32 devices in a mesh: dp: 4 (over y, core), tile: 8 (over z, x).
Axes of the slice: x: 2, y: 2, z: 4, core: 2. Of those that a mesh axis runs over, the one named last changes fastest.
Arguments:
- inputs: bfloat16 [8, 64, 128, 256], P('dp', None, 'tile'), may hold values from -6 to 6
- cotangent: bfloat16 [8, 64, 128, 256], P('dp', None, 'tile'), may hold values from -6 to 6
- mode_weight: bfloat16 [64, 64, 64, 128], P('tile'), may hold values from -0.5 to 0.5
- local_weight: bfloat16 [64, 64], replicated, may hold values from -0.75 to 0.75
Outputs:
- input_grad: bfloat16 [8, 64, 128, 256], P('dp', None, 'tile')
- mode_grad: float32 [64, 64, 64, 128], P('tile')
- local_grad: float32 [64, 64], replicated
The draws below stay inside these ranges and needn't reach their ends.
All inputs are finite; a program needn't handle non-finite values.
Results may differ from the reference program's by a relative error of at most 0.015.
Values may be sent and summed in bfloat16 or wider, within the bound.
No kernel may reach another device: no remote copies, remote signals or barrier semaphores. Data moves between devices by JAX's collectives and lax.ppermute only.
A program may use at most 128 MiB of HBM per device.

```python
import math
import jax
import jax.numpy as jnp
from jax import lax

C = 64
M1 = 64
M2 = 64
W = 256
TH = 16
H = 128
SAMPLES = 8
N_TILE = 8


def shard_levels(key, extent, split, least, top_value):
    factor_of = 1.0
    for position, parts in split:
        draws = jax.random.uniform(jax.random.fold_in(jax.random.fold_in(key, 6), position), (parts,), jnp.float32, least / len(split), top_value / len(split))
        factor_of = factor_of * jnp.repeat(jnp.exp(draws), extent[position] // parts).reshape((-1,) + (1,) * (len(extent) - 1 - position))
    return factor_of


def normal_values(rng, extent, scale, reach, shards=(), kind=jnp.bfloat16):
    gain = shard_levels(rng, extent, shards, -0.22, 0.18) if shards else 1.0
    drawn = jax.random.normal(rng, extent, jnp.float32) * scale * gain
    return jnp.minimum(jnp.maximum(drawn, -reach), reach).astype(kind)


def setup_inputs(seed: int = 0) -> dict:
    keys = jax.random.split(jax.random.key(seed), 5)
    inputs = normal_values(keys[0], (SAMPLES, C, H, W), 1.0, 6.0, ((0, 4), (2, 8)))
    cotangent = normal_values(keys[1], (SAMPLES, C, H, W), 1.0, 6.0, ((0, 4), (2, 8)))
    mode_weight = normal_values(keys[2], (M2, C, C, 2 * M1), (2 * C) ** -0.5, 0.5, ((0, 8),))
    local_weight = normal_values(keys[3], (C, C), C ** -0.5, 0.75)
    return {"inputs": inputs, "cotangent": cotangent, "mode_weight": mode_weight, "local_weight": local_weight}


def row_tables(positions, length):
    modes = jnp.arange(M1, dtype=jnp.int32)
    signed = jnp.where(modes < M1 // 2, modes, modes - M1).astype(jnp.int32)
    phases = jnp.mod(positions[:, None] * signed[None, :], length).astype(jnp.int32)
    angles = phases.astype(jnp.float32) * (2.0 * math.pi / length)
    return jnp.concatenate([jnp.cos(angles), jnp.sin(angles)], axis=1).astype(jnp.bfloat16)

def column_tables():
    modes = jnp.arange(M2, dtype=jnp.int32)
    pixels = jnp.arange(W, dtype=jnp.int32)
    phases = jnp.mod(modes[:, None] * pixels[None, :], W).astype(jnp.int32)
    angles = phases.astype(jnp.float32) * (2.0 * math.pi / W)
    return jnp.concatenate([jnp.cos(angles), -jnp.sin(angles)], axis=0).astype(jnp.bfloat16)

def inverse_rows(tables):
    cosine = tables[:, :M1]
    sine = tables[:, M1:]
    upper = jnp.concatenate([cosine.T, sine.T], axis=1)
    lower = jnp.concatenate([-sine.T, cosine.T], axis=1)
    return jnp.concatenate([upper, lower], axis=0)

def along_rows(halves, tables):
    mixed = jnp.einsum('pqch,hm->pqcm', halves.astype(jnp.float32), tables.astype(jnp.float32))
    real_part = mixed[0]
    imag_part = mixed[1]
    return jnp.concatenate([real_part[..., :M1] + imag_part[..., M1:], imag_part[..., :M1] - real_part[..., M1:]], axis=-1)

def mix_forward(spectra, weights):
    real_in, imag_in = (spectra[..., :M1], spectra[..., M1:])
    real_w, imag_w = (weights[..., :M1], weights[..., M1:])
    real_out = jnp.einsum('qck,qcok->qok', real_in, real_w) - jnp.einsum('qck,qcok->qok', imag_in, imag_w)
    imag_out = jnp.einsum('qck,qcok->qok', real_in, imag_w) + jnp.einsum('qck,qcok->qok', imag_in, real_w)
    return jnp.concatenate([real_out, imag_out], axis=-1)

def mix_backward(grads, weights):
    real_g, imag_g = (grads[..., :M1], grads[..., M1:])
    real_w, imag_w = (weights[..., :M1], weights[..., M1:])
    real_out = jnp.einsum('qok,qcok->qck', real_g, real_w) + jnp.einsum('qok,qcok->qck', imag_g, imag_w)
    imag_out = jnp.einsum('qok,qcok->qck', imag_g, real_w) - jnp.einsum('qok,qcok->qck', real_g, imag_w)
    return jnp.concatenate([real_out, imag_out], axis=-1)

def weight_term(spectra, grads):
    real_in, imag_in = (spectra[..., :M1], spectra[..., M1:])
    real_g, imag_g = (grads[..., :M1], grads[..., M1:])
    real_out = jnp.einsum('qck,qok->qcok', real_in, real_g) + jnp.einsum('qck,qok->qcok', imag_in, imag_g)
    imag_out = jnp.einsum('qck,qok->qcok', real_in, imag_g) - jnp.einsum('qck,qok->qcok', imag_in, real_g)
    return jnp.concatenate([real_out, imag_out], axis=-1)

def gelu_slope(values):
    cumulative = 0.5 * (1.0 + jax.scipy.special.erf(values / math.sqrt(2.0)))
    density = jnp.exp(-0.5 * values * values) / math.sqrt(2.0 * math.pi)
    return cumulative + values * density

def reference(inputs, cotangent, mode_weight, local_weight):
    height = TH * N_TILE
    spec_scale = 1.0 / math.sqrt(height * W)
    mode_scale = 1.0 / math.sqrt(M1 * M2)
    rows_table = row_tables(jnp.arange(height, dtype=jnp.int32), height)
    back_table = inverse_rows(rows_table).astype(jnp.float32)
    col_table = column_tables().astype(jnp.float32)
    col_three = col_table.reshape(2, M2, W)
    weights = mode_weight.astype(jnp.float32)
    local = local_weight.astype(jnp.float32)

    def to_modes(fields, scale):
        halves = jnp.einsum('qw,chw->qch', col_table, fields.astype(jnp.float32)).astype(jnp.bfloat16)
        halves = halves.reshape(2, M2, C, height)
        return (scale * along_rows(halves, rows_table)).astype(jnp.bfloat16)

    def to_pixels(spectra, scale):
        inner = jnp.einsum('qom,mj->qoj', spectra.astype(jnp.float32), back_table).astype(jnp.bfloat16)
        inner = inner.reshape(M2, C, 2, height).astype(jnp.float32)
        return scale * jnp.einsum('qoph,pqw->ohw', inner, col_three)

    def one_sample(carry, pair):
        mode_sum, local_sum = carry
        fields, grads = pair
        fields32 = fields.astype(jnp.float32)
        spectra = to_modes(fields, spec_scale)
        outputs = mix_forward(spectra.astype(jnp.float32), weights).astype(jnp.bfloat16)
        pre = to_pixels(outputs, mode_scale) + jnp.einsum('co,chw->ohw', local, fields32)
        gate_grad = (grads.astype(jnp.float32) * gelu_slope(pre)).astype(jnp.bfloat16)
        gate32 = gate_grad.astype(jnp.float32)
        local_sum = local_sum + jnp.einsum('chw,ohw->co', fields32, gate32)
        back_local = jnp.einsum('co,ohw->chw', local, gate32)
        out_grad = to_modes(gate_grad, mode_scale)
        in_grad = mix_backward(out_grad.astype(jnp.float32), weights).astype(jnp.bfloat16)
        mode_sum = mode_sum + weight_term(spectra.astype(jnp.float32), out_grad.astype(jnp.float32))
        result = (to_pixels(in_grad, spec_scale) + back_local).astype(jnp.bfloat16)
        return ((mode_sum, local_sum), result)
    start = (jnp.zeros((M2, C, C, 2 * M1), jnp.float32), jnp.zeros((C, C), jnp.float32))
    (mode_grad, local_grad), input_grad = lax.scan(one_sample, start, (inputs, cotangent))
    return (input_grad, mode_grad, local_grad)
```

```python
import math

import jax
import jax.numpy as jnp
import numpy as np
from jax import lax
from jax.experimental import pallas as pl
from jax.experimental.pallas import tpu as pltpu
from jax.sharding import PartitionSpec as P

F32 = jnp.float32
BF16 = jnp.bfloat16
LIMIT = 56 * 1024 * 1024


def row_tables(height, modes):
    index = np.arange(modes)
    signed = np.where(index < modes // 2, index, index - modes)
    phases = np.mod(np.arange(height)[:, None] * signed[None, :], height)
    angles = phases * (2.0 * math.pi / height)
    return np.cos(angles), np.sin(angles)


def column_tables(width, modes):
    phases = np.mod(np.arange(modes)[:, None] * np.arange(width)[None, :], width)
    angles = phases * (2.0 * math.pi / width)
    return np.stack([np.cos(angles), -np.sin(angles)])


def constant(table):
    return jnp.asarray(np.asarray(table, np.float32)).astype(BF16)


def tables(tiles, owned, th, width, modes):
    cols = column_tables(width, tiles * owned)
    split = cols.reshape(2, tiles, owned, width)
    send_cols = split.transpose(1, 0, 2, 3).reshape(-1, width)
    back_cols = split.transpose(2, 1, 0, 3).reshape(-1, width)
    cosine, sine = row_tables(th * tiles, modes)
    real = np.concatenate([cosine, -sine], axis=1)
    imag = np.concatenate([sine, cosine], axis=1)
    pair = np.stack([real, imag]).reshape(2, tiles, th, 2 * modes)
    rows = pair.transpose(2, 1, 0, 3).reshape(-1, 2 * modes)
    back_rows = pair.transpose(1, 0, 2, 3).reshape(-1, 2 * modes)
    return constant(send_cols), constant(rows), constant(back_rows), constant(back_cols)


def dot(left, right, dims):
    return lax.dot_general(left, right, (dims, ((), ())), preferred_element_type=F32)


def low_half(shape, half):
    return lax.broadcasted_iota(jnp.int32, shape, 1) < half


def gelu_slope(values):
    size = jnp.abs(values)
    expo = jnp.exp(-0.5 * values * values)
    t = 1.0 / (1.0 + (0.3275911 / math.sqrt(2.0)) * size)
    poly = 0.5 * 1.061405429
    for factor in (-1.453152027, 1.421413741, -0.284496736, 0.254829592):
        poly = poly * t + 0.5 * factor
    tail = poly * t * expo
    cumulative = jnp.where(values < 0.0, tail, 1.0 - tail)
    return cumulative + values * expo * (1.0 / math.sqrt(2.0 * math.pi))


def spread(wide, source, lane_tile):
    for part in range(wide.shape[0]):
        wide[part] = source[:, part * lane_tile : (part + 1) * lane_tile].astype(F32)


def pick(wide, start, count, stride):
    return jnp.concatenate(
        [wide[part, pl.ds(start, count, stride=stride), :] for part in range(wide.shape[0])], axis=1
    ).astype(BF16)


def stack(wide, start, count, stride):
    return jnp.concatenate(
        [wide[part, pl.ds(start, count, stride=stride), :] for part in range(wide.shape[0])], axis=0
    ).astype(BF16)


def columns_kernel(field_ref, table_ref, send_ref, rows_ref, wide):
    heights, lanes, _ = rows_ref.shape
    spread(wide, field_ref, 128)
    for h in range(heights):
        field = pick(wide, h, lanes, heights)
        rows_ref[h] = field
        send_ref[:, h * lanes : (h + 1) * lanes] = dot(table_ref[...], field, ((1,), (1,))).astype(BF16)


def relayout_kernel(field_ref, rows_ref, wide):
    heights, lanes, _ = rows_ref.shape
    spread(wide, field_ref, 128)
    for h in range(heights):
        rows_ref[h] = pick(wide, h, lanes, heights)


def spectrum(recv_ref, rows_ref, wide, scale, owned):
    q = pl.program_id(0)

    @pl.when(q == 0)
    def _():
        spread(wide, recv_ref, wide.shape[2])

    stacked = stack(wide, q, recv_ref.shape[0] // owned, owned)
    return (scale * dot(stacked, rows_ref[...], ((0,), (0,)))).astype(BF16)


def forward_kernel(scale, owned, samples, recv_ref, rows_ref, back_ref, weight_ref, spec_ref, send_ref, wide, real, imag):
    spec = spectrum(recv_ref, rows_ref, wide, scale, owned)
    spec_ref[0] = spec
    channels, outs, both = weight_ref.shape[1:]
    half = both // 2
    value = spec.astype(F32)
    other = pltpu.roll(value, half, 1)
    low = low_half(value.shape, half)
    real[...] = jnp.where(low, value, other)
    imag[...] = jnp.where(low, other, value)
    unroll = 8

    def body(block, carry):
        sums = list(carry)
        for step in range(unroll):
            c = block * unroll + step
            weight = weight_ref[0, c].astype(F32)
            for s in range(samples):
                sums[2 * s] = sums[2 * s] + weight * real[pl.ds(s * channels + c, 1), :]
                sums[2 * s + 1] = sums[2 * s + 1] + weight * imag[pl.ds(s * channels + c, 1), :]
        return tuple(sums)

    zero = jnp.zeros((outs, both), F32)
    sums = lax.fori_loop(0, channels // unroll, body, (zero,) * (2 * samples))
    low = low_half((outs, both), half)
    mixed = []
    for s in range(samples):
        crossed = pltpu.roll(sums[2 * s + 1], half, 1)
        mixed.append(sums[2 * s] + jnp.where(low, -crossed, crossed))
    mixed = jnp.concatenate(mixed, axis=0).astype(BF16)
    send_ref[...] = dot(back_ref[...], mixed, ((1,), (1,))).astype(BF16)


def backward_kernel(scale, owned, samples, recv_ref, rows_ref, back_ref, weight_ref, spec_ref, send_ref, wide, real, imag):
    spec = spectrum(recv_ref, rows_ref, wide, scale, owned)
    spec_ref[0] = spec
    channels, outs, both = weight_ref.shape[1:]
    half = both // 2
    value = spec.astype(F32)
    other = pltpu.roll(value, half, 1)
    low = low_half(value.shape, half)
    grads = (jnp.where(low, value, other), jnp.where(low, other, value))
    unroll = 8

    def body(block, carry):
        for step in range(unroll):
            c = block * unroll + step
            weight = weight_ref[0, c].astype(F32)
            for s in range(samples):
                for grad, store in zip(grads, (real, imag)):
                    product = weight * grad[s * outs : (s + 1) * outs]
                    store[pl.ds(s * channels + c, 1), :] = jnp.sum(product, axis=0, keepdims=True)
        return carry

    lax.fori_loop(0, channels // unroll, body, 0)
    straight = real[...]
    crossed = pltpu.roll(imag[...], half, 1)
    mixed = (jnp.where(low, straight, -straight) + crossed).astype(BF16)
    send_ref[...] = dot(back_ref[...], mixed, ((1,), (1,))).astype(BF16)


def pixels_kernel(scale, recv_ref, back_ref, local_ref, field_ref, cot_ref, table_ref, grad_ref, send_ref, wide):
    heights, lanes, _ = field_ref.shape
    spread(wide, recv_ref, wide.shape[2])
    count = recv_ref.shape[0] // heights
    for h in range(heights):
        inner = stack(wide, h, count, heights)
        pre = scale * dot(inner, back_ref[...], ((0,), (0,)))
        pre = pre + dot(local_ref[...], field_ref[h], ((1,), (0,)))
        grad = (cot_ref[h].astype(F32) * gelu_slope(pre)).astype(BF16)
        grad_ref[h] = grad
        send_ref[:, h * lanes : (h + 1) * lanes] = dot(table_ref[...], grad, ((1,), (1,))).astype(BF16)


def local_kernel(field_ref, grad_ref, out_ref):
    heights = field_ref.shape[0]
    total = jnp.zeros(out_ref.shape, F32)
    for h in range(heights):
        total = total + dot(field_ref[h], grad_ref[h], ((1,), (1,)))
    out_ref[...] = total


def final_kernel(scale, recv_ref, back_ref, local_ref, grad_ref, out_ref, wide, result):
    heights, lanes, width = grad_ref.shape
    spread(wide, recv_ref, wide.shape[2])
    count = recv_ref.shape[0] // heights
    for h in range(heights):
        inner = stack(wide, h, count, heights)
        value = scale * dot(inner, back_ref[...], ((0,), (0,)))
        value = value + dot(local_ref[...], grad_ref[h], ((1,), (0,)))
        for part in range(result.shape[0]):
            result[part, pl.ds(h, lanes, stride=heights), :] = value[:, part * 128 : (part + 1) * 128]
    for part in range(result.shape[0]):
        out_ref[:, part * 128 : (part + 1) * 128] = result[part].astype(BF16)


def outer_kernel(samples, spec_ref, grad_ref, out_ref, real, imag, plain, crossed):
    groups = spec_ref.shape[0]
    channels, outs, both = out_ref.shape[1:]
    half = both // 2
    low = low_half((channels, both), half)
    for g in range(groups):
        for s in range(samples):
            n = g * samples + s
            spec = spec_ref[g, 0, s * channels : (s + 1) * channels, :].astype(F32)
            other = pltpu.roll(spec, half, 1)
            real[n] = jnp.where(low, spec, other)
            imag[n] = jnp.where(low, other, -spec)
            grad = grad_ref[g, 0, s * outs : (s + 1) * outs, :]
            plain[n] = grad
            crossed[n] = pltpu.roll(grad.astype(F32), half, 1).astype(BF16)
    total = groups * samples
    tile = 16

    def body(c, carry):
        left = []
        for n in range(total):
            for store in (real, imag):
                row = jnp.broadcast_to(store[n, pl.ds(c, 1), :], (tile, both))
                left.append(row.astype(BF16))
        for o in range(0, outs, tile):
            terms = []
            for n in range(total):
                terms.append(left[2 * n] * plain[n, o : o + tile, :])
                terms.append(left[2 * n + 1] * crossed[n, o : o + tile, :])
            while len(terms) > 2:
                terms = [a + b for a, b in zip(terms[0::2], terms[1::2])]
            out_ref[0, c, o : o + tile, :] = terms[0].astype(F32) + terms[1].astype(F32)
        return carry

    lax.fori_loop(0, channels, body, 0, unroll=2)


def call(kernel, outs, scratch, name, grid=None, in_specs=None, out_specs=None):
    extra = {}
    if grid is not None:
        extra = dict(grid=grid, in_specs=in_specs, out_specs=out_specs)
    return pl.pallas_call(
        kernel,
        out_shape=outs,
        scratch_shapes=scratch,
        compiler_params=pltpu.CompilerParams(vmem_limit_bytes=LIMIT),
        name=name,
        **extra,
    )


def block_diagonal(matrix, copies):
    zero = jnp.zeros_like(matrix)
    return jnp.concatenate(
        [
            jnp.concatenate([matrix if i == j else zero for j in range(copies)], axis=1)
            for i in range(copies)
        ],
        axis=0,
    )


def sum_over(values, axis):
    size = lax.axis_size(axis)
    step = 1
    while step < size:
        values = values + lax.ppermute(values, axis, [(i, i ^ step) for i in range(size)])
        step *= 2
    return values


def shape(extent, kind=BF16):
    return jax.ShapeDtypeStruct(extent, kind)


def local(inputs, cotangent, mode_weight, local_weight):
    tiles = lax.axis_size("tile")
    samples, channels, th, width = inputs.shape
    owned, _, _, both = mode_weight.shape
    modes = both // 2
    lanes = samples * channels
    parts = width // 128
    spec_scale = 1.0 / math.sqrt(tiles * th * width)
    mode_scale = 1.0 / math.sqrt(modes * tiles * owned)
    send_cols, rows, back_rows, back_cols = tables(tiles, owned, th, width, modes)
    pixel_rows = samples * channels * th
    halves = 2 * tiles * owned
    inverse = 2 * tiles * th

    def exchange(values):
        split = values.reshape(tiles, values.shape[0] // tiles, values.shape[1])
        moved = lax.all_to_all(split, "tile", split_axis=0, concat_axis=0, tiled=False)
        return moved.reshape(values.shape)

    forward_mix = block_diagonal(local_weight.T, samples)
    backward_mix = block_diagonal(local_weight, samples)
    pixel_scratch = pltpu.VMEM((parts, pixel_rows, 128), F32)

    send, field_rows = call(
        columns_kernel,
        (shape((halves, th * lanes)), shape((th, lanes, width))),
        [pixel_scratch],
        "columns",
    )(inputs.reshape(pixel_rows, width), send_cols)
    halves_in = exchange(send)
    cot_rows = call(relayout_kernel, shape((th, lanes, width)), [pixel_scratch], "relayout")(
        cotangent.reshape(pixel_rows, width)
    )

    def mode_call(kernel, name, scale, recv):
        def body(*refs):
            kernel(scale, owned, samples, *refs)

        whole = lambda extent: pl.BlockSpec(extent, lambda q: (0, 0))
        return call(
            body,
            (shape((owned, lanes, both)), shape((inverse, owned * lanes))),
            [
                pltpu.VMEM((th, halves, lanes), F32),
                pltpu.VMEM((lanes, both), F32),
                pltpu.VMEM((lanes, both), F32),
            ],
            name,
            grid=(owned,),
            in_specs=[
                whole(recv.shape),
                whole(rows.shape),
                whole(back_rows.shape),
                pl.BlockSpec((1,) + mode_weight.shape[1:], lambda q: (q, 0, 0, 0)),
            ],
            out_specs=(
                pl.BlockSpec((1, lanes, both), lambda q: (q, 0, 0)),
                pl.BlockSpec((inverse, lanes), lambda q: (0, q)),
            ),
        )(recv, rows, back_rows, mode_weight)

    spectra, send = mode_call(forward_kernel, "mix_forward", spec_scale, halves_in)
    inner = exchange(send)
    all_spectra = lax.all_gather(spectra, "dp")

    inverse_scratch = pltpu.VMEM((owned, inverse, lanes), F32)

    def pixel_body(*refs):
        pixels_kernel(mode_scale, *refs)

    gate_rows, send = call(
        pixel_body,
        (shape((th, lanes, width)), shape((halves, th * lanes))),
        [inverse_scratch],
        "pixels",
    )(inner, back_cols, forward_mix, field_rows, cot_rows, send_cols)
    halves_out = exchange(send)
    local_pairs = call(local_kernel, shape((lanes, lanes), F32), [], "local_grad")(field_rows, gate_rows)
    local_sum = sum(
        local_pairs[s * channels : (s + 1) * channels, s * channels : (s + 1) * channels]
        for s in range(samples)
    )
    local_grad = sum_over(sum_over(local_sum, "dp"), "tile")

    grad_spectra, send = mode_call(backward_kernel, "mix_backward", mode_scale, halves_out)
    all_grads = lax.all_gather(grad_spectra, "dp")
    inner = exchange(send)

    def outer_body(*refs):
        outer_kernel(samples, *refs)

    groups = lax.axis_size("dp")
    total = groups * samples
    gathered = pl.BlockSpec((groups, 1, lanes, both), lambda q: (0, q, 0, 0))
    mode_grad = call(
        outer_body,
        shape(mode_weight.shape, F32),
        [pltpu.VMEM((total, channels, both), F32)] * 2 + [pltpu.VMEM((total, channels, both), BF16)] * 2,
        "mode_grad",
        grid=(owned,),
        in_specs=[gathered, gathered],
        out_specs=pl.BlockSpec((1,) + mode_weight.shape[1:], lambda q: (q, 0, 0, 0)),
    )(all_spectra, all_grads)

    def final_body(*refs):
        final_kernel(spec_scale, *refs)

    input_grad = call(
        final_body,
        shape((pixel_rows, width)),
        [inverse_scratch, pixel_scratch],
        "final",
    )(inner, back_cols, backward_mix, gate_rows).reshape(inputs.shape)
    return (input_grad, mode_grad, local_grad)


def solution(mesh):
    return jax.shard_map(
        local,
        mesh=mesh,
        in_specs=(
            P("dp", None, "tile", None),
            P("dp", None, "tile", None),
            P("tile", None, None, None),
            P(),
        ),
        out_specs=(P("dp", None, "tile", None), P("tile", None, None, None), P()),
        check_vma=False,
    )
```

```python
import math

import jax
import jax.numpy as jnp
import numpy as np
from jax import lax
from jax.experimental import pallas as pl
from jax.experimental.pallas import tpu as pltpu
from jax.sharding import PartitionSpec as P

F32 = jnp.float32
BF16 = jnp.bfloat16
LIMIT = 56 * 1024 * 1024
PACK = 16
GROUP = 8


def row_tables(height, modes):
    index = np.arange(modes)
    signed = np.where(index < modes // 2, index, index - modes)
    phases = np.mod(np.arange(height)[:, None] * signed[None, :], height)
    angles = phases * (2.0 * math.pi / height)
    return np.cos(angles), np.sin(angles)


def column_tables(width, modes):
    phases = np.mod(np.arange(modes)[:, None] * np.arange(width)[None, :], width)
    angles = phases * (2.0 * math.pi / width)
    return np.stack([np.cos(angles), -np.sin(angles)])


def constant(table):
    return jnp.asarray(np.asarray(table, np.float32)).astype(BF16)


def tables(tiles, owned, th, width, modes):
    cols = column_tables(width, tiles * owned)
    split = cols.reshape(2, tiles, owned, width)
    send_cols = split.transpose(1, 0, 2, 3).reshape(-1, width)
    back_cols = split.transpose(2, 1, 0, 3).reshape(-1, width)
    cosine, sine = row_tables(th * tiles, modes)
    real = np.concatenate([cosine, -sine], axis=1)
    imag = np.concatenate([sine, cosine], axis=1)
    pair = np.stack([real, imag]).reshape(2, tiles, th, 2 * modes)
    rows = pair.transpose(2, 1, 0, 3).reshape(-1, 2 * modes)
    back_rows = pair.transpose(1, 0, 2, 3).reshape(-1, 2 * modes)
    return constant(send_cols), constant(rows), constant(back_rows), constant(back_cols)


def dot(left, right, dims):
    return lax.dot_general(left, right, (dims, ((), ())), preferred_element_type=F32)


def low_half(shape, half):
    return lax.broadcasted_iota(jnp.int32, shape, 1) < half


def gelu_slope(values):
    size = jnp.abs(values)
    expo = jnp.exp(-0.5 * values * values)
    t = 1.0 / (1.0 + (0.3275911 / math.sqrt(2.0)) * size)
    poly = 0.5 * 1.061405429
    for factor in (-1.453152027, 1.421413741, -0.284496736, 0.254829592):
        poly = poly * t + 0.5 * factor
    tail = poly * t * expo
    cumulative = jnp.where(values < 0.0, tail, 1.0 - tail)
    return cumulative + values * expo * (1.0 / math.sqrt(2.0 * math.pi))


def spread(wide, source, lane_tile):
    for part in range(wide.shape[0]):
        wide[part] = source[:, part * lane_tile : (part + 1) * lane_tile].astype(F32)


def pick(wide, start, count, stride):
    return jnp.concatenate(
        [wide[part, pl.ds(start, count, stride=stride), :] for part in range(wide.shape[0])], axis=1
    ).astype(BF16)


def stack(wide, start, count, stride):
    return jnp.concatenate(
        [wide[part, pl.ds(start, count, stride=stride), :] for part in range(wide.shape[0])], axis=0
    ).astype(BF16)


def columns_kernel(field_ref, table_ref, send_ref, rows_ref, wide):
    heights, lanes, _ = rows_ref.shape
    spread(wide, field_ref, 128)
    for h in range(heights):
        field = pick(wide, h, lanes, heights)
        rows_ref[h] = field
        send_ref[:, h * lanes : (h + 1) * lanes] = dot(table_ref[...], field, ((1,), (1,))).astype(BF16)


def relayout_kernel(field_ref, rows_ref, wide):
    heights, lanes, _ = rows_ref.shape
    spread(wide, field_ref, 128)
    for h in range(heights):
        rows_ref[h] = pick(wide, h, lanes, heights)


def spectra_kernel(scale, recv_ref, rows_ref, spec_ref, wide):
    owned = spec_ref.shape[0]
    spread(wide, recv_ref, wide.shape[2])
    for q in range(owned):
        stacked = stack(wide, q, recv_ref.shape[0] // owned, owned)
        spec_ref[q] = (scale * dot(stacked, rows_ref[...], ((0,), (0,)))).astype(BF16)


def tree(terms):
    while len(terms) > 1:
        terms = [a + b for a, b in zip(terms[0::2], terms[1::2])]
    return terms[0]


def packed_row(store, index):
    row = store[pl.ds(index, 1), :]
    return jnp.broadcast_to(row, (PACK, row.shape[1])).astype(BF16)


def send_inverse(back_ref, mixed, send_ref):
    @pl.when(pl.program_id(0) == pl.num_programs(0) - 1)
    def _():
        owned, lanes, _ = mixed.shape
        for q in range(owned):
            send_ref[:, q * lanes : (q + 1) * lanes] = dot(back_ref[...], mixed[q], ((1,), (1,))).astype(BF16)


def forward_kernel(samples, spec_ref, back_ref, adder_ref, weight_ref, send_ref, mixed, sums, real, imag):
    channels, outs, both = weight_ref.shape[1:]
    half = both // 2
    value = spec_ref[0].astype(F32)
    other = pltpu.roll(value, half, 1)
    low = low_half(value.shape, half)
    real[...] = jnp.where(low, value, other)
    imag[...] = jnp.where(low, other, value)

    def body(block, carry):
        first = block * GROUP
        rows = [
            [packed_row(store, s * channels + first + step) for step in range(GROUP)]
            for s in range(samples)
            for store in (real, imag)
        ]
        for o in range(0, outs, PACK):
            weights = [weight_ref[0, first + step, o : o + PACK, :] for step in range(GROUP)]
            for n, row in enumerate(rows):
                total = tree([w * r for w, r in zip(weights, row)])
                sums[n, pl.ds(pl.multiple_of(block * outs + o, PACK), PACK), :] = total
        return carry

    lax.fori_loop(0, channels // GROUP, body, 0)
    low = low_half((outs, both), half)
    result = []
    for s in range(samples):
        straight = dot(adder_ref[...], sums[2 * s], ((1,), (0,)))
        crossed = pltpu.roll(dot(adder_ref[...], sums[2 * s + 1], ((1,), (0,))), half, 1)
        result.append(straight + jnp.where(low, -crossed, crossed))
    mixed[pl.program_id(0)] = jnp.concatenate(result, axis=0).astype(BF16)
    send_inverse(back_ref, mixed, send_ref)


def backward_kernel(samples, spec_ref, back_ref, adder_ref, weight_ref, send_ref, mixed, sums, real, imag):
    channels, outs, both = weight_ref.shape[1:]
    half = both // 2
    value = spec_ref[0].astype(F32)
    other = pltpu.roll(value, half, 1)
    low = low_half(value.shape, half)
    real[...] = jnp.where(low, value, other)
    imag[...] = jnp.where(low, other, value)
    grads = [
        [store[s * outs + o : s * outs + o + PACK, :].astype(BF16) for o in range(0, outs, PACK)]
        for s in range(samples)
        for store in (real, imag)
    ]

    def body(block, carry):
        for step in range(GROUP):
            c = block * GROUP + step
            weights = [weight_ref[0, c, o : o + PACK, :] for o in range(0, outs, PACK)]
            for n, grad in enumerate(grads):
                total = tree([w * g for w, g in zip(weights, grad)])
                sums[n, pl.ds(pl.multiple_of(c * PACK, PACK), PACK), :] = total
        return carry

    lax.fori_loop(0, channels // GROUP, body, 0)
    low = low_half((channels, both), half)
    result = []
    for s in range(samples):
        straight = dot(adder_ref[...], sums[2 * s], ((1,), (0,)))
        crossed = pltpu.roll(dot(adder_ref[...], sums[2 * s + 1], ((1,), (0,))), half, 1)
        result.append(jnp.where(low, straight, -straight) + crossed)
    mixed[pl.program_id(0)] = jnp.concatenate(result, axis=0).astype(BF16)
    send_inverse(back_ref, mixed, send_ref)


def pixels_kernel(scale, recv_ref, back_ref, local_ref, field_ref, cot_ref, table_ref, grad_ref, send_ref, wide):
    heights, lanes, _ = field_ref.shape
    spread(wide, recv_ref, wide.shape[2])
    count = recv_ref.shape[0] // heights
    for h in range(heights):
        inner = stack(wide, h, count, heights)
        pre = scale * dot(inner, back_ref[...], ((0,), (0,)))
        pre = pre + dot(local_ref[...], field_ref[h], ((1,), (0,)))
        grad = (cot_ref[h].astype(F32) * gelu_slope(pre)).astype(BF16)
        grad_ref[h] = grad
        send_ref[:, h * lanes : (h + 1) * lanes] = dot(table_ref[...], grad, ((1,), (1,))).astype(BF16)


def local_kernel(field_ref, grad_ref, out_ref):
    heights = field_ref.shape[0]
    total = jnp.zeros(out_ref.shape, F32)
    for h in range(heights):
        total = total + dot(field_ref[h], grad_ref[h], ((1,), (1,)))
    out_ref[...] = total


def final_kernel(scale, recv_ref, back_ref, local_ref, grad_ref, out_ref, wide, result):
    heights, lanes, width = grad_ref.shape
    spread(wide, recv_ref, wide.shape[2])
    count = recv_ref.shape[0] // heights
    for h in range(heights):
        inner = stack(wide, h, count, heights)
        value = scale * dot(inner, back_ref[...], ((0,), (0,)))
        value = value + dot(local_ref[...], grad_ref[h], ((1,), (0,)))
        for part in range(result.shape[0]):
            result[part, pl.ds(h, lanes, stride=heights), :] = value[:, part * 128 : (part + 1) * 128]
    for part in range(result.shape[0]):
        out_ref[:, part * 128 : (part + 1) * 128] = result[part].astype(BF16)


def outer_kernel(samples, spec_ref, grad_ref, out_ref, real, imag, plain, crossed):
    groups = spec_ref.shape[0]
    channels, outs, both = out_ref.shape[1:]
    half = both // 2
    low = low_half((channels, both), half)
    for g in range(groups):
        for s in range(samples):
            n = g * samples + s
            spec = spec_ref[g, 0, s * channels : (s + 1) * channels, :].astype(F32)
            other = pltpu.roll(spec, half, 1)
            real[n] = jnp.where(low, spec, other)
            imag[n] = jnp.where(low, other, -spec)
            grad = grad_ref[g, 0, s * outs : (s + 1) * outs, :]
            plain[n] = grad
            crossed[n] = pltpu.roll(grad.astype(F32), half, 1).astype(BF16)
    total = groups * samples
    pair = 2 * PACK

    for o in range(0, outs, pair):
        tiles = range(o, o + pair, PACK)
        right = [
            [store[n, t : t + PACK, :] for n in range(total) for store in (plain, crossed)] for t in tiles
        ]

        def body(c, carry):
            left = [packed_row(store.at[n], c) for n in range(total) for store in (real, imag)]
            for t, column in zip(tiles, right):
                terms = [a * b for a, b in zip(left, column)]
                middle = len(terms) // 2
                total_sum = tree(terms[:middle]).astype(F32) + tree(terms[middle:]).astype(F32)
                out_ref[0, c, t : t + PACK, :] = total_sum
            return carry

        lax.fori_loop(0, channels, body, 0, unroll=2)


def call(kernel, outs, scratch, name, grid=None, in_specs=None, out_specs=None):
    extra = {}
    if grid is not None:
        extra = dict(grid=grid, in_specs=in_specs, out_specs=out_specs)
    return pl.pallas_call(
        kernel,
        out_shape=outs,
        scratch_shapes=scratch,
        compiler_params=pltpu.CompilerParams(vmem_limit_bytes=LIMIT),
        name=name,
        **extra,
    )


def block_diagonal(matrix, copies):
    zero = jnp.zeros_like(matrix)
    return jnp.concatenate(
        [
            jnp.concatenate([matrix if i == j else zero for j in range(copies)], axis=1)
            for i in range(copies)
        ],
        axis=0,
    )


def shape(extent, kind=BF16):
    return jax.ShapeDtypeStruct(extent, kind)


def local(inputs, cotangent, mode_weight, local_weight):
    tiles = lax.axis_size("tile")
    samples, channels, th, width = inputs.shape
    owned, _, _, both = mode_weight.shape
    modes = both // 2
    lanes = samples * channels
    parts = width // 128
    spec_scale = 1.0 / math.sqrt(tiles * th * width)
    mode_scale = 1.0 / math.sqrt(modes * tiles * owned)
    send_cols, rows, back_rows, back_cols = tables(tiles, owned, th, width, modes)
    pixel_rows = samples * channels * th
    halves = 2 * tiles * owned
    inverse = 2 * tiles * th

    def exchange(values):
        split = values.reshape(tiles, values.shape[0] // tiles, values.shape[1])
        moved = lax.all_to_all(split, "tile", split_axis=0, concat_axis=0, tiled=False)
        return moved.reshape(values.shape)

    forward_mix = block_diagonal(local_weight.T, samples)
    backward_mix = block_diagonal(local_weight, samples)
    pixel_scratch = pltpu.VMEM((parts, pixel_rows, 128), F32)

    send, field_rows = call(
        columns_kernel,
        (shape((halves, th * lanes)), shape((th, lanes, width))),
        [pixel_scratch],
        "columns",
    )(inputs.reshape(pixel_rows, width), send_cols)
    halves_in = exchange(send)
    cot_rows = call(relayout_kernel, shape((th, lanes, width)), [pixel_scratch], "relayout")(
        cotangent.reshape(pixel_rows, width)
    )

    def spectra_call(name, scale, recv):
        def body(*refs):
            spectra_kernel(scale, *refs)

        return call(
            body, shape((owned, lanes, both)), [pltpu.VMEM((th, halves, lanes), F32)], name
        )(recv, rows)

    def mix_call(kernel, name, spec, adder):
        def body(*refs):
            kernel(samples, *refs)

        whole = lambda extent: pl.BlockSpec(extent, lambda q: (0, 0))
        return call(
            body,
            shape((inverse, owned * lanes)),
            [
                pltpu.VMEM((owned, lanes, both), BF16),
                pltpu.VMEM((2 * samples, adder.shape[1], both), BF16),
                pltpu.VMEM((lanes, both), F32),
                pltpu.VMEM((lanes, both), F32),
            ],
            name,
            grid=(owned,),
            in_specs=[
                pl.BlockSpec((1, lanes, both), lambda q: (q, 0, 0)),
                whole(back_rows.shape),
                whole(adder.shape),
                pl.BlockSpec((1,) + mode_weight.shape[1:], lambda q: (q, 0, 0, 0)),
            ],
            out_specs=whole((inverse, owned * lanes)),
        )(spec, back_rows, adder, mode_weight)

    forward_adder = constant(np.tile(np.eye(channels), (1, channels // GROUP)))
    backward_adder = constant(np.repeat(np.eye(channels), PACK, axis=1))
    spectra = spectra_call("spectra", spec_scale, halves_in)
    all_spectra = lax.all_gather(spectra, "dp")
    inner = exchange(mix_call(forward_kernel, "mix_forward", spectra, forward_adder))

    inverse_scratch = pltpu.VMEM((owned, inverse, lanes), F32)

    def pixel_body(*refs):
        pixels_kernel(mode_scale, *refs)

    gate_rows, send = call(
        pixel_body,
        (shape((th, lanes, width)), shape((halves, th * lanes))),
        [inverse_scratch],
        "pixels",
    )(inner, back_cols, forward_mix, field_rows, cot_rows, send_cols)
    halves_out = exchange(send)
    local_pairs = call(local_kernel, shape((lanes, lanes), F32), [], "local_grad")(field_rows, gate_rows)
    local_sum = sum(
        local_pairs[s * channels : (s + 1) * channels, s * channels : (s + 1) * channels]
        for s in range(samples)
    )
    local_grad = jnp.sum(lax.all_gather(local_sum, ("dp", "tile")), axis=0)

    grad_spectra = spectra_call("grad_spectra", mode_scale, halves_out)
    all_grads = lax.all_gather(grad_spectra, "dp")
    inner = exchange(mix_call(backward_kernel, "mix_backward", grad_spectra, backward_adder))

    def outer_body(*refs):
        outer_kernel(samples, *refs)

    groups = lax.axis_size("dp")
    total = groups * samples
    gathered = pl.BlockSpec((groups, 1, lanes, both), lambda q: (0, q, 0, 0))
    mode_grad = call(
        outer_body,
        shape(mode_weight.shape, F32),
        [pltpu.VMEM((total, channels, both), F32)] * 2 + [pltpu.VMEM((total, channels, both), BF16)] * 2,
        "mode_grad",
        grid=(owned,),
        in_specs=[gathered, gathered],
        out_specs=pl.BlockSpec((1,) + mode_weight.shape[1:], lambda q: (q, 0, 0, 0)),
    )(all_spectra, all_grads)

    inner, mode_grad = lax.optimization_barrier((inner, mode_grad))

    def final_body(*refs):
        final_kernel(spec_scale, *refs)

    input_grad = call(
        final_body,
        shape((pixel_rows, width)),
        [inverse_scratch, pixel_scratch],
        "final",
    )(inner, back_cols, backward_mix, gate_rows).reshape(inputs.shape)
    return (input_grad, mode_grad, local_grad)


def solution(mesh):
    return jax.shard_map(
        local,
        mesh=mesh,
        in_specs=(
            P("dp", None, "tile", None),
            P("dp", None, "tile", None),
            P("tile", None, None, None),
            P(),
        ),
        out_specs=(P("dp", None, "tile", None), P("tile", None, None, None), P()),
        check_vma=False,
    )
```

```python
import functools
import math

import jax
import jax.numpy as jnp
import numpy as np
from jax import lax
from jax.experimental import pallas as pl
from jax.experimental.pallas import tpu as pltpu
from jax.sharding import PartitionSpec as P

F32 = jnp.float32
BF16 = jnp.bfloat16
LIMIT = 28 * 1024 * 1024
COPIES = 8
PACK = 16
GROUP = 8


def row_tables(height, modes):
    index = np.arange(modes)
    signed = np.where(index < modes // 2, index, index - modes)
    phases = np.mod(np.arange(height)[:, None] * signed[None, :], height)
    angles = phases * (2.0 * math.pi / height)
    return np.cos(angles), np.sin(angles)


def column_tables(width, modes):
    phases = np.mod(np.arange(modes)[:, None] * np.arange(width)[None, :], width)
    angles = phases * (2.0 * math.pi / width)
    return np.stack([np.cos(angles), -np.sin(angles)])


def constant(table):
    return jnp.asarray(np.asarray(table, np.float32)).astype(BF16)


def tables(tiles, owned, th, width, modes):
    cols = column_tables(width, tiles * owned)
    split = cols.reshape(2, tiles, owned, width)
    send_cols = split.transpose(1, 0, 2, 3).reshape(-1, width)
    back_cols = split.transpose(2, 1, 0, 3).reshape(-1, width)
    cosine, sine = row_tables(th * tiles, modes)
    real = np.concatenate([cosine, -sine], axis=1)
    imag = np.concatenate([sine, cosine], axis=1)
    pair = np.stack([real, imag]).reshape(2, tiles, th, 2 * modes)
    rows = pair.transpose(2, 1, 0, 3).reshape(-1, 2 * modes)
    back_rows = pair.transpose(1, 0, 2, 3).reshape(-1, 2 * modes)
    return constant(send_cols), constant(rows), constant(back_rows), constant(back_cols)


def dot(left, right, dims):
    return lax.dot_general(left, right, (dims, ((), ())), preferred_element_type=F32)


def low_half(shape, half):
    return lax.broadcasted_iota(jnp.int32, shape, 1) < half


def gelu_slope(values):
    size = jnp.abs(values)
    expo = jnp.exp(-0.5 * values * values)
    t = 1.0 / (1.0 + (0.3275911 / math.sqrt(2.0)) * size)
    poly = 0.5 * 1.061405429
    for factor in (-1.453152027, 1.421413741, -0.284496736, 0.254829592):
        poly = poly * t + 0.5 * factor
    tail = poly * t * expo
    cumulative = jnp.where(values < 0.0, tail, 1.0 - tail)
    return cumulative + values * expo * (1.0 / math.sqrt(2.0 * math.pi))


def spread(wide, source, lane_tile):
    for part in range(wide.shape[0]):
        wide[part] = source[:, part * lane_tile : (part + 1) * lane_tile].astype(F32)


def pick(wide, start, count, stride):
    return jnp.concatenate(
        [wide[part, pl.ds(start, count, stride=stride), :] for part in range(wide.shape[0])], axis=1
    ).astype(BF16)


def stack(wide, start, count, stride):
    return jnp.concatenate(
        [wide[part, pl.ds(start, count, stride=stride), :] for part in range(wide.shape[0])], axis=0
    ).astype(BF16)


def copies(source, target, sems):
    piece = target.shape[0] // sems.shape[0]
    moves = []
    for n in range(sems.shape[0]):
        part = pl.ds(n * piece, piece)
        moves.append(pltpu.make_async_copy(source.at[part], target.at[part], sems.at[n]))
    return moves


def load_fields(field_ref, buffer, wide, sems):
    moves = copies(field_ref, buffer, sems)
    for move in moves:
        move.start()
    piece = buffer.shape[0] // len(moves)
    for n, move in enumerate(moves):
        move.wait()
        for part in range(wide.shape[0]):
            wide[part, n * piece : (n + 1) * piece, :] = buffer[
                n * piece : (n + 1) * piece, part * 128 : (part + 1) * 128
            ].astype(F32)


def columns_kernel(field_ref, table_ref, send_ref, rows_ref, buffer, wide, sems):
    heights, lanes, _ = rows_ref.shape
    load_fields(field_ref, buffer, wide, sems)
    for h in range(heights):
        field = pick(wide, h, lanes, heights)
        rows_ref[h] = field
        send_ref[:, h * lanes : (h + 1) * lanes] = dot(table_ref[...], field, ((1,), (1,))).astype(BF16)


def relayout_kernel(field_ref, rows_ref, buffer, wide, sems):
    heights, lanes, _ = rows_ref.shape
    load_fields(field_ref, buffer, wide, sems)
    for h in range(heights):
        rows_ref[h] = pick(wide, h, lanes, heights)


def load_kernel(source_ref, target_ref, sems):
    moves = [
        pltpu.make_async_copy(source_ref.at[n], target_ref.at[n], sems.at[n])
        for n in range(source_ref.shape[0])
    ]
    for move in moves:
        move.start()
    for move in moves:
        move.wait()


def spectra_kernel(scale, owned, recv_ref, rows_ref, spec_ref, wide):
    lanes = wide.shape[2]
    spread(wide, recv_ref, lanes)
    for q in range(owned):
        stacked = stack(wide, q, recv_ref.shape[0] // owned, owned)
        spec_ref[q * lanes : (q + 1) * lanes, :] = (
            scale * dot(stacked, rows_ref[...], ((0,), (0,)))
        ).astype(BF16)


def grad_spectra_kernel(scale, owned, recv_ref, rows_ref, local_ref, spec_ref, wide):
    spectra_kernel(scale, owned, recv_ref, rows_ref, spec_ref, wide)
    value = local_ref[...]
    high = value.astype(BF16)
    low = (value - high.astype(F32)).astype(BF16)
    spec_ref[owned * wide.shape[2] :, :] = jnp.concatenate([high, low], axis=1)


def tree(terms):
    while len(terms) > 1:
        terms = [a + b for a, b in zip(terms[0::2], terms[1::2])]
    return terms[0]


def packed_row(store, index):
    row = store[pl.ds(index, 1), :]
    return jnp.broadcast_to(row, (PACK, row.shape[1])).astype(BF16)


def send_inverse(back_ref, mixed, send_ref):
    owned, lanes, _ = mixed.shape
    for q in range(owned):
        send_ref[:, q * lanes : (q + 1) * lanes] = dot(back_ref[...], mixed[q], ((1,), (1,))).astype(BF16)


def duplicate(spec, real, imag, half):
    value = spec.astype(F32)
    other = pltpu.roll(value, half, 1)
    low = low_half(value.shape, half)
    real[...] = jnp.where(low, value, other)
    imag[...] = jnp.where(low, other, value)


def forward_kernel(samples, spec_ref, back_ref, adder_ref, weight_ref, send_ref, mixed, sums, real, imag):
    owned, channels, outs, both = weight_ref.shape
    half = both // 2
    lanes = mixed.shape[1]

    def mode(q, carry):
        duplicate(spec_ref[pl.ds(pl.multiple_of(q * lanes, lanes), lanes), :], real, imag, half)

        def body(block, carry):
            first = block * GROUP
            rows = [
                [packed_row(store, s * channels + first + step) for step in range(GROUP)]
                for s in range(samples)
                for store in (real, imag)
            ]
            for o in range(0, outs, PACK):
                weights = [weight_ref[q, first + step, o : o + PACK, :] for step in range(GROUP)]
                for n, row in enumerate(rows):
                    total = tree([w * r for w, r in zip(weights, row)])
                    sums[n, pl.ds(pl.multiple_of(block * outs + o, PACK), PACK), :] = total
            return carry

        lax.fori_loop(0, channels // GROUP, body, 0)
        low = low_half((outs, both), half)
        result = []
        for s in range(samples):
            straight = dot(adder_ref[...], sums[2 * s], ((1,), (0,)))
            crossed = pltpu.roll(dot(adder_ref[...], sums[2 * s + 1], ((1,), (0,))), half, 1)
            result.append(straight + jnp.where(low, -crossed, crossed))
        mixed[q] = jnp.concatenate(result, axis=0).astype(BF16)
        return carry

    lax.fori_loop(0, owned, mode, 0)
    send_inverse(back_ref, mixed, send_ref)


def backward_kernel(samples, spec_ref, back_ref, adder_ref, weight_ref, send_ref, mixed, sums, real, imag):
    owned, channels, outs, both = weight_ref.shape
    half = both // 2
    lanes = mixed.shape[1]

    def mode(q, carry):
        duplicate(spec_ref[pl.ds(pl.multiple_of(q * lanes, lanes), lanes), :], real, imag, half)
        grads = [
            [store[s * outs + o : s * outs + o + PACK, :].astype(BF16) for o in range(0, outs, PACK)]
            for s in range(samples)
            for store in (real, imag)
        ]

        def body(block, carry):
            for step in range(GROUP):
                c = block * GROUP + step
                weights = [weight_ref[q, c, o : o + PACK, :] for o in range(0, outs, PACK)]
                for n, grad in enumerate(grads):
                    total = tree([w * g for w, g in zip(weights, grad)])
                    sums[n, pl.ds(pl.multiple_of(c * PACK, PACK), PACK), :] = total
            return carry

        lax.fori_loop(0, channels // GROUP, body, 0)
        low = low_half((channels, both), half)
        result = []
        for s in range(samples):
            straight = dot(adder_ref[...], sums[2 * s], ((1,), (0,)))
            crossed = pltpu.roll(dot(adder_ref[...], sums[2 * s + 1], ((1,), (0,))), half, 1)
            result.append(jnp.where(low, straight, -straight) + crossed)
        mixed[q] = jnp.concatenate(result, axis=0).astype(BF16)
        return carry

    lax.fori_loop(0, owned, mode, 0)
    send_inverse(back_ref, mixed, send_ref)


def pixels_kernel(scale, recv_ref, back_ref, local_ref, field_ref, cot_ref, table_ref, grad_ref, send_ref, wide):
    heights, lanes, _ = field_ref.shape
    spread(wide, recv_ref, wide.shape[2])
    count = recv_ref.shape[0] // heights
    for h in range(heights):
        inner = stack(wide, h, count, heights)
        pre = scale * dot(inner, back_ref[...], ((0,), (0,)))
        pre = pre + dot(local_ref[...], field_ref[h], ((1,), (0,)))
        grad = (cot_ref[h].astype(F32) * gelu_slope(pre)).astype(BF16)
        grad_ref[h] = grad
        send_ref[:, h * lanes : (h + 1) * lanes] = dot(table_ref[...], grad, ((1,), (1,))).astype(BF16)


def local_kernel(samples, field_ref, grad_ref, out_ref):
    heights, lanes, _ = field_ref.shape
    total = jnp.zeros((lanes, lanes), F32)
    for h in range(heights):
        total = total + dot(field_ref[h], grad_ref[h], ((1,), (1,)))
    size = lanes // samples
    out_ref[...] = sum(
        total[s * size : (s + 1) * size, s * size : (s + 1) * size] for s in range(samples)
    )


def final_kernel(scale, recv_ref, back_ref, local_ref, grad_ref, out_ref, wide, result, buffer, sems):
    heights, lanes, width = grad_ref.shape
    spread(wide, recv_ref, wide.shape[2])
    count = recv_ref.shape[0] // heights
    for h in range(heights):
        inner = stack(wide, h, count, heights)
        value = scale * dot(inner, back_ref[...], ((0,), (0,)))
        value = value + dot(local_ref[...], grad_ref[h], ((1,), (0,)))
        for part in range(result.shape[0]):
            result[part, pl.ds(h, lanes, stride=heights), :] = value[:, part * 128 : (part + 1) * 128]
    moves = copies(buffer, out_ref, sems)
    piece = buffer.shape[0] // len(moves)
    for n, move in enumerate(moves):
        for part in range(result.shape[0]):
            buffer[n * piece : (n + 1) * piece, part * 128 : (part + 1) * 128] = result[
                part, n * piece : (n + 1) * piece, :
            ].astype(BF16)
        move.start()
    for move in moves:
        move.wait()


def outer_kernel(samples, groups, owned, channels, *refs):
    specs, grads = refs[:groups], refs[groups : 2 * groups]
    out_ref, local_ref, real, imag, plain, crossed, block, sems = refs[2 * groups :]
    _, outs, both = block.shape[1:]
    half = both // 2
    low = low_half((channels, both), half)
    lanes = samples * channels
    total = groups * samples
    strips = outs // PACK

    local_sum = 0.0
    for grad in grads:
        pair = grad[owned * lanes :, :].astype(F32)
        local_sum = local_sum + pair[:, :channels] + pair[:, channels : 2 * channels]
    local_ref[...] = local_sum

    def move(q, strip):
        rows = pl.ds(strip * PACK, PACK)
        slot = lax.rem(q, 2)
        return pltpu.make_async_copy(
            block.at[slot, :, rows, :], out_ref.at[q, :, rows, :], sems.at[slot, strip]
        )

    def mode(q, carry):
        slot = lax.rem(q, 2)
        for g in range(groups):
            for s in range(samples):
                n = g * samples + s
                rows = pl.ds(pl.multiple_of(q * lanes + s * channels, channels), channels)
                spec = specs[g][rows, :].astype(F32)
                other = pltpu.roll(spec, half, 1)
                real[n] = jnp.where(low, spec, other)
                imag[n] = jnp.where(low, other, -spec)
                grad = grads[g][rows, :].astype(F32)
                plain[n] = grad
                crossed[n] = pltpu.roll(grad, half, 1)
        for strip in range(strips):
            first = strip * PACK

            @pl.when(q >= 2)
            def _():
                move(q - 2, strip).wait()

            right = [store[n, first : first + PACK, :] for n in range(total) for store in (plain, crossed)]

            def body(c, carry):
                left = [store[n, pl.ds(c, 1), :] for n in range(total) for store in (real, imag)]
                value = left[0] * right[0]
                for a, b in zip(left[1:], right[1:]):
                    value = value + a * b
                block[slot, c, first : first + PACK, :] = value
                return carry

            lax.fori_loop(0, channels, body, 0, unroll=4)
            move(q, strip).start()
        return carry

    lax.fori_loop(0, owned, mode, 0)
    for q in range(max(owned - 2, 0), owned):
        for strip in range(strips):
            move(q, strip).wait()


VMEM_SPEC = pl.BlockSpec(memory_space=pltpu.VMEM)
HBM_SPEC = pl.BlockSpec(memory_space=pltpu.HBM)


def call(kernel, name, operands, outs, scratch, far=(), far_outs=()):
    single = not isinstance(outs, tuple)
    specs = [HBM_SPEC if n in far_outs else VMEM_SPEC for n in range(1 if single else len(outs))]
    return pl.pallas_call(
        kernel,
        out_shape=outs,
        in_specs=[HBM_SPEC if n in far else VMEM_SPEC for n in range(len(operands))],
        out_specs=specs[0] if single else tuple(specs),
        scratch_shapes=scratch,
        compiler_params=pltpu.CompilerParams(vmem_limit_bytes=LIMIT),
        name=name,
    )(*operands)


def gather(values, axis):
    size = lax.axis_size(axis)
    return [values] + [
        lax.ppermute(values, axis, [(i, (i + step) % size) for i in range(size)]) for step in range(1, size)
    ]


def sum_over(values, axis):
    size = lax.axis_size(axis)
    step = 1
    while step < size:
        values = values + lax.ppermute(values, axis, [(i, i ^ step) for i in range(size)])
        step *= 2
    return values


def block_diagonal(matrix, copies):
    zero = jnp.zeros_like(matrix)
    return jnp.concatenate(
        [
            jnp.concatenate([matrix if i == j else zero for j in range(copies)], axis=1)
            for i in range(copies)
        ],
        axis=0,
    )


def shape(extent, kind=BF16):
    return jax.ShapeDtypeStruct(extent, kind)


def local(inputs, cotangent, mode_weight, local_weight):
    tiles = lax.axis_size("tile")
    samples, channels, th, width = inputs.shape
    owned, _, _, both = mode_weight.shape
    modes = both // 2
    lanes = samples * channels
    parts = width // 128
    spec_scale = 1.0 / math.sqrt(tiles * th * width)
    mode_scale = 1.0 / math.sqrt(modes * tiles * owned)
    send_cols, rows, back_rows, back_cols = tables(tiles, owned, th, width, modes)
    pixel_rows = samples * channels * th
    halves = 2 * tiles * owned
    inverse = 2 * tiles * th

    def exchange(values):
        split = values.reshape(tiles, values.shape[0] // tiles, values.shape[1])
        moved = lax.all_to_all(split, "tile", split_axis=0, concat_axis=0, tiled=False)
        return moved.reshape(values.shape)

    forward_mix = block_diagonal(local_weight.T, samples)
    backward_mix = block_diagonal(local_weight, samples)
    buffer = pltpu.VMEM((pixel_rows, width), BF16)
    pixel_scratch = pltpu.VMEM((parts, pixel_rows, 128), F32)
    copy_sems = pltpu.SemaphoreType.DMA((COPIES,))
    field_scratch = [buffer, pixel_scratch, copy_sems]
    inverse_scratch = pltpu.VMEM((owned, inverse, lanes), F32)
    spectra_scratch = pltpu.VMEM((th, halves, lanes), F32)

    send, field_rows = call(
        columns_kernel,
        "columns",
        (inputs.reshape(pixel_rows, width), send_cols),
        (shape((halves, th * lanes)), shape((th, lanes, width))),
        field_scratch,
        far=(0,),
    )
    halves_in = exchange(send)
    weights = call(
        load_kernel,
        "weights",
        (mode_weight,),
        shape(mode_weight.shape),
        [pltpu.SemaphoreType.DMA((owned,))],
        far=(0,),
    )
    cot_rows = call(
        relayout_kernel,
        "relayout",
        (cotangent.reshape(pixel_rows, width),),
        shape((th, lanes, width)),
        field_scratch,
        far=(0,),
    )

    def mix_call(kernel, name, spec, adder):
        return call(
            functools.partial(kernel, samples),
            name,
            (spec, back_rows, adder, weights),
            shape((inverse, owned * lanes)),
            [
                pltpu.VMEM((owned, lanes, both), BF16),
                pltpu.VMEM((2 * samples, adder.shape[1], both), BF16),
                pltpu.VMEM((lanes, both), F32),
                pltpu.VMEM((lanes, both), F32),
            ],
        )

    forward_adder = constant(np.tile(np.eye(channels), (1, channels // GROUP)))
    backward_adder = constant(np.repeat(np.eye(channels), PACK, axis=1))
    spectra = call(
        functools.partial(spectra_kernel, spec_scale, owned),
        "spectra",
        (halves_in, rows),
        shape((owned * lanes, both)),
        [spectra_scratch],
    )
    all_spectra = gather(spectra, "dp")
    inner = exchange(mix_call(forward_kernel, "mix_forward", spectra, forward_adder))

    gate_rows, send = call(
        functools.partial(pixels_kernel, mode_scale),
        "pixels",
        (inner, back_cols, forward_mix, field_rows, cot_rows, send_cols),
        (shape((th, lanes, width)), shape((halves, th * lanes))),
        [inverse_scratch],
    )
    halves_out = exchange(send)
    local_sum = call(
        functools.partial(local_kernel, samples),
        "local_grad",
        (field_rows, gate_rows),
        shape((channels, channels), F32),
        [],
    )
    local_sum = sum_over(local_sum, "tile")

    grad_spectra = call(
        functools.partial(grad_spectra_kernel, mode_scale, owned),
        "grad_spectra",
        (halves_out, rows, local_sum),
        shape((owned * lanes + channels, both)),
        [spectra_scratch],
    )
    all_grads = gather(grad_spectra, "dp")
    inner = exchange(mix_call(backward_kernel, "mix_backward", grad_spectra, backward_adder))

    groups = lax.axis_size("dp")
    per_sample = pltpu.VMEM((groups * samples, channels, both), F32)
    mode_grad, local_grad = call(
        functools.partial(outer_kernel, samples, groups, owned, channels),
        "mode_grad",
        (*all_spectra, *all_grads),
        (shape(mode_weight.shape, F32), shape((channels, channels), F32)),
        [per_sample] * 4
        + [pltpu.VMEM((2,) + mode_weight.shape[1:], F32), pltpu.SemaphoreType.DMA((2, channels // PACK))],
        far_outs=(0,),
    )
    inner, mode_grad = lax.optimization_barrier((inner, mode_grad))

    input_grad = call(
        functools.partial(final_kernel, spec_scale),
        "final",
        (inner, back_cols, backward_mix, gate_rows),
        shape((pixel_rows, width)),
        [inverse_scratch, pixel_scratch, buffer, copy_sems],
        far_outs=(0,),
    ).reshape(inputs.shape)
    return (input_grad, mode_grad, local_grad)


def solution(mesh):
    return jax.shard_map(
        local,
        mesh=mesh,
        in_specs=(
            P("dp", None, "tile", None),
            P("dp", None, "tile", None),
            P("tile", None, None, None),
            P(),
        ),
        out_specs=(P("dp", None, "tile", None), P("tile", None, None, None), P()),
        check_vma=False,
    )
```

```python
import functools
import math

import jax
import jax.numpy as jnp
import numpy as np
from jax import lax
from jax.experimental import pallas as pl
from jax.experimental.pallas import tpu as pltpu
from jax.sharding import PartitionSpec as P

F32 = jnp.float32
BF16 = jnp.bfloat16
LIMIT = 28 * 1024 * 1024
ROWS = 8
PACK = 16
GROUP = 8


def row_tables(height, modes):
    index = np.arange(modes)
    signed = np.where(index < modes // 2, index, index - modes)
    phases = np.mod(np.arange(height)[:, None] * signed[None, :], height)
    angles = phases * (2.0 * math.pi / height)
    return np.cos(angles), np.sin(angles)


def column_tables(width, modes):
    phases = np.mod(np.arange(modes)[:, None] * np.arange(width)[None, :], width)
    angles = phases * (2.0 * math.pi / width)
    return np.stack([np.cos(angles), -np.sin(angles)])


def constant(table):
    return jnp.asarray(np.asarray(table, np.float32)).astype(BF16)


def tables(tiles, owned, th, width, modes):
    cols = column_tables(width, tiles * owned)
    split = cols.reshape(2, tiles, owned, width)
    send_cols = split.transpose(1, 0, 2, 3).reshape(-1, width)
    back_cols = split.transpose(2, 1, 0, 3).reshape(-1, width)
    cosine, sine = row_tables(th * tiles, modes)
    real = np.concatenate([cosine, -sine], axis=1)
    imag = np.concatenate([sine, cosine], axis=1)
    pair = np.stack([real, imag]).reshape(2, tiles, th, 2 * modes)
    rows = pair.transpose(2, 1, 0, 3).reshape(-1, 2 * modes)
    back_rows = pair.transpose(1, 0, 2, 3).reshape(-1, 2 * modes)
    return constant(send_cols), constant(rows), constant(back_rows), constant(back_cols)


def order(outer, inner):
    take = np.arange(outer * inner).reshape(outer, inner).T.reshape(-1)
    return constant(np.eye(outer * inner)[take])


def dot(left, right, dims):
    return lax.dot_general(left, right, (dims, ((), ())), preferred_element_type=F32)


def low_half(shape, half):
    return lax.broadcasted_iota(jnp.int32, shape, 1) < half


def gelu_slope(values):
    size = jnp.abs(values)
    expo = jnp.exp(-0.5 * values * values)
    t = 1.0 / (1.0 + (0.3275911 / math.sqrt(2.0)) * size)
    poly = 0.5 * 1.061405429
    for factor in (-1.453152027, 1.421413741, -0.284496736, 0.254829592):
        poly = poly * t + 0.5 * factor
    tail = poly * t * expo
    cumulative = jnp.where(values < 0.0, tail, 1.0 - tail)
    return cumulative + values * expo * (1.0 / math.sqrt(2.0 * math.pi))


def shuffle(order_ref, value):
    return dot(order_ref[...], value, ((1,), (0,))).astype(BF16)


def by_rows(order_ref, field_ref, rows_ref):
    heights, lanes, _ = rows_ref.shape
    block = PACK * heights
    for first in range(0, lanes, PACK):
        moved = shuffle(order_ref, field_ref[first * heights : first * heights + block, :])
        for h in range(heights):
            rows_ref[h, first : first + PACK, :] = moved[h * PACK : (h + 1) * PACK]


def columns_kernel(field_ref, order_ref, table_ref, send_ref, rows_ref):
    heights, lanes, _ = rows_ref.shape
    by_rows(order_ref, field_ref, rows_ref)
    for h in range(heights):
        send_ref[:, h * lanes : (h + 1) * lanes] = dot(table_ref[...], rows_ref[h], ((1,), (1,))).astype(BF16)


def relayout_kernel(field_ref, order_ref, rows_ref):
    by_rows(order_ref, field_ref, rows_ref)


def stack(sorted_rows, index, count, lanes):
    part = sorted_rows[index * count : (index + 1) * count]
    return jnp.concatenate(
        [part[:, n : n + lanes] for n in range(0, part.shape[1], lanes)], axis=0
    )


def spectra_into(scale, owned, recv_ref, order_ref, rows_ref, spec_ref):
    count = recv_ref.shape[0] // owned
    lanes = recv_ref.shape[1] * count // rows_ref.shape[0]
    ordered = shuffle(order_ref, recv_ref[...])
    for q in range(owned):
        stacked = stack(ordered, q, count, lanes)
        spec_ref[q * lanes : (q + 1) * lanes, :] = (
            scale * dot(stacked, rows_ref[...], ((0,), (0,)))
        ).astype(BF16)


def grad_spectra_kernel(scale, owned, recv_ref, order_ref, rows_ref, local_ref, spec_ref):
    spectra_into(scale, owned, recv_ref, order_ref, rows_ref, spec_ref)
    value = local_ref[...]
    high = value.astype(BF16)
    low = (value - high.astype(F32)).astype(BF16)
    spec_ref[spec_ref.shape[0] - value.shape[0] :, :] = jnp.concatenate([high, low], axis=1)


def packed_row(store, index):
    row = store[pl.ds(index, 1), :]
    return jnp.broadcast_to(row, (PACK, row.shape[1])).astype(BF16)


def diagonal_masks(both):
    half = both // 2
    row = lax.broadcasted_iota(jnp.int32, (PACK, both), 0)
    lane = lax.broadcasted_iota(jnp.int32, (PACK, both), 1)
    lane = jnp.where(lane < half, lane, lane - half)
    return [lane == row + first for first in range(0, half, PACK)]


def diagonals(masks, upper, lower):
    zero = jnp.zeros_like(upper)
    parts = [jnp.where(mask, row, zero) for row in (upper, lower) for mask in masks]
    return jnp.concatenate(parts, axis=0)


def send_inverse(back_ref, mixed, send_ref):
    @pl.when(pl.program_id(0) == pl.num_programs(0) - 1)
    def _():
        owned, lanes, _ = mixed.shape
        for q in range(owned):
            send_ref[:, q * lanes : (q + 1) * lanes] = dot(back_ref[...], mixed[q], ((1,), (1,))).astype(BF16)


def forward_kernel(scale, samples, owned, recv_ref, order_ref, rows_ref, back_ref, weight_ref, spec_ref, send_ref, mixed, upper, lower):
    _, channels, outs, both = weight_ref.shape
    half = both // 2
    lanes = mixed.shape[1]
    q = pl.program_id(0)

    @pl.when(q == 0)
    def _():
        spectra_into(scale, owned, recv_ref, order_ref, rows_ref, spec_ref)

    value = spec_ref[pl.ds(pl.multiple_of(q * lanes, lanes), lanes), :].astype(F32)
    other = pltpu.roll(value, half, 1)
    upper[...] = value
    lower[...] = jnp.where(low_half(value.shape, half), -other, other)
    masks = diagonal_masks(both)

    def body(block, total):
        first = block * GROUP
        left = jnp.concatenate([weight_ref[0, first + step] for step in range(GROUP)], axis=1)
        right = [
            jnp.concatenate(
                [
                    diagonals(
                        masks,
                        packed_row(upper, s * channels + first + step),
                        packed_row(lower, s * channels + first + step),
                    )
                    for s in range(samples)
                ],
                axis=1,
            )
            for step in range(GROUP)
        ]
        return total + dot(left, jnp.concatenate(right, axis=0), ((1,), (0,)))

    total = lax.fori_loop(0, channels // GROUP, body, jnp.zeros((outs, samples * both), F32))
    mixed[q] = jnp.concatenate(
        [total[:, s * both : (s + 1) * both] for s in range(samples)], axis=0
    ).astype(BF16)
    send_inverse(back_ref, mixed, send_ref)


def backward_kernel(samples, spec_ref, back_ref, adder_ref, weight_ref, send_ref, mixed, sums):
    _, channels, outs, both = weight_ref.shape
    half = both // 2
    lanes = mixed.shape[1]
    q = pl.program_id(0)
    value = spec_ref[pl.ds(pl.multiple_of(q * lanes, lanes), lanes), :].astype(F32)
    other = pltpu.roll(value, half, 1)
    low = low_half(value.shape, half)
    real = jnp.where(low, value, other)
    imag = jnp.where(low, other, value)
    grads = [part[s * outs : (s + 1) * outs] for s in range(samples) for part in (real, imag)]

    def body(block, carry):
        for step in range(GROUP):
            c = block * GROUP + step
            weight = weight_ref[0, c].astype(F32)
            for n, grad in enumerate(grads):
                product = weight * grad
                total = product[:ROWS]
                for o in range(ROWS, outs, ROWS):
                    total = total + product[o : o + ROWS]
                sums[n, pl.ds(pl.multiple_of(c * ROWS, ROWS), ROWS), :] = total
        return carry

    lax.fori_loop(0, channels // GROUP, body, 0)
    low = low_half((channels, both), half)
    result = []
    for s in range(samples):
        straight = dot(adder_ref[...], sums[2 * s].astype(BF16), ((1,), (0,)))
        crossed = dot(adder_ref[...], sums[2 * s + 1].astype(BF16), ((1,), (0,)))
        result.append(jnp.where(low, straight, -straight) + pltpu.roll(crossed, half, 1))
    mixed[q] = jnp.concatenate(result, axis=0).astype(BF16)
    send_inverse(back_ref, mixed, send_ref)


def pixels_kernel(scale, recv_ref, order_ref, back_ref, local_ref, field_ref, cot_ref, table_ref, grad_ref, send_ref):
    heights, lanes, _ = field_ref.shape
    count = recv_ref.shape[0] // heights
    ordered = shuffle(order_ref, recv_ref[...])
    for h in range(heights):
        inner = stack(ordered, h, count, lanes)
        pre = scale * dot(inner, back_ref[...], ((0,), (0,)))
        pre = pre + dot(local_ref[...], field_ref[h], ((1,), (0,)))
        grad = (cot_ref[h].astype(F32) * gelu_slope(pre)).astype(BF16)
        grad_ref[h] = grad
        send_ref[:, h * lanes : (h + 1) * lanes] = dot(table_ref[...], grad, ((1,), (1,))).astype(BF16)


def local_kernel(samples, field_ref, grad_ref, out_ref):
    heights, lanes, _ = field_ref.shape
    total = jnp.zeros((lanes, lanes), F32)
    for h in range(heights):
        total = total + dot(field_ref[h], grad_ref[h], ((1,), (1,)))
    size = lanes // samples
    out_ref[...] = sum(
        total[s * size : (s + 1) * size, s * size : (s + 1) * size] for s in range(samples)
    )


def final_kernel(scale, recv_ref, order_ref, back_ref, local_ref, grad_ref, restore_ref, out_ref, result):
    heights, lanes, _ = grad_ref.shape
    count = recv_ref.shape[0] // heights
    ordered = shuffle(order_ref, recv_ref[...])
    for h in range(heights):
        inner = stack(ordered, h, count, lanes)
        value = scale * dot(inner, back_ref[...], ((0,), (0,)))
        result[h] = (value + dot(local_ref[...], grad_ref[h], ((1,), (0,)))).astype(BF16)
    block = PACK * heights
    for first in range(0, lanes, PACK):
        part = jnp.concatenate([result[h, first : first + PACK, :] for h in range(heights)], axis=0)
        out_ref[first * heights : first * heights + block, :] = shuffle(restore_ref, part)


def outer_kernel(samples, spec_ref, grad_ref, pair_ref, out_ref, local_ref, upper, lower, left):
    groups = spec_ref.shape[0]
    _, channels, outs, both = out_ref.shape
    half = both // 2
    low = low_half((channels, both), half)

    @pl.when(pl.program_id(0) == 0)
    def _():
        total = 0.0
        for g in range(groups):
            pair = pair_ref[g].astype(F32)
            total = total + pair[:, :channels] + pair[:, channels : 2 * channels]
        local_ref[...] = total

    for g in range(groups):
        for s in range(samples):
            n = g * samples + s
            spec = spec_ref[g, s * channels : (s + 1) * channels, :].astype(F32)
            upper[n] = jnp.where(low, spec, -spec)
            lower[n] = pltpu.roll(spec, half, 1)
            left[:, n * both : (n + 1) * both] = grad_ref[g, s * outs : (s + 1) * outs, :]
    masks = diagonal_masks(both)
    pair = 2

    def body(block, carry):
        first = block * pair
        right = [
            jnp.concatenate(
                [
                    diagonals(masks, packed_row(upper.at[n], first + step), packed_row(lower.at[n], first + step))
                    for step in range(pair)
                ],
                axis=1,
            )
            for n in range(groups * samples)
        ]
        value = dot(left[...], jnp.concatenate(right, axis=0), ((1,), (0,)))
        for step in range(pair):
            out_ref[0, first + step] = value[:, step * both : (step + 1) * both]
        return carry

    lax.fori_loop(0, channels // pair, body, 0)


def whole(extent):
    return pl.BlockSpec(extent, lambda *_: (0,) * len(extent))


def call(kernel, name, operands, outs, scratch=(), near=(), grid=(1,), blocks=None, out_blocks=None):
    blocks, out_blocks = blocks or {}, out_blocks or {}
    single = not isinstance(outs, tuple)
    listed = (outs,) if single else outs
    in_specs = [
        VMEM_SPEC if n in near else blocks.get(n, whole(operand.shape)) for n, operand in enumerate(operands)
    ]
    out_specs = tuple(out_blocks.get(n, whole(out.shape)) for n, out in enumerate(listed))
    return pl.pallas_call(
        kernel,
        out_shape=outs,
        grid=grid,
        in_specs=in_specs,
        out_specs=out_specs[0] if single else out_specs,
        scratch_shapes=list(scratch),
        compiler_params=pltpu.CompilerParams(vmem_limit_bytes=LIMIT),
        name=name,
    )(*operands)


VMEM_SPEC = pl.BlockSpec(memory_space=pltpu.VMEM)


def sum_over(values, axis):
    size = lax.axis_size(axis)
    step = 1
    while step < size:
        values = values + lax.ppermute(values, axis, [(i, i ^ step) for i in range(size)])
        step *= 2
    return values


def block_diagonal(matrix, copies):
    zero = jnp.zeros_like(matrix)
    return jnp.concatenate(
        [
            jnp.concatenate([matrix if i == j else zero for j in range(copies)], axis=1)
            for i in range(copies)
        ],
        axis=0,
    )


def shape(extent, kind=BF16):
    return jax.ShapeDtypeStruct(extent, kind)


def local(inputs, cotangent, mode_weight, local_weight):
    tiles = lax.axis_size("tile")
    samples, channels, th, width = inputs.shape
    owned, _, _, both = mode_weight.shape
    modes = both // 2
    lanes = samples * channels
    parts = width // 128
    spec_scale = 1.0 / math.sqrt(tiles * th * width)
    mode_scale = 1.0 / math.sqrt(modes * tiles * owned)
    send_cols, rows, back_rows, back_cols = tables(tiles, owned, th, width, modes)
    pixel_rows = samples * channels * th
    halves = 2 * tiles * owned
    inverse = 2 * tiles * th

    def exchange(values):
        split = values.reshape(tiles, values.shape[0] // tiles, values.shape[1])
        moved = lax.all_to_all(split, "tile", split_axis=0, concat_axis=0, tiled=False)
        return moved.reshape(values.shape)

    forward_mix = block_diagonal(local_weight.T, samples)
    backward_mix = block_diagonal(local_weight, samples)
    by_row = order(PACK, th)
    by_channel = order(th, PACK)
    by_mode = order(2 * tiles, owned)
    by_height = order(2 * tiles, th)
    mixed = pltpu.VMEM((owned, lanes, both), BF16)
    spectrum_rows = pltpu.VMEM((lanes, both), F32)
    weight_block = pl.BlockSpec((1,) + mode_weight.shape[1:], lambda q: (q, 0, 0, 0))

    send, field_rows = call(
        columns_kernel,
        "columns",
        (inputs.reshape(pixel_rows, width), by_row, send_cols),
        (shape((halves, th * lanes)), shape((th, lanes, width))),
    )
    halves_in = exchange(send)
    cot_rows = call(
        relayout_kernel,
        "relayout",
        (cotangent.reshape(pixel_rows, width), by_row),
        shape((th, lanes, width)),
    )
    spectra, send = call(
        functools.partial(forward_kernel, spec_scale, samples, owned),
        "mix_forward",
        (halves_in, by_mode, rows, back_rows, mode_weight),
        (shape((owned * lanes, both)), shape((inverse, owned * lanes))),
        [mixed, spectrum_rows, spectrum_rows],
        grid=(owned,),
        blocks={4: weight_block},
    )
    all_spectra = lax.all_gather(spectra, "dp")
    inner = exchange(send)
    gate_rows, send = call(
        functools.partial(pixels_kernel, mode_scale),
        "pixels",
        (inner, by_height, back_cols, forward_mix, field_rows, cot_rows, send_cols),
        (shape((th, lanes, width)), shape((halves, th * lanes))),
    )
    halves_out = exchange(send)
    local_sum = call(
        functools.partial(local_kernel, samples),
        "local_grad",
        (field_rows, gate_rows),
        shape((channels, channels), F32),
    )
    local_sum = sum_over(local_sum, "tile")
    grad_spectra = call(
        functools.partial(grad_spectra_kernel, mode_scale, owned),
        "grad_spectra",
        (halves_out, by_mode, rows, local_sum),
        shape((owned * lanes + channels, both)),
    )
    all_grads = lax.all_gather(grad_spectra, "dp")
    adder = constant(np.repeat(np.eye(channels), ROWS, axis=1))
    send = call(
        functools.partial(backward_kernel, samples),
        "mix_backward",
        (grad_spectra, back_rows, adder, mode_weight),
        shape((inverse, owned * lanes)),
        [mixed, pltpu.VMEM((2 * samples, channels * ROWS, both), F32)],
        grid=(owned,),
        blocks={3: weight_block},
    )
    inner = exchange(send)

    groups = lax.axis_size("dp")
    total = groups * samples
    per_mode = pl.BlockSpec((groups, lanes, both), lambda q: (0, q, 0))
    below = owned * lanes // channels
    mode_grad, local_grad = call(
        functools.partial(outer_kernel, samples),
        "mode_grad",
        (all_spectra, all_grads, all_grads),
        (shape(mode_weight.shape, F32), shape((channels, channels), F32)),
        [pltpu.VMEM((total, channels, both), F32)] * 2 + [pltpu.VMEM((channels, total * both), BF16)],
        grid=(owned,),
        blocks={
            0: per_mode,
            1: per_mode,
            2: pl.BlockSpec((groups, channels, both), lambda q: (0, below, 0)),
        },
        out_blocks={0: weight_block},
    )
    inner, mode_grad = lax.optimization_barrier((inner, mode_grad))

    input_grad = call(
        functools.partial(final_kernel, spec_scale),
        "final",
        (inner, by_height, back_cols, backward_mix, gate_rows, by_channel),
        shape((pixel_rows, width)),
        [pltpu.VMEM((th, lanes, width), BF16)],
    ).reshape(inputs.shape)
    return (input_grad, mode_grad, local_grad)


def solution(mesh):
    return jax.shard_map(
        local,
        mesh=mesh,
        in_specs=(
            P("dp", None, "tile", None),
            P("dp", None, "tile", None),
            P("tile", None, None, None),
            P(),
        ),
        out_specs=(P("dp", None, "tile", None), P("tile", None, None, None), P()),
        check_vma=False,
    )
```

```python
import functools
import math

import jax
import jax.numpy as jnp
import numpy as np
from jax import lax
from jax.experimental import pallas as pl
from jax.experimental.pallas import tpu as pltpu
from jax.sharding import PartitionSpec as P

F32 = jnp.float32
BF16 = jnp.bfloat16
LIMIT = 56 * 1024 * 1024
ROWS = 8
PACK = 16
GROUP = 8


def row_tables(height, modes):
    index = np.arange(modes)
    signed = np.where(index < modes // 2, index, index - modes)
    phases = np.mod(np.arange(height)[:, None] * signed[None, :], height)
    angles = phases * (2.0 * math.pi / height)
    return np.cos(angles), np.sin(angles)


def column_tables(width, modes):
    phases = np.mod(np.arange(modes)[:, None] * np.arange(width)[None, :], width)
    angles = phases * (2.0 * math.pi / width)
    return np.stack([np.cos(angles), -np.sin(angles)])


def constant(table):
    return jnp.asarray(np.asarray(table, np.float32)).astype(BF16)


def tables(tiles, owned, th, width, modes):
    cols = column_tables(width, tiles * owned)
    split = cols.reshape(2, tiles, owned, width)
    send_cols = split.transpose(1, 0, 2, 3).reshape(tiles, 2 * owned, width)
    send_cols = np.pad(send_cols, ((0, 0), (0, padded(2 * owned) - 2 * owned), (0, 0))).reshape(-1, width)
    back_cols = split.transpose(2, 1, 0, 3).reshape(-1, width)
    cosine, sine = row_tables(th * tiles, modes)
    real = np.concatenate([cosine, -sine], axis=1)
    imag = np.concatenate([sine, cosine], axis=1)
    pair = np.stack([real, imag]).reshape(2, tiles, th, 2 * modes)
    rows = pair.transpose(2, 1, 0, 3).reshape(-1, 2 * modes)
    back_rows = pair.transpose(1, 0, 2, 3).reshape(-1, 2 * modes)
    return constant(send_cols), constant(rows), constant(back_rows), constant(back_cols)


def padded(rows):
    return -(-rows // PACK) * PACK


def order(outer, inner):
    take = np.arange(outer * inner).reshape(outer, inner).T.reshape(-1)
    return constant(np.eye(outer * inner)[take])


def mode_order(tiles, owned):
    rows = np.arange(tiles * padded(2 * owned)).reshape(tiles, -1)
    take = rows[:, : 2 * owned].reshape(tiles, 2, owned).transpose(2, 0, 1).reshape(-1)
    return constant(np.eye(rows.size)[take])


def dot(left, right, dims):
    return lax.dot_general(left, right, (dims, ((), ())), preferred_element_type=F32)


def low_half(shape, half):
    return lax.broadcasted_iota(jnp.int32, shape, 1) < half


def gelu_slope(values):
    size = jnp.abs(values)
    expo = jnp.exp(-0.5 * values * values)
    t = 1.0 / (1.0 + (0.3275911 / math.sqrt(2.0)) * size)
    poly = 0.5 * 1.061405429
    for factor in (-1.453152027, 1.421413741, -0.284496736, 0.254829592):
        poly = poly * t + 0.5 * factor
    tail = poly * t * expo
    cumulative = jnp.where(values < 0.0, tail, 1.0 - tail)
    return cumulative + values * expo * (1.0 / math.sqrt(2.0 * math.pi))


def piece(me_ref, step, extent):
    return pl.ds(pl.multiple_of((me_ref[0] ^ step) * extent, extent), extent)


def assemble(me_ref, pieces, whole_ref):
    for step, part in enumerate(pieces):
        whole_ref[piece(me_ref, step, part.shape[0]), :] = part[...]


def hand_out(me_ref, whole_ref, pieces):
    for step, part in enumerate(pieces):
        part[...] = whole_ref[piece(me_ref, step, part.shape[0]), :]


def shuffle(order_ref, value):
    return dot(order_ref[...], value, ((1,), (0,))).astype(BF16)


def by_rows(order_ref, field_ref, rows_ref):
    heights, lanes, _ = rows_ref.shape
    block = PACK * heights
    for first in range(0, lanes, PACK):
        moved = shuffle(order_ref, field_ref[first * heights : first * heights + block, :])
        for h in range(heights):
            rows_ref[h, first : first + PACK, :] = moved[h * PACK : (h + 1) * PACK]


def columns_kernel(me_ref, field_ref, order_ref, table_ref, rows_ref, *rest):
    *pieces, send_ref = rest
    heights, lanes, _ = rows_ref.shape
    by_rows(order_ref, field_ref, rows_ref)
    for h in range(heights):
        send_ref[:, h * lanes : (h + 1) * lanes] = dot(table_ref[...], rows_ref[h], ((1,), (1,))).astype(BF16)
    hand_out(me_ref, send_ref, pieces)


def relayout_kernel(field_ref, order_ref, rows_ref):
    by_rows(order_ref, field_ref, rows_ref)


def shuffle_groups(order_ref, recv_ref):
    size = order_ref.shape[0]
    return [shuffle(order_ref, recv_ref[n : n + size, :]) for n in range(0, recv_ref.shape[0], size)]


def stack(groups, index, count, lanes):
    return jnp.concatenate(
        [
            group[index * count : (index + 1) * count, n : n + lanes]
            for n in range(0, groups[0].shape[1], lanes)
            for group in groups
        ],
        axis=0,
    )


def spectra_into(scale, owned, recv_ref, order_ref, rows_ref, spec_ref):
    count = order_ref.shape[0] // owned
    lanes = recv_ref.shape[1] * count // rows_ref.shape[0]
    ordered = [shuffle(order_ref, recv_ref[...])]
    for q in range(owned):
        stacked = stack(ordered, q, count, lanes)
        spec_ref[q * lanes : (q + 1) * lanes, :] = (
            scale * dot(stacked, rows_ref[...], ((0,), (0,)))
        ).astype(BF16)


def grad_spectra_kernel(scale, owned, tiles, me_ref, *refs):
    pieces, (order_ref, rows_ref, local_ref, spec_ref, recv_ref) = refs[:tiles], refs[tiles:]
    assemble(me_ref, pieces, recv_ref)
    spectra_into(scale, owned, recv_ref, order_ref, rows_ref, spec_ref)
    value = local_ref[...]
    high = value.astype(BF16)
    low = (value - high.astype(F32)).astype(BF16)
    spec_ref[spec_ref.shape[0] - value.shape[0] :, :] = jnp.concatenate([high, low], axis=1)


def packed_row(store, index):
    row = store[pl.ds(index, 1), :]
    return jnp.broadcast_to(row, (PACK, row.shape[1])).astype(BF16)


def send_inverse(me_ref, back_ref, mixed, send_ref, pieces):
    @pl.when(pl.program_id(0) == pl.num_programs(0) - 1)
    def _():
        owned, lanes, _ = mixed.shape
        for q in range(owned):
            send_ref[:, q * lanes : (q + 1) * lanes] = dot(back_ref[...], mixed[q], ((1,), (1,))).astype(BF16)
        hand_out(me_ref, send_ref, pieces)


def forward_kernel(scale, samples, owned, tiles, me_ref, *refs):
    arrived, (order_ref, rows_ref, back_ref, weight_ref, spec_ref) = refs[:tiles], refs[tiles : tiles + 5]
    pieces, (recv_ref, send_ref, mixed, real, imag) = refs[tiles + 5 : 2 * tiles + 5], refs[2 * tiles + 5 :]
    _, channels, outs, both = weight_ref.shape
    half = both // 2
    lanes = mixed.shape[1]
    q = pl.program_id(0)

    @pl.when(q == 0)
    def _():
        assemble(me_ref, arrived, recv_ref)
        spectra_into(scale, owned, recv_ref, order_ref, rows_ref, spec_ref)

    value = spec_ref[pl.ds(pl.multiple_of(q * lanes, lanes), lanes), :].astype(F32)
    other = pltpu.roll(value, half, 1)
    low = low_half(value.shape, half)
    real[...] = jnp.where(low, value, other)
    imag[...] = jnp.where(low, other, value)

    def body(block, carry):
        sums = list(carry)
        for step in range(GROUP):
            c = block * GROUP + step
            weight = weight_ref[0, c].astype(F32)
            for s in range(samples):
                sums[2 * s] = sums[2 * s] + weight * real[pl.ds(s * channels + c, 1), :]
                sums[2 * s + 1] = sums[2 * s + 1] + weight * imag[pl.ds(s * channels + c, 1), :]
        return tuple(sums)

    zero = jnp.zeros((outs, both), F32)
    sums = lax.fori_loop(0, channels // GROUP, body, (zero,) * (2 * samples))
    low = low_half((outs, both), half)
    result = []
    for s in range(samples):
        crossed = pltpu.roll(sums[2 * s + 1], half, 1)
        result.append(sums[2 * s] + jnp.where(low, -crossed, crossed))
    mixed[q] = jnp.concatenate(result, axis=0).astype(BF16)
    send_inverse(me_ref, back_ref, mixed, send_ref, pieces)


def backward_kernel(samples, me_ref, spec_ref, back_ref, adder_ref, weight_ref, *rest):
    *pieces, send_ref, mixed, sums = rest
    _, channels, outs, both = weight_ref.shape
    half = both // 2
    lanes = mixed.shape[1]
    q = pl.program_id(0)
    value = spec_ref[pl.ds(pl.multiple_of(q * lanes, lanes), lanes), :].astype(F32)
    other = pltpu.roll(value, half, 1)
    low = low_half(value.shape, half)
    real = jnp.where(low, value, other)
    imag = jnp.where(low, other, value)
    grads = [part[s * outs : (s + 1) * outs] for s in range(samples) for part in (real, imag)]

    def body(block, carry):
        for step in range(GROUP):
            c = block * GROUP + step
            weight = weight_ref[0, c].astype(F32)
            for n, grad in enumerate(grads):
                product = weight * grad
                total = product[:ROWS]
                for o in range(ROWS, outs, ROWS):
                    total = total + product[o : o + ROWS]
                sums[n, pl.ds(pl.multiple_of(c * ROWS, ROWS), ROWS), :] = total
        return carry

    lax.fori_loop(0, channels // GROUP, body, 0)
    low = low_half((channels, both), half)
    result = []
    for s in range(samples):
        straight = dot(adder_ref[...], sums[2 * s].astype(BF16), ((1,), (0,)))
        crossed = dot(adder_ref[...], sums[2 * s + 1].astype(BF16), ((1,), (0,)))
        result.append(jnp.where(low, straight, -straight) + pltpu.roll(crossed, half, 1))
    mixed[q] = jnp.concatenate(result, axis=0).astype(BF16)
    send_inverse(me_ref, back_ref, mixed, send_ref, pieces)


def pixels_kernel(scale, tiles, me_ref, *refs):
    arrived, (order_ref, back_ref, local_ref, field_ref, cot_ref, table_ref, grad_ref) = (
        refs[:tiles],
        refs[tiles : tiles + 7],
    )
    pieces, (recv_ref, send_ref) = refs[tiles + 7 : 2 * tiles + 7], refs[2 * tiles + 7 :]
    assemble(me_ref, arrived, recv_ref)
    heights, lanes, _ = field_ref.shape
    count = order_ref.shape[0] // heights
    ordered = shuffle_groups(order_ref, recv_ref)
    for h in range(heights):
        inner = stack(ordered, h, count, lanes)
        pre = scale * dot(inner, back_ref[...], ((0,), (0,)))
        pre = pre + dot(local_ref[...], field_ref[h], ((1,), (0,)))
        grad = (cot_ref[h].astype(F32) * gelu_slope(pre)).astype(BF16)
        grad_ref[h] = grad
        send_ref[:, h * lanes : (h + 1) * lanes] = dot(table_ref[...], grad, ((1,), (1,))).astype(BF16)
    hand_out(me_ref, send_ref, pieces)


def local_kernel(samples, field_ref, grad_ref, out_ref):
    heights, lanes, _ = field_ref.shape
    total = jnp.zeros((lanes, lanes), F32)
    for h in range(heights):
        total = total + dot(field_ref[h], grad_ref[h], ((1,), (1,)))
    size = lanes // samples
    out_ref[...] = sum(
        total[s * size : (s + 1) * size, s * size : (s + 1) * size] for s in range(samples)
    )


def final_kernel(scale, tiles, me_ref, *refs):
    arrived, (order_ref, back_ref, local_ref, grad_ref, restore_ref, out_ref, recv_ref, result) = (
        refs[:tiles],
        refs[tiles:],
    )
    assemble(me_ref, arrived, recv_ref)
    heights, lanes, _ = grad_ref.shape
    count = order_ref.shape[0] // heights
    ordered = shuffle_groups(order_ref, recv_ref)
    for h in range(heights):
        inner = stack(ordered, h, count, lanes)
        value = scale * dot(inner, back_ref[...], ((0,), (0,)))
        result[h] = (value + dot(local_ref[...], grad_ref[h], ((1,), (0,)))).astype(BF16)
    block = PACK * heights
    for first in range(0, lanes, PACK):
        part = jnp.concatenate([result[h, first : first + PACK, :] for h in range(heights)], axis=0)
        out_ref[first * heights : first * heights + block, :] = shuffle(restore_ref, part)


def tree(terms):
    while len(terms) > 1:
        terms = [a + b for a, b in zip(terms[0::2], terms[1::2])]
    return terms[0]


def outer_kernel(samples, spec_ref, grad_ref, pair_ref, out_ref, local_ref, real, imag, plain, crossed):
    groups = spec_ref.shape[0]
    _, channels, outs, both = out_ref.shape
    half = both // 2
    low = low_half((channels, both), half)
    total = groups * samples

    @pl.when(pl.program_id(0) == 0)
    def _():
        pairs = 0.0
        for g in range(groups):
            pair = pair_ref[g].astype(F32)
            pairs = pairs + pair[:, :channels] + pair[:, channels : 2 * channels]
        local_ref[...] = pairs

    for g in range(groups):
        for s in range(samples):
            n = g * samples + s
            spec = spec_ref[g, s * channels : (s + 1) * channels, :].astype(F32)
            other = pltpu.roll(spec, half, 1)
            real[n] = jnp.where(low, spec, other)
            imag[n] = jnp.where(low, other, -spec)
            grad = grad_ref[g, s * outs : (s + 1) * outs, :]
            plain[n] = grad
            crossed[n] = pltpu.roll(grad.astype(F32), half, 1).astype(BF16)

    def body(c, carry):
        left = [packed_row(store.at[n], c) for n in range(total) for store in (real, imag)]
        for o in range(0, outs, PACK):
            right = [store[n, o : o + PACK, :] for n in range(total) for store in (plain, crossed)]
            terms = [a * b for a, b in zip(left, right)]
            middle = len(terms) // 2
            out_ref[0, c, o : o + PACK, :] = tree(terms[:middle]).astype(F32) + tree(terms[middle:]).astype(F32)
        return carry

    lax.fori_loop(0, channels, body, 0, unroll=2)


def whole(extent):
    return pl.BlockSpec(extent, lambda *_: (0,) * len(extent))


def call(kernel, name, operands, outs, scratch=(), grid=(1,), blocks=None, out_blocks=None, place=None):
    blocks, out_blocks = blocks or {}, out_blocks or {}
    scalars = () if place is None else (place,)
    in_specs = [blocks.get(n, whole(operand.shape)) for n, operand in enumerate(operands)]
    out_specs = [out_blocks.get(n, whole(out.shape)) for n, out in enumerate(outs)]
    return pl.pallas_call(
        kernel,
        out_shape=tuple(outs),
        grid_spec=pltpu.PrefetchScalarGridSpec(
            num_scalar_prefetch=len(scalars),
            grid=grid,
            in_specs=in_specs,
            out_specs=tuple(out_specs),
            scratch_shapes=list(scratch),
        ),
        compiler_params=pltpu.CompilerParams(vmem_limit_bytes=LIMIT),
        name=name,
    )(*scalars, *operands)


def sum_over(values, axis):
    size = lax.axis_size(axis)
    step = 1
    while step < size:
        values = values + lax.ppermute(values, axis, [(i, i ^ step) for i in range(size)])
        step *= 2
    return values


def block_diagonal(matrix, copies):
    zero = jnp.zeros_like(matrix)
    return jnp.concatenate(
        [
            jnp.concatenate([matrix if i == j else zero for j in range(copies)], axis=1)
            for i in range(copies)
        ],
        axis=0,
    )


def shape(extent, kind=BF16):
    return jax.ShapeDtypeStruct(extent, kind)


def local(inputs, cotangent, mode_weight, local_weight):
    tiles = lax.axis_size("tile")
    samples, channels, th, width = inputs.shape
    owned, _, _, both = mode_weight.shape
    modes = both // 2
    lanes = samples * channels
    parts = width // 128
    spec_scale = 1.0 / math.sqrt(tiles * th * width)
    mode_scale = 1.0 / math.sqrt(modes * tiles * owned)
    send_cols, rows, back_rows, back_cols = tables(tiles, owned, th, width, modes)
    pixel_rows = samples * channels * th
    halves = tiles * padded(2 * owned)
    inverse = 2 * tiles * th

    place = lax.axis_index("tile").astype(jnp.int32).reshape(1)

    def exchange(pieces):
        return [pieces[0]] + [
            lax.ppermute(pieces[step], "tile", [(i, i ^ step) for i in range(tiles)]) for step in range(1, tiles)
        ]

    forward_mix = block_diagonal(local_weight.T, samples)
    backward_mix = block_diagonal(local_weight, samples)
    by_row = order(PACK, th)
    by_channel = order(th, PACK)
    by_mode = mode_order(tiles, owned)
    by_height = order(2 * min(tiles, 8), th)
    mixed = pltpu.VMEM((owned, lanes, both), BF16)
    spectrum_rows = pltpu.VMEM((lanes, both), F32)
    weight_block = pl.BlockSpec((1,) + mode_weight.shape[1:], lambda q, _: (q, 0, 0, 0))
    to_modes = pltpu.VMEM((halves, th * lanes), BF16)
    to_pixels = pltpu.VMEM((inverse, owned * lanes), BF16)
    mode_pieces = (shape((halves // tiles, th * lanes)),) * tiles
    pixel_pieces = (shape((inverse // tiles, owned * lanes)),) * tiles
    field_shape = shape((th, lanes, width))

    field_rows, *send = call(
        columns_kernel,
        "columns",
        (inputs.reshape(pixel_rows, width), by_row, send_cols),
        (field_shape, *mode_pieces),
        [to_modes],
        place=place,
    )
    arrived = exchange(send)
    (cot_rows,) = call(
        relayout_kernel, "relayout", (cotangent.reshape(pixel_rows, width), by_row), (field_shape,)
    )
    spectra, *send = call(
        functools.partial(forward_kernel, spec_scale, samples, owned, tiles),
        "mix_forward",
        (*arrived, by_mode, rows, back_rows, mode_weight),
        (shape((owned * lanes, both)), *pixel_pieces),
        [to_modes, to_pixels, mixed, spectrum_rows, spectrum_rows],
        grid=(owned,),
        blocks={tiles + 3: weight_block},
        place=place,
    )
    all_spectra = lax.all_gather(spectra, "dp")
    arrived = exchange(send)
    gate_rows, *send = call(
        functools.partial(pixels_kernel, mode_scale, tiles),
        "pixels",
        (*arrived, by_height, back_cols, forward_mix, field_rows, cot_rows, send_cols),
        (field_shape, *mode_pieces),
        [to_pixels, to_modes],
        place=place,
    )
    arrived = exchange(send)
    (local_sum,) = call(
        functools.partial(local_kernel, samples),
        "local_grad",
        (field_rows, gate_rows),
        (shape((channels, channels), F32),),
    )
    local_sum = sum_over(local_sum, "tile")
    (grad_spectra,) = call(
        functools.partial(grad_spectra_kernel, mode_scale, owned, tiles),
        "grad_spectra",
        (*arrived, by_mode, rows, local_sum),
        (shape((owned * lanes + channels, both)),),
        [to_modes],
        place=place,
    )
    all_grads = lax.all_gather(grad_spectra, "dp")
    adder = constant(np.repeat(np.eye(channels), ROWS, axis=1))
    send = call(
        functools.partial(backward_kernel, samples),
        "mix_backward",
        (grad_spectra, back_rows, adder, mode_weight),
        pixel_pieces,
        [to_pixels, mixed, pltpu.VMEM((2 * samples, channels * ROWS, both), F32)],
        grid=(owned,),
        blocks={3: weight_block},
        place=place,
    )
    arrived = exchange(send)

    groups = lax.axis_size("dp")
    total = groups * samples
    per_mode = pl.BlockSpec((groups, lanes, both), lambda q: (0, q, 0))
    below = owned * lanes // channels
    mode_grad, local_grad = call(
        functools.partial(outer_kernel, samples),
        "mode_grad",
        (all_spectra, all_grads, all_grads),
        (shape(mode_weight.shape, F32), shape((channels, channels), F32)),
        [pltpu.VMEM((total, channels, both), F32)] * 2 + [pltpu.VMEM((total, channels, both), BF16)] * 2,
        grid=(owned,),
        blocks={
            0: per_mode,
            1: per_mode,
            2: pl.BlockSpec((groups, channels, both), lambda q: (0, below, 0)),
        },
        out_blocks={0: pl.BlockSpec((1,) + mode_weight.shape[1:], lambda q: (q, 0, 0, 0))},
    )
    *arrived, mode_grad = lax.optimization_barrier((*arrived, mode_grad))

    (input_grad,) = call(
        functools.partial(final_kernel, spec_scale, tiles),
        "final",
        (*arrived, by_height, back_cols, backward_mix, gate_rows, by_channel),
        (shape((pixel_rows, width)),),
        [to_pixels, pltpu.VMEM((th, lanes, width), BF16)],
        place=place,
    )
    return (input_grad.reshape(inputs.shape), mode_grad, local_grad)


def solution(mesh):
    return jax.shard_map(
        local,
        mesh=mesh,
        in_specs=(
            P("dp", None, "tile", None),
            P("dp", None, "tile", None),
            P("tile", None, None, None),
            P(),
        ),
        out_specs=(P("dp", None, "tile", None), P("tile", None, None, None), P()),
        check_vma=False,
    )
```

```python
import functools
import math

import jax
import jax.numpy as jnp
import numpy as np
from jax import lax
from jax.experimental import pallas as pl
from jax.experimental.pallas import tpu as pltpu
from jax.sharding import PartitionSpec as P

F32 = jnp.float32
BF16 = jnp.bfloat16
LIMIT = 56 * 1024 * 1024
ROWS = 8
PACK = 16
GROUP = 8


def row_tables(height, modes):
    index = np.arange(modes)
    signed = np.where(index < modes // 2, index, index - modes)
    phases = np.mod(np.arange(height)[:, None] * signed[None, :], height)
    angles = phases * (2.0 * math.pi / height)
    return np.cos(angles), np.sin(angles)


def column_tables(width, modes):
    phases = np.mod(np.arange(modes)[:, None] * np.arange(width)[None, :], width)
    angles = phases * (2.0 * math.pi / width)
    return np.stack([np.cos(angles), -np.sin(angles)])


def constant(table):
    return jnp.asarray(np.asarray(table, np.float32)).astype(BF16)


def tables(tiles, owned, th, width, modes):
    cols = column_tables(width, tiles * owned)
    split = cols.reshape(2, tiles, owned, width)
    send_cols = split.transpose(1, 0, 2, 3).reshape(tiles, 2 * owned, width)
    send_cols = np.pad(send_cols, ((0, 0), (0, padded(2 * owned) - 2 * owned), (0, 0))).reshape(-1, width)
    back_cols = split.transpose(2, 1, 0, 3).reshape(-1, width)
    cosine, sine = row_tables(th * tiles, modes)
    real = np.concatenate([cosine, -sine], axis=1)
    imag = np.concatenate([sine, cosine], axis=1)
    pair = np.stack([real, imag]).reshape(2, tiles, th, 2 * modes)
    rows = pair.transpose(2, 1, 0, 3).reshape(-1, 2 * modes)
    back_rows = pair.transpose(1, 0, 2, 3).reshape(-1, 2 * modes)
    return constant(send_cols), constant(rows), constant(back_rows), constant(back_cols)


def padded(rows):
    return -(-rows // PACK) * PACK


def order(outer, inner):
    take = np.arange(outer * inner).reshape(outer, inner).T.reshape(-1)
    return constant(np.eye(outer * inner)[take])


def mode_order(tiles, owned):
    rows = np.arange(tiles * padded(2 * owned)).reshape(tiles, -1)
    take = rows[:, : 2 * owned].reshape(tiles, 2, owned).transpose(2, 0, 1).reshape(-1)
    return constant(np.eye(rows.size)[take])


def dot(left, right, dims):
    return lax.dot_general(left, right, (dims, ((), ())), preferred_element_type=F32)


def low_half(shape, half):
    return lax.broadcasted_iota(jnp.int32, shape, 1) < half


def gelu_slope(values):
    size = jnp.abs(values)
    expo = jnp.exp(-0.5 * values * values)
    t = 1.0 / (1.0 + (0.3275911 / math.sqrt(2.0)) * size)
    poly = 0.5 * 1.061405429
    for factor in (-1.453152027, 1.421413741, -0.284496736, 0.254829592):
        poly = poly * t + 0.5 * factor
    tail = poly * t * expo
    cumulative = jnp.where(values < 0.0, tail, 1.0 - tail)
    return cumulative + values * expo * (1.0 / math.sqrt(2.0 * math.pi))


def shuffle(order_ref, value):
    return dot(order_ref[...], value, ((1,), (0,))).astype(BF16)


def by_rows(order_ref, field_ref, rows_ref):
    heights, lanes, _ = rows_ref.shape
    block = PACK * heights
    for first in range(0, lanes, PACK):
        moved = shuffle(order_ref, field_ref[first * heights : first * heights + block, :])
        for h in range(heights):
            rows_ref[h, first : first + PACK, :] = moved[h * PACK : (h + 1) * PACK]


def columns_kernel(field_ref, order_ref, table_ref, rows_ref, send_ref):
    heights, lanes, _ = rows_ref.shape
    by_rows(order_ref, field_ref, rows_ref)
    for h in range(heights):
        send_ref[:, h * lanes : (h + 1) * lanes] = dot(table_ref[...], rows_ref[h], ((1,), (1,))).astype(BF16)


def relayout_kernel(field_ref, order_ref, rows_ref):
    by_rows(order_ref, field_ref, rows_ref)


def shuffle_groups(order_ref, recv_ref):
    size = order_ref.shape[0]
    return [shuffle(order_ref, recv_ref[n : n + size, :]) for n in range(0, recv_ref.shape[0], size)]


def stack(groups, index, count, lanes):
    return jnp.concatenate(
        [
            group[index * count : (index + 1) * count, n : n + lanes]
            for n in range(0, groups[0].shape[1], lanes)
            for group in groups
        ],
        axis=0,
    )


def spectra_into(scale, owned, recv_ref, order_ref, rows_ref, spec_ref):
    count = order_ref.shape[0] // owned
    lanes = recv_ref.shape[1] * count // rows_ref.shape[0]
    ordered = [shuffle(order_ref, recv_ref[...])]
    for q in range(owned):
        stacked = stack(ordered, q, count, lanes)
        spec_ref[q * lanes : (q + 1) * lanes, :] = (
            scale * dot(stacked, rows_ref[...], ((0,), (0,)))
        ).astype(BF16)


def grad_spectra_kernel(scale, owned, recv_ref, order_ref, rows_ref, local_ref, spec_ref):
    spectra_into(scale, owned, recv_ref, order_ref, rows_ref, spec_ref)
    value = local_ref[...]
    high = value.astype(BF16)
    low = (value - high.astype(F32)).astype(BF16)
    spec_ref[spec_ref.shape[0] - value.shape[0] :, :] = jnp.concatenate([high, low], axis=1)


def send_inverse(back_ref, mixed, send_ref):
    @pl.when(pl.program_id(0) == pl.num_programs(0) - 1)
    def _():
        owned, lanes, _ = mixed.shape
        for q in range(owned):
            send_ref[:, q * lanes : (q + 1) * lanes] = dot(back_ref[...], mixed[q], ((1,), (1,))).astype(BF16)


def over_sublanes(repeat_ref, value):
    return dot(repeat_ref[...], value.astype(BF16), ((1,), (0,)))


def repeated(tile, extent):
    return jnp.concatenate([tile] * (extent // tile.shape[0]), axis=0)


def forward_kernel(scale, samples, owned, recv_ref, order_ref, rows_ref, back_ref, repeat_ref, weight_ref, *rest):
    spec_ref, send_ref, mixed, tiles, sums = rest
    _, channels, outs, both = weight_ref.shape
    half = both // 2
    lanes = mixed.shape[1]
    q = pl.program_id(0)

    @pl.when(q == 0)
    def _():
        spectra_into(scale, owned, recv_ref, order_ref, rows_ref, spec_ref)

    value = spec_ref[pl.ds(pl.multiple_of(q * lanes, lanes), lanes), :].astype(F32)
    other = pltpu.roll(value, half, 1)
    low = low_half(value.shape, half)
    real = jnp.where(low, value, other)
    imag = jnp.where(low, other, value)
    for s in range(samples):
        part = slice(s * channels, (s + 1) * channels)
        tiles[2 * s] = over_sublanes(repeat_ref, real[part])
        tiles[2 * s + 1] = over_sublanes(repeat_ref, imag[part])
    extent = outs // 2
    kinds = 2 * samples

    for first in range(0, outs, extent):

        def body(block, carry):
            totals = list(carry)
            for step in range(GROUP):
                c = block * GROUP + step
                weight = weight_ref[0, c, first : first + extent, :].astype(F32)
                for n in range(kinds):
                    tile = tiles[n, pl.ds(pl.multiple_of(c * ROWS, ROWS), ROWS), :]
                    totals[n] = totals[n] + weight * repeated(tile, extent)
            return tuple(totals)

        zero = jnp.zeros((extent, both), F32)
        totals = lax.fori_loop(0, channels // GROUP, body, (zero,) * kinds)
        for n in range(kinds):
            sums[n, first : first + extent, :] = totals[n]
    low = low_half((outs, both), half)
    result = []
    for s in range(samples):
        crossed = pltpu.roll(sums[2 * s + 1], half, 1)
        result.append(sums[2 * s] + jnp.where(low, -crossed, crossed))
    mixed[q] = jnp.concatenate(result, axis=0).astype(BF16)
    send_inverse(back_ref, mixed, send_ref)


def backward_kernel(samples, spec_ref, back_ref, weight_ref, send_ref, mixed, sums):
    _, channels, outs, both = weight_ref.shape
    half = both // 2
    lanes = mixed.shape[1]
    q = pl.program_id(0)
    value = spec_ref[pl.ds(pl.multiple_of(q * lanes, lanes), lanes), :].astype(F32)
    other = pltpu.roll(value, half, 1)
    low = low_half(value.shape, half)
    real = jnp.where(low, value, other)
    imag = jnp.where(low, other, value)
    grads = [part[s * outs : (s + 1) * outs] for s in range(samples) for part in (real, imag)]

    def body(block, carry):
        for step in range(GROUP):
            c = block * GROUP + step
            totals = [None] * len(grads)
            for o in range(0, outs, PACK):
                weight = weight_ref[0, c, o : o + PACK, :].astype(F32)
                for n, grad in enumerate(grads):
                    product = weight * grad[o : o + PACK]
                    part = product[:ROWS] + product[ROWS:]
                    totals[n] = part if totals[n] is None else totals[n] + part
            for n, total in enumerate(totals):
                sums[n, pl.ds(pl.multiple_of(c * ROWS, ROWS), ROWS), :] = total
        return carry

    lax.fori_loop(0, channels // GROUP, body, 0)
    low = low_half((channels, both), half)
    result = []
    for s in range(samples):
        straight, crossed = (
            sum(sums[n, pl.ds(row, channels, stride=ROWS), :] for row in range(ROWS)) for n in (2 * s, 2 * s + 1)
        )
        result.append(jnp.where(low, straight, -straight) + pltpu.roll(crossed, half, 1))
    mixed[q] = jnp.concatenate(result, axis=0).astype(BF16)
    send_inverse(back_ref, mixed, send_ref)


def pixels_kernel(scale, recv_ref, order_ref, back_ref, local_ref, field_ref, cot_ref, table_ref, grad_ref, send_ref):
    heights, lanes, _ = field_ref.shape
    count = order_ref.shape[0] // heights
    ordered = shuffle_groups(order_ref, recv_ref)
    for h in range(heights):
        inner = stack(ordered, h, count, lanes)
        pre = scale * dot(inner, back_ref[...], ((0,), (0,)))
        pre = pre + dot(local_ref[...], field_ref[h], ((1,), (0,)))
        grad = (cot_ref[h].astype(F32) * gelu_slope(pre)).astype(BF16)
        grad_ref[h] = grad
        send_ref[:, h * lanes : (h + 1) * lanes] = dot(table_ref[...], grad, ((1,), (1,))).astype(BF16)


def local_kernel(samples, field_ref, grad_ref, out_ref):
    heights, lanes, _ = field_ref.shape
    total = jnp.zeros((lanes, lanes), F32)
    for h in range(heights):
        total = total + dot(field_ref[h], grad_ref[h], ((1,), (1,)))
    size = lanes // samples
    out_ref[...] = sum(
        total[s * size : (s + 1) * size, s * size : (s + 1) * size] for s in range(samples)
    )


def final_kernel(scale, recv_ref, order_ref, back_ref, local_ref, grad_ref, restore_ref, out_ref, result):
    heights, lanes, _ = grad_ref.shape
    count = order_ref.shape[0] // heights
    ordered = shuffle_groups(order_ref, recv_ref)
    for h in range(heights):
        inner = stack(ordered, h, count, lanes)
        value = scale * dot(inner, back_ref[...], ((0,), (0,)))
        result[h] = (value + dot(local_ref[...], grad_ref[h], ((1,), (0,)))).astype(BF16)
    block = PACK * heights
    for first in range(0, lanes, PACK):
        part = jnp.concatenate([result[h, first : first + PACK, :] for h in range(heights)], axis=0)
        out_ref[first * heights : first * heights + block, :] = shuffle(restore_ref, part)


def outer_kernel(samples, spec_ref, grad_ref, pair_ref, repeat_ref, out_ref, local_ref, tiles, right):
    groups = spec_ref.shape[0]
    _, channels, outs, both = out_ref.shape
    half = both // 2
    low = low_half((channels, both), half)
    kinds = 2 * groups * samples

    @pl.when(pl.program_id(0) == 0)
    def _():
        pairs = 0.0
        for g in range(groups):
            pair = pair_ref[g].astype(F32)
            pairs = pairs + pair[:, :channels] + pair[:, channels : 2 * channels]
        local_ref[...] = pairs

    for g in range(groups):
        for s in range(samples):
            n = 2 * (g * samples + s)
            spec = spec_ref[g, s * channels : (s + 1) * channels, :].astype(F32)
            other = pltpu.roll(spec, half, 1)
            tiles[n] = over_sublanes(repeat_ref, jnp.where(low, spec, other))
            tiles[n + 1] = over_sublanes(repeat_ref, jnp.where(low, other, -spec))
            grad = grad_ref[g, s * outs : (s + 1) * outs, :].astype(F32)
            right[n] = grad
            right[n + 1] = pltpu.roll(grad, half, 1)

    for first in range(0, outs, PACK):
        strip = [right[n, first : first + PACK, :] for n in range(kinds)]

        def body(c, carry):
            total = None
            for n in range(kinds):
                tile = tiles[n, pl.ds(pl.multiple_of(c * ROWS, ROWS), ROWS), :]
                term = repeated(tile, PACK) * strip[n]
                total = term if total is None else total + term
            out_ref[0, c, first : first + PACK, :] = total
            return carry

        lax.fori_loop(0, channels, body, 0, unroll=4)


def whole(extent):
    return pl.BlockSpec(extent, lambda *_: (0,) * len(extent))


def call(kernel, name, operands, outs, scratch=(), grid=(1,), blocks=None, out_blocks=None):
    blocks, out_blocks = blocks or {}, out_blocks or {}
    in_specs = [blocks.get(n, whole(operand.shape)) for n, operand in enumerate(operands)]
    out_specs = [out_blocks.get(n, whole(out.shape)) for n, out in enumerate(outs)]
    return pl.pallas_call(
        kernel,
        out_shape=tuple(outs),
        grid=grid,
        in_specs=in_specs,
        out_specs=tuple(out_specs),
        scratch_shapes=list(scratch),
        compiler_params=pltpu.CompilerParams(vmem_limit_bytes=LIMIT),
        name=name,
    )(*operands)


def sum_over(values, axis):
    size = lax.axis_size(axis)
    step = 1
    while step < size:
        values = values + lax.ppermute(values, axis, [(i, i ^ step) for i in range(size)])
        step *= 2
    return values


def block_diagonal(matrix, copies):
    zero = jnp.zeros_like(matrix)
    return jnp.concatenate(
        [
            jnp.concatenate([matrix if i == j else zero for j in range(copies)], axis=1)
            for i in range(copies)
        ],
        axis=0,
    )


def shape(extent, kind=BF16):
    return jax.ShapeDtypeStruct(extent, kind)


def local(inputs, cotangent, mode_weight, local_weight):
    tiles = lax.axis_size("tile")
    samples, channels, th, width = inputs.shape
    owned, _, _, both = mode_weight.shape
    modes = both // 2
    lanes = samples * channels
    parts = width // 128
    spec_scale = 1.0 / math.sqrt(tiles * th * width)
    mode_scale = 1.0 / math.sqrt(modes * tiles * owned)
    send_cols, rows, back_rows, back_cols = tables(tiles, owned, th, width, modes)
    pixel_rows = samples * channels * th
    halves = tiles * padded(2 * owned)
    inverse = 2 * tiles * th

    def exchange(values):
        split = values.reshape(tiles, values.shape[0] // tiles, values.shape[1])
        moved = lax.all_to_all(split, "tile", split_axis=0, concat_axis=0, tiled=False)
        return moved.reshape(values.shape)

    forward_mix = block_diagonal(local_weight.T, samples)
    backward_mix = block_diagonal(local_weight, samples)
    by_row = order(PACK, th)
    by_channel = order(th, PACK)
    by_mode = mode_order(tiles, owned)
    by_height = order(2 * min(tiles, 8), th)
    mixed = pltpu.VMEM((owned, lanes, both), BF16)
    weight_block = pl.BlockSpec((1,) + mode_weight.shape[1:], lambda q: (q, 0, 0, 0))
    repeat = constant(np.repeat(np.eye(channels), ROWS, axis=0))
    to_modes = shape((halves, th * lanes))
    to_pixels = shape((inverse, owned * lanes))
    field_shape = shape((th, lanes, width))

    field_rows, send = call(
        columns_kernel,
        "columns",
        (inputs.reshape(pixel_rows, width), by_row, send_cols),
        (field_shape, to_modes),
    )
    arrived = exchange(send)
    (cot_rows,) = call(
        relayout_kernel, "relayout", (cotangent.reshape(pixel_rows, width), by_row), (field_shape,)
    )
    spectra, send = call(
        functools.partial(forward_kernel, spec_scale, samples, owned),
        "mix_forward",
        (arrived, by_mode, rows, back_rows, repeat, mode_weight),
        (shape((owned * lanes, both)), to_pixels),
        [
            mixed,
            pltpu.VMEM((2 * samples, channels * ROWS, both), F32),
            pltpu.VMEM((2 * samples, channels, both), F32),
        ],
        grid=(owned,),
        blocks={5: weight_block},
    )
    all_spectra = lax.all_gather(spectra, "dp")
    arrived = exchange(send)
    gate_rows, send = call(
        functools.partial(pixels_kernel, mode_scale),
        "pixels",
        (arrived, by_height, back_cols, forward_mix, field_rows, cot_rows, send_cols),
        (field_shape, to_modes),
    )
    arrived = exchange(send)
    (local_sum,) = call(
        functools.partial(local_kernel, samples),
        "local_grad",
        (field_rows, gate_rows),
        (shape((channels, channels), F32),),
    )
    local_sum = sum_over(local_sum, "tile")
    (grad_spectra,) = call(
        functools.partial(grad_spectra_kernel, mode_scale, owned),
        "grad_spectra",
        (arrived, by_mode, rows, local_sum),
        (shape((owned * lanes + channels, both)),),
    )
    all_grads = lax.all_gather(grad_spectra, "dp")
    (send,) = call(
        functools.partial(backward_kernel, samples),
        "mix_backward",
        (grad_spectra, back_rows, mode_weight),
        (to_pixels,),
        [mixed, pltpu.VMEM((2 * samples, channels * ROWS, both), F32)],
        grid=(owned,),
        blocks={2: weight_block},
    )
    arrived = exchange(send)

    groups = lax.axis_size("dp")
    kinds = 2 * groups * samples
    per_mode = pl.BlockSpec((groups, lanes, both), lambda q: (0, q, 0))
    below = owned * lanes // channels
    mode_grad, local_grad = call(
        functools.partial(outer_kernel, samples),
        "mode_grad",
        (all_spectra, all_grads, all_grads, repeat),
        (shape(mode_weight.shape, F32), shape((channels, channels), F32)),
        [pltpu.VMEM((kinds, channels * ROWS, both), F32), pltpu.VMEM((kinds, channels, both), F32)],
        grid=(owned,),
        blocks={
            0: per_mode,
            1: per_mode,
            2: pl.BlockSpec((groups, channels, both), lambda q: (0, below, 0)),
        },
        out_blocks={0: weight_block},
    )
    arrived, mode_grad = lax.optimization_barrier((arrived, mode_grad))

    (input_grad,) = call(
        functools.partial(final_kernel, spec_scale),
        "final",
        (arrived, by_height, back_cols, backward_mix, gate_rows, by_channel),
        (shape((pixel_rows, width)),),
        [pltpu.VMEM((th, lanes, width), BF16)],
    )
    return (input_grad.reshape(inputs.shape), mode_grad, local_grad)


def solution(mesh):
    return jax.shard_map(
        local,
        mesh=mesh,
        in_specs=(
            P("dp", None, "tile", None),
            P("dp", None, "tile", None),
            P("tile", None, None, None),
            P(),
        ),
        out_specs=(P("dp", None, "tile", None), P("tile", None, None, None), P()),
        check_vma=False,
    )
```

```python
import functools
import math

import jax
import jax.numpy as jnp
import numpy as np
from jax import lax
from jax.experimental import pallas as pl
from jax.experimental.pallas import tpu as pltpu
from jax.sharding import PartitionSpec as P

F32 = jnp.float32
BF16 = jnp.bfloat16
LIMIT = 56 * 1024 * 1024
ROWS = 8
PACK = 16
GROUP = 8


def row_tables(height, modes):
    index = np.arange(modes)
    signed = np.where(index < modes // 2, index, index - modes)
    phases = np.mod(np.arange(height)[:, None] * signed[None, :], height)
    angles = phases * (2.0 * math.pi / height)
    return np.cos(angles), np.sin(angles)


def column_tables(width, modes):
    phases = np.mod(np.arange(modes)[:, None] * np.arange(width)[None, :], width)
    angles = phases * (2.0 * math.pi / width)
    return np.stack([np.cos(angles), -np.sin(angles)])


def constant(table):
    return jnp.asarray(np.asarray(table, np.float32)).astype(BF16)


def tables(tiles, owned, th, width, modes):
    cols = column_tables(width, tiles * owned)
    split = cols.reshape(2, tiles, owned, width)
    send_cols = split.transpose(1, 0, 2, 3).reshape(tiles, 2 * owned, width)
    send_cols = np.pad(send_cols, ((0, 0), (0, padded(2 * owned) - 2 * owned), (0, 0))).reshape(-1, width)
    back_cols = split.transpose(2, 1, 0, 3).reshape(-1, width)
    cosine, sine = row_tables(th * tiles, modes)
    real = np.concatenate([cosine, -sine], axis=1)
    imag = np.concatenate([sine, cosine], axis=1)
    pair = np.stack([real, imag]).reshape(2, tiles, th, 2 * modes)
    rows = pair.transpose(2, 1, 0, 3).reshape(-1, 2 * modes)
    back_rows = pair.transpose(1, 0, 2, 3).reshape(-1, 2 * modes)
    return constant(send_cols), constant(rows), constant(back_rows), constant(back_cols)


def padded(rows):
    return -(-rows // PACK) * PACK


def order(outer, inner):
    take = np.arange(outer * inner).reshape(outer, inner).T.reshape(-1)
    return constant(np.eye(outer * inner)[take])


def mode_order(tiles, owned):
    rows = np.arange(tiles * padded(2 * owned)).reshape(tiles, -1)
    take = rows[:, : 2 * owned].reshape(tiles, 2, owned).transpose(2, 0, 1).reshape(-1)
    return constant(np.eye(rows.size)[take])


def dot(left, right, dims):
    return lax.dot_general(left, right, (dims, ((), ())), preferred_element_type=F32)


def low_half(shape, half):
    return lax.broadcasted_iota(jnp.int32, shape, 1) < half


def gelu_slope(values):
    size = jnp.abs(values)
    expo = jnp.exp(-0.5 * values * values)
    t = 1.0 / (1.0 + (0.3275911 / math.sqrt(2.0)) * size)
    poly = 0.5 * 1.061405429
    for factor in (-1.453152027, 1.421413741, -0.284496736, 0.254829592):
        poly = poly * t + 0.5 * factor
    tail = poly * t * expo
    cumulative = jnp.where(values < 0.0, tail, 1.0 - tail)
    return cumulative + values * expo * (1.0 / math.sqrt(2.0 * math.pi))


def shuffle(order_ref, value):
    return dot(order_ref[...], value, ((1,), (0,))).astype(BF16)


def by_rows(order_ref, field_ref, rows_ref):
    heights, lanes, _ = rows_ref.shape
    block = PACK * heights
    for first in range(0, lanes, PACK):
        moved = shuffle(order_ref, field_ref[first * heights : first * heights + block, :])
        for h in range(heights):
            rows_ref[h, first : first + PACK, :] = moved[h * PACK : (h + 1) * PACK]


def columns_kernel(field_ref, order_ref, table_ref, rows_ref, send_ref):
    heights, lanes, _ = rows_ref.shape
    by_rows(order_ref, field_ref, rows_ref)
    for h in range(heights):
        send_ref[:, h * lanes : (h + 1) * lanes] = dot(table_ref[...], rows_ref[h], ((1,), (1,))).astype(BF16)


def relayout_kernel(field_ref, order_ref, rows_ref):
    by_rows(order_ref, field_ref, rows_ref)


def shuffle_groups(order_ref, recv_ref):
    size = order_ref.shape[0]
    return [shuffle(order_ref, recv_ref[n : n + size, :]) for n in range(0, recv_ref.shape[0], size)]


def stack(groups, index, count, lanes):
    return jnp.concatenate(
        [
            group[index * count : (index + 1) * count, n : n + lanes]
            for n in range(0, groups[0].shape[1], lanes)
            for group in groups
        ],
        axis=0,
    )


def spectra_into(scale, owned, recv_ref, order_ref, rows_ref, spec_ref):
    count = order_ref.shape[0] // owned
    lanes = recv_ref.shape[1] * count // rows_ref.shape[0]
    ordered = [shuffle(order_ref, recv_ref[...])]
    for q in range(owned):
        stacked = stack(ordered, q, count, lanes)
        spec_ref[q * lanes : (q + 1) * lanes, :] = (
            scale * dot(stacked, rows_ref[...], ((0,), (0,)))
        ).astype(BF16)


def grad_spectra_kernel(scale, owned, recv_ref, order_ref, rows_ref, local_ref, spec_ref):
    spectra_into(scale, owned, recv_ref, order_ref, rows_ref, spec_ref)
    value = local_ref[...]
    high = value.astype(BF16)
    low = (value - high.astype(F32)).astype(BF16)
    spec_ref[spec_ref.shape[0] - value.shape[0] :, :] = jnp.concatenate([high, low], axis=1)


def send_inverse(back_ref, mixed, send_ref):
    @pl.when(pl.program_id(0) == pl.num_programs(0) - 1)
    def _():
        owned, lanes, _ = mixed.shape
        for q in range(owned):
            send_ref[:, q * lanes : (q + 1) * lanes] = dot(back_ref[...], mixed[q], ((1,), (1,))).astype(BF16)


def tree(terms):
    while len(terms) > 1:
        terms = [a + b for a, b in zip(terms[0::2], terms[1::2])]
    return terms[0]


def packed_row(store, index):
    row = store[pl.ds(index, 1), :]
    return jnp.broadcast_to(row, (PACK, row.shape[1])).astype(BF16)


def duplicates(spec, half):
    value = spec.astype(F32)
    other = pltpu.roll(value, half, 1)
    low = low_half(value.shape, half)
    return jnp.where(low, value, other), jnp.where(low, other, value)


def forward_kernel(scale, samples, owned, recv_ref, order_ref, rows_ref, back_ref, weight_ref, *rest):
    spec_ref, send_ref, mixed, real, imag, sums = rest
    _, channels, outs, both = weight_ref.shape
    half = both // 2
    lanes = mixed.shape[1]
    q = pl.program_id(0)

    @pl.when(q == 0)
    def _():
        spectra_into(scale, owned, recv_ref, order_ref, rows_ref, spec_ref)

    spec = spec_ref[pl.ds(pl.multiple_of(q * lanes, lanes), lanes), :]
    real[...], imag[...] = duplicates(spec, half)
    sums[...] = jnp.zeros_like(sums)

    def body(block, carry):
        first = block * GROUP
        rows = [
            [packed_row(store, s * channels + first + step) for step in range(GROUP)]
            for s in range(samples)
            for store in (real, imag)
        ]
        for o in range(0, outs, PACK):
            weights = [weight_ref[0, first + step, o : o + PACK, :] for step in range(GROUP)]
            for n, row in enumerate(rows):
                total = tree([w * r for w, r in zip(weights, row)])
                sums[n, o : o + PACK, :] += total.astype(F32)
        return carry

    lax.fori_loop(0, channels // GROUP, body, 0)
    low = low_half((outs, both), half)
    result = []
    for s in range(samples):
        crossed = pltpu.roll(sums[2 * s + 1], half, 1)
        result.append(sums[2 * s] + jnp.where(low, -crossed, crossed))
    mixed[q] = jnp.concatenate(result, axis=0).astype(BF16)
    send_inverse(back_ref, mixed, send_ref)


def backward_kernel(samples, spec_ref, back_ref, weight_ref, send_ref, mixed, sums):
    _, channels, outs, both = weight_ref.shape
    half = both // 2
    lanes = mixed.shape[1]
    q = pl.program_id(0)
    spec = spec_ref[pl.ds(pl.multiple_of(q * lanes, lanes), lanes), :]
    parts = [part.astype(BF16) for part in duplicates(spec, half)]
    grads = [
        [part[s * outs + o : s * outs + o + PACK] for o in range(0, outs, PACK)]
        for s in range(samples)
        for part in parts
    ]

    def body(block, carry):
        for step in range(GROUP):
            c = block * GROUP + step
            weights = [weight_ref[0, c, o : o + PACK, :] for o in range(0, outs, PACK)]
            for n, grad in enumerate(grads):
                total = tree([w * g for w, g in zip(weights, grad)]).astype(F32)
                sums[n, pl.ds(pl.multiple_of(c * ROWS, ROWS), ROWS), :] = total[:ROWS] + total[ROWS:]
        return carry

    lax.fori_loop(0, channels // GROUP, body, 0)
    low = low_half((channels, both), half)
    result = []
    for s in range(samples):
        straight, crossed = (
            sum(sums[n, pl.ds(row, channels, stride=ROWS), :] for row in range(ROWS)) for n in (2 * s, 2 * s + 1)
        )
        result.append(jnp.where(low, straight, -straight) + pltpu.roll(crossed, half, 1))
    mixed[q] = jnp.concatenate(result, axis=0).astype(BF16)
    send_inverse(back_ref, mixed, send_ref)


def pixels_kernel(scale, heights, recv_ref, order_ref, back_ref, local_ref, field_ref, cot_ref, table_ref, *rest):
    grad_ref, send_ref, ordered = rest
    steps, lanes, _ = field_ref.shape
    count = order_ref.shape[0] // heights
    size = order_ref.shape[0]
    group = pl.program_id(0)

    @pl.when(group == 0)
    def _():
        for n in range(0, recv_ref.shape[0], size):
            ordered[n : n + size, :] = shuffle(order_ref, recv_ref[n : n + size, :])

    for step in range(steps):
        parts = []
        for n in range(0, recv_ref.shape[0], size):
            first = pl.multiple_of(n + (group * steps + step) * count, count)
            parts.append(ordered[pl.ds(first, count), :])
        inner = stack(parts, 0, count, lanes)
        pre = scale * dot(inner, back_ref[...], ((0,), (0,)))
        pre = pre + dot(local_ref[...], field_ref[step], ((1,), (0,)))
        grad = (cot_ref[step].astype(F32) * gelu_slope(pre)).astype(BF16)
        grad_ref[step] = grad
        send_ref[:, step * lanes : (step + 1) * lanes] = dot(table_ref[...], grad, ((1,), (1,))).astype(BF16)


def local_kernel(samples, field_ref, grad_ref, out_ref):
    heights, lanes, _ = field_ref.shape
    total = jnp.zeros((lanes, lanes), F32)
    for h in range(heights):
        total = total + dot(field_ref[h], grad_ref[h], ((1,), (1,)))
    size = lanes // samples
    out_ref[...] = sum(
        total[s * size : (s + 1) * size, s * size : (s + 1) * size] for s in range(samples)
    )


def final_kernel(scale, recv_ref, order_ref, back_ref, local_ref, grad_ref, restore_ref, out_ref, result):
    heights, lanes, _ = grad_ref.shape
    count = order_ref.shape[0] // heights
    ordered = shuffle_groups(order_ref, recv_ref)
    for h in range(heights):
        inner = stack(ordered, h, count, lanes)
        value = scale * dot(inner, back_ref[...], ((0,), (0,)))
        result[h] = (value + dot(local_ref[...], grad_ref[h], ((1,), (0,)))).astype(BF16)
    block = PACK * heights
    for first in range(0, lanes, PACK):
        part = jnp.concatenate([result[h, first : first + PACK, :] for h in range(heights)], axis=0)
        out_ref[first * heights : first * heights + block, :] = shuffle(restore_ref, part)


def outer_kernel(samples, spec_ref, grad_ref, pair_ref, out_ref, local_ref, real, imag, plain, crossed):
    groups = spec_ref.shape[0]
    _, channels, outs, both = out_ref.shape
    half = both // 2
    low = low_half((channels, both), half)
    total = groups * samples

    @pl.when(pl.program_id(0) == 0)
    def _():
        pairs = 0.0
        for g in range(groups):
            pair = pair_ref[g].astype(F32)
            pairs = pairs + pair[:, :channels] + pair[:, channels : 2 * channels]
        local_ref[...] = pairs

    for g in range(groups):
        for s in range(samples):
            n = g * samples + s
            spec = spec_ref[g, s * channels : (s + 1) * channels, :].astype(F32)
            other = pltpu.roll(spec, half, 1)
            real[n] = jnp.where(low, spec, other)
            imag[n] = jnp.where(low, other, -spec)
            grad = grad_ref[g, s * outs : (s + 1) * outs, :]
            plain[n] = grad
            crossed[n] = pltpu.roll(grad.astype(F32), half, 1).astype(BF16)

    def body(c, carry):
        left = [packed_row(store.at[n], c) for n in range(total) for store in (real, imag)]
        for o in range(0, outs, PACK):
            right = [store[n, o : o + PACK, :] for n in range(total) for store in (plain, crossed)]
            out_ref[0, c, o : o + PACK, :] = tree([a * b for a, b in zip(left, right)]).astype(F32)
        return carry

    lax.fori_loop(0, channels, body, 0, unroll=2)


IN_VMEM = pl.BlockSpec(memory_space=pltpu.VMEM)


def whole(extent):
    return pl.BlockSpec(extent, lambda *_: (0,) * len(extent))


def call(kernel, name, operands, outs, scratch=(), grid=(1,), blocks=None, out_blocks=None):
    blocks, out_blocks = blocks or {}, out_blocks or {}
    in_specs = [blocks.get(n) or whole(operand.shape) for n, operand in enumerate(operands)]
    out_specs = [out_blocks.get(n, whole(out.shape)) for n, out in enumerate(outs)]
    return pl.pallas_call(
        kernel,
        out_shape=tuple(outs),
        grid=grid,
        in_specs=in_specs,
        out_specs=tuple(out_specs),
        scratch_shapes=list(scratch),
        compiler_params=pltpu.CompilerParams(vmem_limit_bytes=LIMIT),
        name=name,
    )(*operands)


def sum_over(values, axis):
    size = lax.axis_size(axis)
    step = 1
    while step < size:
        values = values + lax.ppermute(values, axis, [(i, i ^ step) for i in range(size)])
        step *= 2
    return values


def block_diagonal(matrix, copies):
    zero = jnp.zeros_like(matrix)
    return jnp.concatenate(
        [
            jnp.concatenate([matrix if i == j else zero for j in range(copies)], axis=1)
            for i in range(copies)
        ],
        axis=0,
    )


def shape(extent, kind=BF16):
    return jax.ShapeDtypeStruct(extent, kind)


def local(inputs, cotangent, mode_weight, local_weight):
    tiles = lax.axis_size("tile")
    samples, channels, th, width = inputs.shape
    owned, _, _, both = mode_weight.shape
    modes = both // 2
    lanes = samples * channels
    parts = width // 128
    spec_scale = 1.0 / math.sqrt(tiles * th * width)
    mode_scale = 1.0 / math.sqrt(modes * tiles * owned)
    send_cols, rows, back_rows, back_cols = tables(tiles, owned, th, width, modes)
    pixel_rows = samples * channels * th
    halves = tiles * padded(2 * owned)
    inverse = 2 * tiles * th

    def exchange(values):
        split = values.reshape(tiles, values.shape[0] // tiles, values.shape[1])
        moved = lax.all_to_all(split, "tile", split_axis=0, concat_axis=0, tiled=False)
        return moved.reshape(values.shape)

    forward_mix = block_diagonal(local_weight.T, samples)
    backward_mix = block_diagonal(local_weight, samples)
    by_row = order(PACK, th)
    by_channel = order(th, PACK)
    by_mode = mode_order(tiles, owned)
    by_height = order(2 * min(tiles, 8), th)
    mixed = pltpu.VMEM((owned, lanes, both), BF16)
    weight_block = pl.BlockSpec((1,) + mode_weight.shape[1:], lambda q: (q, 0, 0, 0))
    to_modes = shape((halves, th * lanes))
    to_pixels = shape((inverse, owned * lanes))
    field_shape = shape((th, lanes, width))

    field_rows, send = call(
        columns_kernel,
        "columns",
        (inputs.reshape(pixel_rows, width), by_row, send_cols),
        (field_shape, to_modes),
    )
    arrived = exchange(send)
    (cot_rows,) = call(
        relayout_kernel, "relayout", (cotangent.reshape(pixel_rows, width), by_row), (field_shape,)
    )
    spectra, send = call(
        functools.partial(forward_kernel, spec_scale, samples, owned),
        "mix_forward",
        (arrived, by_mode, rows, back_rows, mode_weight),
        (shape((owned * lanes, both)), to_pixels),
        [
            mixed,
            pltpu.VMEM((lanes, both), F32),
            pltpu.VMEM((lanes, both), F32),
            pltpu.VMEM((2 * samples, channels, both), F32),
        ],
        grid=(owned,),
        blocks={0: IN_VMEM, 4: weight_block},
    )
    all_spectra = lax.all_gather(spectra, "dp")
    arrived = exchange(send)
    steps = 4
    row_block = pl.BlockSpec((steps, lanes, width), lambda n: (n, 0, 0))
    gate_rows, send = call(
        functools.partial(pixels_kernel, mode_scale, th),
        "pixels",
        (arrived, by_height, back_cols, forward_mix, field_rows, cot_rows, send_cols),
        (field_shape, to_modes),
        [pltpu.VMEM((inverse, owned * lanes), BF16)],
        grid=(th // steps,),
        blocks={0: IN_VMEM, 4: row_block, 5: row_block},
        out_blocks={0: row_block, 1: pl.BlockSpec((halves, steps * lanes), lambda n: (0, n))},
    )
    arrived = exchange(send)
    (local_sum,) = call(
        functools.partial(local_kernel, samples),
        "local_grad",
        (field_rows, gate_rows),
        (shape((channels, channels), F32),),
    )
    local_sum = sum_over(local_sum, "tile")
    (grad_spectra,) = call(
        functools.partial(grad_spectra_kernel, mode_scale, owned),
        "grad_spectra",
        (arrived, by_mode, rows, local_sum),
        (shape((owned * lanes + channels, both)),),
        blocks={0: IN_VMEM},
    )
    all_grads = lax.all_gather(grad_spectra, "dp")
    (send,) = call(
        functools.partial(backward_kernel, samples),
        "mix_backward",
        (grad_spectra, back_rows, mode_weight),
        (to_pixels,),
        [mixed, pltpu.VMEM((2 * samples, channels * ROWS, both), F32)],
        grid=(owned,),
        blocks={2: weight_block},
    )
    arrived = exchange(send)

    groups = lax.axis_size("dp")
    total = groups * samples
    per_mode = pl.BlockSpec((groups, lanes, both), lambda q: (0, q, 0))
    below = owned * lanes // channels
    mode_grad, local_grad = call(
        functools.partial(outer_kernel, samples),
        "mode_grad",
        (all_spectra, all_grads, all_grads),
        (shape(mode_weight.shape, F32), shape((channels, channels), F32)),
        [pltpu.VMEM((total, channels, both), F32)] * 2 + [pltpu.VMEM((total, channels, both), BF16)] * 2,
        grid=(owned,),
        blocks={
            0: per_mode,
            1: per_mode,
            2: pl.BlockSpec((groups, channels, both), lambda q: (0, below, 0)),
        },
        out_blocks={0: weight_block},
    )
    arrived, mode_grad = lax.optimization_barrier((arrived, mode_grad))

    (input_grad,) = call(
        functools.partial(final_kernel, spec_scale),
        "final",
        (arrived, by_height, back_cols, backward_mix, gate_rows, by_channel),
        (shape((pixel_rows, width)),),
        [pltpu.VMEM((th, lanes, width), BF16)],
        blocks={0: IN_VMEM},
    )
    return (input_grad.reshape(inputs.shape), mode_grad, local_grad)


def solution(mesh):
    return jax.shard_map(
        local,
        mesh=mesh,
        in_specs=(
            P("dp", None, "tile", None),
            P("dp", None, "tile", None),
            P("tile", None, None, None),
            P(),
        ),
        out_specs=(P("dp", None, "tile", None), P("tile", None, None, None), P()),
        check_vma=False,
    )
```

```python
import functools
import math

import jax
import jax.numpy as jnp
import numpy as np
from jax import lax
from jax.experimental import pallas as pl
from jax.experimental.pallas import tpu as pltpu
from jax.sharding import PartitionSpec as P

F32 = jnp.float32
BF16 = jnp.bfloat16
LIMIT = 56 * 1024 * 1024
ROWS = 8
PACK = 16
GROUP = 8
SPLIT = 4


def row_tables(height, modes):
    index = np.arange(modes)
    signed = np.where(index < modes // 2, index, index - modes)
    phases = np.mod(np.arange(height)[:, None] * signed[None, :], height)
    angles = phases * (2.0 * math.pi / height)
    return np.cos(angles), np.sin(angles)


def column_tables(width, modes):
    phases = np.mod(np.arange(modes)[:, None] * np.arange(width)[None, :], width)
    angles = phases * (2.0 * math.pi / width)
    return np.stack([np.cos(angles), -np.sin(angles)])


def constant(table):
    return jnp.asarray(np.asarray(table, np.float32)).astype(BF16)


def tables(tiles, owned, th, width, modes):
    cols = column_tables(width, tiles * owned)
    split = cols.reshape(2, tiles, owned, width)
    send_cols = split.transpose(1, 0, 2, 3).reshape(tiles, 2 * owned, width)
    send_cols = np.pad(send_cols, ((0, 0), (0, padded(2 * owned) - 2 * owned), (0, 0))).reshape(-1, width)
    back_cols = split.transpose(2, 1, 0, 3).reshape(-1, width)
    cosine, sine = row_tables(th * tiles, modes)
    real = np.concatenate([cosine, -sine], axis=1)
    imag = np.concatenate([sine, cosine], axis=1)
    pair = np.stack([real, imag]).reshape(2, tiles, th, 2 * modes)
    rows = pair.transpose(2, 1, 0, 3).reshape(-1, 2 * modes)
    back_rows = pair.transpose(1, 0, 2, 3).reshape(-1, 2 * modes)
    return constant(send_cols), constant(rows), constant(back_rows), constant(back_cols)


def padded(rows):
    return -(-rows // PACK) * PACK


def order(outer, inner):
    take = np.arange(outer * inner).reshape(outer, inner).T.reshape(-1)
    return constant(np.eye(outer * inner)[take])


def mode_order(tiles, owned):
    rows = np.arange(tiles * padded(2 * owned)).reshape(tiles, -1)
    take = rows[:, : 2 * owned].reshape(tiles, 2, owned).transpose(2, 0, 1).reshape(-1)
    return constant(np.eye(rows.size)[take])


def dot(left, right, dims):
    return lax.dot_general(left, right, (dims, ((), ())), preferred_element_type=F32)


def low_half(shape, half):
    return lax.broadcasted_iota(jnp.int32, shape, 1) < half


def gelu_slope(values):
    size = jnp.abs(values)
    expo = jnp.exp(-0.5 * values * values)
    t = 1.0 / (1.0 + (0.3275911 / math.sqrt(2.0)) * size)
    poly = 0.5 * 1.061405429
    for factor in (-1.453152027, 1.421413741, -0.284496736, 0.254829592):
        poly = poly * t + 0.5 * factor
    tail = poly * t * expo
    cumulative = jnp.where(values < 0.0, tail, 1.0 - tail)
    return cumulative + values * expo * (1.0 / math.sqrt(2.0 * math.pi))


def shuffle(order_ref, value):
    return dot(order_ref[...], value, ((1,), (0,))).astype(BF16)


def by_rows(order_ref, field_refs, rows_ref):
    heights, lanes, _ = rows_ref.shape
    block = PACK * heights
    quarter = lanes // len(field_refs)
    for first in range(0, lanes, PACK):
        start = first % quarter * heights
        moved = shuffle(order_ref, field_refs[first // quarter][start : start + block, :])
        for h in range(heights):
            rows_ref[h, first : first + PACK, :] = moved[h * PACK : (h + 1) * PACK]


def columns_kernel(order_ref, table_ref, *rest):
    field_refs, (rows_ref, send_ref) = rest[:SPLIT], rest[SPLIT:]
    heights, lanes, _ = rows_ref.shape
    by_rows(order_ref, field_refs, rows_ref)
    for h in range(heights):
        send_ref[:, h * lanes : (h + 1) * lanes] = dot(table_ref[...], rows_ref[h], ((1,), (1,))).astype(BF16)


def relayout_kernel(order_ref, *rest):
    by_rows(order_ref, rest[:SPLIT], rest[SPLIT])


def shuffle_groups(order_ref, recv_ref):
    size = order_ref.shape[0]
    return [shuffle(order_ref, recv_ref[n : n + size, :]) for n in range(0, recv_ref.shape[0], size)]


def stack(groups, index, count, lanes):
    return jnp.concatenate(
        [
            group[index * count : (index + 1) * count, n : n + lanes]
            for n in range(0, groups[0].shape[1], lanes)
            for group in groups
        ],
        axis=0,
    )


def spectra_into(scale, owned, recv_ref, order_ref, rows_ref, spec_ref):
    count = order_ref.shape[0] // owned
    lanes = recv_ref.shape[1] * count // rows_ref.shape[0]
    ordered = [shuffle(order_ref, recv_ref[...])]
    for q in range(owned):
        stacked = stack(ordered, q, count, lanes)
        spec_ref[q * lanes : (q + 1) * lanes, :] = (
            scale * dot(stacked, rows_ref[...], ((0,), (0,)))
        ).astype(BF16)


def grad_spectra_kernel(scale, owned, recv_ref, order_ref, rows_ref, local_ref, spec_ref):
    spectra_into(scale, owned, recv_ref, order_ref, rows_ref, spec_ref)
    value = local_ref[...]
    high = value.astype(BF16)
    low = (value - high.astype(F32)).astype(BF16)
    spec_ref[spec_ref.shape[0] - value.shape[0] :, :] = jnp.concatenate([high, low], axis=1)


def send_inverse(back_ref, mixed, send_ref):
    @pl.when(pl.program_id(0) == pl.num_programs(0) - 1)
    def _():
        owned, lanes, _ = mixed.shape
        for q in range(owned):
            send_ref[:, q * lanes : (q + 1) * lanes] = dot(back_ref[...], mixed[q], ((1,), (1,))).astype(BF16)


def tree(terms):
    while len(terms) > 1:
        terms = [a + b for a, b in zip(terms[0::2], terms[1::2])]
    return terms[0]


def packed_row(store, index):
    row = store[pl.ds(index, 1), :]
    return jnp.broadcast_to(row, (PACK, row.shape[1])).astype(BF16)


def duplicates(spec, half):
    value = spec.astype(F32)
    other = pltpu.roll(value, half, 1)
    low = low_half(value.shape, half)
    return jnp.where(low, value, other), jnp.where(low, other, value)


def forward_kernel(scale, samples, owned, recv_ref, order_ref, rows_ref, back_ref, *rest):
    weight_refs, (spec_ref, send_ref, mixed, real, imag, sums) = rest[:SPLIT], rest[SPLIT:]
    _, quarter, outs, both = weight_refs[0].shape
    channels = quarter * SPLIT
    half = both // 2
    lanes = mixed.shape[1]
    q = pl.program_id(0)

    @pl.when(q == 0)
    def _():
        spectra_into(scale, owned, recv_ref, order_ref, rows_ref, spec_ref)

    spec = spec_ref[pl.ds(pl.multiple_of(q * lanes, lanes), lanes), :]
    real[...], imag[...] = duplicates(spec, half)
    sums[...] = jnp.zeros_like(sums)

    for part, weight_ref in enumerate(weight_refs):

        def body(block, carry):
            first = block * GROUP
            rows = [
                [packed_row(store, s * channels + part * quarter + first + step) for step in range(GROUP)]
                for s in range(samples)
                for store in (real, imag)
            ]
            for o in range(0, outs, PACK):
                weights = [weight_ref[0, first + step, o : o + PACK, :] for step in range(GROUP)]
                for n, row in enumerate(rows):
                    total = tree([w * r for w, r in zip(weights, row)])
                    sums[n, o : o + PACK, :] += total.astype(F32)
            return carry

        lax.fori_loop(0, quarter // GROUP, body, 0)
    low = low_half((outs, both), half)
    result = []
    for s in range(samples):
        crossed = pltpu.roll(sums[2 * s + 1], half, 1)
        result.append(sums[2 * s] + jnp.where(low, -crossed, crossed))
    mixed[q] = jnp.concatenate(result, axis=0).astype(BF16)
    send_inverse(back_ref, mixed, send_ref)


def backward_kernel(samples, spec_ref, back_ref, *rest):
    weight_refs, (send_ref, mixed, sums) = rest[:SPLIT], rest[SPLIT:]
    _, quarter, outs, both = weight_refs[0].shape
    channels = quarter * SPLIT
    half = both // 2
    lanes = mixed.shape[1]
    q = pl.program_id(0)
    spec = spec_ref[pl.ds(pl.multiple_of(q * lanes, lanes), lanes), :]
    parts = [part.astype(BF16) for part in duplicates(spec, half)]
    grads = [
        [part[s * outs + o : s * outs + o + PACK] for o in range(0, outs, PACK)]
        for s in range(samples)
        for part in parts
    ]

    for part, weight_ref in enumerate(weight_refs):

        def body(block, carry):
            for step in range(GROUP):
                c = block * GROUP + step
                weights = [weight_ref[0, c, o : o + PACK, :] for o in range(0, outs, PACK)]
                for n, grad in enumerate(grads):
                    total = tree([w * g for w, g in zip(weights, grad)]).astype(F32)
                    row = pl.multiple_of((part * quarter + c) * ROWS, ROWS)
                    sums[n, pl.ds(row, ROWS), :] = total[:ROWS] + total[ROWS:]
            return carry

        lax.fori_loop(0, quarter // GROUP, body, 0)
    low = low_half((channels, both), half)
    result = []
    for s in range(samples):
        straight, crossed = (
            sum(sums[n, pl.ds(row, channels, stride=ROWS), :] for row in range(ROWS)) for n in (2 * s, 2 * s + 1)
        )
        result.append(jnp.where(low, straight, -straight) + pltpu.roll(crossed, half, 1))
    mixed[q] = jnp.concatenate(result, axis=0).astype(BF16)
    send_inverse(back_ref, mixed, send_ref)


def pixels_kernel(scale, heights, recv_ref, order_ref, back_ref, local_ref, field_ref, cot_ref, table_ref, *rest):
    grad_ref, send_ref, ordered = rest
    steps, lanes, _ = field_ref.shape
    count = order_ref.shape[0] // heights
    size = order_ref.shape[0]
    group = pl.program_id(0)

    @pl.when(group == 0)
    def _():
        for n in range(0, recv_ref.shape[0], size):
            ordered[n : n + size, :] = shuffle(order_ref, recv_ref[n : n + size, :])

    for step in range(steps):
        parts = []
        for n in range(0, recv_ref.shape[0], size):
            first = pl.multiple_of(n + (group * steps + step) * count, count)
            parts.append(ordered[pl.ds(first, count), :])
        inner = stack(parts, 0, count, lanes)
        pre = scale * dot(inner, back_ref[...], ((0,), (0,)))
        pre = pre + dot(local_ref[...], field_ref[step], ((1,), (0,)))
        grad = (cot_ref[step].astype(F32) * gelu_slope(pre)).astype(BF16)
        grad_ref[step] = grad
        send_ref[:, step * lanes : (step + 1) * lanes] = dot(table_ref[...], grad, ((1,), (1,))).astype(BF16)


def local_kernel(samples, field_ref, grad_ref, out_ref):
    heights, lanes, _ = field_ref.shape
    total = jnp.zeros((lanes, lanes), F32)
    for h in range(heights):
        total = total + dot(field_ref[h], grad_ref[h], ((1,), (1,)))
    size = lanes // samples
    out_ref[...] = sum(
        total[s * size : (s + 1) * size, s * size : (s + 1) * size] for s in range(samples)
    )


def final_kernel(scale, recv_ref, order_ref, back_ref, local_ref, grad_ref, restore_ref, out_ref, result):
    heights, lanes, _ = grad_ref.shape
    count = order_ref.shape[0] // heights
    ordered = shuffle_groups(order_ref, recv_ref)
    for h in range(heights):
        inner = stack(ordered, h, count, lanes)
        value = scale * dot(inner, back_ref[...], ((0,), (0,)))
        result[h] = (value + dot(local_ref[...], grad_ref[h], ((1,), (0,)))).astype(BF16)
    block = PACK * heights
    for first in range(0, lanes, PACK):
        part = jnp.concatenate([result[h, first : first + PACK, :] for h in range(heights)], axis=0)
        out_ref[first * heights : first * heights + block, :] = shuffle(restore_ref, part)


def outer_kernel(samples, spec_ref, grad_ref, pair_ref, out_ref, local_ref, real, imag, plain, crossed, slots, sems):
    groups = spec_ref.shape[0]
    _, channels, outs, both = slots.shape
    pieces = sems.shape[1]
    size = channels // pieces
    q = pl.program_id(0)
    slot = lax.rem(q, 2)

    def move(mode, n):
        part = pl.ds(n * size, size)
        place = lax.rem(mode, 2)
        return pltpu.make_async_copy(slots.at[place, part], out_ref.at[mode, part], sems.at[place, n])

    half = both // 2
    low = low_half((channels, both), half)
    total = groups * samples

    @pl.when(q == 0)
    def _():
        pairs = 0.0
        for g in range(groups):
            pair = pair_ref[g].astype(F32)
            pairs = pairs + pair[:, :channels] + pair[:, channels : 2 * channels]
        local_ref[...] = pairs

    for g in range(groups):
        for s in range(samples):
            n = g * samples + s
            spec = spec_ref[g, s * channels : (s + 1) * channels, :].astype(F32)
            other = pltpu.roll(spec, half, 1)
            real[n] = jnp.where(low, spec, other)
            imag[n] = jnp.where(low, other, -spec)
            grad = grad_ref[g, s * outs : (s + 1) * outs, :]
            plain[n] = grad
            crossed[n] = pltpu.roll(grad.astype(F32), half, 1).astype(BF16)

    def body(c, carry):
        left = [packed_row(store.at[n], c) for n in range(total) for store in (real, imag)]
        for o in range(0, outs, PACK):
            right = [store[n, o : o + PACK, :] for n in range(total) for store in (plain, crossed)]
            slots[slot, c, o : o + PACK, :] = tree([a * b for a, b in zip(left, right)]).astype(F32)
        return carry

    for n in range(pieces):

        @pl.when(q >= 2)
        def _():
            move(q - 2, n).wait()

        lax.fori_loop(n * size, (n + 1) * size, body, 0, unroll=2)
        move(q, n).start()

    last = pl.num_programs(0) - 1

    @pl.when(jnp.logical_and(q == last, q >= 1))
    def _():
        for n in range(pieces):
            move(q - 1, n).wait()

    @pl.when(q == last)
    def _():
        for n in range(pieces):
            move(q, n).wait()


def whole(extent):
    return pl.BlockSpec(extent, lambda *_: (0,) * len(extent))


def call(kernel, name, operands, outs, scratch=(), grid=(1,), blocks=None, out_blocks=None):
    blocks, out_blocks = blocks or {}, out_blocks or {}
    in_specs = [blocks.get(n) or whole(operand.shape) for n, operand in enumerate(operands)]
    out_specs = [out_blocks.get(n, whole(out.shape)) for n, out in enumerate(outs)]
    return pl.pallas_call(
        kernel,
        out_shape=tuple(outs),
        grid=grid,
        in_specs=in_specs,
        out_specs=tuple(out_specs),
        scratch_shapes=list(scratch),
        compiler_params=pltpu.CompilerParams(vmem_limit_bytes=LIMIT),
        name=name,
    )(*operands)


def sum_over(values, axis):
    size = lax.axis_size(axis)
    step = 1
    while step < size:
        values = values + lax.ppermute(values, axis, [(i, i ^ step) for i in range(size)])
        step *= 2
    return values


def block_diagonal(matrix, copies):
    zero = jnp.zeros_like(matrix)
    return jnp.concatenate(
        [
            jnp.concatenate([matrix if i == j else zero for j in range(copies)], axis=1)
            for i in range(copies)
        ],
        axis=0,
    )


def shape(extent, kind=BF16):
    return jax.ShapeDtypeStruct(extent, kind)


def local(inputs, cotangent, mode_weight, local_weight):
    tiles = lax.axis_size("tile")
    samples, channels, th, width = inputs.shape
    owned, _, _, both = mode_weight.shape
    modes = both // 2
    lanes = samples * channels
    parts = width // 128
    spec_scale = 1.0 / math.sqrt(tiles * th * width)
    mode_scale = 1.0 / math.sqrt(modes * tiles * owned)
    send_cols, rows, back_rows, back_cols = tables(tiles, owned, th, width, modes)
    pixel_rows = samples * channels * th
    halves = tiles * padded(2 * owned)
    inverse = 2 * tiles * th

    def exchange(values):
        split = values.reshape(tiles, values.shape[0] // tiles, values.shape[1])
        moved = lax.all_to_all(split, "tile", split_axis=0, concat_axis=0, tiled=False)
        return moved.reshape(values.shape)

    forward_mix = block_diagonal(local_weight.T, samples)
    backward_mix = block_diagonal(local_weight, samples)
    by_row = order(PACK, th)
    by_channel = order(th, PACK)
    by_mode = mode_order(tiles, owned)
    by_height = order(2 * min(tiles, 8), th)
    mixed = pltpu.VMEM((owned, lanes, both), BF16)
    weight_extent = (1, channels // SPLIT) + mode_weight.shape[2:]

    def weight_blocks(first):
        return {
            first + n: pl.BlockSpec(weight_extent, lambda q, n=n: (q, n, 0, 0)) for n in range(SPLIT)
        }

    to_modes = shape((halves, th * lanes))
    to_pixels = shape((inverse, owned * lanes))
    field_shape = shape((th, lanes, width))

    def field_blocks(first):
        return {first + n: pl.BlockSpec((pixel_rows // SPLIT, width), lambda _, n=n: (n, 0)) for n in range(SPLIT)}

    field_rows, send = call(
        columns_kernel,
        "columns",
        (by_row, send_cols, *[inputs.reshape(pixel_rows, width)] * SPLIT),
        (field_shape, to_modes),
        blocks=field_blocks(2),
    )
    arrived = exchange(send)
    (cot_rows,) = call(
        relayout_kernel,
        "relayout",
        (by_row, *[cotangent.reshape(pixel_rows, width)] * SPLIT),
        (field_shape,),
        blocks=field_blocks(1),
    )
    spectra, send = call(
        functools.partial(forward_kernel, spec_scale, samples, owned),
        "mix_forward",
        (arrived, by_mode, rows, back_rows, *[mode_weight] * SPLIT),
        (shape((owned * lanes, both)), to_pixels),
        [
            mixed,
            pltpu.VMEM((lanes, both), F32),
            pltpu.VMEM((lanes, both), F32),
            pltpu.VMEM((2 * samples, channels, both), F32),
        ],
        grid=(owned,),
        blocks=weight_blocks(4),
    )
    all_spectra = lax.all_gather(spectra, "dp")
    arrived = exchange(send)
    steps = 4
    row_block = pl.BlockSpec((steps, lanes, width), lambda n: (n, 0, 0))
    gate_rows, send = call(
        functools.partial(pixels_kernel, mode_scale, th),
        "pixels",
        (arrived, by_height, back_cols, forward_mix, field_rows, cot_rows, send_cols),
        (field_shape, to_modes),
        [pltpu.VMEM((inverse, owned * lanes), BF16)],
        grid=(th // steps,),
        blocks={4: row_block, 5: row_block},
        out_blocks={0: row_block, 1: pl.BlockSpec((halves, steps * lanes), lambda n: (0, n))},
    )
    arrived = exchange(send)
    (local_sum,) = call(
        functools.partial(local_kernel, samples),
        "local_grad",
        (field_rows, gate_rows),
        (shape((channels, channels), F32),),
    )
    local_sum = sum_over(local_sum, "tile")
    (grad_spectra,) = call(
        functools.partial(grad_spectra_kernel, mode_scale, owned),
        "grad_spectra",
        (arrived, by_mode, rows, local_sum),
        (shape((owned * lanes + channels, both)),),
    )
    all_grads = lax.all_gather(grad_spectra, "dp")
    (send,) = call(
        functools.partial(backward_kernel, samples),
        "mix_backward",
        (grad_spectra, back_rows, *[mode_weight] * SPLIT),
        (to_pixels,),
        [mixed, pltpu.VMEM((2 * samples, channels * ROWS, both), F32)],
        grid=(owned,),
        blocks=weight_blocks(2),
    )
    arrived = exchange(send)

    groups = lax.axis_size("dp")
    total = groups * samples
    per_mode = pl.BlockSpec((groups, lanes, both), lambda q: (0, q, 0))
    below = owned * lanes // channels
    mode_grad, local_grad = call(
        functools.partial(outer_kernel, samples),
        "mode_grad",
        (all_spectra, all_grads, all_grads),
        (shape(mode_weight.shape, F32), shape((channels, channels), F32)),
        [pltpu.VMEM((total, channels, both), F32)] * 2
        + [pltpu.VMEM((total, channels, both), BF16)] * 2
        + [pltpu.VMEM((2,) + mode_weight.shape[1:], F32), pltpu.SemaphoreType.DMA((2, channels // GROUP))],
        grid=(owned,),
        blocks={
            0: per_mode,
            1: per_mode,
            2: pl.BlockSpec((groups, channels, both), lambda q: (0, below, 0)),
        },
        out_blocks={0: pl.BlockSpec(memory_space=pl.ANY)},
    )
    arrived, mode_grad = lax.optimization_barrier((arrived, mode_grad))

    (input_grad,) = call(
        functools.partial(final_kernel, spec_scale),
        "final",
        (arrived, by_height, back_cols, backward_mix, gate_rows, by_channel),
        (shape((pixel_rows, width)),),
        [pltpu.VMEM((th, lanes, width), BF16)],
    )
    return (input_grad.reshape(inputs.shape), mode_grad, local_grad)


def solution(mesh):
    return jax.shard_map(
        local,
        mesh=mesh,
        in_specs=(
            P("dp", None, "tile", None),
            P("dp", None, "tile", None),
            P("tile", None, None, None),
            P(),
        ),
        out_specs=(P("dp", None, "tile", None), P("tile", None, None, None), P()),
        check_vma=False,
    )
```

```python
import functools
import math

import jax
import jax.numpy as jnp
import numpy as np
from jax import lax
from jax.experimental import pallas as pl
from jax.experimental.pallas import tpu as pltpu
from jax.sharding import PartitionSpec as P

F32 = jnp.float32
BF16 = jnp.bfloat16
LIMIT = 56 * 1024 * 1024
ROWS = 8
PACK = 16
GROUP = 8
SPLIT = 4


def row_tables(height, modes):
    index = np.arange(modes)
    signed = np.where(index < modes // 2, index, index - modes)
    phases = np.mod(np.arange(height)[:, None] * signed[None, :], height)
    angles = phases * (2.0 * math.pi / height)
    return np.cos(angles), np.sin(angles)


def column_tables(width, modes):
    phases = np.mod(np.arange(modes)[:, None] * np.arange(width)[None, :], width)
    angles = phases * (2.0 * math.pi / width)
    return np.stack([np.cos(angles), -np.sin(angles)])


def constant(table):
    return jnp.asarray(np.asarray(table, np.float32)).astype(BF16)


def tables(tiles, owned, th, width, modes):
    cols = column_tables(width, tiles * owned)
    split = cols.reshape(2, tiles, owned, width)
    send_cols = split.transpose(1, 0, 2, 3).reshape(tiles, 2 * owned, width)
    send_cols = np.pad(send_cols, ((0, 0), (0, padded(2 * owned) - 2 * owned), (0, 0))).reshape(-1, width)
    back_cols = split.transpose(2, 1, 0, 3).reshape(-1, width)
    cosine, sine = row_tables(th * tiles, modes)
    real = np.concatenate([cosine, -sine], axis=1)
    imag = np.concatenate([sine, cosine], axis=1)
    pair = np.stack([real, imag]).reshape(2, tiles, th, 2 * modes)
    rows = pair.transpose(2, 1, 0, 3).reshape(-1, 2 * modes)
    back_rows = pair.transpose(1, 0, 2, 3).reshape(-1, 2 * modes)
    return constant(send_cols), constant(rows), constant(back_rows), constant(back_cols)


def padded(rows):
    return -(-rows // PACK) * PACK


def order(outer, inner):
    take = np.arange(outer * inner).reshape(outer, inner).T.reshape(-1)
    return constant(np.eye(outer * inner)[take])


def mode_order(tiles, owned):
    rows = np.arange(tiles * padded(2 * owned)).reshape(tiles, -1)
    take = rows[:, : 2 * owned].reshape(tiles, 2, owned).transpose(2, 0, 1).reshape(-1)
    return constant(np.eye(rows.size)[take])


def dot(left, right, dims):
    return lax.dot_general(left, right, (dims, ((), ())), preferred_element_type=F32)


def low_half(shape, half):
    return lax.broadcasted_iota(jnp.int32, shape, 1) < half


def gelu_slope(values):
    size = jnp.abs(values)
    expo = jnp.exp(-0.5 * values * values)
    t = 1.0 / (1.0 + (0.3275911 / math.sqrt(2.0)) * size)
    poly = 0.5 * 1.061405429
    for factor in (-1.453152027, 1.421413741, -0.284496736, 0.254829592):
        poly = poly * t + 0.5 * factor
    tail = poly * t * expo
    cumulative = jnp.where(values < 0.0, tail, 1.0 - tail)
    return cumulative + values * expo * (1.0 / math.sqrt(2.0 * math.pi))


def shuffle(order_ref, value):
    return dot(order_ref[...], value, ((1,), (0,))).astype(BF16)


def by_rows(order_ref, field_refs, rows_ref):
    heights, lanes, _ = rows_ref.shape
    block = PACK * heights
    quarter = lanes // len(field_refs)
    for first in range(0, lanes, PACK):
        start = first % quarter * heights
        moved = shuffle(order_ref, field_refs[first // quarter][start : start + block, :])
        for h in range(heights):
            rows_ref[h, first : first + PACK, :] = moved[h * PACK : (h + 1) * PACK]


def columns_kernel(order_ref, table_ref, *rest):
    field_refs, (rows_ref, send_ref) = rest[:SPLIT], rest[SPLIT:]
    heights, lanes, _ = rows_ref.shape
    by_rows(order_ref, field_refs, rows_ref)
    for h in range(heights):
        send_ref[:, h * lanes : (h + 1) * lanes] = dot(table_ref[...], rows_ref[h], ((1,), (1,))).astype(BF16)


def relayout_kernel(order_ref, *rest):
    by_rows(order_ref, rest[:SPLIT], rest[SPLIT])


def shuffle_groups(order_ref, recv_ref):
    size = order_ref.shape[0]
    return [shuffle(order_ref, recv_ref[n : n + size, :]) for n in range(0, recv_ref.shape[0], size)]


def stack(groups, index, count, lanes):
    return jnp.concatenate(
        [
            group[index * count : (index + 1) * count, n : n + lanes]
            for n in range(0, groups[0].shape[1], lanes)
            for group in groups
        ],
        axis=0,
    )


def spectra_into(scale, owned, recv_ref, order_ref, rows_ref, spec_ref):
    count = order_ref.shape[0] // owned
    lanes = recv_ref.shape[1] * count // rows_ref.shape[0]
    ordered = [shuffle(order_ref, recv_ref[...])]
    for q in range(owned):
        stacked = stack(ordered, q, count, lanes)
        spec_ref[q * lanes : (q + 1) * lanes, :] = (
            scale * dot(stacked, rows_ref[...], ((0,), (0,)))
        ).astype(BF16)


def grad_spectra_kernel(scale, owned, recv_ref, order_ref, rows_ref, local_ref, spec_ref):
    spectra_into(scale, owned, recv_ref, order_ref, rows_ref, spec_ref)
    value = local_ref[...]
    high = value.astype(BF16)
    low = (value - high.astype(F32)).astype(BF16)
    spec_ref[spec_ref.shape[0] - value.shape[0] :, :] = jnp.concatenate([high, low], axis=1)


def send_inverse(back_ref, mixed, send_ref):
    @pl.when(pl.program_id(0) == pl.num_programs(0) - 1)
    def _():
        owned, lanes, _ = mixed.shape
        for q in range(owned):
            send_ref[:, q * lanes : (q + 1) * lanes] = dot(back_ref[...], mixed[q], ((1,), (1,))).astype(BF16)


def tree(terms):
    while len(terms) > 1:
        terms = [a + b for a, b in zip(terms[0::2], terms[1::2])]
    return terms[0]


def packed_row(store, index):
    row = store[pl.ds(index, 1), :]
    return jnp.broadcast_to(row, (PACK, row.shape[1])).astype(BF16)


def duplicates(spec, half):
    value = spec.astype(F32)
    other = pltpu.roll(value, half, 1)
    low = low_half(value.shape, half)
    return jnp.where(low, value, other), jnp.where(low, other, value)


def fetch_weights(source_ref, weights, sems):
    q = pl.program_id(0)
    owned, channels = weights.shape[:2]
    pieces = sems.shape[1]
    size = channels // pieces

    def move(mode, n):
        part = pl.ds(n * size, size)
        return pltpu.make_async_copy(source_ref.at[mode, part], weights.at[mode, part], sems.at[mode, n])

    @pl.when(q == 0)
    def _():
        for mode in range(owned):
            for n in range(pieces):
                move(mode, n).start(priority=n)

    for n in range(pieces):
        move(q, n).wait()


def forward_kernel(scale, samples, owned, recv_ref, order_ref, rows_ref, back_ref, source_ref, *rest):
    spec_ref, send_ref, mixed, real, imag, sums, weights, sems = rest
    _, channels, outs, both = weights.shape
    half = both // 2
    lanes = mixed.shape[1]
    q = pl.program_id(0)
    fetch_weights(source_ref, weights, sems)

    @pl.when(q == 0)
    def _():
        spectra_into(scale, owned, recv_ref, order_ref, rows_ref, spec_ref)

    spec = spec_ref[pl.ds(pl.multiple_of(q * lanes, lanes), lanes), :]
    real[...], imag[...] = duplicates(spec, half)
    sums[...] = jnp.zeros_like(sums)

    def body(block, carry):
        first = block * GROUP
        rows = [
            [packed_row(store, s * channels + first + step) for step in range(GROUP)]
            for s in range(samples)
            for store in (real, imag)
        ]
        for o in range(0, outs, PACK):
            column = [weights[q, first + step, o : o + PACK, :] for step in range(GROUP)]
            for n, row in enumerate(rows):
                total = tree([w * r for w, r in zip(column, row)])
                sums[n, o : o + PACK, :] += total.astype(F32)
        return carry

    lax.fori_loop(0, channels // GROUP, body, 0)
    low = low_half((outs, both), half)
    result = []
    for s in range(samples):
        crossed = pltpu.roll(sums[2 * s + 1], half, 1)
        result.append(sums[2 * s] + jnp.where(low, -crossed, crossed))
    mixed[q] = jnp.concatenate(result, axis=0).astype(BF16)
    send_inverse(back_ref, mixed, send_ref)


def backward_kernel(samples, spec_ref, back_ref, source_ref, send_ref, mixed, sums, weights, sems):
    _, channels, outs, both = weights.shape
    half = both // 2
    lanes = mixed.shape[1]
    q = pl.program_id(0)
    fetch_weights(source_ref, weights, sems)
    spec = spec_ref[pl.ds(pl.multiple_of(q * lanes, lanes), lanes), :]
    parts = [part.astype(BF16) for part in duplicates(spec, half)]
    grads = [
        [part[s * outs + o : s * outs + o + PACK] for o in range(0, outs, PACK)]
        for s in range(samples)
        for part in parts
    ]

    def body(block, carry):
        for step in range(GROUP):
            c = block * GROUP + step
            column = [weights[q, c, o : o + PACK, :] for o in range(0, outs, PACK)]
            for n, grad in enumerate(grads):
                total = tree([w * g for w, g in zip(column, grad)]).astype(F32)
                sums[n, pl.ds(pl.multiple_of(c * ROWS, ROWS), ROWS), :] = total[:ROWS] + total[ROWS:]
        return carry

    lax.fori_loop(0, channels // GROUP, body, 0)
    low = low_half((channels, both), half)
    result = []
    for s in range(samples):
        straight, crossed = (
            sum(sums[n, pl.ds(row, channels, stride=ROWS), :] for row in range(ROWS)) for n in (2 * s, 2 * s + 1)
        )
        result.append(jnp.where(low, straight, -straight) + pltpu.roll(crossed, half, 1))
    mixed[q] = jnp.concatenate(result, axis=0).astype(BF16)
    send_inverse(back_ref, mixed, send_ref)


def pixels_kernel(scale, heights, recv_ref, order_ref, back_ref, local_ref, field_ref, cot_ref, table_ref, *rest):
    grad_ref, send_ref, ordered = rest
    steps, lanes, _ = field_ref.shape
    count = order_ref.shape[0] // heights
    size = order_ref.shape[0]
    group = pl.program_id(0)

    @pl.when(group == 0)
    def _():
        for n in range(0, recv_ref.shape[0], size):
            ordered[n : n + size, :] = shuffle(order_ref, recv_ref[n : n + size, :])

    for step in range(steps):
        parts = []
        for n in range(0, recv_ref.shape[0], size):
            first = pl.multiple_of(n + (group * steps + step) * count, count)
            parts.append(ordered[pl.ds(first, count), :])
        inner = stack(parts, 0, count, lanes)
        pre = scale * dot(inner, back_ref[...], ((0,), (0,)))
        pre = pre + dot(local_ref[...], field_ref[step], ((1,), (0,)))
        grad = (cot_ref[step].astype(F32) * gelu_slope(pre)).astype(BF16)
        grad_ref[step] = grad
        send_ref[:, step * lanes : (step + 1) * lanes] = dot(table_ref[...], grad, ((1,), (1,))).astype(BF16)


def local_kernel(samples, field_ref, grad_ref, out_ref):
    heights, lanes, _ = field_ref.shape
    total = jnp.zeros((lanes, lanes), F32)
    for h in range(heights):
        total = total + dot(field_ref[h], grad_ref[h], ((1,), (1,)))
    size = lanes // samples
    out_ref[...] = sum(
        total[s * size : (s + 1) * size, s * size : (s + 1) * size] for s in range(samples)
    )


def final_kernel(scale, recv_ref, order_ref, back_ref, local_ref, grad_ref, restore_ref, out_ref, result):
    heights, lanes, _ = grad_ref.shape
    count = order_ref.shape[0] // heights
    ordered = shuffle_groups(order_ref, recv_ref)
    for h in range(heights):
        inner = stack(ordered, h, count, lanes)
        value = scale * dot(inner, back_ref[...], ((0,), (0,)))
        result[h] = (value + dot(local_ref[...], grad_ref[h], ((1,), (0,)))).astype(BF16)
    block = PACK * heights
    for first in range(0, lanes, PACK):
        part = jnp.concatenate([result[h, first : first + PACK, :] for h in range(heights)], axis=0)
        out_ref[first * heights : first * heights + block, :] = shuffle(restore_ref, part)


def outer_kernel(samples, spec_ref, grad_ref, pair_ref, out_ref, local_ref, real, imag, plain, crossed, slots, sems):
    groups = spec_ref.shape[0]
    _, channels, outs, both = slots.shape
    pieces = sems.shape[1]
    size = channels // pieces
    q = pl.program_id(0)
    slot = lax.rem(q, 2)

    def move(mode, n):
        part = pl.ds(n * size, size)
        place = lax.rem(mode, 2)
        return pltpu.make_async_copy(slots.at[place, part], out_ref.at[mode, part], sems.at[place, n])

    half = both // 2
    low = low_half((channels, both), half)
    total = groups * samples

    @pl.when(q == 0)
    def _():
        pairs = 0.0
        for g in range(groups):
            pair = pair_ref[g].astype(F32)
            pairs = pairs + pair[:, :channels] + pair[:, channels : 2 * channels]
        local_ref[...] = pairs

    for g in range(groups):
        for s in range(samples):
            n = g * samples + s
            spec = spec_ref[g, s * channels : (s + 1) * channels, :].astype(F32)
            other = pltpu.roll(spec, half, 1)
            real[n] = jnp.where(low, spec, other)
            imag[n] = jnp.where(low, other, -spec)
            grad = grad_ref[g, s * outs : (s + 1) * outs, :]
            plain[n] = grad
            crossed[n] = pltpu.roll(grad.astype(F32), half, 1).astype(BF16)

    def body(c, carry):
        left = [packed_row(store.at[n], c) for n in range(total) for store in (real, imag)]
        for o in range(0, outs, PACK):
            right = [store[n, o : o + PACK, :] for n in range(total) for store in (plain, crossed)]
            slots[slot, c, o : o + PACK, :] = tree([a * b for a, b in zip(left, right)]).astype(F32)
        return carry

    for n in range(pieces):

        @pl.when(q >= 2)
        def _():
            move(q - 2, n).wait()

        lax.fori_loop(n * size, (n + 1) * size, body, 0, unroll=2)
        move(q, n).start(priority=n % 2)

    last = pl.num_programs(0) - 1

    @pl.when(jnp.logical_and(q == last, q >= 1))
    def _():
        for n in range(pieces):
            move(q - 1, n).wait()

    @pl.when(q == last)
    def _():
        for n in range(pieces):
            move(q, n).wait()


def whole(extent):
    return pl.BlockSpec(extent, lambda *_: (0,) * len(extent))


def call(kernel, name, operands, outs, scratch=(), grid=(1,), blocks=None, out_blocks=None):
    blocks, out_blocks = blocks or {}, out_blocks or {}
    in_specs = [blocks.get(n) or whole(operand.shape) for n, operand in enumerate(operands)]
    out_specs = [out_blocks.get(n, whole(out.shape)) for n, out in enumerate(outs)]
    return pl.pallas_call(
        kernel,
        out_shape=tuple(outs),
        grid=grid,
        in_specs=in_specs,
        out_specs=tuple(out_specs),
        scratch_shapes=list(scratch),
        compiler_params=pltpu.CompilerParams(vmem_limit_bytes=LIMIT),
        name=name,
    )(*operands)


def sum_over(values, axis):
    size = lax.axis_size(axis)
    step = 1
    while step < size:
        values = values + lax.ppermute(values, axis, [(i, i ^ step) for i in range(size)])
        step *= 2
    return values


def block_diagonal(matrix, copies):
    zero = jnp.zeros_like(matrix)
    return jnp.concatenate(
        [
            jnp.concatenate([matrix if i == j else zero for j in range(copies)], axis=1)
            for i in range(copies)
        ],
        axis=0,
    )


def shape(extent, kind=BF16):
    return jax.ShapeDtypeStruct(extent, kind)


def local(inputs, cotangent, mode_weight, local_weight):
    tiles = lax.axis_size("tile")
    samples, channels, th, width = inputs.shape
    owned, _, _, both = mode_weight.shape
    modes = both // 2
    lanes = samples * channels
    parts = width // 128
    spec_scale = 1.0 / math.sqrt(tiles * th * width)
    mode_scale = 1.0 / math.sqrt(modes * tiles * owned)
    send_cols, rows, back_rows, back_cols = tables(tiles, owned, th, width, modes)
    pixel_rows = samples * channels * th
    halves = tiles * padded(2 * owned)
    inverse = 2 * tiles * th

    def exchange(values):
        split = values.reshape(tiles, values.shape[0] // tiles, values.shape[1])
        moved = lax.all_to_all(split, "tile", split_axis=0, concat_axis=0, tiled=False)
        return moved.reshape(values.shape)

    forward_mix = block_diagonal(local_weight.T, samples)
    backward_mix = block_diagonal(local_weight, samples)
    by_row = order(PACK, th)
    by_channel = order(th, PACK)
    by_mode = mode_order(tiles, owned)
    by_height = order(2 * min(tiles, 8), th)
    mixed = pltpu.VMEM((owned, lanes, both), BF16)
    weight_scratch = [pltpu.VMEM(mode_weight.shape, BF16), pltpu.SemaphoreType.DMA((owned, 2))]
    in_place = pl.BlockSpec(memory_space=pl.ANY)
    to_modes = shape((halves, th * lanes))
    to_pixels = shape((inverse, owned * lanes))
    field_shape = shape((th, lanes, width))

    def field_blocks(first):
        return {first + n: pl.BlockSpec((pixel_rows // SPLIT, width), lambda _, n=n: (n, 0)) for n in range(SPLIT)}

    field_rows, send = call(
        columns_kernel,
        "columns",
        (by_row, send_cols, *[inputs.reshape(pixel_rows, width)] * SPLIT),
        (field_shape, to_modes),
        blocks=field_blocks(2),
    )
    arrived = exchange(send)
    (cot_rows,) = call(
        relayout_kernel,
        "relayout",
        (by_row, *[cotangent.reshape(pixel_rows, width)] * SPLIT),
        (field_shape,),
        blocks=field_blocks(1),
    )
    spectra, send = call(
        functools.partial(forward_kernel, spec_scale, samples, owned),
        "mix_forward",
        (arrived, by_mode, rows, back_rows, mode_weight),
        (shape((owned * lanes, both)), to_pixels),
        [
            mixed,
            pltpu.VMEM((lanes, both), F32),
            pltpu.VMEM((lanes, both), F32),
            pltpu.VMEM((2 * samples, channels, both), F32),
            *weight_scratch,
        ],
        grid=(owned,),
        blocks={4: in_place},
    )
    all_spectra = lax.all_gather(spectra, "dp")
    arrived = exchange(send)
    steps = 4
    row_block = pl.BlockSpec((steps, lanes, width), lambda n: (n, 0, 0))
    gate_rows, send = call(
        functools.partial(pixels_kernel, mode_scale, th),
        "pixels",
        (arrived, by_height, back_cols, forward_mix, field_rows, cot_rows, send_cols),
        (field_shape, to_modes),
        [pltpu.VMEM((inverse, owned * lanes), BF16)],
        grid=(th // steps,),
        blocks={4: row_block, 5: row_block},
        out_blocks={0: row_block, 1: pl.BlockSpec((halves, steps * lanes), lambda n: (0, n))},
    )
    arrived = exchange(send)
    (local_sum,) = call(
        functools.partial(local_kernel, samples),
        "local_grad",
        (field_rows, gate_rows),
        (shape((channels, channels), F32),),
    )
    local_sum = sum_over(local_sum, "tile")
    (grad_spectra,) = call(
        functools.partial(grad_spectra_kernel, mode_scale, owned),
        "grad_spectra",
        (arrived, by_mode, rows, local_sum),
        (shape((owned * lanes + channels, both)),),
    )
    all_grads = lax.all_gather(grad_spectra, "dp")
    (send,) = call(
        functools.partial(backward_kernel, samples),
        "mix_backward",
        (grad_spectra, back_rows, mode_weight),
        (to_pixels,),
        [mixed, pltpu.VMEM((2 * samples, channels * ROWS, both), F32), *weight_scratch],
        grid=(owned,),
        blocks={2: in_place},
    )
    arrived = exchange(send)

    groups = lax.axis_size("dp")
    total = groups * samples
    per_mode = pl.BlockSpec((groups, lanes, both), lambda q: (0, q, 0))
    below = owned * lanes // channels
    mode_grad, local_grad = call(
        functools.partial(outer_kernel, samples),
        "mode_grad",
        (all_spectra, all_grads, all_grads),
        (shape(mode_weight.shape, F32), shape((channels, channels), F32)),
        [pltpu.VMEM((total, channels, both), F32)] * 2
        + [pltpu.VMEM((total, channels, both), BF16)] * 2
        + [pltpu.VMEM((2,) + mode_weight.shape[1:], F32), pltpu.SemaphoreType.DMA((2, channels // GROUP))],
        grid=(owned,),
        blocks={
            0: per_mode,
            1: per_mode,
            2: pl.BlockSpec((groups, channels, both), lambda q: (0, below, 0)),
        },
        out_blocks={0: in_place},
    )
    arrived, mode_grad = lax.optimization_barrier((arrived, mode_grad))

    (input_grad,) = call(
        functools.partial(final_kernel, spec_scale),
        "final",
        (arrived, by_height, back_cols, backward_mix, gate_rows, by_channel),
        (shape((pixel_rows, width)),),
        [pltpu.VMEM((th, lanes, width), BF16)],
    )
    return (input_grad.reshape(inputs.shape), mode_grad, local_grad)


def solution(mesh):
    return jax.shard_map(
        local,
        mesh=mesh,
        in_specs=(
            P("dp", None, "tile", None),
            P("dp", None, "tile", None),
            P("tile", None, None, None),
            P(),
        ),
        out_specs=(P("dp", None, "tile", None), P("tile", None, None, None), P()),
        check_vma=False,
    )
```

```python
import functools
import math

import jax
import jax.numpy as jnp
import numpy as np
from jax import lax
from jax.experimental import pallas as pl
from jax.experimental.pallas import tpu as pltpu
from jax.sharding import PartitionSpec as P

F32 = jnp.float32
BF16 = jnp.bfloat16
LIMIT = 56 * 1024 * 1024
ROWS = 8
PACK = 16
GROUP = 8
SPLIT = 4


def row_tables(height, modes):
    index = np.arange(modes)
    signed = np.where(index < modes // 2, index, index - modes)
    phases = np.mod(np.arange(height)[:, None] * signed[None, :], height)
    angles = phases * (2.0 * math.pi / height)
    return np.cos(angles), np.sin(angles)


def column_tables(width, modes):
    phases = np.mod(np.arange(modes)[:, None] * np.arange(width)[None, :], width)
    angles = phases * (2.0 * math.pi / width)
    return np.stack([np.cos(angles), -np.sin(angles)])


def constant(table):
    return jnp.asarray(np.asarray(table, np.float32)).astype(BF16)


def tables(tiles, owned, th, width, modes):
    cols = column_tables(width, tiles * owned)
    split = cols.reshape(2, tiles, owned, width)
    send_cols = split.transpose(1, 0, 2, 3).reshape(tiles, 2 * owned, width)
    send_cols = np.pad(send_cols, ((0, 0), (0, padded(2 * owned) - 2 * owned), (0, 0))).reshape(-1, width)
    back_cols = split.transpose(2, 1, 0, 3).reshape(-1, width)
    cosine, sine = row_tables(th * tiles, modes)
    real = np.concatenate([cosine, -sine], axis=1)
    imag = np.concatenate([sine, cosine], axis=1)
    pair = np.stack([real, imag]).reshape(2, tiles, th, 2 * modes)
    rows = pair.transpose(2, 1, 0, 3).reshape(-1, 2 * modes)
    back_rows = pair.transpose(1, 0, 2, 3).reshape(-1, 2 * modes)
    return constant(send_cols), constant(rows), constant(back_rows), constant(back_cols)


def padded(rows):
    return -(-rows // PACK) * PACK


def order(outer, inner):
    take = np.arange(outer * inner).reshape(outer, inner).T.reshape(-1)
    return constant(np.eye(outer * inner)[take])


def mode_order(tiles, owned):
    rows = np.arange(tiles * padded(2 * owned)).reshape(tiles, -1)
    take = rows[:, : 2 * owned].reshape(tiles, 2, owned).transpose(2, 0, 1).reshape(-1)
    return constant(np.eye(rows.size)[take])


def dot(left, right, dims):
    return lax.dot_general(left, right, (dims, ((), ())), preferred_element_type=F32)


def low_half(shape, half):
    return lax.broadcasted_iota(jnp.int32, shape, 1) < half


def gelu_slope(values):
    size = jnp.abs(values)
    expo = jnp.exp(-0.5 * values * values)
    t = 1.0 / (1.0 + (0.3275911 / math.sqrt(2.0)) * size)
    poly = 0.5 * 1.061405429
    for factor in (-1.453152027, 1.421413741, -0.284496736, 0.254829592):
        poly = poly * t + 0.5 * factor
    tail = poly * t * expo
    cumulative = jnp.where(values < 0.0, tail, 1.0 - tail)
    return cumulative + values * expo * (1.0 / math.sqrt(2.0 * math.pi))


def shuffle(order_ref, value):
    return dot(order_ref[...], value, ((1,), (0,))).astype(BF16)


def by_rows(order_ref, field_refs, rows_ref):
    heights, lanes, _ = rows_ref.shape
    block = PACK * heights
    quarter = lanes // len(field_refs)
    for first in range(0, lanes, PACK):
        start = first % quarter * heights
        moved = shuffle(order_ref, field_refs[first // quarter][start : start + block, :])
        for h in range(heights):
            rows_ref[h, first : first + PACK, :] = moved[h * PACK : (h + 1) * PACK]


def columns_kernel(order_ref, table_ref, *rest):
    field_refs, (rows_ref, send_ref) = rest[:SPLIT], rest[SPLIT:]
    heights, lanes, _ = rows_ref.shape
    by_rows(order_ref, field_refs, rows_ref)
    for h in range(heights):
        send_ref[:, h * lanes : (h + 1) * lanes] = dot(table_ref[...], rows_ref[h], ((1,), (1,))).astype(BF16)


def relayout_kernel(order_ref, *rest):
    by_rows(order_ref, rest[:SPLIT], rest[SPLIT])


def shuffle_groups(order_ref, recv_ref):
    size = order_ref.shape[0]
    return [shuffle(order_ref, recv_ref[n : n + size, :]) for n in range(0, recv_ref.shape[0], size)]


def stack(groups, index, count, lanes):
    return jnp.concatenate(
        [
            group[index * count : (index + 1) * count, n : n + lanes]
            for n in range(0, groups[0].shape[1], lanes)
            for group in groups
        ],
        axis=0,
    )


def spectra_into(scale, owned, recv_ref, order_ref, rows_ref, spec_ref):
    count = order_ref.shape[0] // owned
    lanes = recv_ref.shape[1] * count // rows_ref.shape[0]
    ordered = [shuffle(order_ref, recv_ref[...])]
    for q in range(owned):
        stacked = stack(ordered, q, count, lanes)
        spec_ref[q * lanes : (q + 1) * lanes, :] = (
            scale * dot(stacked, rows_ref[...], ((0,), (0,)))
        ).astype(BF16)


def grad_spectra_kernel(scale, owned, recv_ref, order_ref, rows_ref, local_ref, spec_ref):
    spectra_into(scale, owned, recv_ref, order_ref, rows_ref, spec_ref)
    value = local_ref[...]
    high = value.astype(BF16)
    low = (value - high.astype(F32)).astype(BF16)
    spec_ref[spec_ref.shape[0] - value.shape[0] :, :] = jnp.concatenate([high, low], axis=1)


def send_inverse(back_ref, mixed, send_ref):
    @pl.when(pl.program_id(0) == pl.num_programs(0) - 1)
    def _():
        owned, lanes, _ = mixed.shape
        for q in range(owned):
            send_ref[:, q * lanes : (q + 1) * lanes] = dot(back_ref[...], mixed[q], ((1,), (1,))).astype(BF16)


def tree(terms):
    while len(terms) > 1:
        terms = [a + b for a, b in zip(terms[0::2], terms[1::2])]
    return terms[0]


def packed_row(store, index):
    row = store[pl.ds(index, 1), :]
    return jnp.broadcast_to(row, (PACK, row.shape[1])).astype(BF16)


def duplicates(spec, half):
    value = spec.astype(F32)
    other = pltpu.roll(value, half, 1)
    low = low_half(value.shape, half)
    return jnp.where(low, value, other), jnp.where(low, other, value)


def forward_kernel(scale, samples, owned, recv_ref, order_ref, rows_ref, back_ref, weight_ref, *rest):
    spec_ref, send_ref, mixed, real, imag, sums = rest
    _, outs, both = sums.shape
    channels = weight_ref.shape[0] // outs
    half = both // 2
    lanes = mixed.shape[1]
    q = pl.program_id(0)

    @pl.when(q == 0)
    def _():
        spectra_into(scale, owned, recv_ref, order_ref, rows_ref, spec_ref)

    spec = spec_ref[pl.ds(pl.multiple_of(q * lanes, lanes), lanes), :]
    real[...], imag[...] = duplicates(spec, half)
    sums[...] = jnp.zeros_like(sums)

    def window(c, o):
        return pl.ds(pl.multiple_of(c * outs + o, PACK), PACK)

    def body(block, carry):
        first = block * GROUP
        rows = [
            [packed_row(store, s * channels + first + step) for step in range(GROUP)]
            for s in range(samples)
            for store in (real, imag)
        ]
        for o in range(0, outs, PACK):
            column = [weight_ref[window(first + step, o), :] for step in range(GROUP)]
            for n, row in enumerate(rows):
                total = tree([w * r for w, r in zip(column, row)])
                sums[n, o : o + PACK, :] += total.astype(F32)
        return carry

    lax.fori_loop(0, channels // GROUP, body, 0)
    low = low_half((outs, both), half)
    result = []
    for s in range(samples):
        crossed = pltpu.roll(sums[2 * s + 1], half, 1)
        result.append(sums[2 * s] + jnp.where(low, -crossed, crossed))
    mixed[q] = jnp.concatenate(result, axis=0).astype(BF16)
    send_inverse(back_ref, mixed, send_ref)


def backward_kernel(samples, spec_ref, back_ref, weight_ref, send_ref, mixed, sums):
    channels, both = sums.shape[1] // ROWS, sums.shape[2]
    outs = weight_ref.shape[0] // channels
    half = both // 2
    lanes = mixed.shape[1]
    q = pl.program_id(0)
    spec = spec_ref[pl.ds(pl.multiple_of(q * lanes, lanes), lanes), :]
    parts = [part.astype(BF16) for part in duplicates(spec, half)]
    grads = [
        [part[s * outs + o : s * outs + o + PACK] for o in range(0, outs, PACK)]
        for s in range(samples)
        for part in parts
    ]

    def window(c, o):
        return pl.ds(pl.multiple_of(c * outs + o, PACK), PACK)

    def body(block, carry):
        for step in range(GROUP):
            c = block * GROUP + step
            column = [weight_ref[window(c, o), :] for o in range(0, outs, PACK)]
            for n, grad in enumerate(grads):
                total = tree([w * g for w, g in zip(column, grad)]).astype(F32)
                sums[n, pl.ds(pl.multiple_of(c * ROWS, ROWS), ROWS), :] = total[:ROWS] + total[ROWS:]
        return carry

    lax.fori_loop(0, channels // GROUP, body, 0)
    low = low_half((channels, both), half)
    result = []
    for s in range(samples):
        straight, crossed = (
            sum(sums[n, pl.ds(row, channels, stride=ROWS), :] for row in range(ROWS)) for n in (2 * s, 2 * s + 1)
        )
        result.append(jnp.where(low, straight, -straight) + pltpu.roll(crossed, half, 1))
    mixed[q] = jnp.concatenate(result, axis=0).astype(BF16)
    send_inverse(back_ref, mixed, send_ref)


def pixels_kernel(scale, heights, recv_ref, order_ref, back_ref, local_ref, field_ref, cot_ref, table_ref, *rest):
    grad_ref, send_ref, ordered = rest
    steps, lanes, _ = field_ref.shape
    count = order_ref.shape[0] // heights
    size = order_ref.shape[0]
    group = pl.program_id(0)

    @pl.when(group == 0)
    def _():
        for n in range(0, recv_ref.shape[0], size):
            ordered[n : n + size, :] = shuffle(order_ref, recv_ref[n : n + size, :])

    for step in range(steps):
        parts = []
        for n in range(0, recv_ref.shape[0], size):
            first = pl.multiple_of(n + (group * steps + step) * count, count)
            parts.append(ordered[pl.ds(first, count), :])
        inner = stack(parts, 0, count, lanes)
        pre = scale * dot(inner, back_ref[...], ((0,), (0,)))
        pre = pre + dot(local_ref[...], field_ref[step], ((1,), (0,)))
        grad = (cot_ref[step].astype(F32) * gelu_slope(pre)).astype(BF16)
        grad_ref[step] = grad
        send_ref[:, step * lanes : (step + 1) * lanes] = dot(table_ref[...], grad, ((1,), (1,))).astype(BF16)


def local_kernel(samples, field_ref, grad_ref, out_ref):
    heights, lanes, _ = field_ref.shape
    total = jnp.zeros((lanes, lanes), F32)
    for h in range(heights):
        total = total + dot(field_ref[h], grad_ref[h], ((1,), (1,)))
    size = lanes // samples
    out_ref[...] = sum(
        total[s * size : (s + 1) * size, s * size : (s + 1) * size] for s in range(samples)
    )


def final_kernel(scale, recv_ref, order_ref, back_ref, local_ref, grad_ref, restore_ref, out_ref, result):
    heights, lanes, _ = grad_ref.shape
    count = order_ref.shape[0] // heights
    ordered = shuffle_groups(order_ref, recv_ref)
    for h in range(heights):
        inner = stack(ordered, h, count, lanes)
        value = scale * dot(inner, back_ref[...], ((0,), (0,)))
        result[h] = (value + dot(local_ref[...], grad_ref[h], ((1,), (0,)))).astype(BF16)
    block = PACK * heights
    for first in range(0, lanes, PACK):
        part = jnp.concatenate([result[h, first : first + PACK, :] for h in range(heights)], axis=0)
        out_ref[first * heights : first * heights + block, :] = shuffle(restore_ref, part)


def outer_kernel(samples, spec_ref, grad_ref, pair_ref, out_ref, local_ref, real, imag, plain, crossed):
    groups = spec_ref.shape[0]
    total, channels, both = real.shape
    outs = plain.shape[1]
    half = both // 2
    low = low_half((channels, both), half)

    @pl.when(pl.program_id(0) == 0)
    def _():
        pairs = 0.0
        for g in range(groups):
            pair = pair_ref[g].astype(F32)
            pairs = pairs + pair[:, :channels] + pair[:, channels : 2 * channels]
        local_ref[...] = pairs

    for g in range(groups):
        for s in range(samples):
            n = g * samples + s
            spec = spec_ref[g, s * channels : (s + 1) * channels, :].astype(F32)
            other = pltpu.roll(spec, half, 1)
            real[n] = jnp.where(low, spec, other)
            imag[n] = jnp.where(low, other, -spec)
            grad = grad_ref[g, s * outs : (s + 1) * outs, :]
            plain[n] = grad
            crossed[n] = pltpu.roll(grad.astype(F32), half, 1).astype(BF16)

    def body(c, carry):
        left = [packed_row(store.at[n], c) for n in range(total) for store in (real, imag)]
        for o in range(0, outs, PACK):
            right = [store[n, o : o + PACK, :] for n in range(total) for store in (plain, crossed)]
            row = pl.multiple_of(c * outs + o, PACK)
            out_ref[pl.ds(row, PACK), :] = tree([a * b for a, b in zip(left, right)]).astype(F32)
        return carry

    lax.fori_loop(0, channels, body, 0, unroll=2)


def whole(extent):
    return pl.BlockSpec(extent, lambda *_: (0,) * len(extent))


def call(kernel, name, operands, outs, scratch=(), grid=(1,), blocks=None, out_blocks=None):
    blocks, out_blocks = blocks or {}, out_blocks or {}
    in_specs = [blocks.get(n) or whole(operand.shape) for n, operand in enumerate(operands)]
    out_specs = [out_blocks.get(n, whole(out.shape)) for n, out in enumerate(outs)]
    return pl.pallas_call(
        kernel,
        out_shape=tuple(outs),
        grid=grid,
        in_specs=in_specs,
        out_specs=tuple(out_specs),
        scratch_shapes=list(scratch),
        compiler_params=pltpu.CompilerParams(vmem_limit_bytes=LIMIT),
        name=name,
    )(*operands)


def sum_over(values, axis):
    size = lax.axis_size(axis)
    step = 1
    while step < size:
        values = values + lax.ppermute(values, axis, [(i, i ^ step) for i in range(size)])
        step *= 2
    return values


def block_diagonal(matrix, copies):
    zero = jnp.zeros_like(matrix)
    return jnp.concatenate(
        [
            jnp.concatenate([matrix if i == j else zero for j in range(copies)], axis=1)
            for i in range(copies)
        ],
        axis=0,
    )


def shape(extent, kind=BF16):
    return jax.ShapeDtypeStruct(extent, kind)


def local(inputs, cotangent, mode_weight, local_weight):
    tiles = lax.axis_size("tile")
    samples, channels, th, width = inputs.shape
    owned, _, _, both = mode_weight.shape
    modes = both // 2
    lanes = samples * channels
    parts = width // 128
    spec_scale = 1.0 / math.sqrt(tiles * th * width)
    mode_scale = 1.0 / math.sqrt(modes * tiles * owned)
    send_cols, rows, back_rows, back_cols = tables(tiles, owned, th, width, modes)
    pixel_rows = samples * channels * th
    halves = tiles * padded(2 * owned)
    inverse = 2 * tiles * th

    def exchange(values):
        split = values.reshape(tiles, values.shape[0] // tiles, values.shape[1])
        moved = lax.all_to_all(split, "tile", split_axis=0, concat_axis=0, tiled=False)
        return moved.reshape(values.shape)

    forward_mix = block_diagonal(local_weight.T, samples)
    backward_mix = block_diagonal(local_weight, samples)
    by_row = order(PACK, th)
    by_channel = order(th, PACK)
    by_mode = mode_order(tiles, owned)
    by_height = order(2 * min(tiles, 8), th)
    mixed = pltpu.VMEM((owned, lanes, both), BF16)
    flat_weight = mode_weight.reshape(-1, both)
    weight_block = pl.BlockSpec((flat_weight.shape[0] // owned, both), lambda q: (q, 0))
    to_modes = shape((halves, th * lanes))
    to_pixels = shape((inverse, owned * lanes))
    field_shape = shape((th, lanes, width))

    def field_blocks(first):
        return {first + n: pl.BlockSpec((pixel_rows // SPLIT, width), lambda _, n=n: (n, 0)) for n in range(SPLIT)}

    field_rows, send = call(
        columns_kernel,
        "columns",
        (by_row, send_cols, *[inputs.reshape(pixel_rows, width)] * SPLIT),
        (field_shape, to_modes),
        blocks=field_blocks(2),
    )
    arrived = exchange(send)
    (cot_rows,) = call(
        relayout_kernel,
        "relayout",
        (by_row, *[cotangent.reshape(pixel_rows, width)] * SPLIT),
        (field_shape,),
        blocks=field_blocks(1),
    )
    spectra, send = call(
        functools.partial(forward_kernel, spec_scale, samples, owned),
        "mix_forward",
        (arrived, by_mode, rows, back_rows, flat_weight),
        (shape((owned * lanes, both)), to_pixels),
        [
            mixed,
            pltpu.VMEM((lanes, both), F32),
            pltpu.VMEM((lanes, both), F32),
            pltpu.VMEM((2 * samples, channels, both), F32),
        ],
        grid=(owned,),
        blocks={4: weight_block},
    )
    all_spectra = lax.all_gather(spectra, "dp")
    arrived = exchange(send)
    steps = 4
    row_block = pl.BlockSpec((steps, lanes, width), lambda n: (n, 0, 0))
    gate_rows, send = call(
        functools.partial(pixels_kernel, mode_scale, th),
        "pixels",
        (arrived, by_height, back_cols, forward_mix, field_rows, cot_rows, send_cols),
        (field_shape, to_modes),
        [pltpu.VMEM((inverse, owned * lanes), BF16)],
        grid=(th // steps,),
        blocks={4: row_block, 5: row_block},
        out_blocks={0: row_block, 1: pl.BlockSpec((halves, steps * lanes), lambda n: (0, n))},
    )
    arrived = exchange(send)
    (local_sum,) = call(
        functools.partial(local_kernel, samples),
        "local_grad",
        (field_rows, gate_rows),
        (shape((channels, channels), F32),),
    )
    local_sum = sum_over(local_sum, "tile")
    (grad_spectra,) = call(
        functools.partial(grad_spectra_kernel, mode_scale, owned),
        "grad_spectra",
        (arrived, by_mode, rows, local_sum),
        (shape((owned * lanes + channels, both)),),
    )
    all_grads = lax.all_gather(grad_spectra, "dp")
    (send,) = call(
        functools.partial(backward_kernel, samples),
        "mix_backward",
        (grad_spectra, back_rows, flat_weight),
        (to_pixels,),
        [mixed, pltpu.VMEM((2 * samples, channels * ROWS, both), F32)],
        grid=(owned,),
        blocks={2: weight_block},
    )
    arrived = exchange(send)

    groups = lax.axis_size("dp")
    total = groups * samples
    per_mode = pl.BlockSpec((groups, lanes, both), lambda q: (0, q, 0))
    below = owned * lanes // channels
    mode_grad, local_grad = call(
        functools.partial(outer_kernel, samples),
        "mode_grad",
        (all_spectra, all_grads, all_grads),
        (shape(flat_weight.shape, F32), shape((channels, channels), F32)),
        [pltpu.VMEM((total, channels, both), F32)] * 2 + [pltpu.VMEM((total, channels, both), BF16)] * 2,
        grid=(owned,),
        blocks={
            0: per_mode,
            1: per_mode,
            2: pl.BlockSpec((groups, channels, both), lambda q: (0, below, 0)),
        },
        out_blocks={0: weight_block},
    )
    arrived, mode_grad = lax.optimization_barrier((arrived, mode_grad))

    (input_grad,) = call(
        functools.partial(final_kernel, spec_scale),
        "final",
        (arrived, by_height, back_cols, backward_mix, gate_rows, by_channel),
        (shape((pixel_rows, width)),),
        [pltpu.VMEM((th, lanes, width), BF16)],
    )
    return (input_grad.reshape(inputs.shape), mode_grad.reshape(mode_weight.shape), local_grad)


def solution(mesh):
    return jax.shard_map(
        local,
        mesh=mesh,
        in_specs=(
            P("dp", None, "tile", None),
            P("dp", None, "tile", None),
            P("tile", None, None, None),
            P(),
        ),
        out_specs=(P("dp", None, "tile", None), P("tile", None, None, None), P()),
        check_vma=False,
    )
```

```python
import functools
import math

import jax
import jax.numpy as jnp
import numpy as np
from jax import lax
from jax.experimental import pallas as pl
from jax.experimental.pallas import tpu as pltpu
from jax.sharding import PartitionSpec as P

F32 = jnp.float32
BF16 = jnp.bfloat16
LIMIT = 56 * 1024 * 1024
ROWS = 8
PACK = 16
GROUP = 8
SPLIT = 4


def row_tables(height, modes):
    index = np.arange(modes)
    signed = np.where(index < modes // 2, index, index - modes)
    phases = np.mod(np.arange(height)[:, None] * signed[None, :], height)
    angles = phases * (2.0 * math.pi / height)
    return np.cos(angles), np.sin(angles)


def column_tables(width, modes):
    phases = np.mod(np.arange(modes)[:, None] * np.arange(width)[None, :], width)
    angles = phases * (2.0 * math.pi / width)
    return np.stack([np.cos(angles), -np.sin(angles)])


def constant(table):
    return jnp.asarray(np.asarray(table, np.float32)).astype(BF16)


def tables(tiles, owned, th, width, modes):
    cols = column_tables(width, tiles * owned)
    split = cols.reshape(2, tiles, owned, width)
    send_cols = split.transpose(1, 0, 2, 3).reshape(tiles, 2 * owned, width)
    send_cols = np.pad(send_cols, ((0, 0), (0, padded(2 * owned) - 2 * owned), (0, 0))).reshape(-1, width)
    back_cols = split.transpose(2, 1, 0, 3).reshape(-1, width)
    cosine, sine = row_tables(th * tiles, modes)
    real = np.concatenate([cosine, -sine], axis=1)
    imag = np.concatenate([sine, cosine], axis=1)
    pair = np.stack([real, imag]).reshape(2, tiles, th, 2 * modes)
    rows = pair.transpose(2, 1, 0, 3).reshape(-1, 2 * modes)
    back_rows = pair.transpose(1, 0, 2, 3).reshape(-1, 2 * modes)
    return constant(send_cols), constant(rows), constant(back_rows), constant(back_cols)


def padded(rows):
    return -(-rows // PACK) * PACK


def order(outer, inner):
    take = np.arange(outer * inner).reshape(outer, inner).T.reshape(-1)
    return constant(np.eye(outer * inner)[take])


def mode_order(tiles, owned):
    rows = np.arange(tiles * padded(2 * owned)).reshape(tiles, -1)
    take = rows[:, : 2 * owned].reshape(tiles, 2, owned).transpose(2, 0, 1).reshape(-1)
    return constant(np.eye(rows.size)[take])


def dot(left, right, dims):
    return lax.dot_general(left, right, (dims, ((), ())), preferred_element_type=F32)


def low_half(shape, half):
    return lax.broadcasted_iota(jnp.int32, shape, 1) < half


def gelu_slope(values):
    size = jnp.abs(values)
    expo = jnp.exp(-0.5 * values * values)
    t = 1.0 / (1.0 + (0.3275911 / math.sqrt(2.0)) * size)
    poly = 0.5 * 1.061405429
    for factor in (-1.453152027, 1.421413741, -0.284496736, 0.254829592):
        poly = poly * t + 0.5 * factor
    tail = poly * t * expo
    cumulative = jnp.where(values < 0.0, tail, 1.0 - tail)
    return cumulative + values * expo * (1.0 / math.sqrt(2.0 * math.pi))


def shuffle(order_ref, value):
    return dot(order_ref[...], value, ((1,), (0,))).astype(BF16)


def by_rows(order_ref, field_refs, rows_ref):
    heights, lanes, _ = rows_ref.shape
    block = PACK * heights
    quarter = lanes // len(field_refs)
    for first in range(0, lanes, PACK):
        start = first % quarter * heights
        moved = shuffle(order_ref, field_refs[first // quarter][start : start + block, :])
        for h in range(heights):
            rows_ref[h, first : first + PACK, :] = moved[h * PACK : (h + 1) * PACK]


def columns_kernel(order_ref, table_ref, *rest):
    field_refs, (rows_ref, send_ref) = rest[:SPLIT], rest[SPLIT:]
    heights, lanes, _ = rows_ref.shape
    by_rows(order_ref, field_refs, rows_ref)
    for h in range(heights):
        send_ref[:, h * lanes : (h + 1) * lanes] = dot(table_ref[...], rows_ref[h], ((1,), (1,))).astype(BF16)


def relayout_kernel(order_ref, *rest):
    by_rows(order_ref, rest[:SPLIT], rest[SPLIT])


def shuffle_groups(order_ref, recv_ref):
    size = order_ref.shape[0]
    return [shuffle(order_ref, recv_ref[n : n + size, :]) for n in range(0, recv_ref.shape[0], size)]


def stack(groups, index, count, lanes):
    return jnp.concatenate(
        [
            group[index * count : (index + 1) * count, n : n + lanes]
            for n in range(0, groups[0].shape[1], lanes)
            for group in groups
        ],
        axis=0,
    )


def spectra_into(scale, owned, recv_ref, order_ref, rows_ref, spec_ref):
    count = order_ref.shape[0] // owned
    lanes = recv_ref.shape[1] * count // rows_ref.shape[0]
    ordered = [shuffle(order_ref, recv_ref[...])]
    for q in range(owned):
        stacked = stack(ordered, q, count, lanes)
        spec_ref[q * lanes : (q + 1) * lanes, :] = (
            scale * dot(stacked, rows_ref[...], ((0,), (0,)))
        ).astype(BF16)


def grad_spectra_kernel(scale, owned, recv_ref, order_ref, rows_ref, local_ref, spec_ref):
    spectra_into(scale, owned, recv_ref, order_ref, rows_ref, spec_ref)
    value = local_ref[...]
    high = value.astype(BF16)
    low = (value - high.astype(F32)).astype(BF16)
    spec_ref[spec_ref.shape[0] - value.shape[0] :, :] = jnp.concatenate([high, low], axis=1)


def send_inverse(back_ref, mixed, send_ref):
    @pl.when(pl.program_id(0) == pl.num_programs(0) - 1)
    def _():
        owned, lanes, _ = mixed.shape
        for q in range(owned):
            send_ref[:, q * lanes : (q + 1) * lanes] = dot(back_ref[...], mixed[q], ((1,), (1,))).astype(BF16)


def tree(terms):
    while len(terms) > 1:
        terms = [a + b for a, b in zip(terms[0::2], terms[1::2])]
    return terms[0]


def packed_row(store, index):
    row = store[pl.ds(index, 1), :]
    return jnp.broadcast_to(row, (PACK, row.shape[1])).astype(BF16)


def duplicates(spec, half):
    value = spec.astype(F32)
    other = pltpu.roll(value, half, 1)
    low = low_half(value.shape, half)
    return jnp.where(low, value, other), jnp.where(low, other, value)


def forward_kernel(scale, samples, owned, recv_ref, order_ref, rows_ref, back_ref, weight_ref, *rest):
    spec_ref, send_ref, mixed, real, imag, sums = rest
    _, outs, both = sums.shape
    channels = weight_ref.shape[0] // outs
    half = both // 2
    lanes = mixed.shape[1]
    q = pl.program_id(0)

    @pl.when(q == 0)
    def _():
        spectra_into(scale, owned, recv_ref, order_ref, rows_ref, spec_ref)

    spec = spec_ref[pl.ds(pl.multiple_of(q * lanes, lanes), lanes), :]
    real[...], imag[...] = duplicates(spec, half)
    sums[...] = jnp.zeros_like(sums)

    def window(c, o):
        return pl.ds(pl.multiple_of(c * outs + o, PACK), PACK)

    def body(block, carry):
        first = block * GROUP
        rows = [
            [packed_row(store, s * channels + first + step) for step in range(GROUP)]
            for s in range(samples)
            for store in (real, imag)
        ]
        for start in range(0, outs, 2 * PACK):
            totals = []
            for o in (start, start + PACK):
                column = [weight_ref[window(first + step, o), :] for step in range(GROUP)]
                for n, row in enumerate(rows):
                    totals.append((n, o, tree([w * r for w, r in zip(column, row)])))
            updated = [(n, o, sums[n, o : o + PACK, :] + total.astype(F32)) for n, o, total in totals]
            for n, o, total in updated:
                sums[n, o : o + PACK, :] = total
        return carry

    lax.fori_loop(0, channels // GROUP, body, 0)
    low = low_half((outs, both), half)
    result = []
    for s in range(samples):
        crossed = pltpu.roll(sums[2 * s + 1], half, 1)
        result.append(sums[2 * s] + jnp.where(low, -crossed, crossed))
    mixed[q] = jnp.concatenate(result, axis=0).astype(BF16)
    send_inverse(back_ref, mixed, send_ref)


def backward_kernel(samples, spec_ref, back_ref, weight_ref, send_ref, mixed, sums):
    channels, both = sums.shape[1] // ROWS, sums.shape[2]
    outs = weight_ref.shape[0] // channels
    half = both // 2
    lanes = mixed.shape[1]
    q = pl.program_id(0)
    spec = spec_ref[pl.ds(pl.multiple_of(q * lanes, lanes), lanes), :]
    parts = [part.astype(BF16) for part in duplicates(spec, half)]
    grads = [
        [part[s * outs + o : s * outs + o + PACK] for o in range(0, outs, PACK)]
        for s in range(samples)
        for part in parts
    ]

    def window(c, o):
        return pl.ds(pl.multiple_of(c * outs + o, PACK), PACK)

    def body(block, carry):
        totals = []
        for step in range(GROUP // 2):
            c = block * (GROUP // 2) + step
            column = [weight_ref[window(c, o), :] for o in range(0, outs, PACK)]
            for n, grad in enumerate(grads):
                total = tree([w * g for w, g in zip(column, grad)]).astype(F32)
                totals.append((n, c, total[:ROWS] + total[ROWS:]))
        for n, c, total in totals:
            sums[n, pl.ds(pl.multiple_of(c * ROWS, ROWS), ROWS), :] = total
        return carry

    lax.fori_loop(0, channels // (GROUP // 2), body, 0)
    low = low_half((channels, both), half)
    result = []
    for s in range(samples):
        straight, crossed = (
            sum(sums[n, pl.ds(row, channels, stride=ROWS), :] for row in range(ROWS)) for n in (2 * s, 2 * s + 1)
        )
        result.append(jnp.where(low, straight, -straight) + pltpu.roll(crossed, half, 1))
    mixed[q] = jnp.concatenate(result, axis=0).astype(BF16)
    send_inverse(back_ref, mixed, send_ref)


def pixels_kernel(scale, heights, recv_ref, order_ref, back_ref, local_ref, field_ref, cot_ref, table_ref, *rest):
    grad_ref, send_ref, ordered = rest
    steps, lanes, _ = field_ref.shape
    count = order_ref.shape[0] // heights
    size = order_ref.shape[0]
    group = pl.program_id(0)

    @pl.when(group == 0)
    def _():
        for n in range(0, recv_ref.shape[0], size):
            ordered[n : n + size, :] = shuffle(order_ref, recv_ref[n : n + size, :])

    for step in range(steps):
        parts = []
        for n in range(0, recv_ref.shape[0], size):
            first = pl.multiple_of(n + (group * steps + step) * count, count)
            parts.append(ordered[pl.ds(first, count), :])
        inner = stack(parts, 0, count, lanes)
        pre = scale * dot(inner, back_ref[...], ((0,), (0,)))
        pre = pre + dot(local_ref[...], field_ref[step], ((1,), (0,)))
        grad = (cot_ref[step].astype(F32) * gelu_slope(pre)).astype(BF16)
        grad_ref[step] = grad
        send_ref[:, step * lanes : (step + 1) * lanes] = dot(table_ref[...], grad, ((1,), (1,))).astype(BF16)


def local_kernel(samples, field_ref, grad_ref, out_ref):
    heights, lanes, _ = field_ref.shape
    total = jnp.zeros((lanes, lanes), F32)
    for h in range(heights):
        total = total + dot(field_ref[h], grad_ref[h], ((1,), (1,)))
    size = lanes // samples
    out_ref[...] = sum(
        total[s * size : (s + 1) * size, s * size : (s + 1) * size] for s in range(samples)
    )


def final_kernel(scale, recv_ref, order_ref, back_ref, local_ref, grad_ref, restore_ref, out_ref, result):
    heights, lanes, _ = grad_ref.shape
    count = order_ref.shape[0] // heights
    ordered = shuffle_groups(order_ref, recv_ref)
    for h in range(heights):
        inner = stack(ordered, h, count, lanes)
        value = scale * dot(inner, back_ref[...], ((0,), (0,)))
        result[h] = (value + dot(local_ref[...], grad_ref[h], ((1,), (0,)))).astype(BF16)
    block = PACK * heights
    for first in range(0, lanes, PACK):
        part = jnp.concatenate([result[h, first : first + PACK, :] for h in range(heights)], axis=0)
        out_ref[first * heights : first * heights + block, :] = shuffle(restore_ref, part)


def outer_kernel(samples, spec_ref, grad_ref, pair_ref, out_ref, local_ref, real, imag, plain, crossed):
    groups = spec_ref.shape[0]
    total, channels, both = real.shape
    outs = plain.shape[1]
    half = both // 2
    low = low_half((channels, both), half)

    @pl.when(pl.program_id(0) == 0)
    def _():
        pairs = 0.0
        for g in range(groups):
            pair = pair_ref[g].astype(F32)
            pairs = pairs + pair[:, :channels] + pair[:, channels : 2 * channels]
        local_ref[...] = pairs

    for g in range(groups):
        for s in range(samples):
            n = g * samples + s
            spec = spec_ref[g, s * channels : (s + 1) * channels, :].astype(F32)
            other = pltpu.roll(spec, half, 1)
            real[n] = jnp.where(low, spec, other)
            imag[n] = jnp.where(low, other, -spec)
            grad = grad_ref[g, s * outs : (s + 1) * outs, :]
            plain[n] = grad
            crossed[n] = pltpu.roll(grad.astype(F32), half, 1).astype(BF16)

    def body(pair, carry):
        lefts = [
            [packed_row(store.at[n], 2 * pair + c) for n in range(total) for store in (real, imag)] for c in range(2)
        ]
        results = []
        for o in range(0, outs, PACK):
            right = [store[n, o : o + PACK, :] for n in range(total) for store in (plain, crossed)]
            for c, left in enumerate(lefts):
                results.append((c, o, tree([a * b for a, b in zip(left, right)])))
        for c, o, result in results:
            row = pl.multiple_of((2 * pair + c) * outs + o, PACK)
            out_ref[pl.ds(row, PACK), :] = result.astype(F32)
        return carry

    lax.fori_loop(0, channels // 2, body, 0)


def whole(extent):
    return pl.BlockSpec(extent, lambda *_: (0,) * len(extent))


def call(kernel, name, operands, outs, scratch=(), grid=(1,), blocks=None, out_blocks=None):
    blocks, out_blocks = blocks or {}, out_blocks or {}
    in_specs = [blocks.get(n) or whole(operand.shape) for n, operand in enumerate(operands)]
    out_specs = [out_blocks.get(n, whole(out.shape)) for n, out in enumerate(outs)]
    return pl.pallas_call(
        kernel,
        out_shape=tuple(outs),
        grid=grid,
        in_specs=in_specs,
        out_specs=tuple(out_specs),
        scratch_shapes=list(scratch),
        compiler_params=pltpu.CompilerParams(vmem_limit_bytes=LIMIT),
        name=name,
    )(*operands)


def sum_over(values, axis):
    size = lax.axis_size(axis)
    step = 1
    while step < size:
        values = values + lax.ppermute(values, axis, [(i, i ^ step) for i in range(size)])
        step *= 2
    return values


def block_diagonal(matrix, copies):
    zero = jnp.zeros_like(matrix)
    return jnp.concatenate(
        [
            jnp.concatenate([matrix if i == j else zero for j in range(copies)], axis=1)
            for i in range(copies)
        ],
        axis=0,
    )


def shape(extent, kind=BF16):
    return jax.ShapeDtypeStruct(extent, kind)


def local(inputs, cotangent, mode_weight, local_weight):
    tiles = lax.axis_size("tile")
    samples, channels, th, width = inputs.shape
    owned, _, _, both = mode_weight.shape
    modes = both // 2
    lanes = samples * channels
    parts = width // 128
    spec_scale = 1.0 / math.sqrt(tiles * th * width)
    mode_scale = 1.0 / math.sqrt(modes * tiles * owned)
    send_cols, rows, back_rows, back_cols = tables(tiles, owned, th, width, modes)
    pixel_rows = samples * channels * th
    halves = tiles * padded(2 * owned)
    inverse = 2 * tiles * th

    def exchange(values):
        split = values.reshape(tiles, values.shape[0] // tiles, values.shape[1])
        moved = lax.all_to_all(split, "tile", split_axis=0, concat_axis=0, tiled=False)
        return moved.reshape(values.shape)

    forward_mix = block_diagonal(local_weight.T, samples)
    backward_mix = block_diagonal(local_weight, samples)
    by_row = order(PACK, th)
    by_channel = order(th, PACK)
    by_mode = mode_order(tiles, owned)
    by_height = order(2 * min(tiles, 8), th)
    mixed = pltpu.VMEM((owned, lanes, both), BF16)
    flat_weight = mode_weight.reshape(-1, both)
    weight_block = pl.BlockSpec((flat_weight.shape[0] // owned, both), lambda q: (q, 0))
    to_modes = shape((halves, th * lanes))
    to_pixels = shape((inverse, owned * lanes))
    field_shape = shape((th, lanes, width))

    def field_blocks(first):
        return {first + n: pl.BlockSpec((pixel_rows // SPLIT, width), lambda _, n=n: (n, 0)) for n in range(SPLIT)}

    field_rows, send = call(
        columns_kernel,
        "columns",
        (by_row, send_cols, *[inputs.reshape(pixel_rows, width)] * SPLIT),
        (field_shape, to_modes),
        blocks=field_blocks(2),
    )
    arrived = exchange(send)
    (cot_rows,) = call(
        relayout_kernel,
        "relayout",
        (by_row, *[cotangent.reshape(pixel_rows, width)] * SPLIT),
        (field_shape,),
        blocks=field_blocks(1),
    )
    spectra, send = call(
        functools.partial(forward_kernel, spec_scale, samples, owned),
        "mix_forward",
        (arrived, by_mode, rows, back_rows, flat_weight),
        (shape((owned * lanes, both)), to_pixels),
        [
            mixed,
            pltpu.VMEM((lanes, both), F32),
            pltpu.VMEM((lanes, both), F32),
            pltpu.VMEM((2 * samples, channels, both), F32),
        ],
        grid=(owned,),
        blocks={4: weight_block},
    )
    all_spectra = lax.all_gather(spectra, "dp")
    arrived = exchange(send)
    steps = 4
    row_block = pl.BlockSpec((steps, lanes, width), lambda n: (n, 0, 0))
    gate_rows, send = call(
        functools.partial(pixels_kernel, mode_scale, th),
        "pixels",
        (arrived, by_height, back_cols, forward_mix, field_rows, cot_rows, send_cols),
        (field_shape, to_modes),
        [pltpu.VMEM((inverse, owned * lanes), BF16)],
        grid=(th // steps,),
        blocks={4: row_block, 5: row_block},
        out_blocks={0: row_block, 1: pl.BlockSpec((halves, steps * lanes), lambda n: (0, n))},
    )
    arrived = exchange(send)
    (local_sum,) = call(
        functools.partial(local_kernel, samples),
        "local_grad",
        (field_rows, gate_rows),
        (shape((channels, channels), F32),),
    )
    local_sum = sum_over(local_sum, "tile")
    (grad_spectra,) = call(
        functools.partial(grad_spectra_kernel, mode_scale, owned),
        "grad_spectra",
        (arrived, by_mode, rows, local_sum),
        (shape((owned * lanes + channels, both)),),
    )
    all_grads = lax.all_gather(grad_spectra, "dp")
    (send,) = call(
        functools.partial(backward_kernel, samples),
        "mix_backward",
        (grad_spectra, back_rows, flat_weight),
        (to_pixels,),
        [mixed, pltpu.VMEM((2 * samples, channels * ROWS, both), F32)],
        grid=(owned,),
        blocks={2: weight_block},
    )
    arrived = exchange(send)

    groups = lax.axis_size("dp")
    total = groups * samples
    per_mode = pl.BlockSpec((groups, lanes, both), lambda q: (0, q, 0))
    below = owned * lanes // channels
    mode_grad, local_grad = call(
        functools.partial(outer_kernel, samples),
        "mode_grad",
        (all_spectra, all_grads, all_grads),
        (shape(flat_weight.shape, F32), shape((channels, channels), F32)),
        [pltpu.VMEM((total, channels, both), F32)] * 2 + [pltpu.VMEM((total, channels, both), BF16)] * 2,
        grid=(owned,),
        blocks={
            0: per_mode,
            1: per_mode,
            2: pl.BlockSpec((groups, channels, both), lambda q: (0, below, 0)),
        },
        out_blocks={0: weight_block},
    )
    arrived, mode_grad = lax.optimization_barrier((arrived, mode_grad))

    (input_grad,) = call(
        functools.partial(final_kernel, spec_scale),
        "final",
        (arrived, by_height, back_cols, backward_mix, gate_rows, by_channel),
        (shape((pixel_rows, width)),),
        [pltpu.VMEM((th, lanes, width), BF16)],
    )
    return (input_grad.reshape(inputs.shape), mode_grad.reshape(mode_weight.shape), local_grad)


def solution(mesh):
    return jax.shard_map(
        local,
        mesh=mesh,
        in_specs=(
            P("dp", None, "tile", None),
            P("dp", None, "tile", None),
            P("tile", None, None, None),
            P(),
        ),
        out_specs=(P("dp", None, "tile", None), P("tile", None, None, None), P()),
        check_vma=False,
    )
```

```python
import functools
import math

import jax
import jax.numpy as jnp
import numpy as np
from jax import lax
from jax.experimental import pallas as pl
from jax.experimental.pallas import tpu as pltpu
from jax.sharding import PartitionSpec as P

F32 = jnp.float32
BF16 = jnp.bfloat16
LIMIT = 56 * 1024 * 1024
SMALL = 24 * 1024 * 1024
ROWS = 8
PACK = 16
GROUP = 8
SPLIT = 4


def row_tables(height, modes):
    index = np.arange(modes)
    signed = np.where(index < modes // 2, index, index - modes)
    phases = np.mod(np.arange(height)[:, None] * signed[None, :], height)
    angles = phases * (2.0 * math.pi / height)
    return np.cos(angles), np.sin(angles)


def column_tables(width, modes):
    phases = np.mod(np.arange(modes)[:, None] * np.arange(width)[None, :], width)
    angles = phases * (2.0 * math.pi / width)
    return np.stack([np.cos(angles), -np.sin(angles)])


def constant(table):
    return jnp.asarray(np.asarray(table, np.float32)).astype(BF16)


def tables(tiles, owned, th, width, modes):
    cols = column_tables(width, tiles * owned)
    split = cols.reshape(2, tiles, owned, width)
    send_cols = split.transpose(1, 0, 2, 3).reshape(tiles, 2 * owned, width)
    send_cols = np.pad(send_cols, ((0, 0), (0, padded(2 * owned) - 2 * owned), (0, 0))).reshape(-1, width)
    back_cols = split.transpose(2, 1, 0, 3).reshape(-1, width)
    cosine, sine = row_tables(th * tiles, modes)
    real = np.concatenate([cosine, -sine], axis=1)
    imag = np.concatenate([sine, cosine], axis=1)
    pair = np.stack([real, imag]).reshape(2, tiles, th, 2 * modes)
    rows = pair.transpose(2, 1, 0, 3).reshape(-1, 2 * modes)
    back_rows = pair.transpose(1, 0, 2, 3).reshape(-1, 2 * modes)
    return constant(send_cols), constant(rows), constant(back_rows), constant(back_cols)


def padded(rows):
    return -(-rows // PACK) * PACK


def order(outer, inner):
    take = np.arange(outer * inner).reshape(outer, inner).T.reshape(-1)
    return constant(np.eye(outer * inner)[take])


def mode_order(tiles, owned):
    rows = np.arange(tiles * padded(2 * owned)).reshape(tiles, -1)
    take = rows[:, : 2 * owned].reshape(tiles, 2, owned).transpose(2, 0, 1).reshape(-1)
    return constant(np.eye(rows.size)[take])


def dot(left, right, dims):
    return lax.dot_general(left, right, (dims, ((), ())), preferred_element_type=F32)


def low_half(shape, half):
    return lax.broadcasted_iota(jnp.int32, shape, 1) < half


def gelu_slope(values):
    size = jnp.abs(values)
    expo = jnp.exp(-0.5 * values * values)
    t = 1.0 / (1.0 + (0.3275911 / math.sqrt(2.0)) * size)
    poly = 0.5 * 1.061405429
    for factor in (-1.453152027, 1.421413741, -0.284496736, 0.254829592):
        poly = poly * t + 0.5 * factor
    tail = poly * t * expo
    cumulative = jnp.where(values < 0.0, tail, 1.0 - tail)
    return cumulative + values * expo * (1.0 / math.sqrt(2.0 * math.pi))


def shuffle(order_ref, value):
    return dot(order_ref[...], value, ((1,), (0,))).astype(BF16)


def by_rows(order_ref, field_refs, rows_ref):
    heights, lanes, _ = rows_ref.shape
    block = PACK * heights
    quarter = lanes // len(field_refs)
    for first in range(0, lanes, PACK):
        start = first % quarter * heights
        moved = shuffle(order_ref, field_refs[first // quarter][start : start + block, :])
        for h in range(heights):
            rows_ref[h, first : first + PACK, :] = moved[h * PACK : (h + 1) * PACK]


def columns_kernel(order_ref, table_ref, *rest):
    field_refs, (rows_ref, send_ref) = rest[:SPLIT], rest[SPLIT:]
    heights, lanes, _ = rows_ref.shape
    by_rows(order_ref, field_refs, rows_ref)
    for h in range(heights):
        send_ref[:, h * lanes : (h + 1) * lanes] = dot(table_ref[...], rows_ref[h], ((1,), (1,))).astype(BF16)


def relayout_kernel(order_ref, *rest):
    by_rows(order_ref, rest[:SPLIT], rest[SPLIT])


def shuffle_groups(order_ref, recv_ref):
    size = order_ref.shape[0]
    return [shuffle(order_ref, recv_ref[n : n + size, :]) for n in range(0, recv_ref.shape[0], size)]


def stack(groups, index, count, lanes):
    return jnp.concatenate(
        [
            group[index * count : (index + 1) * count, n : n + lanes]
            for n in range(0, groups[0].shape[1], lanes)
            for group in groups
        ],
        axis=0,
    )


def spectra_into(scale, owned, recv_ref, order_ref, rows_ref, spec_ref):
    count = order_ref.shape[0] // owned
    lanes = recv_ref.shape[1] * count // rows_ref.shape[0]
    ordered = [shuffle(order_ref, recv_ref[...])]
    for q in range(owned):
        stacked = stack(ordered, q, count, lanes)
        spec_ref[q * lanes : (q + 1) * lanes, :] = (
            scale * dot(stacked, rows_ref[...], ((0,), (0,)))
        ).astype(BF16)


def grad_spectra_kernel(scale, owned, recv_ref, order_ref, rows_ref, local_ref, spec_ref):
    spectra_into(scale, owned, recv_ref, order_ref, rows_ref, spec_ref)
    value = local_ref[...]
    high = value.astype(BF16)
    low = (value - high.astype(F32)).astype(BF16)
    spec_ref[spec_ref.shape[0] - value.shape[0] :, :] = jnp.concatenate([high, low], axis=1)


def tree(terms):
    while len(terms) > 1:
        terms = [a + b for a, b in zip(terms[0::2], terms[1::2])]
    return terms[0]


def packed_row(store, index):
    row = store[pl.ds(index, 1), :]
    return jnp.broadcast_to(row, (PACK, row.shape[1])).astype(BF16)


def duplicates(spec, half):
    value = spec.astype(F32)
    other = pltpu.roll(value, half, 1)
    low = low_half(value.shape, half)
    return jnp.where(low, value, other), jnp.where(low, other, value)


def finish(back_ref, sums, send_ref, mix):
    @pl.when(pl.program_id(0) == pl.num_programs(0) - 1)
    def _():
        owned = sums.shape[0]
        lanes = send_ref.shape[1] // owned
        for q in range(owned):
            mixed = mix(sums.at[q]).astype(BF16)
            send_ref[:, q * lanes : (q + 1) * lanes] = dot(back_ref[...], mixed, ((1,), (1,))).astype(BF16)


def forward_kernel(scale, samples, owned, recv_ref, order_ref, rows_ref, back_ref, weight_ref, *rest):
    spec_ref, send_ref, real, imag, sums = rest
    _, _, outs, both = sums.shape
    channels = weight_ref.shape[0] // outs
    half = both // 2
    lanes = samples * channels
    q = pl.program_id(0)

    @pl.when(q == 0)
    def _():
        spectra_into(scale, owned, recv_ref, order_ref, rows_ref, spec_ref)
        real[...], imag[...] = duplicates(spec_ref[...], half)
        sums[...] = jnp.zeros_like(sums)

    def window(c, o):
        return pl.ds(pl.multiple_of(c * outs + o, PACK), PACK)

    def body(block, carry):
        first = block * GROUP
        rows = [
            [packed_row(store, q * lanes + s * channels + first + step) for step in range(GROUP)]
            for s in range(samples)
            for store in (real, imag)
        ]
        for start in range(0, outs, 2 * PACK):
            totals = []
            for o in (start, start + PACK):
                column = [weight_ref[window(first + step, o), :] for step in range(GROUP)]
                for n, row in enumerate(rows):
                    totals.append((n, o, tree([w * r for w, r in zip(column, row)])))
            updated = [(n, o, sums[q, n, o : o + PACK, :] + total.astype(F32)) for n, o, total in totals]
            for n, o, total in updated:
                sums[q, n, o : o + PACK, :] = total
        return carry

    lax.fori_loop(0, channels // GROUP, body, 0)

    def mix(parts):
        low = low_half((outs, both), half)
        result = []
        for s in range(samples):
            crossed = pltpu.roll(parts[2 * s + 1], half, 1)
            result.append(parts[2 * s] + jnp.where(low, -crossed, crossed))
        return jnp.concatenate(result, axis=0)

    finish(back_ref, sums, send_ref, mix)


def backward_kernel(samples, spec_ref, back_ref, weight_ref, send_ref, real, imag, sums):
    channels, both = sums.shape[2] // ROWS, sums.shape[3]
    outs = weight_ref.shape[0] // channels
    half = both // 2
    lanes = samples * outs
    q = pl.program_id(0)

    @pl.when(q == 0)
    def _():
        first, second = duplicates(spec_ref[: real.shape[0], :], half)
        real[...], imag[...] = first.astype(BF16), second.astype(BF16)

    grads = [
        [store[pl.ds(pl.multiple_of(q * lanes + s * outs + o, PACK), PACK), :] for o in range(0, outs, PACK)]
        for s in range(samples)
        for store in (real, imag)
    ]

    def window(c, o):
        return pl.ds(pl.multiple_of(c * outs + o, PACK), PACK)

    def body(block, carry):
        totals = []
        for step in range(GROUP):
            c = block * GROUP + step
            column = [weight_ref[window(c, o), :] for o in range(0, outs, PACK)]
            for n, grad in enumerate(grads):
                total = tree([w * g for w, g in zip(column, grad)]).astype(F32)
                totals.append((n, c, total[:ROWS] + total[ROWS:]))
        for n, c, total in totals:
            sums[q, n, pl.ds(pl.multiple_of(c * ROWS, ROWS), ROWS), :] = total
        return carry

    lax.fori_loop(0, channels // GROUP, body, 0)

    def mix(parts):
        low = low_half((channels, both), half)
        result = []
        for s in range(samples):
            straight, crossed = (
                sum(parts[n, pl.ds(row, channels, stride=ROWS), :] for row in range(ROWS)) for n in (2 * s, 2 * s + 1)
            )
            result.append(jnp.where(low, straight, -straight) + pltpu.roll(crossed, half, 1))
        return jnp.concatenate(result, axis=0)

    finish(back_ref, sums, send_ref, mix)


def pixels_kernel(scale, heights, recv_ref, order_ref, back_ref, local_ref, field_ref, cot_ref, table_ref, *rest):
    grad_ref, send_ref, sum_ref, ordered, total = rest
    steps, lanes, _ = field_ref.shape
    count = order_ref.shape[0] // heights
    size = order_ref.shape[0]
    group = pl.program_id(0)

    @pl.when(group == 0)
    def _():
        for n in range(0, recv_ref.shape[0], size):
            ordered[n : n + size, :] = shuffle(order_ref, recv_ref[n : n + size, :])
        total[...] = jnp.zeros_like(total)

    local = jnp.zeros(total.shape, F32)
    for step in range(steps):
        parts = []
        for n in range(0, recv_ref.shape[0], size):
            first = pl.multiple_of(n + (group * steps + step) * count, count)
            parts.append(ordered[pl.ds(first, count), :])
        inner = stack(parts, 0, count, lanes)
        pre = scale * dot(inner, back_ref[...], ((0,), (0,)))
        pre = pre + dot(local_ref[...], field_ref[step], ((1,), (0,)))
        grad = (cot_ref[step].astype(F32) * gelu_slope(pre)).astype(BF16)
        grad_ref[step] = grad
        send_ref[:, step * lanes : (step + 1) * lanes] = dot(table_ref[...], grad, ((1,), (1,))).astype(BF16)
        local = local + dot(field_ref[step], grad, ((1,), (1,)))
    total[...] += local

    @pl.when(group == pl.num_programs(0) - 1)
    def _():
        extent = sum_ref.shape[0]
        sum_ref[...] = sum(total[n : n + extent, n : n + extent] for n in range(0, lanes, extent))


def final_kernel(scale, recv_ref, order_ref, back_ref, local_ref, grad_ref, restore_ref, out_ref, result):
    heights, lanes, _ = grad_ref.shape
    count = order_ref.shape[0] // heights
    ordered = shuffle_groups(order_ref, recv_ref)
    for h in range(heights):
        inner = stack(ordered, h, count, lanes)
        value = scale * dot(inner, back_ref[...], ((0,), (0,)))
        result[h] = (value + dot(local_ref[...], grad_ref[h], ((1,), (0,)))).astype(BF16)
    block = PACK * heights
    for first in range(0, lanes, PACK):
        part = jnp.concatenate([result[h, first : first + PACK, :] for h in range(heights)], axis=0)
        out_ref[first * heights : first * heights + block, :] = shuffle(restore_ref, part)


def outer_kernel(samples, spec_ref, grad_ref, pair_ref, out_ref, local_ref, real, imag, plain, crossed):
    groups = spec_ref.shape[0]
    total, channels, both = real.shape
    outs = plain.shape[1]
    half = both // 2
    low = low_half((channels, both), half)

    @pl.when(pl.program_id(0) == 0)
    def _():
        pairs = 0.0
        for g in range(groups):
            pair = pair_ref[g].astype(F32)
            pairs = pairs + pair[:, :channels] + pair[:, channels : 2 * channels]
        local_ref[...] = pairs

    for g in range(groups):
        for s in range(samples):
            n = g * samples + s
            spec = spec_ref[g, s * channels : (s + 1) * channels, :].astype(F32)
            other = pltpu.roll(spec, half, 1)
            real[n] = jnp.where(low, spec, other)
            imag[n] = jnp.where(low, other, -spec)
            grad = grad_ref[g, s * outs : (s + 1) * outs, :]
            plain[n] = grad
            crossed[n] = pltpu.roll(grad.astype(F32), half, 1).astype(BF16)

    def body(pair, carry):
        lefts = [
            [packed_row(store.at[n], 2 * pair + c) for n in range(total) for store in (real, imag)] for c in range(2)
        ]
        results = []
        for o in range(0, outs, PACK):
            right = [store[n, o : o + PACK, :] for n in range(total) for store in (plain, crossed)]
            for c, left in enumerate(lefts):
                results.append((c, o, tree([a * b for a, b in zip(left, right)])))
        for c, o, result in results:
            row = pl.multiple_of((2 * pair + c) * outs + o, PACK)
            out_ref[pl.ds(row, PACK), :] = result.astype(F32)
        return carry

    lax.fori_loop(0, channels // 2, body, 0)


def whole(extent):
    return pl.BlockSpec(extent, lambda *_: (0,) * len(extent))


def call(kernel, name, operands, outs, scratch=(), grid=(1,), blocks=None, out_blocks=None, limit=LIMIT):
    blocks, out_blocks = blocks or {}, out_blocks or {}
    in_specs = [blocks.get(n) or whole(operand.shape) for n, operand in enumerate(operands)]
    out_specs = [out_blocks.get(n, whole(out.shape)) for n, out in enumerate(outs)]
    return pl.pallas_call(
        kernel,
        out_shape=tuple(outs),
        grid=grid,
        in_specs=in_specs,
        out_specs=tuple(out_specs),
        scratch_shapes=list(scratch),
        compiler_params=pltpu.CompilerParams(vmem_limit_bytes=limit),
        name=name,
    )(*operands)


def sum_over(values, axis):
    size = lax.axis_size(axis)
    step = 1
    while step < size:
        values = values + lax.ppermute(values, axis, [(i, i ^ step) for i in range(size)])
        step *= 2
    return values


def block_diagonal(matrix, copies):
    zero = jnp.zeros_like(matrix)
    return jnp.concatenate(
        [
            jnp.concatenate([matrix if i == j else zero for j in range(copies)], axis=1)
            for i in range(copies)
        ],
        axis=0,
    )


def shape(extent, kind=BF16):
    return jax.ShapeDtypeStruct(extent, kind)


def local(inputs, cotangent, mode_weight, local_weight):
    tiles = lax.axis_size("tile")
    samples, channels, th, width = inputs.shape
    owned, _, _, both = mode_weight.shape
    modes = both // 2
    lanes = samples * channels
    parts = width // 128
    spec_scale = 1.0 / math.sqrt(tiles * th * width)
    mode_scale = 1.0 / math.sqrt(modes * tiles * owned)
    send_cols, rows, back_rows, back_cols = tables(tiles, owned, th, width, modes)
    pixel_rows = samples * channels * th
    halves = tiles * padded(2 * owned)
    inverse = 2 * tiles * th

    def exchange(values):
        split = values.reshape(tiles, values.shape[0] // tiles, values.shape[1])
        moved = lax.all_to_all(split, "tile", split_axis=0, concat_axis=0, tiled=False)
        return moved.reshape(values.shape)

    forward_mix = block_diagonal(local_weight.T, samples)
    backward_mix = block_diagonal(local_weight, samples)
    by_row = order(PACK, th)
    by_channel = order(th, PACK)
    by_mode = mode_order(tiles, owned)
    by_height = order(2 * min(tiles, 8), th)
    flat_weight = mode_weight.reshape(-1, both)
    weight_block = pl.BlockSpec((flat_weight.shape[0] // owned, both), lambda q: (q, 0))
    to_modes = shape((halves, th * lanes))
    to_pixels = shape((inverse, owned * lanes))
    field_shape = shape((th, lanes, width))

    def field_blocks(first):
        return {first + n: pl.BlockSpec((pixel_rows // SPLIT, width), lambda _, n=n: (n, 0)) for n in range(SPLIT)}

    field_rows, send = call(
        columns_kernel,
        "columns",
        (by_row, send_cols, *[inputs.reshape(pixel_rows, width)] * SPLIT),
        (field_shape, to_modes),
        blocks=field_blocks(2),
    )
    arrived = exchange(send)
    (cot_rows,) = call(
        relayout_kernel,
        "relayout",
        (by_row, *[cotangent.reshape(pixel_rows, width)] * SPLIT),
        (field_shape,),
        blocks=field_blocks(1),
    )
    spectra, send = call(
        functools.partial(forward_kernel, spec_scale, samples, owned),
        "mix_forward",
        (arrived, by_mode, rows, back_rows, flat_weight),
        (shape((owned * lanes, both)), to_pixels),
        [
            pltpu.VMEM((owned * lanes, both), F32),
            pltpu.VMEM((owned * lanes, both), F32),
            pltpu.VMEM((owned, 2 * samples, channels, both), F32),
        ],
        grid=(owned,),
        blocks={4: weight_block},
    )
    all_spectra = lax.all_gather(spectra, "dp")
    arrived = exchange(send)
    steps = 4
    row_block = pl.BlockSpec((steps, lanes, width), lambda n: (n, 0, 0))
    gate_rows, send, local_sum = call(
        functools.partial(pixels_kernel, mode_scale, th),
        "pixels",
        (arrived, by_height, back_cols, forward_mix, field_rows, cot_rows, send_cols),
        (field_shape, to_modes, shape((channels, channels), F32)),
        [pltpu.VMEM((inverse, owned * lanes), BF16), pltpu.VMEM((lanes, lanes), F32)],
        grid=(th // steps,),
        blocks={4: row_block, 5: row_block},
        out_blocks={0: row_block, 1: pl.BlockSpec((halves, steps * lanes), lambda n: (0, n))},
        limit=SMALL,
    )
    arrived = exchange(send)
    local_sum = sum_over(local_sum, "tile")
    (grad_spectra,) = call(
        functools.partial(grad_spectra_kernel, mode_scale, owned),
        "grad_spectra",
        (arrived, by_mode, rows, local_sum),
        (shape((owned * lanes + channels, both)),),
        limit=SMALL,
    )
    all_grads = lax.all_gather(grad_spectra, "dp")
    (send,) = call(
        functools.partial(backward_kernel, samples),
        "mix_backward",
        (grad_spectra, back_rows, flat_weight),
        (to_pixels,),
        [
            pltpu.VMEM((owned * lanes, both), BF16),
            pltpu.VMEM((owned * lanes, both), BF16),
            pltpu.VMEM((owned, 2 * samples, channels * ROWS, both), F32),
        ],
        grid=(owned,),
        blocks={2: weight_block},
    )
    arrived = exchange(send)

    groups = lax.axis_size("dp")
    total = groups * samples
    per_mode = pl.BlockSpec((groups, lanes, both), lambda q: (0, q, 0))
    below = owned * lanes // channels
    mode_grad, local_grad = call(
        functools.partial(outer_kernel, samples),
        "mode_grad",
        (all_spectra, all_grads, all_grads),
        (shape(flat_weight.shape, F32), shape((channels, channels), F32)),
        [pltpu.VMEM((total, channels, both), F32)] * 2 + [pltpu.VMEM((total, channels, both), BF16)] * 2,
        grid=(owned,),
        blocks={
            0: per_mode,
            1: per_mode,
            2: pl.BlockSpec((groups, channels, both), lambda q: (0, below, 0)),
        },
        out_blocks={0: weight_block},
    )
    arrived, mode_grad = lax.optimization_barrier((arrived, mode_grad))

    (input_grad,) = call(
        functools.partial(final_kernel, spec_scale),
        "final",
        (arrived, by_height, back_cols, backward_mix, gate_rows, by_channel),
        (shape((pixel_rows, width)),),
        [pltpu.VMEM((th, lanes, width), BF16)],
        limit=SMALL,
    )
    return (input_grad.reshape(inputs.shape), mode_grad.reshape(mode_weight.shape), local_grad)


def solution(mesh):
    return jax.shard_map(
        local,
        mesh=mesh,
        in_specs=(
            P("dp", None, "tile", None),
            P("dp", None, "tile", None),
            P("tile", None, None, None),
            P(),
        ),
        out_specs=(P("dp", None, "tile", None), P("tile", None, None, None), P()),
        check_vma=False,
    )
```

```python
import functools
import math

import jax
import jax.numpy as jnp
import numpy as np
from jax import lax
from jax.experimental import pallas as pl
from jax.experimental.pallas import tpu as pltpu
from jax.sharding import PartitionSpec as P

F32 = jnp.float32
BF16 = jnp.bfloat16
LIMIT = 56 * 1024 * 1024
SMALL = 24 * 1024 * 1024
ROWS = 8
PACK = 16
GROUP = 8
SPLIT = 4


def row_tables(height, modes):
    index = np.arange(modes)
    signed = np.where(index < modes // 2, index, index - modes)
    phases = np.mod(np.arange(height)[:, None] * signed[None, :], height)
    angles = phases * (2.0 * math.pi / height)
    return np.cos(angles), np.sin(angles)


def column_tables(width, modes):
    phases = np.mod(np.arange(modes)[:, None] * np.arange(width)[None, :], width)
    angles = phases * (2.0 * math.pi / width)
    return np.stack([np.cos(angles), -np.sin(angles)])


def constant(table):
    return jnp.asarray(np.asarray(table, np.float32)).astype(BF16)


def tables(tiles, owned, th, width, modes):
    cols = column_tables(width, tiles * owned)
    split = cols.reshape(2, tiles, owned, width)
    send_cols = split.transpose(1, 0, 2, 3).reshape(tiles, 2 * owned, width)
    send_cols = np.pad(send_cols, ((0, 0), (0, padded(2 * owned) - 2 * owned), (0, 0))).reshape(-1, width)
    back_cols = split.transpose(2, 1, 0, 3).reshape(-1, width)
    cosine, sine = row_tables(th * tiles, modes)
    real = np.concatenate([cosine, -sine], axis=1)
    imag = np.concatenate([sine, cosine], axis=1)
    pair = np.stack([real, imag]).reshape(2, tiles, th, 2 * modes)
    rows = pair.transpose(2, 1, 0, 3).reshape(-1, 2 * modes)
    back_rows = pair.transpose(1, 0, 2, 3).reshape(-1, 2 * modes)
    return constant(send_cols), constant(rows), constant(back_rows), constant(back_cols)


def padded(rows):
    return -(-rows // PACK) * PACK


def order(outer, inner):
    take = np.arange(outer * inner).reshape(outer, inner).T.reshape(-1)
    return constant(np.eye(outer * inner)[take])


def mode_order(tiles, owned):
    rows = np.arange(tiles * padded(2 * owned)).reshape(tiles, -1)
    take = rows[:, : 2 * owned].reshape(tiles, 2, owned).transpose(2, 0, 1).reshape(-1)
    return constant(np.eye(rows.size)[take])


def dot(left, right, dims):
    return lax.dot_general(left, right, (dims, ((), ())), preferred_element_type=F32)


def low_half(shape, half):
    return lax.broadcasted_iota(jnp.int32, shape, 1) < half


def gelu_slope(values):
    size = jnp.abs(values)
    expo = jnp.exp(-0.5 * values * values)
    t = 1.0 / (1.0 + (0.3275911 / math.sqrt(2.0)) * size)
    poly = 0.5 * 1.061405429
    for factor in (-1.453152027, 1.421413741, -0.284496736, 0.254829592):
        poly = poly * t + 0.5 * factor
    tail = poly * t * expo
    cumulative = jnp.where(values < 0.0, tail, 1.0 - tail)
    return cumulative + values * expo * (1.0 / math.sqrt(2.0 * math.pi))


def shuffle(order_ref, value):
    return dot(order_ref[...], value, ((1,), (0,))).astype(BF16)


def by_rows(order_ref, field_refs, rows_ref):
    heights, lanes, _ = rows_ref.shape
    block = PACK * heights
    quarter = lanes // len(field_refs)
    for first in range(0, lanes, PACK):
        start = first % quarter * heights
        moved = shuffle(order_ref, field_refs[first // quarter][start : start + block, :])
        for h in range(heights):
            rows_ref[h, first : first + PACK, :] = moved[h * PACK : (h + 1) * PACK]


def columns_kernel(order_ref, table_ref, *rest):
    field_refs, (rows_ref, send_ref) = rest[:SPLIT], rest[SPLIT:]
    heights, lanes, _ = rows_ref.shape
    by_rows(order_ref, field_refs, rows_ref)
    for h in range(heights):
        send_ref[:, h * lanes : (h + 1) * lanes] = dot(table_ref[...], rows_ref[h], ((1,), (1,))).astype(BF16)


def relayout_kernel(order_ref, *rest):
    by_rows(order_ref, rest[:SPLIT], rest[SPLIT])


def shuffle_groups(order_ref, recv_ref):
    size = order_ref.shape[0]
    return [shuffle(order_ref, recv_ref[n : n + size, :]) for n in range(0, recv_ref.shape[0], size)]


def stack(groups, index, count, lanes):
    return jnp.concatenate(
        [
            group[index * count : (index + 1) * count, n : n + lanes]
            for n in range(0, groups[0].shape[1], lanes)
            for group in groups
        ],
        axis=0,
    )


def spectra_into(scale, owned, recv_ref, order_ref, rows_ref, spec_ref):
    count = order_ref.shape[0] // owned
    lanes = recv_ref.shape[1] * count // rows_ref.shape[0]
    ordered = [shuffle(order_ref, recv_ref[...])]
    for q in range(owned):
        stacked = stack(ordered, q, count, lanes)
        spec_ref[q * lanes : (q + 1) * lanes, :] = (
            scale * dot(stacked, rows_ref[...], ((0,), (0,)))
        ).astype(BF16)


def grad_spectra_kernel(scale, owned, recv_ref, order_ref, rows_ref, local_ref, spec_ref):
    spectra_into(scale, owned, recv_ref, order_ref, rows_ref, spec_ref)
    value = local_ref[...]
    high = value.astype(BF16)
    low = (value - high.astype(F32)).astype(BF16)
    spec_ref[spec_ref.shape[0] - value.shape[0] :, :] = jnp.concatenate([high, low], axis=1)


def tree(terms):
    while len(terms) > 1:
        terms = [a + b for a, b in zip(terms[0::2], terms[1::2])]
    return terms[0]


def packed_row(store, index):
    row = store[pl.ds(index, 1), :]
    return jnp.broadcast_to(row, (PACK, row.shape[1])).astype(BF16)


def duplicates(spec, half):
    value = spec.astype(F32)
    other = pltpu.roll(value, half, 1)
    low = low_half(value.shape, half)
    return jnp.where(low, value, other), jnp.where(low, other, value)


def finish(back_ref, sums, send_ref, mix):
    @pl.when(pl.program_id(0) == pl.num_programs(0) - 1)
    def _():
        owned = sums.shape[0]
        lanes = send_ref.shape[1] // owned
        for q in range(owned):
            mixed = mix(sums.at[q]).astype(BF16)
            send_ref[:, q * lanes : (q + 1) * lanes] = dot(back_ref[...], mixed, ((1,), (1,))).astype(BF16)


def forward_kernel(scale, samples, owned, recv_ref, order_ref, rows_ref, back_ref, weight_ref, *rest):
    spec_ref, send_ref, real, imag, sums = rest
    _, _, outs, both = sums.shape
    channels = weight_ref.shape[0] // outs
    half = both // 2
    lanes = samples * channels
    q = pl.program_id(0)

    @pl.when(q == 0)
    def _():
        spectra_into(scale, owned, recv_ref, order_ref, rows_ref, spec_ref)
        real[...], imag[...] = duplicates(spec_ref[...], half)
        sums[...] = jnp.zeros_like(sums)

    def window(c, o):
        return pl.ds(pl.multiple_of(c * outs + o, PACK), PACK)

    def body(block, carry):
        first = block * GROUP
        rows = [
            [packed_row(store, q * lanes + s * channels + first + step) for step in range(GROUP)]
            for s in range(samples)
            for store in (real, imag)
        ]
        for start in range(0, outs, 2 * PACK):
            totals = []
            for o in (start, start + PACK):
                column = [weight_ref[window(first + step, o), :] for step in range(GROUP)]
                for n, row in enumerate(rows):
                    totals.append((n, o, tree([w * r for w, r in zip(column, row)])))
            updated = [(n, o, sums[q, n, o : o + PACK, :] + total.astype(F32)) for n, o, total in totals]
            for n, o, total in updated:
                sums[q, n, o : o + PACK, :] = total
        return carry

    lax.fori_loop(0, channels // GROUP, body, 0)

    def mix(parts):
        low = low_half((outs, both), half)
        result = []
        for s in range(samples):
            crossed = pltpu.roll(parts[2 * s + 1], half, 1)
            result.append(parts[2 * s] + jnp.where(low, -crossed, crossed))
        return jnp.concatenate(result, axis=0)

    finish(back_ref, sums, send_ref, mix)


def backward_kernel(samples, spec_ref, back_ref, weight_ref, send_ref, real, imag, sums):
    channels, both = sums.shape[2] // ROWS, sums.shape[3]
    outs = weight_ref.shape[0] // channels
    half = both // 2
    lanes = samples * outs
    q = pl.program_id(0)

    @pl.when(q == 0)
    def _():
        first, second = duplicates(spec_ref[: real.shape[0], :], half)
        real[...], imag[...] = first.astype(BF16), second.astype(BF16)

    grads = [
        [store[pl.ds(pl.multiple_of(q * lanes + s * outs + o, PACK), PACK), :] for o in range(0, outs, PACK)]
        for s in range(samples)
        for store in (real, imag)
    ]

    def window(c, o):
        return pl.ds(pl.multiple_of(c * outs + o, PACK), PACK)

    def body(block, carry):
        totals = []
        for step in range(GROUP):
            c = block * GROUP + step
            column = [weight_ref[window(c, o), :] for o in range(0, outs, PACK)]
            for n, grad in enumerate(grads):
                total = tree([w * g for w, g in zip(column, grad)]).astype(F32)
                totals.append((n, c, total[:ROWS] + total[ROWS:]))
        for n, c, total in totals:
            sums[q, n, pl.ds(pl.multiple_of(c * ROWS, ROWS), ROWS), :] = total
        return carry

    lax.fori_loop(0, channels // GROUP, body, 0)

    def mix(parts):
        low = low_half((channels, both), half)
        result = []
        for s in range(samples):
            straight, crossed = (
                sum(parts[n, pl.ds(row, channels, stride=ROWS), :] for row in range(ROWS)) for n in (2 * s, 2 * s + 1)
            )
            result.append(jnp.where(low, straight, -straight) + pltpu.roll(crossed, half, 1))
        return jnp.concatenate(result, axis=0)

    finish(back_ref, sums, send_ref, mix)


def pixels_kernel(scale, heights, recv_ref, order_ref, back_ref, local_ref, field_ref, cot_ref, table_ref, *rest):
    grad_ref, send_ref, sum_ref, ordered, total = rest
    steps, lanes, _ = field_ref.shape
    count = order_ref.shape[0] // heights
    size = order_ref.shape[0]
    group = pl.program_id(0)

    @pl.when(group == 0)
    def _():
        for n in range(0, recv_ref.shape[0], size):
            ordered[n : n + size, :] = shuffle(order_ref, recv_ref[n : n + size, :])
        total[...] = jnp.zeros_like(total)

    local = jnp.zeros(total.shape, F32)
    for step in range(steps):
        parts = []
        for n in range(0, recv_ref.shape[0], size):
            first = pl.multiple_of(n + (group * steps + step) * count, count)
            parts.append(ordered[pl.ds(first, count), :])
        inner = stack(parts, 0, count, lanes)
        pre = scale * dot(inner, back_ref[...], ((0,), (0,)))
        pre = pre + dot(local_ref[...], field_ref[step], ((1,), (0,)))
        grad = (cot_ref[step].astype(F32) * gelu_slope(pre)).astype(BF16)
        grad_ref[step] = grad
        send_ref[:, step * lanes : (step + 1) * lanes] = dot(table_ref[...], grad, ((1,), (1,))).astype(BF16)
        local = local + dot(field_ref[step], grad, ((1,), (1,)))
    total[...] += local

    @pl.when(group == pl.num_programs(0) - 1)
    def _():
        extent = sum_ref.shape[0]
        sum_ref[...] = sum(total[n : n + extent, n : n + extent] for n in range(0, lanes, extent))


def final_kernel(scale, recv_ref, order_ref, back_ref, local_ref, grad_ref, restore_ref, out_ref, result):
    heights, lanes, _ = grad_ref.shape
    count = order_ref.shape[0] // heights
    ordered = shuffle_groups(order_ref, recv_ref)
    for h in range(heights):
        inner = stack(ordered, h, count, lanes)
        value = scale * dot(inner, back_ref[...], ((0,), (0,)))
        result[h] = (value + dot(local_ref[...], grad_ref[h], ((1,), (0,)))).astype(BF16)
    block = PACK * heights
    for first in range(0, lanes, PACK):
        part = jnp.concatenate([result[h, first : first + PACK, :] for h in range(heights)], axis=0)
        out_ref[first * heights : first * heights + block, :] = shuffle(restore_ref, part)


def outer_kernel(samples, groups, *refs):
    specs, grads, pairs = refs[:groups], refs[groups : 2 * groups], refs[2 * groups : 3 * groups]
    out_ref, local_ref, real, imag, plain, crossed = refs[3 * groups :]
    total, channels, both = real.shape
    outs = plain.shape[1]
    half = both // 2
    low = low_half((channels, both), half)

    @pl.when(pl.program_id(0) == 0)
    def _():
        value = 0.0
        for pair_ref in pairs:
            pair = pair_ref[...].astype(F32)
            value = value + pair[:, :channels] + pair[:, channels : 2 * channels]
        local_ref[...] = value

    for g in range(groups):
        for s in range(samples):
            n = g * samples + s
            spec = specs[g][s * channels : (s + 1) * channels, :].astype(F32)
            other = pltpu.roll(spec, half, 1)
            real[n] = jnp.where(low, spec, other)
            imag[n] = jnp.where(low, other, -spec)
            grad = grads[g][s * outs : (s + 1) * outs, :]
            plain[n] = grad
            crossed[n] = pltpu.roll(grad.astype(F32), half, 1).astype(BF16)

    def body(pair, carry):
        lefts = [
            [packed_row(store.at[n], 2 * pair + c) for n in range(total) for store in (real, imag)] for c in range(2)
        ]
        results = []
        for o in range(0, outs, PACK):
            right = [store[n, o : o + PACK, :] for n in range(total) for store in (plain, crossed)]
            for c, left in enumerate(lefts):
                results.append((c, o, tree([a * b for a, b in zip(left, right)])))
        for c, o, result in results:
            row = pl.multiple_of((2 * pair + c) * outs + o, PACK)
            out_ref[pl.ds(row, PACK), :] = result.astype(F32)
        return carry

    lax.fori_loop(0, channels // 2, body, 0)


def whole(extent):
    return pl.BlockSpec(extent, lambda *_: (0,) * len(extent))


def call(kernel, name, operands, outs, scratch=(), grid=(1,), blocks=None, out_blocks=None, limit=LIMIT):
    blocks, out_blocks = blocks or {}, out_blocks or {}
    in_specs = [blocks.get(n) or whole(operand.shape) for n, operand in enumerate(operands)]
    out_specs = [out_blocks.get(n, whole(out.shape)) for n, out in enumerate(outs)]
    return pl.pallas_call(
        kernel,
        out_shape=tuple(outs),
        grid=grid,
        in_specs=in_specs,
        out_specs=tuple(out_specs),
        scratch_shapes=list(scratch),
        compiler_params=pltpu.CompilerParams(vmem_limit_bytes=limit),
        name=name,
    )(*operands)


def gather(values, axis):
    size = lax.axis_size(axis)
    return [values] + [
        lax.ppermute(values, axis, [(i, i ^ step) for i in range(size)]) for step in range(1, size)
    ]


def sum_over(values, axis):
    size = lax.axis_size(axis)
    step = 1
    while step < size:
        values = values + lax.ppermute(values, axis, [(i, i ^ step) for i in range(size)])
        step *= 2
    return values


def block_diagonal(matrix, copies):
    zero = jnp.zeros_like(matrix)
    return jnp.concatenate(
        [
            jnp.concatenate([matrix if i == j else zero for j in range(copies)], axis=1)
            for i in range(copies)
        ],
        axis=0,
    )


def shape(extent, kind=BF16):
    return jax.ShapeDtypeStruct(extent, kind)


def local(inputs, cotangent, mode_weight, local_weight):
    tiles = lax.axis_size("tile")
    samples, channels, th, width = inputs.shape
    owned, _, _, both = mode_weight.shape
    modes = both // 2
    lanes = samples * channels
    parts = width // 128
    spec_scale = 1.0 / math.sqrt(tiles * th * width)
    mode_scale = 1.0 / math.sqrt(modes * tiles * owned)
    send_cols, rows, back_rows, back_cols = tables(tiles, owned, th, width, modes)
    pixel_rows = samples * channels * th
    halves = tiles * padded(2 * owned)
    inverse = 2 * tiles * th

    def exchange(values):
        split = values.reshape(tiles, values.shape[0] // tiles, values.shape[1])
        moved = lax.all_to_all(split, "tile", split_axis=0, concat_axis=0, tiled=False)
        return moved.reshape(values.shape)

    forward_mix = block_diagonal(local_weight.T, samples)
    backward_mix = block_diagonal(local_weight, samples)
    by_row = order(PACK, th)
    by_channel = order(th, PACK)
    by_mode = mode_order(tiles, owned)
    by_height = order(2 * min(tiles, 8), th)
    flat_weight = mode_weight.reshape(-1, both)
    weight_block = pl.BlockSpec((flat_weight.shape[0] // owned, both), lambda q: (q, 0))
    to_modes = shape((halves, th * lanes))
    to_pixels = shape((inverse, owned * lanes))
    field_shape = shape((th, lanes, width))

    def field_blocks(first):
        return {first + n: pl.BlockSpec((pixel_rows // SPLIT, width), lambda _, n=n: (n, 0)) for n in range(SPLIT)}

    field_rows, send = call(
        columns_kernel,
        "columns",
        (by_row, send_cols, *[inputs.reshape(pixel_rows, width)] * SPLIT),
        (field_shape, to_modes),
        blocks=field_blocks(2),
    )
    arrived = exchange(send)
    (cot_rows,) = call(
        relayout_kernel,
        "relayout",
        (by_row, *[cotangent.reshape(pixel_rows, width)] * SPLIT),
        (field_shape,),
        blocks=field_blocks(1),
    )
    spectra, send = call(
        functools.partial(forward_kernel, spec_scale, samples, owned),
        "mix_forward",
        (arrived, by_mode, rows, back_rows, flat_weight),
        (shape((owned * lanes, both)), to_pixels),
        [
            pltpu.VMEM((owned * lanes, both), F32),
            pltpu.VMEM((owned * lanes, both), F32),
            pltpu.VMEM((owned, 2 * samples, channels, both), F32),
        ],
        grid=(owned,),
        blocks={4: weight_block},
    )
    all_spectra = gather(spectra, "dp")
    arrived = exchange(send)
    arrived, *all_spectra = lax.optimization_barrier((arrived, *all_spectra))
    steps = 4
    row_block = pl.BlockSpec((steps, lanes, width), lambda n: (n, 0, 0))
    gate_rows, send, local_sum = call(
        functools.partial(pixels_kernel, mode_scale, th),
        "pixels",
        (arrived, by_height, back_cols, forward_mix, field_rows, cot_rows, send_cols),
        (field_shape, to_modes, shape((channels, channels), F32)),
        [pltpu.VMEM((inverse, owned * lanes), BF16), pltpu.VMEM((lanes, lanes), F32)],
        grid=(th // steps,),
        blocks={4: row_block, 5: row_block},
        out_blocks={0: row_block, 1: pl.BlockSpec((halves, steps * lanes), lambda n: (0, n))},
        limit=SMALL,
    )
    arrived = exchange(send)
    local_sum = sum_over(local_sum, "tile")
    (grad_spectra,) = call(
        functools.partial(grad_spectra_kernel, mode_scale, owned),
        "grad_spectra",
        (arrived, by_mode, rows, local_sum),
        (shape((owned * lanes + channels, both)),),
        limit=SMALL,
    )
    all_grads = gather(grad_spectra, "dp")
    (send,) = call(
        functools.partial(backward_kernel, samples),
        "mix_backward",
        (grad_spectra, back_rows, flat_weight),
        (to_pixels,),
        [
            pltpu.VMEM((owned * lanes, both), BF16),
            pltpu.VMEM((owned * lanes, both), BF16),
            pltpu.VMEM((owned, 2 * samples, channels * ROWS, both), F32),
        ],
        grid=(owned,),
        blocks={2: weight_block},
    )
    send, *all_grads = lax.optimization_barrier((send, *all_grads))
    arrived = exchange(send)

    groups = lax.axis_size("dp")
    total = groups * samples
    per_mode = pl.BlockSpec((lanes, both), lambda q: (q, 0))
    below = owned * lanes // channels
    pair_block = pl.BlockSpec((channels, both), lambda q: (below, 0))
    mode_grad, local_grad = call(
        functools.partial(outer_kernel, samples, groups),
        "mode_grad",
        (*all_spectra, *all_grads, *all_grads),
        (shape(flat_weight.shape, F32), shape((channels, channels), F32)),
        [pltpu.VMEM((total, channels, both), F32)] * 2 + [pltpu.VMEM((total, channels, both), BF16)] * 2,
        grid=(owned,),
        blocks={n: per_mode if n < 2 * groups else pair_block for n in range(3 * groups)},
        out_blocks={0: weight_block},
    )
    arrived, mode_grad = lax.optimization_barrier((arrived, mode_grad))

    (input_grad,) = call(
        functools.partial(final_kernel, spec_scale),
        "final",
        (arrived, by_height, back_cols, backward_mix, gate_rows, by_channel),
        (shape((pixel_rows, width)),),
        [pltpu.VMEM((th, lanes, width), BF16)],
        limit=SMALL,
    )
    return (input_grad.reshape(inputs.shape), mode_grad.reshape(mode_weight.shape), local_grad)


def solution(mesh):
    return jax.shard_map(
        local,
        mesh=mesh,
        in_specs=(
            P("dp", None, "tile", None),
            P("dp", None, "tile", None),
            P("tile", None, None, None),
            P(),
        ),
        out_specs=(P("dp", None, "tile", None), P("tile", None, None, None), P()),
        check_vma=False,
    )
```

```python
import functools
import math

import jax
import jax.numpy as jnp
import numpy as np
from jax import lax
from jax.experimental import pallas as pl
from jax.experimental.pallas import tpu as pltpu
from jax.sharding import PartitionSpec as P

F32 = jnp.float32
BF16 = jnp.bfloat16
LIMIT = 56 * 1024 * 1024
SMALL = 24 * 1024 * 1024
ROWS = 8
PACK = 16
GROUP = 8
SPLIT = 4


def row_tables(height, modes):
    index = np.arange(modes)
    signed = np.where(index < modes // 2, index, index - modes)
    phases = np.mod(np.arange(height)[:, None] * signed[None, :], height)
    angles = phases * (2.0 * math.pi / height)
    return np.cos(angles), np.sin(angles)


def column_tables(width, modes):
    phases = np.mod(np.arange(modes)[:, None] * np.arange(width)[None, :], width)
    angles = phases * (2.0 * math.pi / width)
    return np.stack([np.cos(angles), -np.sin(angles)])


def constant(table):
    return jnp.asarray(np.asarray(table, np.float32)).astype(BF16)


def tables(tiles, owned, th, width, modes):
    cols = column_tables(width, tiles * owned)
    split = cols.reshape(2, tiles, owned, width)
    send_cols = split.transpose(1, 0, 2, 3).reshape(tiles, 2 * owned, width)
    send_cols = np.pad(send_cols, ((0, 0), (0, padded(2 * owned) - 2 * owned), (0, 0))).reshape(-1, width)
    back_cols = split.transpose(2, 1, 0, 3).reshape(-1, width)
    cosine, sine = row_tables(th * tiles, modes)
    real = np.concatenate([cosine, -sine], axis=1)
    imag = np.concatenate([sine, cosine], axis=1)
    pair = np.stack([real, imag]).reshape(2, tiles, th, 2 * modes)
    rows = pair.transpose(2, 1, 0, 3).reshape(-1, 2 * modes)
    back_rows = pair.transpose(1, 0, 2, 3).reshape(-1, 2 * modes)
    return constant(send_cols), constant(rows), constant(back_rows), constant(back_cols)


def padded(rows):
    return -(-rows // PACK) * PACK


def order(outer, inner):
    take = np.arange(outer * inner).reshape(outer, inner).T.reshape(-1)
    return constant(np.eye(outer * inner)[take])


def mode_order(tiles, owned):
    rows = np.arange(tiles * padded(2 * owned)).reshape(tiles, -1)
    take = rows[:, : 2 * owned].reshape(tiles, 2, owned).transpose(2, 0, 1).reshape(-1)
    return constant(np.eye(rows.size)[take])


def dot(left, right, dims):
    return lax.dot_general(left, right, (dims, ((), ())), preferred_element_type=F32)


def low_half(shape, half):
    return lax.broadcasted_iota(jnp.int32, shape, 1) < half


def gelu_slope(values):
    size = jnp.abs(values)
    expo = jnp.exp(-0.5 * values * values)
    t = 1.0 / (1.0 + (0.3275911 / math.sqrt(2.0)) * size)
    poly = 0.5 * 1.061405429
    for factor in (-1.453152027, 1.421413741, -0.284496736, 0.254829592):
        poly = poly * t + 0.5 * factor
    tail = poly * t * expo
    cumulative = jnp.where(values < 0.0, tail, 1.0 - tail)
    return cumulative + values * expo * (1.0 / math.sqrt(2.0 * math.pi))


def shuffle(order_ref, value):
    return dot(order_ref[...], value, ((1,), (0,))).astype(BF16)


def by_rows(order_ref, field_refs, rows_ref):
    heights, lanes, _ = rows_ref.shape
    block = PACK * heights
    quarter = lanes // len(field_refs)
    for first in range(0, lanes, PACK):
        start = first % quarter * heights
        moved = shuffle(order_ref, field_refs[first // quarter][start : start + block, :])
        for h in range(heights):
            rows_ref[h, first : first + PACK, :] = moved[h * PACK : (h + 1) * PACK]


def columns_kernel(order_ref, table_ref, *rest):
    field_refs, (rows_ref, send_ref) = rest[:SPLIT], rest[SPLIT:]
    heights, lanes, _ = rows_ref.shape
    by_rows(order_ref, field_refs, rows_ref)
    for h in range(heights):
        send_ref[:, h * lanes : (h + 1) * lanes] = dot(table_ref[...], rows_ref[h], ((1,), (1,))).astype(BF16)


def relayout_kernel(order_ref, *rest):
    by_rows(order_ref, rest[:SPLIT], rest[SPLIT])


def shuffle_groups(order_ref, recv_ref):
    size = order_ref.shape[0]
    return [shuffle(order_ref, recv_ref[n : n + size, :]) for n in range(0, recv_ref.shape[0], size)]


def stack(groups, index, count, lanes):
    return jnp.concatenate(
        [
            group[index * count : (index + 1) * count, n : n + lanes]
            for n in range(0, groups[0].shape[1], lanes)
            for group in groups
        ],
        axis=0,
    )


def spectra_into(scale, owned, recv_ref, order_ref, rows_ref, spec_ref):
    count = order_ref.shape[0] // owned
    lanes = recv_ref.shape[1] * count // rows_ref.shape[0]
    ordered = [shuffle(order_ref, recv_ref[...])]
    for q in range(owned):
        stacked = stack(ordered, q, count, lanes)
        spec_ref[q * lanes : (q + 1) * lanes, :] = (
            scale * dot(stacked, rows_ref[...], ((0,), (0,)))
        ).astype(BF16)


def grad_spectra_kernel(scale, owned, recv_ref, order_ref, rows_ref, local_ref, spec_ref):
    spectra_into(scale, owned, recv_ref, order_ref, rows_ref, spec_ref)
    value = local_ref[...]
    high = value.astype(BF16)
    low = (value - high.astype(F32)).astype(BF16)
    spec_ref[spec_ref.shape[0] - value.shape[0] :, :] = jnp.concatenate([high, low], axis=1)


def tree(terms):
    while len(terms) > 1:
        terms = [a + b for a, b in zip(terms[0::2], terms[1::2])]
    return terms[0]


def rows_of(store, block, extent):
    return store.at[pl.ds(pl.multiple_of(block * extent, extent), extent), :]


def packed_row(view, index):
    row = view[index : index + 1, :]
    return jnp.broadcast_to(row, (PACK, row.shape[1])).astype(BF16)


def duplicates(spec, half):
    value = spec.astype(F32)
    other = pltpu.roll(value, half, 1)
    low = low_half(value.shape, half)
    return jnp.where(low, value, other), jnp.where(low, other, value)


def finish(back_ref, sums, send_ref, mix):
    @pl.when(pl.program_id(0) == pl.num_programs(0) - 1)
    def _():
        owned = sums.shape[0]
        lanes = send_ref.shape[1] // owned
        for q in range(owned):
            mixed = mix(sums.at[q]).astype(BF16)
            send_ref[:, q * lanes : (q + 1) * lanes] = dot(back_ref[...], mixed, ((1,), (1,))).astype(BF16)


def forward_kernel(scale, samples, owned, recv_ref, order_ref, rows_ref, back_ref, weight_ref, *rest):
    spec_ref, send_ref, real, imag, sums = rest
    _, _, outs, both = sums.shape
    channels = weight_ref.shape[0] // outs
    half = both // 2
    lanes = samples * channels
    q = pl.program_id(0)

    @pl.when(q == 0)
    def _():
        spectra_into(scale, owned, recv_ref, order_ref, rows_ref, spec_ref)
        real[...], imag[...] = duplicates(spec_ref[...], half)
        sums[...] = jnp.zeros_like(sums)

    def body(block, carry):
        view = rows_of(weight_ref, block, GROUP * outs)
        rows = []
        for s in range(samples):
            for store in (real, imag):
                part = rows_of(store, (q * lanes + s * channels) // GROUP + block, GROUP)
                rows.append([packed_row(part, step) for step in range(GROUP)])
        into = sums.at[q]
        for start in range(0, outs, 2 * PACK):
            totals = []
            for o in (start, start + PACK):
                column = [view[step * outs + o : step * outs + o + PACK, :] for step in range(GROUP)]
                for n, row in enumerate(rows):
                    totals.append((n, o, tree([w * r for w, r in zip(column, row)])))
            updated = [(n, o, into[n, o : o + PACK, :] + total.astype(F32)) for n, o, total in totals]
            for n, o, total in updated:
                into[n, o : o + PACK, :] = total
        return carry

    lax.fori_loop(0, channels // GROUP, body, 0)

    def mix(parts):
        low = low_half((outs, both), half)
        result = []
        for s in range(samples):
            crossed = pltpu.roll(parts[2 * s + 1], half, 1)
            result.append(parts[2 * s] + jnp.where(low, -crossed, crossed))
        return jnp.concatenate(result, axis=0)

    finish(back_ref, sums, send_ref, mix)


def backward_kernel(samples, spec_ref, back_ref, weight_ref, send_ref, real, imag, sums):
    channels, both = sums.shape[2] // ROWS, sums.shape[3]
    outs = weight_ref.shape[0] // channels
    half = both // 2
    lanes = samples * outs
    q = pl.program_id(0)

    @pl.when(q == 0)
    def _():
        first, second = duplicates(spec_ref[: real.shape[0], :], half)
        real[...], imag[...] = first.astype(BF16), second.astype(BF16)

    grads = [
        [store[pl.ds(pl.multiple_of(q * lanes + s * outs + o, PACK), PACK), :] for o in range(0, outs, PACK)]
        for s in range(samples)
        for store in (real, imag)
    ]

    def body(block, carry):
        view = rows_of(weight_ref, block, GROUP * outs)
        totals = []
        for step in range(GROUP):
            column = [view[step * outs + o : step * outs + o + PACK, :] for o in range(0, outs, PACK)]
            for n, grad in enumerate(grads):
                total = tree([w * g for w, g in zip(column, grad)]).astype(F32)
                totals.append((n, step, total[:ROWS] + total[ROWS:]))
        into = [rows_of(sums.at[q, n], block, GROUP * ROWS) for n in range(len(grads))]
        for n, step, total in totals:
            into[n][step * ROWS : (step + 1) * ROWS, :] = total
        return carry

    lax.fori_loop(0, channels // GROUP, body, 0)

    def mix(parts):
        low = low_half((channels, both), half)
        result = []
        for s in range(samples):
            straight, crossed = (
                sum(parts[n, pl.ds(row, channels, stride=ROWS), :] for row in range(ROWS)) for n in (2 * s, 2 * s + 1)
            )
            result.append(jnp.where(low, straight, -straight) + pltpu.roll(crossed, half, 1))
        return jnp.concatenate(result, axis=0)

    finish(back_ref, sums, send_ref, mix)


def pixels_kernel(scale, heights, recv_ref, order_ref, back_ref, local_ref, field_ref, cot_ref, table_ref, *rest):
    grad_ref, send_ref, sum_ref, ordered, total = rest
    steps, lanes, _ = field_ref.shape
    count = order_ref.shape[0] // heights
    size = order_ref.shape[0]
    group = pl.program_id(0)

    @pl.when(group == 0)
    def _():
        for n in range(0, recv_ref.shape[0], size):
            ordered[n : n + size, :] = shuffle(order_ref, recv_ref[n : n + size, :])
        total[...] = jnp.zeros_like(total)

    local = jnp.zeros(total.shape, F32)
    for step in range(steps):
        parts = []
        for n in range(0, recv_ref.shape[0], size):
            first = pl.multiple_of(n + (group * steps + step) * count, count)
            parts.append(ordered[pl.ds(first, count), :])
        inner = stack(parts, 0, count, lanes)
        pre = scale * dot(inner, back_ref[...], ((0,), (0,)))
        pre = pre + dot(local_ref[...], field_ref[step], ((1,), (0,)))
        grad = (cot_ref[step].astype(F32) * gelu_slope(pre)).astype(BF16)
        grad_ref[step] = grad
        send_ref[:, step * lanes : (step + 1) * lanes] = dot(table_ref[...], grad, ((1,), (1,))).astype(BF16)
        local = local + dot(field_ref[step], grad, ((1,), (1,)))
    total[...] += local

    @pl.when(group == pl.num_programs(0) - 1)
    def _():
        extent = sum_ref.shape[0]
        sum_ref[...] = sum(total[n : n + extent, n : n + extent] for n in range(0, lanes, extent))


def final_kernel(scale, recv_ref, order_ref, back_ref, local_ref, grad_ref, restore_ref, out_ref, result):
    heights, lanes, _ = grad_ref.shape
    count = order_ref.shape[0] // heights
    ordered = shuffle_groups(order_ref, recv_ref)
    for h in range(heights):
        inner = stack(ordered, h, count, lanes)
        value = scale * dot(inner, back_ref[...], ((0,), (0,)))
        result[h] = (value + dot(local_ref[...], grad_ref[h], ((1,), (0,)))).astype(BF16)
    block = PACK * heights
    for first in range(0, lanes, PACK):
        part = jnp.concatenate([result[h, first : first + PACK, :] for h in range(heights)], axis=0)
        out_ref[first * heights : first * heights + block, :] = shuffle(restore_ref, part)


def outer_kernel(samples, groups, *refs):
    specs, grads, pairs = refs[:groups], refs[groups : 2 * groups], refs[2 * groups : 3 * groups]
    out_ref, local_ref, real, imag, plain, crossed = refs[3 * groups :]
    total, channels, both = real.shape
    outs = plain.shape[1]
    half = both // 2
    low = low_half((channels, both), half)

    @pl.when(pl.program_id(0) == 0)
    def _():
        value = 0.0
        for pair_ref in pairs:
            pair = pair_ref[...].astype(F32)
            value = value + pair[:, :channels] + pair[:, channels : 2 * channels]
        local_ref[...] = value

    for g in range(groups):
        for s in range(samples):
            n = g * samples + s
            spec = specs[g][s * channels : (s + 1) * channels, :].astype(F32)
            other = pltpu.roll(spec, half, 1)
            real[n] = jnp.where(low, spec, other)
            imag[n] = jnp.where(low, other, -spec)
            grad = grads[g][s * outs : (s + 1) * outs, :]
            plain[n] = grad
            crossed[n] = pltpu.roll(grad.astype(F32), half, 1).astype(BF16)

    def body(block, carry):
        into = rows_of(out_ref, block, GROUP * outs)
        views = [rows_of(store.at[n], block, GROUP) for n in range(total) for store in (real, imag)]
        for first in range(0, GROUP, 2):
            pair = range(first, first + 2)
            lefts = [[packed_row(view, c) for view in views] for c in pair]
            results = []
            for o in range(0, outs, PACK):
                right = [store[n, o : o + PACK, :] for n in range(total) for store in (plain, crossed)]
                for c, left in zip(pair, lefts):
                    results.append((c * outs + o, tree([a * b for a, b in zip(left, right)])))
            for row, result in results:
                into[row : row + PACK, :] = result.astype(F32)
        return carry

    lax.fori_loop(0, channels // GROUP, body, 0)


def whole(extent):
    return pl.BlockSpec(extent, lambda *_: (0,) * len(extent))


def call(kernel, name, operands, outs, scratch=(), grid=(1,), blocks=None, out_blocks=None, limit=LIMIT):
    blocks, out_blocks = blocks or {}, out_blocks or {}
    in_specs = [blocks.get(n) or whole(operand.shape) for n, operand in enumerate(operands)]
    out_specs = [out_blocks.get(n, whole(out.shape)) for n, out in enumerate(outs)]
    return pl.pallas_call(
        kernel,
        out_shape=tuple(outs),
        grid=grid,
        in_specs=in_specs,
        out_specs=tuple(out_specs),
        scratch_shapes=list(scratch),
        compiler_params=pltpu.CompilerParams(vmem_limit_bytes=limit),
        name=name,
    )(*operands)


def gather(values, axis):
    size = lax.axis_size(axis)
    return [values] + [
        lax.ppermute(values, axis, [(i, i ^ step) for i in range(size)]) for step in range(1, size)
    ]


def sum_over(values, axis):
    size = lax.axis_size(axis)
    top = size
    while top > 1:
        low = max(top // 4, 1)
        values = sum(
            (lax.ppermute(values, axis, [(i, i ^ step) for i in range(size)]) for step in range(low, top, low)),
            values,
        )
        top = low
    return values


def block_diagonal(matrix, copies):
    zero = jnp.zeros_like(matrix)
    return jnp.concatenate(
        [
            jnp.concatenate([matrix if i == j else zero for j in range(copies)], axis=1)
            for i in range(copies)
        ],
        axis=0,
    )


def shape(extent, kind=BF16):
    return jax.ShapeDtypeStruct(extent, kind)


def local(inputs, cotangent, mode_weight, local_weight):
    tiles = lax.axis_size("tile")
    samples, channels, th, width = inputs.shape
    owned, _, _, both = mode_weight.shape
    modes = both // 2
    lanes = samples * channels
    parts = width // 128
    spec_scale = 1.0 / math.sqrt(tiles * th * width)
    mode_scale = 1.0 / math.sqrt(modes * tiles * owned)
    send_cols, rows, back_rows, back_cols = tables(tiles, owned, th, width, modes)
    pixel_rows = samples * channels * th
    halves = tiles * padded(2 * owned)
    inverse = 2 * tiles * th

    def exchange(values):
        split = values.reshape(tiles, values.shape[0] // tiles, values.shape[1])
        moved = lax.all_to_all(split, "tile", split_axis=0, concat_axis=0, tiled=False)
        return moved.reshape(values.shape)

    forward_mix = block_diagonal(local_weight.T, samples)
    backward_mix = block_diagonal(local_weight, samples)
    by_row = order(PACK, th)
    by_channel = order(th, PACK)
    by_mode = mode_order(tiles, owned)
    by_height = order(2 * min(tiles, 8), th)
    flat_weight = mode_weight.reshape(-1, both)
    weight_block = pl.BlockSpec((flat_weight.shape[0] // owned, both), lambda q: (q, 0))
    to_modes = shape((halves, th * lanes))
    to_pixels = shape((inverse, owned * lanes))
    field_shape = shape((th, lanes, width))

    def field_blocks(first):
        return {first + n: pl.BlockSpec((pixel_rows // SPLIT, width), lambda _, n=n: (n, 0)) for n in range(SPLIT)}

    field_rows, send = call(
        columns_kernel,
        "columns",
        (by_row, send_cols, *[inputs.reshape(pixel_rows, width)] * SPLIT),
        (field_shape, to_modes),
        blocks=field_blocks(2),
    )
    arrived = exchange(send)
    (cot_rows,) = call(
        relayout_kernel,
        "relayout",
        (by_row, *[cotangent.reshape(pixel_rows, width)] * SPLIT),
        (field_shape,),
        blocks=field_blocks(1),
    )
    spectra, send = call(
        functools.partial(forward_kernel, spec_scale, samples, owned),
        "mix_forward",
        (arrived, by_mode, rows, back_rows, flat_weight),
        (shape((owned * lanes, both)), to_pixels),
        [
            pltpu.VMEM((owned * lanes, both), F32),
            pltpu.VMEM((owned * lanes, both), F32),
            pltpu.VMEM((owned, 2 * samples, channels, both), F32),
        ],
        grid=(owned,),
        blocks={4: weight_block},
    )
    all_spectra = gather(spectra, "dp")
    arrived = exchange(send)
    arrived, *all_spectra = lax.optimization_barrier((arrived, *all_spectra))
    steps = 4
    row_block = pl.BlockSpec((steps, lanes, width), lambda n: (n, 0, 0))
    gate_rows, send, local_sum = call(
        functools.partial(pixels_kernel, mode_scale, th),
        "pixels",
        (arrived, by_height, back_cols, forward_mix, field_rows, cot_rows, send_cols),
        (field_shape, to_modes, shape((channels, channels), F32)),
        [pltpu.VMEM((inverse, owned * lanes), BF16), pltpu.VMEM((lanes, lanes), F32)],
        grid=(th // steps,),
        blocks={4: row_block, 5: row_block},
        out_blocks={0: row_block, 1: pl.BlockSpec((halves, steps * lanes), lambda n: (0, n))},
        limit=SMALL,
    )
    arrived = exchange(send)
    local_sum = sum_over(local_sum, "tile")
    (grad_spectra,) = call(
        functools.partial(grad_spectra_kernel, mode_scale, owned),
        "grad_spectra",
        (arrived, by_mode, rows, local_sum),
        (shape((owned * lanes + channels, both)),),
        limit=SMALL,
    )
    all_grads = gather(grad_spectra, "dp")
    (send,) = call(
        functools.partial(backward_kernel, samples),
        "mix_backward",
        (grad_spectra, back_rows, flat_weight),
        (to_pixels,),
        [
            pltpu.VMEM((owned * lanes, both), BF16),
            pltpu.VMEM((owned * lanes, both), BF16),
            pltpu.VMEM((owned, 2 * samples, channels * ROWS, both), F32),
        ],
        grid=(owned,),
        blocks={2: weight_block},
    )
    send, *all_grads = lax.optimization_barrier((send, *all_grads))
    arrived = exchange(send)

    groups = lax.axis_size("dp")
    total = groups * samples
    per_mode = pl.BlockSpec((lanes, both), lambda q: (q, 0))
    below = owned * lanes // channels
    pair_block = pl.BlockSpec((channels, both), lambda q: (below, 0))
    mode_grad, local_grad = call(
        functools.partial(outer_kernel, samples, groups),
        "mode_grad",
        (*all_spectra, *all_grads, *all_grads),
        (shape(flat_weight.shape, F32), shape((channels, channels), F32)),
        [pltpu.VMEM((total, channels, both), F32)] * 2 + [pltpu.VMEM((total, channels, both), BF16)] * 2,
        grid=(owned,),
        blocks={n: per_mode if n < 2 * groups else pair_block for n in range(3 * groups)},
        out_blocks={0: weight_block},
    )
    arrived, mode_grad = lax.optimization_barrier((arrived, mode_grad))

    (input_grad,) = call(
        functools.partial(final_kernel, spec_scale),
        "final",
        (arrived, by_height, back_cols, backward_mix, gate_rows, by_channel),
        (shape((pixel_rows, width)),),
        [pltpu.VMEM((th, lanes, width), BF16)],
        limit=SMALL,
    )
    return (input_grad.reshape(inputs.shape), mode_grad.reshape(mode_weight.shape), local_grad)


def solution(mesh):
    return jax.shard_map(
        local,
        mesh=mesh,
        in_specs=(
            P("dp", None, "tile", None),
            P("dp", None, "tile", None),
            P("tile", None, None, None),
            P(),
        ),
        out_specs=(P("dp", None, "tile", None), P("tile", None, None, None), P()),
        check_vma=False,
    )
```

```python
import functools
import math

import jax
import jax.numpy as jnp
import numpy as np
from jax import lax
from jax.experimental import pallas as pl
from jax.experimental.pallas import tpu as pltpu
from jax.sharding import PartitionSpec as P

F32 = jnp.float32
BF16 = jnp.bfloat16
LIMIT = 56 * 1024 * 1024
SMALL = 24 * 1024 * 1024
ROWS = 8
PACK = 16
GROUP = 8
SPLIT = 4


def row_tables(height, modes):
    index = np.arange(modes)
    signed = np.where(index < modes // 2, index, index - modes)
    phases = np.mod(np.arange(height)[:, None] * signed[None, :], height)
    angles = phases * (2.0 * math.pi / height)
    return np.cos(angles), np.sin(angles)


def column_tables(width, modes):
    phases = np.mod(np.arange(modes)[:, None] * np.arange(width)[None, :], width)
    angles = phases * (2.0 * math.pi / width)
    return np.stack([np.cos(angles), -np.sin(angles)])


def constant(table):
    return jnp.asarray(np.asarray(table, np.float32)).astype(BF16)


def tables(tiles, owned, th, width, modes):
    cols = column_tables(width, tiles * owned)
    split = cols.reshape(2, tiles, owned, width)
    send_cols = split.transpose(1, 0, 2, 3).reshape(tiles, 2 * owned, width)
    send_cols = np.pad(send_cols, ((0, 0), (0, padded(2 * owned) - 2 * owned), (0, 0))).reshape(-1, width)
    back_cols = split.transpose(2, 1, 0, 3).reshape(-1, width)
    cosine, sine = row_tables(th * tiles, modes)
    real = np.concatenate([cosine, -sine], axis=1)
    imag = np.concatenate([sine, cosine], axis=1)
    pair = np.stack([real, imag]).reshape(2, tiles, th, 2 * modes)
    rows = pair.transpose(2, 1, 0, 3).reshape(-1, 2 * modes)
    back_rows = pair.transpose(1, 0, 2, 3).reshape(-1, 2 * modes)
    return constant(send_cols), constant(rows), constant(back_rows), constant(back_cols)


def padded(rows):
    return -(-rows // PACK) * PACK


def order(outer, inner):
    take = np.arange(outer * inner).reshape(outer, inner).T.reshape(-1)
    return constant(np.eye(outer * inner)[take])


def mode_order(tiles, owned):
    rows = np.arange(tiles * padded(2 * owned)).reshape(tiles, -1)
    take = rows[:, : 2 * owned].reshape(tiles, 2, owned).transpose(2, 0, 1).reshape(-1)
    return constant(np.eye(rows.size)[take])


def dot(left, right, dims):
    return lax.dot_general(left, right, (dims, ((), ())), preferred_element_type=F32)


def low_half(shape, half):
    return lax.broadcasted_iota(jnp.int32, shape, 1) < half


def gelu_slope(values):
    size = jnp.abs(values)
    expo = jnp.exp(-0.5 * values * values)
    t = 1.0 / (1.0 + (0.3275911 / math.sqrt(2.0)) * size)
    poly = 0.5 * 1.061405429
    for factor in (-1.453152027, 1.421413741, -0.284496736, 0.254829592):
        poly = poly * t + 0.5 * factor
    tail = poly * t * expo
    cumulative = jnp.where(values < 0.0, tail, 1.0 - tail)
    return cumulative + values * expo * (1.0 / math.sqrt(2.0 * math.pi))


def shuffle(order_ref, value):
    return dot(order_ref[...], value, ((1,), (0,))).astype(BF16)


def by_rows(order_ref, field_refs, rows_ref):
    heights, lanes, _ = rows_ref.shape
    block = PACK * heights
    quarter = lanes // len(field_refs)
    for first in range(0, lanes, PACK):
        start = first % quarter * heights
        moved = shuffle(order_ref, field_refs[first // quarter][start : start + block, :])
        for h in range(heights):
            rows_ref[h, first : first + PACK, :] = moved[h * PACK : (h + 1) * PACK]


def columns_kernel(order_ref, table_ref, *rest):
    field_refs, (rows_ref, send_ref) = rest[:SPLIT], rest[SPLIT:]
    heights, lanes, _ = rows_ref.shape
    by_rows(order_ref, field_refs, rows_ref)
    for h in range(heights):
        send_ref[:, h * lanes : (h + 1) * lanes] = dot(table_ref[...], rows_ref[h], ((1,), (1,))).astype(BF16)


def relayout_kernel(order_ref, *rest):
    by_rows(order_ref, rest[:SPLIT], rest[SPLIT])


def shuffle_groups(order_ref, recv_ref):
    size = order_ref.shape[0]
    return [shuffle(order_ref, recv_ref[n : n + size, :]) for n in range(0, recv_ref.shape[0], size)]


def stack(groups, index, count, lanes):
    return jnp.concatenate(
        [
            group[index * count : (index + 1) * count, n : n + lanes]
            for n in range(0, groups[0].shape[1], lanes)
            for group in groups
        ],
        axis=0,
    )


def spectra_into(scale, owned, lanes, recv_ref, order_ref, rows_ref, spec_ref):
    count = order_ref.shape[0] // owned
    fields = rows_ref.shape[0] // count * lanes
    ordered = [shuffle(order_ref, recv_ref[:, :fields])]
    for q in range(owned):
        stacked = stack(ordered, q, count, lanes)
        spec_ref[q * lanes : (q + 1) * lanes, :] = (
            scale * dot(stacked, rows_ref[...], ((0,), (0,)))
        ).astype(BF16)


def to_piece(value):
    return jnp.concatenate([value[n : n + PACK] for n in range(0, value.shape[0], PACK)], axis=1)


def from_piece(value, extent):
    return jnp.concatenate([value[:, n : n + extent] for n in range(0, value.shape[1], extent)], axis=0)


def grad_spectra_kernel(scale, owned, lanes, channels, recv_ref, order_ref, rows_ref, spec_ref):
    spectra_into(scale, owned, lanes, recv_ref, order_ref, rows_ref, spec_ref)
    rows, width = recv_ref.shape
    first = width - channels * channels // PACK
    total = sum(recv_ref[n : n + PACK, first:].astype(F32) for n in range(0, rows, PACK))
    value = from_piece(total, channels)
    high = value.astype(BF16)
    low = (value - high.astype(F32)).astype(BF16)
    spec_ref[spec_ref.shape[0] - channels :, :] = jnp.concatenate([high, low], axis=1)


def tree(terms):
    while len(terms) > 1:
        terms = [a + b for a, b in zip(terms[0::2], terms[1::2])]
    return terms[0]


def rows_of(store, block, extent):
    return store.at[pl.ds(pl.multiple_of(block * extent, extent), extent), :]


def packed_row(view, index):
    row = view[index : index + 1, :]
    return jnp.broadcast_to(row, (PACK, row.shape[1])).astype(BF16)


def duplicates(spec, half):
    value = spec.astype(F32)
    other = pltpu.roll(value, half, 1)
    low = low_half(value.shape, half)
    return jnp.where(low, value, other), jnp.where(low, other, value)


def finish(back_ref, sums, send_ref, mix):
    @pl.when(pl.program_id(0) == pl.num_programs(0) - 1)
    def _():
        owned = sums.shape[0]
        lanes = send_ref.shape[1] // owned
        for q in range(owned):
            mixed = mix(sums.at[q]).astype(BF16)
            send_ref[:, q * lanes : (q + 1) * lanes] = dot(back_ref[...], mixed, ((1,), (1,))).astype(BF16)


def forward_kernel(scale, samples, owned, recv_ref, order_ref, rows_ref, back_ref, weight_ref, *rest):
    spec_ref, send_ref, real, imag, sums = rest
    _, _, outs, both = sums.shape
    channels = weight_ref.shape[0] // outs // owned
    half = both // 2
    lanes = samples * channels
    q = pl.program_id(0)

    @pl.when(q == 0)
    def _():
        spectra_into(scale, owned, lanes, recv_ref, order_ref, rows_ref, spec_ref)
        real[...], imag[...] = duplicates(spec_ref[...], half)
        sums[...] = jnp.zeros_like(sums)

    def body(block, carry):
        view = rows_of(weight_ref, q * (channels // GROUP) + block, GROUP * outs)
        rows = []
        for s in range(samples):
            for store in (real, imag):
                part = rows_of(store, (q * lanes + s * channels) // GROUP + block, GROUP)
                rows.append([packed_row(part, step) for step in range(GROUP)])
        into = sums.at[q]
        for start in range(0, outs, 2 * PACK):
            totals = []
            for o in (start, start + PACK):
                column = [view[step * outs + o : step * outs + o + PACK, :] for step in range(GROUP)]
                for n, row in enumerate(rows):
                    totals.append((n, o, tree([w * r for w, r in zip(column, row)])))
            updated = [(n, o, into[n, o : o + PACK, :] + total.astype(F32)) for n, o, total in totals]
            for n, o, total in updated:
                into[n, o : o + PACK, :] = total
        return carry

    lax.fori_loop(0, channels // GROUP, body, 0)

    def mix(parts):
        low = low_half((outs, both), half)
        result = []
        for s in range(samples):
            crossed = pltpu.roll(parts[2 * s + 1], half, 1)
            result.append(parts[2 * s] + jnp.where(low, -crossed, crossed))
        return jnp.concatenate(result, axis=0)

    finish(back_ref, sums, send_ref, mix)


def backward_kernel(samples, spec_ref, back_ref, weight_ref, send_ref, real, imag, sums):
    channels, both = sums.shape[2] // ROWS, sums.shape[3]
    outs = weight_ref.shape[0] // channels // sums.shape[0]
    half = both // 2
    lanes = samples * outs
    q = pl.program_id(0)

    @pl.when(q == 0)
    def _():
        first, second = duplicates(spec_ref[: real.shape[0], :], half)
        real[...], imag[...] = first.astype(BF16), second.astype(BF16)

    grads = [
        [store[pl.ds(pl.multiple_of(q * lanes + s * outs + o, PACK), PACK), :] for o in range(0, outs, PACK)]
        for s in range(samples)
        for store in (real, imag)
    ]

    def body(block, carry):
        view = rows_of(weight_ref, q * (channels // GROUP) + block, GROUP * outs)
        totals = []
        for step in range(GROUP):
            column = [view[step * outs + o : step * outs + o + PACK, :] for o in range(0, outs, PACK)]
            for n, grad in enumerate(grads):
                total = tree([w * g for w, g in zip(column, grad)]).astype(F32)
                totals.append((n, step, total[:ROWS] + total[ROWS:]))
        into = [rows_of(sums.at[q, n], block, GROUP * ROWS) for n in range(len(grads))]
        for n, step, total in totals:
            into[n][step * ROWS : (step + 1) * ROWS, :] = total
        return carry

    lax.fori_loop(0, channels // GROUP, body, 0)

    def mix(parts):
        low = low_half((channels, both), half)
        result = []
        for s in range(samples):
            straight, crossed = (
                sum(parts[n, pl.ds(row, channels, stride=ROWS), :] for row in range(ROWS)) for n in (2 * s, 2 * s + 1)
            )
            result.append(jnp.where(low, straight, -straight) + pltpu.roll(crossed, half, 1))
        return jnp.concatenate(result, axis=0)

    finish(back_ref, sums, send_ref, mix)


def pixels_kernel(scale, heights, samples, recv_ref, order_ref, back_ref, local_ref, field_ref, cot_ref, table_ref, *rest):
    grad_ref, send_ref, ordered, total = rest
    steps, lanes, _ = field_ref.shape
    count = order_ref.shape[0] // heights
    size = order_ref.shape[0]
    group = pl.program_id(0)

    @pl.when(group == 0)
    def _():
        for n in range(0, recv_ref.shape[0], size):
            ordered[n : n + size, :] = shuffle(order_ref, recv_ref[n : n + size, :])
        total[...] = jnp.zeros_like(total)

    local = jnp.zeros(total.shape, F32)
    for step in range(steps):
        parts = []
        for n in range(0, recv_ref.shape[0], size):
            first = pl.multiple_of(n + (group * steps + step) * count, count)
            parts.append(ordered[pl.ds(first, count), :])
        inner = stack(parts, 0, count, lanes)
        pre = scale * dot(inner, back_ref[...], ((0,), (0,)))
        pre = pre + dot(local_ref[...], field_ref[step], ((1,), (0,)))
        grad = (cot_ref[step].astype(F32) * gelu_slope(pre)).astype(BF16)
        grad_ref[step] = grad
        column = pl.ds(pl.multiple_of((group * steps + step) * lanes, lanes), lanes)
        send_ref[:, column] = dot(table_ref[...], grad, ((1,), (1,))).astype(BF16)
        local = local + dot(field_ref[step], grad, ((1,), (1,)))
    total[...] += local

    @pl.when(group == pl.num_programs(0) - 1)
    def _():
        extent = lanes // samples
        partial = sum(total[n : n + extent, n : n + extent] for n in range(0, lanes, extent))
        partial = to_piece(partial.astype(BF16))
        for n in range(0, send_ref.shape[0], PACK):
            send_ref[n : n + PACK, heights * lanes :] = partial


def final_kernel(scale, recv_ref, order_ref, back_ref, local_ref, grad_ref, restore_ref, out_ref, result):
    heights, lanes, _ = grad_ref.shape
    count = order_ref.shape[0] // heights
    ordered = shuffle_groups(order_ref, recv_ref)
    for h in range(heights):
        inner = stack(ordered, h, count, lanes)
        value = scale * dot(inner, back_ref[...], ((0,), (0,)))
        result[h] = (value + dot(local_ref[...], grad_ref[h], ((1,), (0,)))).astype(BF16)
    block = PACK * heights
    for first in range(0, lanes, PACK):
        part = jnp.concatenate([result[h, first : first + PACK, :] for h in range(heights)], axis=0)
        out_ref[first * heights : first * heights + block, :] = shuffle(restore_ref, part)


def outer_kernel(samples, groups, *refs):
    specs, grads, pairs = refs[:groups], refs[groups : 2 * groups], refs[2 * groups : 3 * groups]
    out_ref, local_ref, real, imag, plain, crossed = refs[3 * groups :]
    total, channels, both = real.shape
    outs = plain.shape[1]
    half = both // 2
    low = low_half((channels, both), half)

    @pl.when(pl.program_id(0) == 0)
    def _():
        value = 0.0
        for pair_ref in pairs:
            pair = pair_ref[...].astype(F32)
            value = value + pair[:, :channels] + pair[:, channels : 2 * channels]
        local_ref[...] = value

    for g in range(groups):
        for s in range(samples):
            n = g * samples + s
            spec = specs[g][s * channels : (s + 1) * channels, :].astype(F32)
            other = pltpu.roll(spec, half, 1)
            real[n] = jnp.where(low, spec, other)
            imag[n] = jnp.where(low, other, -spec)
            grad = grads[g][s * outs : (s + 1) * outs, :]
            plain[n] = grad
            crossed[n] = pltpu.roll(grad.astype(F32), half, 1).astype(BF16)

    def body(block, carry):
        into = rows_of(out_ref, block, GROUP * outs)
        views = [rows_of(store.at[n], block, GROUP) for n in range(total) for store in (real, imag)]
        for first in range(0, GROUP, 2):
            pair = range(first, first + 2)
            lefts = [[packed_row(view, c) for view in views] for c in pair]
            results = []
            for o in range(0, outs, PACK):
                right = [store[n, o : o + PACK, :] for n in range(total) for store in (plain, crossed)]
                for c, left in zip(pair, lefts):
                    results.append((c * outs + o, tree([a * b for a, b in zip(left, right)])))
            for row, result in results:
                into[row : row + PACK, :] = result.astype(F32)
        return carry

    lax.fori_loop(0, channels // GROUP, body, 0)


IN_VMEM = pl.BlockSpec(memory_space=pltpu.VMEM)


def whole(extent):
    return pl.BlockSpec(extent, lambda *_: (0,) * len(extent))


def call(kernel, name, operands, outs, scratch=(), grid=(1,), blocks=None, out_blocks=None, limit=LIMIT):
    blocks, out_blocks = blocks or {}, out_blocks or {}
    in_specs = [blocks.get(n) or whole(operand.shape) for n, operand in enumerate(operands)]
    out_specs = [out_blocks.get(n, whole(out.shape)) for n, out in enumerate(outs)]
    return pl.pallas_call(
        kernel,
        out_shape=tuple(outs),
        grid=grid,
        in_specs=in_specs,
        out_specs=tuple(out_specs),
        scratch_shapes=list(scratch),
        compiler_params=pltpu.CompilerParams(vmem_limit_bytes=limit),
        name=name,
    )(*operands)


def gather(values, axis):
    size = lax.axis_size(axis)
    return [values] + [
        lax.ppermute(values, axis, [(i, i ^ step) for i in range(size)]) for step in range(1, size)
    ]


def block_diagonal(matrix, copies):
    zero = jnp.zeros_like(matrix)
    return jnp.concatenate(
        [
            jnp.concatenate([matrix if i == j else zero for j in range(copies)], axis=1)
            for i in range(copies)
        ],
        axis=0,
    )


def shape(extent, kind=BF16):
    return jax.ShapeDtypeStruct(extent, kind)


def local(inputs, cotangent, mode_weight, local_weight):
    tiles = lax.axis_size("tile")
    samples, channels, th, width = inputs.shape
    owned, _, _, both = mode_weight.shape
    modes = both // 2
    lanes = samples * channels
    parts = width // 128
    spec_scale = 1.0 / math.sqrt(tiles * th * width)
    mode_scale = 1.0 / math.sqrt(modes * tiles * owned)
    send_cols, rows, back_rows, back_cols = tables(tiles, owned, th, width, modes)
    pixel_rows = samples * channels * th
    halves = tiles * padded(2 * owned)
    inverse = 2 * tiles * th

    def exchange(values):
        split = values.reshape(tiles, values.shape[0] // tiles, values.shape[1])
        moved = lax.all_to_all(split, "tile", split_axis=0, concat_axis=0, tiled=False)
        return moved.reshape(values.shape)

    forward_mix = block_diagonal(local_weight.T, samples)
    backward_mix = block_diagonal(local_weight, samples)
    by_row = order(PACK, th)
    by_channel = order(th, PACK)
    by_mode = mode_order(tiles, owned)
    by_height = order(2 * min(tiles, 8), th)
    flat_weight = mode_weight.reshape(-1, both)
    weight_block = pl.BlockSpec((flat_weight.shape[0] // owned, both), lambda q: (q, 0))
    to_modes = shape((halves, th * lanes))
    to_pixels = shape((inverse, owned * lanes))
    field_shape = shape((th, lanes, width))

    def field_blocks(first):
        return {first + n: pl.BlockSpec((pixel_rows // SPLIT, width), lambda _, n=n: (n, 0)) for n in range(SPLIT)}

    field_rows, send = call(
        columns_kernel,
        "columns",
        (by_row, send_cols, *[inputs.reshape(pixel_rows, width)] * SPLIT),
        (field_shape, to_modes),
        blocks=field_blocks(2),
    )
    arrived = exchange(send)
    (cot_rows,) = call(
        relayout_kernel,
        "relayout",
        (by_row, *[cotangent.reshape(pixel_rows, width)] * SPLIT),
        (field_shape,),
        blocks=field_blocks(1),
    )
    spectra, send = call(
        functools.partial(forward_kernel, spec_scale, samples, owned),
        "mix_forward",
        (arrived, by_mode, rows, back_rows, flat_weight),
        (shape((owned * lanes, both)), to_pixels),
        [
            pltpu.VMEM((owned * lanes, both), F32),
            pltpu.VMEM((owned * lanes, both), F32),
            pltpu.VMEM((owned, 2 * samples, channels, both), F32),
        ],
        grid=(owned,),
        blocks={4: IN_VMEM},
        limit=SMALL,
    )
    all_spectra = gather(spectra, "dp")
    arrived = exchange(send)
    arrived, *all_spectra = lax.optimization_barrier((arrived, *all_spectra))
    steps = 4
    row_block = pl.BlockSpec((steps, lanes, width), lambda n: (n, 0, 0))
    gate_rows, send = call(
        functools.partial(pixels_kernel, mode_scale, th, samples),
        "pixels",
        (arrived, by_height, back_cols, forward_mix, field_rows, cot_rows, send_cols),
        (field_shape, shape((halves, th * lanes + channels * channels // PACK))),
        [pltpu.VMEM((inverse, owned * lanes), BF16), pltpu.VMEM((lanes, lanes), F32)],
        grid=(th // steps,),
        blocks={4: row_block, 5: row_block},
        out_blocks={0: row_block},
        limit=SMALL,
    )
    arrived = exchange(send)
    (grad_spectra,) = call(
        functools.partial(grad_spectra_kernel, mode_scale, owned, lanes, channels),
        "grad_spectra",
        (arrived, by_mode, rows),
        (shape((owned * lanes + channels, both)),),
        limit=SMALL,
    )
    all_grads = gather(grad_spectra, "dp")
    (send,) = call(
        functools.partial(backward_kernel, samples),
        "mix_backward",
        (grad_spectra, back_rows, flat_weight),
        (to_pixels,),
        [
            pltpu.VMEM((owned * lanes, both), BF16),
            pltpu.VMEM((owned * lanes, both), BF16),
            pltpu.VMEM((owned, 2 * samples, channels * ROWS, both), F32),
        ],
        grid=(owned,),
        blocks={2: IN_VMEM},
        limit=SMALL,
    )
    send, *all_grads = lax.optimization_barrier((send, *all_grads))
    arrived = exchange(send)

    groups = lax.axis_size("dp")
    total = groups * samples
    per_mode = pl.BlockSpec((lanes, both), lambda q: (q, 0))
    below = owned * lanes // channels
    pair_block = pl.BlockSpec((channels, both), lambda q: (below, 0))
    mode_grad, local_grad = call(
        functools.partial(outer_kernel, samples, groups),
        "mode_grad",
        (*all_spectra, *all_grads, *all_grads),
        (shape(flat_weight.shape, F32), shape((channels, channels), F32)),
        [pltpu.VMEM((total, channels, both), F32)] * 2 + [pltpu.VMEM((total, channels, both), BF16)] * 2,
        grid=(owned,),
        blocks={n: per_mode if n < 2 * groups else pair_block for n in range(3 * groups)},
        out_blocks={0: weight_block},
    )
    arrived, mode_grad = lax.optimization_barrier((arrived, mode_grad))

    (input_grad,) = call(
        functools.partial(final_kernel, spec_scale),
        "final",
        (arrived, by_height, back_cols, backward_mix, gate_rows, by_channel),
        (shape((pixel_rows, width)),),
        [pltpu.VMEM((th, lanes, width), BF16)],
        limit=SMALL,
    )
    return (input_grad.reshape(inputs.shape), mode_grad.reshape(mode_weight.shape), local_grad)


def solution(mesh):
    return jax.shard_map(
        local,
        mesh=mesh,
        in_specs=(
            P("dp", None, "tile", None),
            P("dp", None, "tile", None),
            P("tile", None, None, None),
            P(),
        ),
        out_specs=(P("dp", None, "tile", None), P("tile", None, None, None), P()),
        check_vma=False,
    )
```

```python
import functools
import math

import jax
import jax.numpy as jnp
import numpy as np
from jax import lax
from jax.experimental import pallas as pl
from jax.experimental.pallas import tpu as pltpu
from jax.sharding import PartitionSpec as P

F32 = jnp.float32
BF16 = jnp.bfloat16
LIMIT = 56 * 1024 * 1024
SMALL = 24 * 1024 * 1024
ROWS = 8
PACK = 16
GROUP = 8
SPLIT = 4
AHEAD = 3


def row_tables(height, modes):
    index = np.arange(modes)
    signed = np.where(index < modes // 2, index, index - modes)
    phases = np.mod(np.arange(height)[:, None] * signed[None, :], height)
    angles = phases * (2.0 * math.pi / height)
    return np.cos(angles), np.sin(angles)


def column_tables(width, modes):
    phases = np.mod(np.arange(modes)[:, None] * np.arange(width)[None, :], width)
    angles = phases * (2.0 * math.pi / width)
    return np.stack([np.cos(angles), -np.sin(angles)])


def constant(table):
    return jnp.asarray(np.asarray(table, np.float32)).astype(BF16)


def tables(tiles, owned, th, width, modes):
    cols = column_tables(width, tiles * owned)
    split = cols.reshape(2, tiles, owned, width)
    send_cols = split.transpose(1, 0, 2, 3).reshape(tiles, 2 * owned, width)
    send_cols = np.pad(send_cols, ((0, 0), (0, padded(2 * owned) - 2 * owned), (0, 0))).reshape(-1, width)
    back_cols = split.transpose(2, 1, 0, 3).reshape(-1, width)
    cosine, sine = row_tables(th * tiles, modes)
    real = np.concatenate([cosine, -sine], axis=1)
    imag = np.concatenate([sine, cosine], axis=1)
    pair = np.stack([real, imag]).reshape(2, tiles, th, 2 * modes)
    rows = pair.transpose(2, 1, 0, 3).reshape(-1, 2 * modes)
    back_rows = pair.transpose(1, 0, 2, 3).reshape(-1, 2 * modes)
    return constant(send_cols), constant(rows), constant(back_rows), constant(back_cols)


def padded(rows):
    return -(-rows // PACK) * PACK


def order(outer, inner):
    take = np.arange(outer * inner).reshape(outer, inner).T.reshape(-1)
    return constant(np.eye(outer * inner)[take])


def mode_order(tiles, owned):
    rows = np.arange(tiles * padded(2 * owned)).reshape(tiles, -1)
    take = rows[:, : 2 * owned].reshape(tiles, 2, owned).transpose(2, 0, 1).reshape(-1)
    return constant(np.eye(rows.size)[take])


def dot(left, right, dims):
    return lax.dot_general(left, right, (dims, ((), ())), preferred_element_type=F32)


def low_half(shape, half):
    return lax.broadcasted_iota(jnp.int32, shape, 1) < half


def gelu_slope(values):
    size = jnp.abs(values)
    expo = jnp.exp(-0.5 * values * values)
    t = 1.0 / (1.0 + (0.3275911 / math.sqrt(2.0)) * size)
    poly = 0.5 * 1.061405429
    for factor in (-1.453152027, 1.421413741, -0.284496736, 0.254829592):
        poly = poly * t + 0.5 * factor
    tail = poly * t * expo
    cumulative = jnp.where(values < 0.0, tail, 1.0 - tail)
    return cumulative + values * expo * (1.0 / math.sqrt(2.0 * math.pi))


def shuffle(order_ref, value):
    return dot(order_ref[...], value, ((1,), (0,))).astype(BF16)


def by_rows(order_ref, field_refs, rows_ref):
    heights, lanes, _ = rows_ref.shape
    block = PACK * heights
    quarter = lanes // len(field_refs)
    for first in range(0, lanes, PACK):
        start = first % quarter * heights
        moved = shuffle(order_ref, field_refs[first // quarter][start : start + block, :])
        for h in range(heights):
            rows_ref[h, first : first + PACK, :] = moved[h * PACK : (h + 1) * PACK]


def columns_kernel(order_ref, table_ref, *rest):
    field_refs, (rows_ref, send_ref) = rest[:SPLIT], rest[SPLIT:]
    heights, lanes, _ = rows_ref.shape
    by_rows(order_ref, field_refs, rows_ref)
    for h in range(heights):
        send_ref[:, h * lanes : (h + 1) * lanes] = dot(table_ref[...], rows_ref[h], ((1,), (1,))).astype(BF16)


def relayout_kernel(order_ref, *rest):
    by_rows(order_ref, rest[:SPLIT], rest[SPLIT])


def shuffle_groups(order_ref, recv_ref, width):
    size = order_ref.shape[0]
    return [shuffle(order_ref, recv_ref[n : n + size, :width]) for n in range(0, recv_ref.shape[0], size)]


def stack(groups, index, count, lanes):
    return jnp.concatenate(
        [
            group[index * count : (index + 1) * count, n : n + lanes]
            for n in range(0, groups[0].shape[1], lanes)
            for group in groups
        ],
        axis=0,
    )


def spectra_into(scale, owned, lanes, recv_ref, order_ref, rows_ref, spec_ref):
    count = order_ref.shape[0] // owned
    fields = rows_ref.shape[0] // count * lanes
    ordered = [shuffle(order_ref, recv_ref[:, :fields])]
    for q in range(owned):
        stacked = stack(ordered, q, count, lanes)
        spec_ref[q * lanes : (q + 1) * lanes, :] = (
            scale * dot(stacked, rows_ref[...], ((0,), (0,)))
        ).astype(BF16)


def to_piece(value, rows):
    return jnp.concatenate([value[n : n + rows] for n in range(0, value.shape[0], rows)], axis=1)


def from_piece(value, extent):
    return jnp.concatenate([value[:, n : n + extent] for n in range(0, value.shape[1], extent)], axis=0)


def spectra_kernel(scale, owned, lanes, recv_ref, order_ref, rows_ref, spec_ref):
    spectra_into(scale, owned, lanes, recv_ref, order_ref, rows_ref, spec_ref)


def tree(terms):
    while len(terms) > 1:
        terms = [a + b for a, b in zip(terms[0::2], terms[1::2])]
    return terms[0]


def rows_of(store, block, extent):
    return store.at[pl.ds(pl.multiple_of(block * extent, extent), extent), :]


def packed_row(view, index):
    row = view[index : index + 1, :]
    return jnp.broadcast_to(row, (PACK, row.shape[1])).astype(BF16)


def duplicates(spec, half):
    value = spec.astype(F32)
    other = pltpu.roll(value, half, 1)
    low = low_half(value.shape, half)
    return jnp.where(low, value, other), jnp.where(low, other, value)


def finish(back_ref, sums, send_ref, mix):
    @pl.when(pl.program_id(0) == pl.num_programs(0) - 1)
    def _():
        owned = sums.shape[0]
        for q in range(owned):
            mixed = mix(sums.at[q]).astype(BF16)
            lanes = mixed.shape[0]
            send_ref[:, q * lanes : (q + 1) * lanes] = dot(back_ref[...], mixed, ((1,), (1,))).astype(BF16)


def fetch_weights(source_ref, weights, sems):
    q = pl.program_id(0)
    owned = sems.shape[0]
    size = weights.shape[0] // owned

    def move(mode):
        part = pl.ds(pl.multiple_of(mode * size, size), size)
        return pltpu.make_async_copy(source_ref.at[part, :], weights.at[part, :], sems.at[mode])

    @pl.when(q == 0)
    def _():
        for mode in range(min(AHEAD, owned)):
            move(mode).start()

    @pl.when(q + AHEAD < owned)
    def _():
        move(q + AHEAD).start()

    return move(q), weights.at[pl.ds(pl.multiple_of(q * size, size), size), :]


def forward_kernel(scale, samples, owned, recv_ref, order_ref, rows_ref, back_ref, source_ref, *rest):
    spec_ref, send_ref, real, imag, sums, weights, sems = rest
    _, _, outs, both = sums.shape
    channels = weights.shape[0] // outs // owned
    half = both // 2
    lanes = samples * channels
    q = pl.program_id(0)
    coming, weight_ref = fetch_weights(source_ref, weights, sems)

    @pl.when(q == 0)
    def _():
        spectra_into(scale, owned, lanes, recv_ref, order_ref, rows_ref, spec_ref)
        real[...], imag[...] = duplicates(spec_ref[...], half)
        sums[...] = jnp.zeros_like(sums)

    coming.wait()

    def body(block, carry):
        view = rows_of(weight_ref, block, GROUP * outs)
        rows = []
        for s in range(samples):
            for store in (real, imag):
                part = rows_of(store, (q * lanes + s * channels) // GROUP + block, GROUP)
                rows.append([packed_row(part, step) for step in range(GROUP)])
        into = sums.at[q]
        for start in range(0, outs, 2 * PACK):
            totals = []
            for o in (start, start + PACK):
                column = [view[step * outs + o : step * outs + o + PACK, :] for step in range(GROUP)]
                for n, row in enumerate(rows):
                    totals.append((n, o, tree([w * r for w, r in zip(column, row)])))
            updated = [(n, o, into[n, o : o + PACK, :] + total.astype(F32)) for n, o, total in totals]
            for n, o, total in updated:
                into[n, o : o + PACK, :] = total
        return carry

    lax.fori_loop(0, channels // GROUP, body, 0)

    def mix(parts):
        low = low_half((outs, both), half)
        result = []
        for s in range(samples):
            crossed = pltpu.roll(parts[2 * s + 1], half, 1)
            result.append(parts[2 * s] + jnp.where(low, -crossed, crossed))
        return jnp.concatenate(result, axis=0)

    finish(back_ref, sums, send_ref, mix)


def backward_kernel(samples, tiles, spec_ref, back_ref, local_ref, source_ref, *rest):
    send_ref, real, imag, sums, weights, sems = rest
    channels, both = sums.shape[2] // ROWS, sums.shape[3]
    outs = weights.shape[0] // channels // sums.shape[0]
    half = both // 2
    lanes = samples * outs
    q = pl.program_id(0)
    coming, weight_ref = fetch_weights(source_ref, weights, sems)

    @pl.when(q == 0)
    def _():
        first, second = duplicates(spec_ref[...], half)
        real[...], imag[...] = first.astype(BF16), second.astype(BF16)
        extent = send_ref.shape[0] // tiles
        partial = to_piece(local_ref[...].astype(BF16), extent)
        for n in range(0, send_ref.shape[0], extent):
            send_ref[n : n + extent, sums.shape[0] * lanes :] = partial

    coming.wait()
    grads = [
        [store[pl.ds(pl.multiple_of(q * lanes + s * outs + o, PACK), PACK), :] for o in range(0, outs, PACK)]
        for s in range(samples)
        for store in (real, imag)
    ]

    def body(block, carry):
        view = rows_of(weight_ref, block, GROUP * outs)
        totals = []
        for step in range(GROUP):
            column = [view[step * outs + o : step * outs + o + PACK, :] for o in range(0, outs, PACK)]
            for n, grad in enumerate(grads):
                total = tree([w * g for w, g in zip(column, grad)]).astype(F32)
                totals.append((n, step, total[:ROWS] + total[ROWS:]))
        into = [rows_of(sums.at[q, n], block, GROUP * ROWS) for n in range(len(grads))]
        for n, step, total in totals:
            into[n][step * ROWS : (step + 1) * ROWS, :] = total
        return carry

    lax.fori_loop(0, channels // GROUP, body, 0)

    def mix(parts):
        low = low_half((channels, both), half)
        result = []
        for s in range(samples):
            straight, crossed = (
                sum(parts[n, pl.ds(row, channels, stride=ROWS), :] for row in range(ROWS)) for n in (2 * s, 2 * s + 1)
            )
            result.append(jnp.where(low, straight, -straight) + pltpu.roll(crossed, half, 1))
        return jnp.concatenate(result, axis=0)

    finish(back_ref, sums, send_ref, mix)


def pixels_kernel(scale, heights, recv_ref, order_ref, back_ref, local_ref, field_ref, cot_ref, table_ref, *rest):
    grad_ref, send_ref, sum_ref, ordered, total = rest
    steps, lanes, _ = field_ref.shape
    count = order_ref.shape[0] // heights
    size = order_ref.shape[0]
    group = pl.program_id(0)

    @pl.when(group == 0)
    def _():
        for n in range(0, recv_ref.shape[0], size):
            ordered[n : n + size, :] = shuffle(order_ref, recv_ref[n : n + size, :])
        total[...] = jnp.zeros_like(total)

    local = jnp.zeros(total.shape, F32)
    for step in range(steps):
        parts = []
        for n in range(0, recv_ref.shape[0], size):
            first = pl.multiple_of(n + (group * steps + step) * count, count)
            parts.append(ordered[pl.ds(first, count), :])
        inner = stack(parts, 0, count, lanes)
        pre = scale * dot(inner, back_ref[...], ((0,), (0,)))
        pre = pre + dot(local_ref[...], field_ref[step], ((1,), (0,)))
        grad = (cot_ref[step].astype(F32) * gelu_slope(pre)).astype(BF16)
        grad_ref[step] = grad
        send_ref[:, step * lanes : (step + 1) * lanes] = dot(table_ref[...], grad, ((1,), (1,))).astype(BF16)
        local = local + dot(field_ref[step], grad, ((1,), (1,)))
    total[...] += local

    @pl.when(group == pl.num_programs(0) - 1)
    def _():
        extent = sum_ref.shape[0]
        sum_ref[...] = sum(total[n : n + extent, n : n + extent] for n in range(0, lanes, extent))


def final_kernel(scale, tiles, recv_ref, order_ref, back_ref, local_ref, grad_ref, restore_ref, *rest):
    out_ref, sum_ref, result = rest
    heights, lanes, _ = grad_ref.shape
    extent = recv_ref.shape[0] // tiles
    first = back_ref.shape[0] // (2 * tiles) * lanes
    partials = sum(recv_ref[n : n + extent, first:].astype(F32) for n in range(0, recv_ref.shape[0], extent))
    sum_ref[...] = from_piece(partials, sum_ref.shape[1])
    count = order_ref.shape[0] // heights
    ordered = shuffle_groups(order_ref, recv_ref, first)
    for h in range(heights):
        inner = stack(ordered, h, count, lanes)
        value = scale * dot(inner, back_ref[...], ((0,), (0,)))
        result[h] = (value + dot(local_ref[...], grad_ref[h], ((1,), (0,)))).astype(BF16)
    block = PACK * heights
    for first in range(0, lanes, PACK):
        part = jnp.concatenate([result[h, first : first + PACK, :] for h in range(heights)], axis=0)
        out_ref[first * heights : first * heights + block, :] = shuffle(restore_ref, part)


def outer_kernel(samples, groups, *refs):
    specs, grads = refs[:groups], refs[groups : 2 * groups]
    out_ref, real, imag, plain, crossed = refs[2 * groups :]
    total, channels, both = real.shape
    outs = plain.shape[1]
    half = both // 2
    low = low_half((channels, both), half)

    for g in range(groups):
        for s in range(samples):
            n = g * samples + s
            spec = specs[g][s * channels : (s + 1) * channels, :].astype(F32)
            other = pltpu.roll(spec, half, 1)
            real[n] = jnp.where(low, spec, other)
            imag[n] = jnp.where(low, other, -spec)
            grad = grads[g][s * outs : (s + 1) * outs, :]
            plain[n] = grad
            crossed[n] = pltpu.roll(grad.astype(F32), half, 1).astype(BF16)

    def body(block, carry):
        into = rows_of(out_ref, block, GROUP * outs)
        views = [rows_of(store.at[n], block, GROUP) for n in range(total) for store in (real, imag)]
        for first in range(0, GROUP, 2):
            pair = range(first, first + 2)
            lefts = [[packed_row(view, c) for view in views] for c in pair]
            results = []
            for o in range(0, outs, PACK):
                right = [store[n, o : o + PACK, :] for n in range(total) for store in (plain, crossed)]
                for c, left in zip(pair, lefts):
                    results.append((c * outs + o, tree([a * b for a, b in zip(left, right)])))
            for row, result in results:
                into[row : row + PACK, :] = result.astype(F32)
        return carry

    lax.fori_loop(0, channels // GROUP, body, 0)


def whole(extent):
    return pl.BlockSpec(extent, lambda *_: (0,) * len(extent))


def call(kernel, name, operands, outs, scratch=(), grid=(1,), blocks=None, out_blocks=None, limit=LIMIT):
    blocks, out_blocks = blocks or {}, out_blocks or {}
    in_specs = [blocks.get(n) or whole(operand.shape) for n, operand in enumerate(operands)]
    out_specs = [out_blocks.get(n, whole(out.shape)) for n, out in enumerate(outs)]
    return pl.pallas_call(
        kernel,
        out_shape=tuple(outs),
        grid=grid,
        in_specs=in_specs,
        out_specs=tuple(out_specs),
        scratch_shapes=list(scratch),
        compiler_params=pltpu.CompilerParams(vmem_limit_bytes=limit),
        name=name,
    )(*operands)


def swap(values, axis, step):
    return lax.ppermute(values, axis, [(i, i ^ step) for i in range(lax.axis_size(axis))])


def gather_near(values, axis):
    size = lax.axis_size(axis)
    return {0: values} | {1 << bit: swap(values, axis, 1 << bit) for bit in range(size.bit_length() - 1)}


def gather_far(near, axis):
    whole_set = dict(near)
    for step in range(1, lax.axis_size(axis)):
        if step not in whole_set:
            whole_set[step] = swap(whole_set[step & (step - 1)], axis, step & -step)
    return [whole_set[step] for step in sorted(whole_set)]


def sum_over(values, axis):
    step = 1
    while step < lax.axis_size(axis):
        values = values + swap(values, axis, step)
        step *= 2
    return values


def block_diagonal(matrix, copies):
    zero = jnp.zeros_like(matrix)
    return jnp.concatenate(
        [
            jnp.concatenate([matrix if i == j else zero for j in range(copies)], axis=1)
            for i in range(copies)
        ],
        axis=0,
    )


def shape(extent, kind=BF16):
    return jax.ShapeDtypeStruct(extent, kind)


def local(inputs, cotangent, mode_weight, local_weight):
    tiles = lax.axis_size("tile")
    samples, channels, th, width = inputs.shape
    owned, _, _, both = mode_weight.shape
    modes = both // 2
    lanes = samples * channels
    parts = width // 128
    spec_scale = 1.0 / math.sqrt(tiles * th * width)
    mode_scale = 1.0 / math.sqrt(modes * tiles * owned)
    send_cols, rows, back_rows, back_cols = tables(tiles, owned, th, width, modes)
    pixel_rows = samples * channels * th
    halves = tiles * padded(2 * owned)
    inverse = 2 * tiles * th

    def exchange(values):
        split = values.reshape(tiles, values.shape[0] // tiles, values.shape[1])
        moved = lax.all_to_all(split, "tile", split_axis=0, concat_axis=0, tiled=False)
        return moved.reshape(values.shape)

    forward_mix = block_diagonal(local_weight.T, samples)
    backward_mix = block_diagonal(local_weight, samples)
    by_row = order(PACK, th)
    by_channel = order(th, PACK)
    by_mode = mode_order(tiles, owned)
    by_height = order(2 * min(tiles, 8), th)
    flat_weight = mode_weight.reshape(-1, both)
    weight_block = pl.BlockSpec((flat_weight.shape[0] // owned, both), lambda q: (q, 0))
    weight_scratch = [pltpu.VMEM(flat_weight.shape, BF16), pltpu.SemaphoreType.DMA((owned,))]
    in_place = pl.BlockSpec(memory_space=pl.ANY)
    to_modes = shape((halves, th * lanes))
    to_pixels = shape((inverse, owned * lanes))
    field_shape = shape((th, lanes, width))

    def field_blocks(first):
        return {first + n: pl.BlockSpec((pixel_rows // SPLIT, width), lambda _, n=n: (n, 0)) for n in range(SPLIT)}

    field_rows, send = call(
        columns_kernel,
        "columns",
        (by_row, send_cols, *[inputs.reshape(pixel_rows, width)] * SPLIT),
        (field_shape, to_modes),
        blocks=field_blocks(2),
    )
    arrived = exchange(send)
    (cot_rows,) = call(
        relayout_kernel,
        "relayout",
        (by_row, *[cotangent.reshape(pixel_rows, width)] * SPLIT),
        (field_shape,),
        blocks=field_blocks(1),
    )
    spectra, send = call(
        functools.partial(forward_kernel, spec_scale, samples, owned),
        "mix_forward",
        (arrived, by_mode, rows, back_rows, flat_weight),
        (shape((owned * lanes, both)), to_pixels),
        [
            pltpu.VMEM((owned * lanes, both), F32),
            pltpu.VMEM((owned * lanes, both), F32),
            pltpu.VMEM((owned, 2 * samples, channels, both), F32),
            *weight_scratch,
        ],
        grid=(owned,),
        blocks={4: in_place},
    )
    all_spectra = gather_far(gather_near(spectra, "dp"), "dp")
    arrived = exchange(send)
    steps = 4
    row_block = pl.BlockSpec((steps, lanes, width), lambda n: (n, 0, 0))
    gate_rows, send, local_sum = call(
        functools.partial(pixels_kernel, mode_scale, th),
        "pixels",
        (arrived, by_height, back_cols, forward_mix, field_rows, cot_rows, send_cols),
        (field_shape, to_modes, shape((channels, channels), F32)),
        [pltpu.VMEM((inverse, owned * lanes), BF16), pltpu.VMEM((lanes, lanes), F32)],
        grid=(th // steps,),
        blocks={4: row_block, 5: row_block},
        out_blocks={0: row_block, 1: pl.BlockSpec((halves, steps * lanes), lambda n: (0, n))},
        limit=SMALL,
    )
    send, *all_spectra = lax.optimization_barrier((send, *all_spectra))
    arrived = exchange(send)
    local_sum = sum_over(local_sum, "dp")
    (grad_spectra,) = call(
        functools.partial(spectra_kernel, mode_scale, owned, lanes),
        "grad_spectra",
        (arrived, by_mode, rows),
        (shape((owned * lanes, both)),),
        limit=SMALL,
    )
    near = gather_near(grad_spectra, "dp")
    (send,) = call(
        functools.partial(backward_kernel, samples, tiles),
        "mix_backward",
        (grad_spectra, back_rows, local_sum, flat_weight),
        (shape((inverse, owned * lanes + channels * channels * tiles // inverse)),),
        [
            pltpu.VMEM((owned * lanes, both), BF16),
            pltpu.VMEM((owned * lanes, both), BF16),
            pltpu.VMEM((owned, 2 * samples, channels * ROWS, both), F32),
            *weight_scratch,
        ],
        grid=(owned,),
        blocks={3: in_place},
    )
    send, near = lax.optimization_barrier((send, near))
    all_grads = gather_far(near, "dp")
    arrived = exchange(send)

    groups = lax.axis_size("dp")
    total = groups * samples
    per_mode = pl.BlockSpec((lanes, both), lambda q: (q, 0))
    (mode_grad,) = call(
        functools.partial(outer_kernel, samples, groups),
        "mode_grad",
        (*all_spectra, *all_grads),
        (shape(flat_weight.shape, F32),),
        [pltpu.VMEM((total, channels, both), F32)] * 2 + [pltpu.VMEM((total, channels, both), BF16)] * 2,
        grid=(owned,),
        blocks={n: per_mode for n in range(2 * groups)},
        out_blocks={0: weight_block},
    )
    arrived, mode_grad = lax.optimization_barrier((arrived, mode_grad))

    input_grad, local_grad = call(
        functools.partial(final_kernel, spec_scale, tiles),
        "final",
        (arrived, by_height, back_cols, backward_mix, gate_rows, by_channel),
        (shape((pixel_rows, width)), shape((channels, channels), F32)),
        [pltpu.VMEM((th, lanes, width), BF16)],
        limit=SMALL,
    )
    return (input_grad.reshape(inputs.shape), mode_grad.reshape(mode_weight.shape), local_grad)


def solution(mesh):
    return jax.shard_map(
        local,
        mesh=mesh,
        in_specs=(
            P("dp", None, "tile", None),
            P("dp", None, "tile", None),
            P("tile", None, None, None),
            P(),
        ),
        out_specs=(P("dp", None, "tile", None), P("tile", None, None, None), P()),
        check_vma=False,
    )
```

```python
import functools
import math

import jax
import jax.numpy as jnp
import numpy as np
from jax import lax
from jax.experimental import pallas as pl
from jax.experimental.pallas import tpu as pltpu
from jax.sharding import PartitionSpec as P

F32 = jnp.float32
BF16 = jnp.bfloat16
LIMIT = 56 * 1024 * 1024
SMALL = 24 * 1024 * 1024
ROWS = 8
PACK = 16
GROUP = 8
SPLIT = 4
AHEAD = 3


def row_tables(height, modes):
    index = np.arange(modes)
    signed = np.where(index < modes // 2, index, index - modes)
    phases = np.mod(np.arange(height)[:, None] * signed[None, :], height)
    angles = phases * (2.0 * math.pi / height)
    return np.cos(angles), np.sin(angles)


def column_tables(width, modes):
    phases = np.mod(np.arange(modes)[:, None] * np.arange(width)[None, :], width)
    angles = phases * (2.0 * math.pi / width)
    return np.stack([np.cos(angles), -np.sin(angles)])


def constant(table):
    return jnp.asarray(np.asarray(table, np.float32)).astype(BF16)


def tables(tiles, owned, th, width, modes):
    cols = column_tables(width, tiles * owned)
    split = cols.reshape(2, tiles, owned, width)
    send_cols = split.transpose(1, 0, 2, 3).reshape(tiles, 2 * owned, width)
    send_cols = np.pad(send_cols, ((0, 0), (0, padded(2 * owned) - 2 * owned), (0, 0))).reshape(-1, width)
    back_cols = split.transpose(2, 1, 0, 3).reshape(-1, width)
    cosine, sine = row_tables(th * tiles, modes)
    real = np.concatenate([cosine, -sine], axis=1)
    imag = np.concatenate([sine, cosine], axis=1)
    pair = np.stack([real, imag]).reshape(2, tiles, th, 2 * modes)
    rows = pair.transpose(2, 1, 0, 3).reshape(-1, 2 * modes)
    back_rows = pair.transpose(1, 0, 2, 3).reshape(-1, 2 * modes)
    return constant(send_cols), constant(rows), constant(back_rows), constant(back_cols)


def padded(rows):
    return -(-rows // PACK) * PACK


def order(outer, inner):
    take = np.arange(outer * inner).reshape(outer, inner).T.reshape(-1)
    return constant(np.eye(outer * inner)[take])


def mode_order(tiles, owned):
    rows = np.arange(tiles * padded(2 * owned)).reshape(tiles, -1)
    take = rows[:, : 2 * owned].reshape(tiles, 2, owned).transpose(2, 0, 1).reshape(-1)
    return constant(np.eye(rows.size)[take])


def dot(left, right, dims):
    return lax.dot_general(left, right, (dims, ((), ())), preferred_element_type=F32)


def low_half(shape, half):
    return lax.broadcasted_iota(jnp.int32, shape, 1) < half


def gelu_slope(values):
    root = values * math.sqrt(0.5 * math.log2(math.e))
    expo = jnp.exp2(-(root * root))
    base = 1.0 + (0.3275911 / math.sqrt(2.0)) * jnp.abs(values)
    t = pl.reciprocal(base, approx=True)
    t = t * (2.0 - base * t)
    poly = 0.5 * 1.061405429
    for factor in (-1.453152027, 1.421413741, -0.284496736, 0.254829592):
        poly = poly * t + 0.5 * factor
    tail = poly * t * expo
    cumulative = jnp.where(values < 0.0, tail, 1.0 - tail)
    return cumulative + values * expo * (1.0 / math.sqrt(2.0 * math.pi))


def shuffle(order_ref, value):
    return dot(order_ref[...], value, ((1,), (0,))).astype(BF16)


def by_rows(order_ref, field_refs, rows_ref):
    heights, lanes, _ = rows_ref.shape
    block = PACK * heights
    quarter = lanes // len(field_refs)
    for first in range(0, lanes, PACK):
        start = first % quarter * heights
        moved = shuffle(order_ref, field_refs[first // quarter][start : start + block, :])
        for h in range(heights):
            rows_ref[h, first : first + PACK, :] = moved[h * PACK : (h + 1) * PACK]


def columns_kernel(order_ref, table_ref, *rest):
    field_refs, (rows_ref, send_ref) = rest[:SPLIT], rest[SPLIT:]
    heights, lanes, _ = rows_ref.shape
    by_rows(order_ref, field_refs, rows_ref)
    for h in range(heights):
        send_ref[:, h * lanes : (h + 1) * lanes] = dot(table_ref[...], rows_ref[h], ((1,), (1,))).astype(BF16)


def relayout_kernel(order_ref, *rest):
    by_rows(order_ref, rest[:SPLIT], rest[SPLIT])


def shuffle_groups(order_ref, recv_ref, width):
    size = order_ref.shape[0]
    return [shuffle(order_ref, recv_ref[n : n + size, :width]) for n in range(0, recv_ref.shape[0], size)]


def stack(groups, index, count, lanes):
    return jnp.concatenate(
        [
            group[index * count : (index + 1) * count, n : n + lanes]
            for n in range(0, groups[0].shape[1], lanes)
            for group in groups
        ],
        axis=0,
    )


def spectra_into(scale, owned, lanes, recv_ref, order_ref, rows_ref, spec_ref):
    count = order_ref.shape[0] // owned
    fields = rows_ref.shape[0] // count * lanes
    ordered = [shuffle(order_ref, recv_ref[:, :fields])]
    for q in range(owned):
        stacked = stack(ordered, q, count, lanes)
        spec_ref[q * lanes : (q + 1) * lanes, :] = (
            scale * dot(stacked, rows_ref[...], ((0,), (0,)))
        ).astype(BF16)


def to_piece(value, rows):
    return jnp.concatenate([value[n : n + rows] for n in range(0, value.shape[0], rows)], axis=1)


def from_piece(value, extent):
    return jnp.concatenate([value[:, n : n + extent] for n in range(0, value.shape[1], extent)], axis=0)


def spectra_kernel(scale, owned, lanes, recv_ref, order_ref, rows_ref, spec_ref):
    spectra_into(scale, owned, lanes, recv_ref, order_ref, rows_ref, spec_ref)


def tree(terms):
    while len(terms) > 1:
        terms = [a + b for a, b in zip(terms[0::2], terms[1::2])]
    return terms[0]


def rows_of(store, block, extent):
    return store.at[pl.ds(pl.multiple_of(block * extent, extent), extent), :]


def packed_row(view, index):
    row = view[index : index + 1, :]
    return jnp.broadcast_to(row, (PACK, row.shape[1])).astype(BF16)


def duplicates(spec, half):
    value = spec.astype(F32)
    other = pltpu.roll(value, half, 1)
    low = low_half(value.shape, half)
    return jnp.where(low, value, other), jnp.where(low, other, value)


def finish(back_ref, sums, send_ref, mix):
    @pl.when(pl.program_id(0) == pl.num_programs(0) - 1)
    def _():
        owned = sums.shape[0]
        for q in range(owned):
            mixed = mix(sums.at[q]).astype(BF16)
            lanes = mixed.shape[0]
            send_ref[:, q * lanes : (q + 1) * lanes] = dot(back_ref[...], mixed, ((1,), (1,))).astype(BF16)


def fetch(sources, targets, sems):
    moves = [
        pltpu.make_async_copy(source, target, sems.at[n]) for n, (source, target) in enumerate(zip(sources, targets))
    ]

    @pl.when(pl.program_id(0) == 0)
    def _():
        for move in moves:
            move.start()

    return moves


def fetch_weights(source_ref, weights, sems):
    q = pl.program_id(0)
    owned = sems.shape[0]
    size = weights.shape[0] // owned

    def move(mode):
        part = pl.ds(pl.multiple_of(mode * size, size), size)
        return pltpu.make_async_copy(source_ref.at[part, :], weights.at[part, :], sems.at[mode])

    @pl.when(q == 0)
    def _():
        for mode in range(min(AHEAD, owned)):
            move(mode).start()

    @pl.when(q + AHEAD < owned)
    def _():
        move(q + AHEAD).start()

    return move(q), weights.at[pl.ds(pl.multiple_of(q * size, size), size), :]


def forward_kernel(scale, samples, owned, *rest):
    sources, source_ref, spec_ref, send_ref, real, imag, sums, weights, sems = rest[:4], *rest[4:12]
    targets, early = rest[12:16], rest[16]
    recv_ref, order_ref, rows_ref, back_ref = targets
    _, _, outs, both = sums.shape
    channels = weights.shape[0] // outs // owned
    half = both // 2
    lanes = samples * channels
    q = pl.program_id(0)
    moves = fetch(sources, targets, early)
    coming, weight_ref = fetch_weights(source_ref, weights, sems)

    @pl.when(q == 0)
    def _():
        for move in moves:
            move.wait()
        spectra_into(scale, owned, lanes, recv_ref, order_ref, rows_ref, spec_ref)
        real[...], imag[...] = duplicates(spec_ref[...], half)
        sums[...] = jnp.zeros_like(sums)

    coming.wait()

    def body(block, carry):
        view = rows_of(weight_ref, block, GROUP * outs)
        rows = []
        for s in range(samples):
            for store in (real, imag):
                part = rows_of(store, (q * lanes + s * channels) // GROUP + block, GROUP)
                rows.append([packed_row(part, step) for step in range(GROUP)])
        into = sums.at[q]
        for start in range(0, outs, 2 * PACK):
            totals = []
            for o in (start, start + PACK):
                column = [view[step * outs + o : step * outs + o + PACK, :] for step in range(GROUP)]
                for n, row in enumerate(rows):
                    totals.append((n, o, tree([w * r for w, r in zip(column, row)])))
            updated = [(n, o, into[n, o : o + PACK, :] + total.astype(F32)) for n, o, total in totals]
            for n, o, total in updated:
                into[n, o : o + PACK, :] = total
        return carry

    lax.fori_loop(0, channels // GROUP, body, 0)

    def mix(parts):
        low = low_half((outs, both), half)
        result = []
        for s in range(samples):
            crossed = pltpu.roll(parts[2 * s + 1], half, 1)
            result.append(parts[2 * s] + jnp.where(low, -crossed, crossed))
        return jnp.concatenate(result, axis=0)

    finish(back_ref, sums, send_ref, mix)


def backward_kernel(samples, tiles, *rest):
    sources, source_ref, send_ref, real, imag, sums, weights, sems = rest[:3], *rest[3:10]
    targets, early = rest[10:13], rest[13]
    spec_ref, back_ref, local_ref = targets
    channels, both = sums.shape[2] // ROWS, sums.shape[3]
    outs = weights.shape[0] // channels // sums.shape[0]
    half = both // 2
    lanes = samples * outs
    q = pl.program_id(0)
    moves = fetch(sources, targets, early)
    coming, weight_ref = fetch_weights(source_ref, weights, sems)

    @pl.when(q == 0)
    def _():
        for move in moves:
            move.wait()
        first, second = duplicates(spec_ref[...], half)
        real[...], imag[...] = first.astype(BF16), second.astype(BF16)
        extent = send_ref.shape[0] // tiles
        partial = to_piece(local_ref[...].astype(BF16), extent)
        for n in range(0, send_ref.shape[0], extent):
            send_ref[n : n + extent, sums.shape[0] * lanes :] = partial

    coming.wait()
    grads = [
        [store[pl.ds(pl.multiple_of(q * lanes + s * outs + o, PACK), PACK), :] for o in range(0, outs, PACK)]
        for s in range(samples)
        for store in (real, imag)
    ]

    def body(block, carry):
        view = rows_of(weight_ref, block, GROUP * outs)
        totals = []
        for step in range(GROUP):
            column = [view[step * outs + o : step * outs + o + PACK, :] for o in range(0, outs, PACK)]
            for n, grad in enumerate(grads):
                total = tree([w * g for w, g in zip(column, grad)]).astype(F32)
                totals.append((n, step, total[:ROWS] + total[ROWS:]))
        into = [rows_of(sums.at[q, n], block, GROUP * ROWS) for n in range(len(grads))]
        for n, step, total in totals:
            into[n][step * ROWS : (step + 1) * ROWS, :] = total
        return carry

    lax.fori_loop(0, channels // GROUP, body, 0)

    def mix(parts):
        low = low_half((channels, both), half)
        result = []
        for s in range(samples):
            straight, crossed = (
                sum(parts[n, pl.ds(row, channels, stride=ROWS), :] for row in range(ROWS)) for n in (2 * s, 2 * s + 1)
            )
            result.append(jnp.where(low, straight, -straight) + pltpu.roll(crossed, half, 1))
        return jnp.concatenate(result, axis=0)

    finish(back_ref, sums, send_ref, mix)


def pixels_kernel(scale, heights, recv_ref, order_ref, back_ref, local_ref, field_ref, cot_ref, table_ref, *rest):
    grad_ref, send_ref, sum_ref, ordered, total = rest
    steps, lanes, _ = field_ref.shape
    count = order_ref.shape[0] // heights
    size = order_ref.shape[0]
    group = pl.program_id(0)

    @pl.when(group == 0)
    def _():
        for n in range(0, recv_ref.shape[0], size):
            ordered[n : n + size, :] = shuffle(order_ref, recv_ref[n : n + size, :])
        total[...] = jnp.zeros_like(total)

    local = jnp.zeros(total.shape, F32)
    for step in range(steps):
        parts = []
        for n in range(0, recv_ref.shape[0], size):
            first = pl.multiple_of(n + (group * steps + step) * count, count)
            parts.append(ordered[pl.ds(first, count), :])
        inner = stack(parts, 0, count, lanes)
        pre = scale * dot(inner, back_ref[...], ((0,), (0,)))
        pre = pre + dot(local_ref[...], field_ref[step], ((1,), (0,)))
        grad = (cot_ref[step].astype(F32) * gelu_slope(pre)).astype(BF16)
        grad_ref[step] = grad
        send_ref[:, step * lanes : (step + 1) * lanes] = dot(table_ref[...], grad, ((1,), (1,))).astype(BF16)
        local = local + dot(field_ref[step], grad, ((1,), (1,)))
    total[...] += local

    @pl.when(group == pl.num_programs(0) - 1)
    def _():
        extent = sum_ref.shape[0]
        sum_ref[...] = sum(total[n : n + extent, n : n + extent] for n in range(0, lanes, extent))


def final_kernel(scale, tiles, recv_ref, order_ref, back_ref, local_ref, grad_ref, restore_ref, *rest):
    out_ref, sum_ref, result = rest
    heights, lanes, _ = grad_ref.shape
    extent = recv_ref.shape[0] // tiles
    first = back_ref.shape[0] // (2 * tiles) * lanes
    partials = sum(recv_ref[n : n + extent, first:].astype(F32) for n in range(0, recv_ref.shape[0], extent))
    sum_ref[...] = from_piece(partials, sum_ref.shape[1])
    count = order_ref.shape[0] // heights
    ordered = shuffle_groups(order_ref, recv_ref, first)
    for h in range(heights):
        inner = stack(ordered, h, count, lanes)
        value = scale * dot(inner, back_ref[...], ((0,), (0,)))
        result[h] = (value + dot(local_ref[...], grad_ref[h], ((1,), (0,)))).astype(BF16)
    block = PACK * heights
    for first in range(0, lanes, PACK):
        part = jnp.concatenate([result[h, first : first + PACK, :] for h in range(heights)], axis=0)
        out_ref[first * heights : first * heights + block, :] = shuffle(restore_ref, part)


def outer_kernel(samples, groups, *refs):
    specs, grads = refs[:groups], refs[groups : 2 * groups]
    out_ref, real, imag, plain, crossed = refs[2 * groups :]
    total, channels, both = real.shape
    outs = plain.shape[1]
    half = both // 2
    low = low_half((channels, both), half)

    for g in range(groups):
        for s in range(samples):
            n = g * samples + s
            spec = specs[g][s * channels : (s + 1) * channels, :].astype(F32)
            other = pltpu.roll(spec, half, 1)
            real[n] = jnp.where(low, spec, other)
            imag[n] = jnp.where(low, other, -spec)
            grad = grads[g][s * outs : (s + 1) * outs, :]
            plain[n] = grad
            crossed[n] = pltpu.roll(grad.astype(F32), half, 1).astype(BF16)

    def body(block, carry):
        into = rows_of(out_ref, block, GROUP * outs)
        views = [rows_of(store.at[n], block, GROUP) for n in range(total) for store in (real, imag)]
        for first in range(0, GROUP, 2):
            pair = range(first, first + 2)
            lefts = [[packed_row(view, c) for view in views] for c in pair]
            results = []
            for o in range(0, outs, PACK):
                right = [store[n, o : o + PACK, :] for n in range(total) for store in (plain, crossed)]
                for c, left in zip(pair, lefts):
                    results.append((c * outs + o, tree([a * b for a, b in zip(left, right)])))
            for row, result in results:
                into[row : row + PACK, :] = result.astype(F32)
        return carry

    lax.fori_loop(0, channels // GROUP, body, 0)


def whole(extent):
    return pl.BlockSpec(extent, lambda *_: (0,) * len(extent))


def call(kernel, name, operands, outs, scratch=(), grid=(1,), blocks=None, out_blocks=None, limit=LIMIT):
    blocks, out_blocks = blocks or {}, out_blocks or {}
    in_specs = [blocks.get(n) or whole(operand.shape) for n, operand in enumerate(operands)]
    out_specs = [out_blocks.get(n, whole(out.shape)) for n, out in enumerate(outs)]
    return pl.pallas_call(
        kernel,
        out_shape=tuple(outs),
        grid=grid,
        in_specs=in_specs,
        out_specs=tuple(out_specs),
        scratch_shapes=list(scratch),
        compiler_params=pltpu.CompilerParams(vmem_limit_bytes=limit),
        name=name,
    )(*operands)


def swap(values, axis, step):
    return lax.ppermute(values, axis, [(i, i ^ step) for i in range(lax.axis_size(axis))])


def gather_near(values, axis):
    size = lax.axis_size(axis)
    return {0: values} | {1 << bit: swap(values, axis, 1 << bit) for bit in range(size.bit_length() - 1)}


def gather_far(near, axis):
    whole_set = dict(near)
    for step in range(1, lax.axis_size(axis)):
        if step not in whole_set:
            whole_set[step] = swap(whole_set[step & (step - 1)], axis, step & -step)
    return [whole_set[step] for step in sorted(whole_set)]


def sum_over(values, axis):
    step = 1
    while step < lax.axis_size(axis):
        values = values + swap(values, axis, step)
        step *= 2
    return values


def block_diagonal(matrix, copies):
    zero = jnp.zeros_like(matrix)
    return jnp.concatenate(
        [
            jnp.concatenate([matrix if i == j else zero for j in range(copies)], axis=1)
            for i in range(copies)
        ],
        axis=0,
    )


def shape(extent, kind=BF16):
    return jax.ShapeDtypeStruct(extent, kind)


def local(inputs, cotangent, mode_weight, local_weight):
    tiles = lax.axis_size("tile")
    samples, channels, th, width = inputs.shape
    owned, _, _, both = mode_weight.shape
    modes = both // 2
    lanes = samples * channels
    parts = width // 128
    spec_scale = 1.0 / math.sqrt(tiles * th * width)
    mode_scale = 1.0 / math.sqrt(modes * tiles * owned)
    send_cols, rows, back_rows, back_cols = tables(tiles, owned, th, width, modes)
    pixel_rows = samples * channels * th
    halves = tiles * padded(2 * owned)
    inverse = 2 * tiles * th

    def exchange(values):
        split = values.reshape(tiles, values.shape[0] // tiles, values.shape[1])
        moved = lax.all_to_all(split, "tile", split_axis=0, concat_axis=0, tiled=False)
        return moved.reshape(values.shape)

    forward_mix = block_diagonal(local_weight.T, samples)
    backward_mix = block_diagonal(local_weight, samples)
    by_row = order(PACK, th)
    by_channel = order(th, PACK)
    by_mode = mode_order(tiles, owned)
    by_height = order(2 * min(tiles, 8), th)
    flat_weight = mode_weight.reshape(-1, both)
    weight_block = pl.BlockSpec((flat_weight.shape[0] // owned, both), lambda q: (q, 0))
    weight_scratch = [pltpu.VMEM(flat_weight.shape, BF16), pltpu.SemaphoreType.DMA((owned,))]
    in_place = pl.BlockSpec(memory_space=pl.ANY)
    to_modes = shape((halves, th * lanes))
    to_pixels = shape((inverse, owned * lanes))
    field_shape = shape((th, lanes, width))

    def field_blocks(first):
        return {first + n: pl.BlockSpec((pixel_rows // SPLIT, width), lambda _, n=n: (n, 0)) for n in range(SPLIT)}

    field_rows, send = call(
        columns_kernel,
        "columns",
        (by_row, send_cols, *[inputs.reshape(pixel_rows, width)] * SPLIT),
        (field_shape, to_modes),
        blocks=field_blocks(2),
    )
    arrived = exchange(send)
    (cot_rows,) = call(
        relayout_kernel,
        "relayout",
        (by_row, *[cotangent.reshape(pixel_rows, width)] * SPLIT),
        (field_shape,),
        blocks=field_blocks(1),
    )
    def early(*operands):
        kept = [pltpu.VMEM(operand.shape, operand.dtype) for operand in operands]
        return kept + [pltpu.SemaphoreType.DMA((len(operands),))]

    spectra, send = call(
        functools.partial(forward_kernel, spec_scale, samples, owned),
        "mix_forward",
        (arrived, by_mode, rows, back_rows, flat_weight),
        (shape((owned * lanes, both)), to_pixels),
        [
            pltpu.VMEM((owned * lanes, both), F32),
            pltpu.VMEM((owned * lanes, both), F32),
            pltpu.VMEM((owned, 2 * samples, channels, both), F32),
            *weight_scratch,
            *early(arrived, by_mode, rows, back_rows),
        ],
        grid=(owned,),
        blocks={n: in_place for n in range(5)},
    )
    all_spectra = gather_far(gather_near(spectra, "dp"), "dp")
    arrived = exchange(send)
    steps = 4
    row_block = pl.BlockSpec((steps, lanes, width), lambda n: (n, 0, 0))
    gate_rows, send, local_sum = call(
        functools.partial(pixels_kernel, mode_scale, th),
        "pixels",
        (arrived, by_height, back_cols, forward_mix, field_rows, cot_rows, send_cols),
        (field_shape, to_modes, shape((channels, channels), F32)),
        [pltpu.VMEM((inverse, owned * lanes), BF16), pltpu.VMEM((lanes, lanes), F32)],
        grid=(th // steps,),
        blocks={4: row_block, 5: row_block},
        out_blocks={0: row_block, 1: pl.BlockSpec((halves, steps * lanes), lambda n: (0, n))},
        limit=SMALL,
    )
    send, *all_spectra = lax.optimization_barrier((send, *all_spectra))
    arrived, local_sum = lax.optimization_barrier((exchange(send), sum_over(local_sum, "dp")))
    (grad_spectra,) = call(
        functools.partial(spectra_kernel, mode_scale, owned, lanes),
        "grad_spectra",
        (arrived, by_mode, rows),
        (shape((owned * lanes, both)),),
        limit=SMALL,
    )
    near = gather_near(grad_spectra, "dp")
    (send,) = call(
        functools.partial(backward_kernel, samples, tiles),
        "mix_backward",
        (grad_spectra, back_rows, local_sum, flat_weight),
        (shape((inverse, owned * lanes + channels * channels * tiles // inverse)),),
        [
            pltpu.VMEM((owned * lanes, both), BF16),
            pltpu.VMEM((owned * lanes, both), BF16),
            pltpu.VMEM((owned, 2 * samples, channels * ROWS, both), F32),
            *weight_scratch,
            *early(grad_spectra, back_rows, local_sum),
        ],
        grid=(owned,),
        blocks={n: in_place for n in range(4)},
    )
    send, near = lax.optimization_barrier((send, near))
    all_grads = gather_far(near, "dp")
    arrived = exchange(send)

    groups = lax.axis_size("dp")
    total = groups * samples
    per_mode = pl.BlockSpec((lanes, both), lambda q: (q, 0))
    (mode_grad,) = call(
        functools.partial(outer_kernel, samples, groups),
        "mode_grad",
        (*all_spectra, *all_grads),
        (shape(flat_weight.shape, F32),),
        [pltpu.VMEM((total, channels, both), F32)] * 2 + [pltpu.VMEM((total, channels, both), BF16)] * 2,
        grid=(owned,),
        blocks={n: per_mode for n in range(2 * groups)},
        out_blocks={0: weight_block},
    )
    arrived, mode_grad = lax.optimization_barrier((arrived, mode_grad))

    input_grad, local_grad = call(
        functools.partial(final_kernel, spec_scale, tiles),
        "final",
        (arrived, by_height, back_cols, backward_mix, gate_rows, by_channel),
        (shape((pixel_rows, width)), shape((channels, channels), F32)),
        [pltpu.VMEM((th, lanes, width), BF16)],
        limit=SMALL,
    )
    return (input_grad.reshape(inputs.shape), mode_grad.reshape(mode_weight.shape), local_grad)


def solution(mesh):
    return jax.shard_map(
        local,
        mesh=mesh,
        in_specs=(
            P("dp", None, "tile", None),
            P("dp", None, "tile", None),
            P("tile", None, None, None),
            P(),
        ),
        out_specs=(P("dp", None, "tile", None), P("tile", None, None, None), P()),
        check_vma=False,
    )
```

```python
import functools
import math

import jax
import jax.numpy as jnp
import numpy as np
from jax import lax
from jax.experimental import pallas as pl
from jax.experimental.pallas import tpu as pltpu
from jax.sharding import PartitionSpec as P

F32 = jnp.float32
BF16 = jnp.bfloat16
LIMIT = 56 * 1024 * 1024
SMALL = 24 * 1024 * 1024
ROWS = 8
PACK = 16
GROUP = 8
SPLIT = 4
AHEAD = 3


def row_tables(height, modes):
    index = np.arange(modes)
    signed = np.where(index < modes // 2, index, index - modes)
    phases = np.mod(np.arange(height)[:, None] * signed[None, :], height)
    angles = phases * (2.0 * math.pi / height)
    return np.cos(angles), np.sin(angles)


def column_tables(width, modes):
    phases = np.mod(np.arange(modes)[:, None] * np.arange(width)[None, :], width)
    angles = phases * (2.0 * math.pi / width)
    return np.stack([np.cos(angles), -np.sin(angles)])


def constant(table):
    return jnp.asarray(np.asarray(table, np.float32)).astype(BF16)


def tables(tiles, owned, th, width, modes):
    cols = column_tables(width, tiles * owned)
    split = cols.reshape(2, tiles, owned, width)
    send_cols = split.transpose(1, 0, 2, 3).reshape(tiles, 2 * owned, width)
    send_cols = np.pad(send_cols, ((0, 0), (0, padded(2 * owned) - 2 * owned), (0, 0))).reshape(-1, width)
    back_cols = split.transpose(2, 1, 0, 3).reshape(-1, width)
    cosine, sine = row_tables(th * tiles, modes)
    real = np.concatenate([cosine, -sine], axis=1)
    imag = np.concatenate([sine, cosine], axis=1)
    pair = np.stack([real, imag]).reshape(2, tiles, th, 2 * modes)
    rows = pair.transpose(2, 1, 0, 3).reshape(-1, 2 * modes)
    back_rows = pair.transpose(1, 0, 2, 3).reshape(-1, 2 * modes)
    return constant(send_cols), constant(rows), constant(back_rows), constant(back_cols)


def padded(rows):
    return -(-rows // PACK) * PACK


def order(outer, inner):
    take = np.arange(outer * inner).reshape(outer, inner).T.reshape(-1)
    return constant(np.eye(outer * inner)[take])


def mode_order(tiles, owned):
    rows = np.arange(tiles * padded(2 * owned)).reshape(tiles, -1)
    take = rows[:, : 2 * owned].reshape(tiles, 2, owned).transpose(2, 0, 1).reshape(-1)
    return constant(np.eye(rows.size)[take])


def dot(left, right, dims):
    return lax.dot_general(left, right, (dims, ((), ())), preferred_element_type=F32)


def low_half(shape, half):
    return lax.broadcasted_iota(jnp.int32, shape, 1) < half


def gelu_slope(values):
    size = jnp.abs(values)
    expo = jnp.exp(-0.5 * values * values)
    t = 1.0 / (1.0 + (0.3275911 / math.sqrt(2.0)) * size)
    poly = 0.5 * 1.061405429
    for factor in (-1.453152027, 1.421413741, -0.284496736, 0.254829592):
        poly = poly * t + 0.5 * factor
    tail = poly * t * expo
    cumulative = jnp.where(values < 0.0, tail, 1.0 - tail)
    return cumulative + values * expo * (1.0 / math.sqrt(2.0 * math.pi))


def shuffle(order_ref, value):
    return dot(order_ref[...], value, ((1,), (0,))).astype(BF16)


def by_rows(order_ref, field_refs, rows_ref):
    heights, lanes, _ = rows_ref.shape
    block = PACK * heights
    quarter = lanes // len(field_refs)
    for first in range(0, lanes, PACK):
        start = first % quarter * heights
        moved = shuffle(order_ref, field_refs[first // quarter][start : start + block, :])
        for h in range(heights):
            rows_ref[h, first : first + PACK, :] = moved[h * PACK : (h + 1) * PACK]


def columns_kernel(order_src, table_src, field_src, rows_out, send_out, *rest):
    order_ref, table_ref, field, rows, send, early, late = rest
    heights, lanes, _ = rows.shape
    block = PACK * heights
    first = [
        pltpu.make_async_copy(order_src, order_ref, early.at[0]),
        pltpu.make_async_copy(table_src, table_ref, early.at[1]),
    ]
    blocks = [
        pltpu.make_async_copy(field_src.at[pl.ds(n, block), :], field.at[pl.ds(n, block), :], early.at[2 + n // block])
        for n in range(0, lanes * heights, block)
    ]
    for move in first + blocks:
        move.start()
    for move in first:
        move.wait()
    for n, move in enumerate(blocks):
        move.wait()
        moved = shuffle(order_ref, field[n * block : (n + 1) * block, :])
        for h in range(heights):
            rows[h, n * PACK : (n + 1) * PACK, :] = moved[h * PACK : (h + 1) * PACK]
    outgoing = []
    part = heights // SPLIT
    for n in range(SPLIT):
        for h in range(n * part, (n + 1) * part):
            send[:, h * lanes : (h + 1) * lanes] = dot(table_ref[...], rows[h], ((1,), (1,))).astype(BF16)
        column = pl.ds(n * part * lanes, part * lanes)
        outgoing.append(pltpu.make_async_copy(send.at[:, column], send_out.at[:, column], late.at[2 * n]))
        layers = pl.ds(n * part, part)
        outgoing.append(pltpu.make_async_copy(rows.at[layers], rows_out.at[layers], late.at[2 * n + 1]))
        for move in outgoing[-2:]:
            move.start()
    for move in outgoing:
        move.wait()


def relayout_kernel(order_ref, *rest):
    by_rows(order_ref, rest[:SPLIT], rest[SPLIT])


def shuffle_groups(order_ref, recv_ref, width):
    size = order_ref.shape[0]
    return [shuffle(order_ref, recv_ref[n : n + size, :width]) for n in range(0, recv_ref.shape[0], size)]


def stack(groups, index, count, lanes):
    return jnp.concatenate(
        [
            group[index * count : (index + 1) * count, n : n + lanes]
            for n in range(0, groups[0].shape[1], lanes)
            for group in groups
        ],
        axis=0,
    )


def spectra_into(scale, owned, lanes, recv_ref, order_ref, rows_ref, spec_ref):
    count = order_ref.shape[0] // owned
    fields = rows_ref.shape[0] // count * lanes
    ordered = [shuffle(order_ref, recv_ref[:, :fields])]
    for q in range(owned):
        stacked = stack(ordered, q, count, lanes)
        spec_ref[q * lanes : (q + 1) * lanes, :] = (
            scale * dot(stacked, rows_ref[...], ((0,), (0,)))
        ).astype(BF16)


def to_piece(value, rows):
    return jnp.concatenate([value[n : n + rows] for n in range(0, value.shape[0], rows)], axis=1)


def from_piece(value, extent):
    return jnp.concatenate([value[:, n : n + extent] for n in range(0, value.shape[1], extent)], axis=0)


def spectra_kernel(scale, owned, lanes, recv_ref, order_ref, rows_ref, spec_ref):
    spectra_into(scale, owned, lanes, recv_ref, order_ref, rows_ref, spec_ref)


def tree(terms):
    while len(terms) > 1:
        terms = [a + b for a, b in zip(terms[0::2], terms[1::2])]
    return terms[0]


def rows_of(store, block, extent):
    return store.at[pl.ds(pl.multiple_of(block * extent, extent), extent), :]


def packed_row(view, index):
    row = view[index : index + 1, :]
    return jnp.broadcast_to(row, (PACK, row.shape[1])).astype(BF16)


def duplicates(spec, half):
    value = spec.astype(F32)
    other = pltpu.roll(value, half, 1)
    low = low_half(value.shape, half)
    return jnp.where(low, value, other), jnp.where(low, other, value)


def finish(back_ref, sums, send_ref, stage, sems, mix):
    @pl.when(pl.program_id(0) == pl.num_programs(0) - 1)
    def _():
        moves = []
        for q in range(sums.shape[0]):
            mixed = mix(sums.at[q]).astype(BF16)
            column = pl.ds(q * mixed.shape[0], mixed.shape[0])
            stage[:, column] = dot(back_ref[...], mixed, ((1,), (1,))).astype(BF16)
            moves.append(pltpu.make_async_copy(stage.at[:, column], send_ref.at[:, column], sems.at[q]))
            moves[-1].start()
        for move in moves:
            move.wait()


def fetch(sources, targets, sems):
    moves = [
        pltpu.make_async_copy(source, target, sems.at[n]) for n, (source, target) in enumerate(zip(sources, targets))
    ]

    @pl.when(pl.program_id(0) == 0)
    def _():
        for move in moves:
            move.start()

    return moves


def fetch_weights(moves, source_ref, weights, sems):
    q = pl.program_id(0)
    owned = sems.shape[0]
    size = weights.shape[0] // owned

    def move(mode):
        part = pl.ds(pl.multiple_of(mode * size, size), size)
        return pltpu.make_async_copy(source_ref.at[part, :], weights.at[part, :], sems.at[mode])

    @pl.when(q == 0)
    def _():
        move(0).start()
        for early in moves:
            early.wait()
        for mode in range(1, min(AHEAD, owned)):
            move(mode).start()

    @pl.when(q + AHEAD < owned)
    def _():
        move(q + AHEAD).start()

    return move(q), weights.at[pl.ds(pl.multiple_of(q * size, size), size), :]


def forward_kernel(scale, samples, owned, *rest):
    sources, source_ref, spec_ref, send_ref, real, imag, sums, weights, sems = rest[:4], *rest[4:12]
    targets, early, stage, late = rest[12:16], *rest[16:19]
    recv_ref, order_ref, rows_ref, back_ref = targets
    _, _, outs, both = sums.shape
    channels = weights.shape[0] // outs // owned
    half = both // 2
    lanes = samples * channels
    q = pl.program_id(0)
    moves = fetch(sources, targets, early)
    coming, weight_ref = fetch_weights(moves, source_ref, weights, sems)

    @pl.when(q == 0)
    def _():
        spectra_into(scale, owned, lanes, recv_ref, order_ref, rows_ref, spec_ref)
        real[...], imag[...] = duplicates(spec_ref[...], half)
        sums[...] = jnp.zeros_like(sums)

    coming.wait()

    def body(block, carry):
        view = rows_of(weight_ref, block, GROUP * outs)
        rows = []
        for s in range(samples):
            for store in (real, imag):
                part = rows_of(store, (q * lanes + s * channels) // GROUP + block, GROUP)
                rows.append([packed_row(part, step) for step in range(GROUP)])
        into = sums.at[q]
        for start in range(0, outs, 2 * PACK):
            totals = []
            for o in (start, start + PACK):
                column = [view[step * outs + o : step * outs + o + PACK, :] for step in range(GROUP)]
                for n, row in enumerate(rows):
                    totals.append((n, o, tree([w * r for w, r in zip(column, row)])))
            updated = [(n, o, into[n, o : o + PACK, :] + total.astype(F32)) for n, o, total in totals]
            for n, o, total in updated:
                into[n, o : o + PACK, :] = total
        return carry

    lax.fori_loop(0, channels // GROUP, body, 0)

    def mix(parts):
        low = low_half((outs, both), half)
        result = []
        for s in range(samples):
            crossed = pltpu.roll(parts[2 * s + 1], half, 1)
            result.append(parts[2 * s] + jnp.where(low, -crossed, crossed))
        return jnp.concatenate(result, axis=0)

    finish(back_ref, sums, send_ref, stage, late, mix)


def backward_kernel(samples, tiles, *rest):
    sources, source_ref, send_ref, real, imag, sums, weights, sems = rest[:3], *rest[3:10]
    targets, early, stage, late = rest[10:13], *rest[13:16]
    spec_ref, back_ref, local_ref = targets

    def carried():
        column = pl.ds(sums.shape[0] * lanes, stage.shape[1] - sums.shape[0] * lanes)
        return pltpu.make_async_copy(stage.at[:, column], send_ref.at[:, column], late.at[0])

    channels, both = sums.shape[2] // ROWS, sums.shape[3]
    outs = weights.shape[0] // channels // sums.shape[0]
    half = both // 2
    lanes = samples * outs
    q = pl.program_id(0)
    moves = fetch(sources, targets, early)
    coming, weight_ref = fetch_weights(moves, source_ref, weights, sems)

    @pl.when(q == 0)
    def _():
        first, second = duplicates(spec_ref[...], half)
        real[...], imag[...] = first.astype(BF16), second.astype(BF16)
        extent = stage.shape[0] // tiles
        partial = to_piece(local_ref[...].astype(BF16), extent)
        for n in range(0, stage.shape[0], extent):
            stage[n : n + extent, sums.shape[0] * lanes :] = partial
        move = carried()
        move.start()
        move.wait()

    coming.wait()
    grads = [
        [store[pl.ds(pl.multiple_of(q * lanes + s * outs + o, PACK), PACK), :] for o in range(0, outs, PACK)]
        for s in range(samples)
        for store in (real, imag)
    ]

    def body(block, carry):
        view = rows_of(weight_ref, block, GROUP * outs)
        totals = []
        for step in range(GROUP):
            column = [view[step * outs + o : step * outs + o + PACK, :] for o in range(0, outs, PACK)]
            for n, grad in enumerate(grads):
                total = tree([w * g for w, g in zip(column, grad)]).astype(F32)
                totals.append((n, step, total[:ROWS] + total[ROWS:]))
        into = [rows_of(sums.at[q, n], block, GROUP * ROWS) for n in range(len(grads))]
        for n, step, total in totals:
            into[n][step * ROWS : (step + 1) * ROWS, :] = total
        return carry

    lax.fori_loop(0, channels // GROUP, body, 0)

    def mix(parts):
        low = low_half((channels, both), half)
        result = []
        for s in range(samples):
            straight, crossed = (
                sum(parts[n, pl.ds(row, channels, stride=ROWS), :] for row in range(ROWS)) for n in (2 * s, 2 * s + 1)
            )
            result.append(jnp.where(low, straight, -straight) + pltpu.roll(crossed, half, 1))
        return jnp.concatenate(result, axis=0)

    finish(back_ref, sums, send_ref, stage, late, mix)


def pixels_kernel(scale, heights, recv_ref, order_ref, back_ref, local_ref, field_ref, cot_ref, table_ref, *rest):
    grad_ref, send_ref, sum_ref, ordered, total = rest
    steps, lanes, _ = field_ref.shape
    count = order_ref.shape[0] // heights
    size = order_ref.shape[0]
    group = pl.program_id(0)

    @pl.when(group == 0)
    def _():
        for n in range(0, recv_ref.shape[0], size):
            ordered[n : n + size, :] = shuffle(order_ref, recv_ref[n : n + size, :])
        total[...] = jnp.zeros_like(total)

    local = jnp.zeros(total.shape, F32)
    for step in range(steps):
        parts = []
        for n in range(0, recv_ref.shape[0], size):
            first = pl.multiple_of(n + (group * steps + step) * count, count)
            parts.append(ordered[pl.ds(first, count), :])
        inner = stack(parts, 0, count, lanes)
        pre = scale * dot(inner, back_ref[...], ((0,), (0,)))
        pre = pre + dot(local_ref[...], field_ref[step], ((1,), (0,)))
        grad = (cot_ref[step].astype(F32) * gelu_slope(pre)).astype(BF16)
        grad_ref[step] = grad
        send_ref[:, step * lanes : (step + 1) * lanes] = dot(table_ref[...], grad, ((1,), (1,))).astype(BF16)
        local = local + dot(field_ref[step], grad, ((1,), (1,)))
    total[...] += local

    @pl.when(group == pl.num_programs(0) - 1)
    def _():
        extent = sum_ref.shape[0]
        sum_ref[...] = sum(total[n : n + extent, n : n + extent] for n in range(0, lanes, extent))


def final_kernel(scale, tiles, recv_ref, order_ref, back_ref, local_ref, grad_ref, restore_ref, *rest):
    out_ref, sum_ref, result, stage, late = rest
    heights, lanes, _ = grad_ref.shape
    extent = recv_ref.shape[0] // tiles
    first = back_ref.shape[0] // (2 * tiles) * lanes
    partials = sum(recv_ref[n : n + extent, first:].astype(F32) for n in range(0, recv_ref.shape[0], extent))
    sum_ref[...] = from_piece(partials, sum_ref.shape[1])
    count = order_ref.shape[0] // heights
    ordered = shuffle_groups(order_ref, recv_ref, first)
    for h in range(heights):
        inner = stack(ordered, h, count, lanes)
        value = scale * dot(inner, back_ref[...], ((0,), (0,)))
        result[h] = (value + dot(local_ref[...], grad_ref[h], ((1,), (0,)))).astype(BF16)
    block = PACK * heights
    moves = []
    for first in range(0, lanes, PACK):
        part = jnp.concatenate([result[h, first : first + PACK, :] for h in range(heights)], axis=0)
        rows = pl.ds(first * heights, block)
        stage[rows, :] = shuffle(restore_ref, part)
        moves.append(pltpu.make_async_copy(stage.at[rows, :], out_ref.at[rows, :], late.at[first // PACK]))
        moves[-1].start()
    for move in moves:
        move.wait()


def outer_kernel(samples, groups, *refs):
    specs, grads = refs[:groups], refs[groups : 2 * groups]
    out_ref, real, imag, plain, crossed = refs[2 * groups :]
    total, channels, both = real.shape
    outs = plain.shape[1]
    half = both // 2
    low = low_half((channels, both), half)

    for g in range(groups):
        for s in range(samples):
            n = g * samples + s
            spec = specs[g][s * channels : (s + 1) * channels, :].astype(F32)
            other = pltpu.roll(spec, half, 1)
            real[n] = jnp.where(low, spec, other)
            imag[n] = jnp.where(low, other, -spec)
            grad = grads[g][s * outs : (s + 1) * outs, :]
            plain[n] = grad
            crossed[n] = pltpu.roll(grad.astype(F32), half, 1).astype(BF16)

    def body(block, carry):
        into = rows_of(out_ref, block, GROUP * outs)
        views = [rows_of(store.at[n], block, GROUP) for n in range(total) for store in (real, imag)]
        for first in range(0, GROUP, 2):
            pair = range(first, first + 2)
            lefts = [[packed_row(view, c) for view in views] for c in pair]
            results = []
            for o in range(0, outs, PACK):
                right = [store[n, o : o + PACK, :] for n in range(total) for store in (plain, crossed)]
                for c, left in zip(pair, lefts):
                    results.append((c * outs + o, tree([a * b for a, b in zip(left, right)])))
            for row, result in results:
                into[row : row + PACK, :] = result.astype(F32)
        return carry

    lax.fori_loop(0, channels // GROUP, body, 0)


def whole(extent):
    return pl.BlockSpec(extent, lambda *_: (0,) * len(extent))


def call(kernel, name, operands, outs, scratch=(), grid=(1,), blocks=None, out_blocks=None, limit=LIMIT):
    blocks, out_blocks = blocks or {}, out_blocks or {}
    in_specs = [blocks.get(n) or whole(operand.shape) for n, operand in enumerate(operands)]
    out_specs = [out_blocks.get(n, whole(out.shape)) for n, out in enumerate(outs)]
    return pl.pallas_call(
        kernel,
        out_shape=tuple(outs),
        grid=grid,
        in_specs=in_specs,
        out_specs=tuple(out_specs),
        scratch_shapes=list(scratch),
        compiler_params=pltpu.CompilerParams(vmem_limit_bytes=limit),
        name=name,
    )(*operands)


def swap(values, axis, step):
    return lax.ppermute(values, axis, [(i, i ^ step) for i in range(lax.axis_size(axis))])


def gather_near(values, axis):
    size = lax.axis_size(axis)
    return {0: values} | {1 << bit: swap(values, axis, 1 << bit) for bit in range(size.bit_length() - 1)}


def gather_far(near, axis):
    whole_set = dict(near)
    for step in range(1, lax.axis_size(axis)):
        if step not in whole_set:
            whole_set[step] = swap(whole_set[step & (step - 1)], axis, step & -step)
    return [whole_set[step] for step in sorted(whole_set)]


def sum_over(values, axis):
    step = 1
    while step < lax.axis_size(axis):
        values = values + swap(values, axis, step)
        step *= 2
    return values


def block_diagonal(matrix, copies):
    zero = jnp.zeros_like(matrix)
    return jnp.concatenate(
        [
            jnp.concatenate([matrix if i == j else zero for j in range(copies)], axis=1)
            for i in range(copies)
        ],
        axis=0,
    )


def shape(extent, kind=BF16):
    return jax.ShapeDtypeStruct(extent, kind)


def local(inputs, cotangent, mode_weight, local_weight):
    tiles = lax.axis_size("tile")
    samples, channels, th, width = inputs.shape
    owned, _, _, both = mode_weight.shape
    modes = both // 2
    lanes = samples * channels
    parts = width // 128
    spec_scale = 1.0 / math.sqrt(tiles * th * width)
    mode_scale = 1.0 / math.sqrt(modes * tiles * owned)
    send_cols, rows, back_rows, back_cols = tables(tiles, owned, th, width, modes)
    pixel_rows = samples * channels * th
    halves = tiles * padded(2 * owned)
    inverse = 2 * tiles * th

    def exchange(values):
        split = values.reshape(tiles, values.shape[0] // tiles, values.shape[1])
        moved = lax.all_to_all(split, "tile", split_axis=0, concat_axis=0, tiled=False)
        return moved.reshape(values.shape)

    forward_mix = block_diagonal(local_weight.T, samples)
    backward_mix = block_diagonal(local_weight, samples)
    by_row = order(PACK, th)
    by_channel = order(th, PACK)
    by_mode = mode_order(tiles, owned)
    by_height = order(2 * min(tiles, 8), th)
    flat_weight = mode_weight.reshape(-1, both)
    weight_block = pl.BlockSpec((flat_weight.shape[0] // owned, both), lambda q: (q, 0))
    weight_scratch = [pltpu.VMEM(flat_weight.shape, BF16), pltpu.SemaphoreType.DMA((owned,))]
    in_place = pl.BlockSpec(memory_space=pl.ANY)
    to_modes = shape((halves, th * lanes))
    to_pixels = shape((inverse, owned * lanes))
    field_shape = shape((th, lanes, width))

    def kept(*operands):
        return [pltpu.VMEM(operand.shape, operand.dtype) for operand in operands]

    def early(*operands):
        return kept(*operands) + [pltpu.SemaphoreType.DMA((len(operands),))]

    def field_blocks(first):
        return {first + n: pl.BlockSpec((pixel_rows // SPLIT, width), lambda _, n=n: (n, 0)) for n in range(SPLIT)}

    field_rows, send = call(
        columns_kernel,
        "columns",
        (by_row, send_cols, inputs.reshape(pixel_rows, width)),
        (field_shape, to_modes),
        [
            *kept(by_row, send_cols, inputs.reshape(pixel_rows, width), field_shape, to_modes),
            pltpu.SemaphoreType.DMA((2 + lanes // PACK,)),
            pltpu.SemaphoreType.DMA((2 * SPLIT,)),
        ],
        blocks={n: in_place for n in range(3)},
        out_blocks={n: in_place for n in range(2)},
    )
    arrived = exchange(send)
    (cot_rows,) = call(
        relayout_kernel,
        "relayout",
        (by_row, *[cotangent.reshape(pixel_rows, width)] * SPLIT),
        (field_shape,),
        blocks=field_blocks(1),
    )
    spectra, send = call(
        functools.partial(forward_kernel, spec_scale, samples, owned),
        "mix_forward",
        (arrived, by_mode, rows, back_rows, flat_weight),
        (shape((owned * lanes, both)), to_pixels),
        [
            pltpu.VMEM((owned * lanes, both), F32),
            pltpu.VMEM((owned * lanes, both), F32),
            pltpu.VMEM((owned, 2 * samples, channels, both), F32),
            *weight_scratch,
            *early(arrived, by_mode, rows, back_rows),
            pltpu.VMEM((inverse, owned * lanes), BF16),
            pltpu.SemaphoreType.DMA((owned,)),
        ],
        grid=(owned,),
        blocks={n: in_place for n in range(5)},
        out_blocks={1: in_place},
    )
    all_spectra = gather_far(gather_near(spectra, "dp"), "dp")
    arrived = exchange(send)
    steps = 4
    row_block = pl.BlockSpec((steps, lanes, width), lambda n: (n, 0, 0))
    gate_rows, send, local_sum = call(
        functools.partial(pixels_kernel, mode_scale, th),
        "pixels",
        (arrived, by_height, back_cols, forward_mix, field_rows, cot_rows, send_cols),
        (field_shape, to_modes, shape((channels, channels), F32)),
        [pltpu.VMEM((inverse, owned * lanes), BF16), pltpu.VMEM((lanes, lanes), F32)],
        grid=(th // steps,),
        blocks={4: row_block, 5: row_block},
        out_blocks={0: row_block, 1: pl.BlockSpec((halves, steps * lanes), lambda n: (0, n))},
        limit=SMALL,
    )
    send, *all_spectra = lax.optimization_barrier((send, *all_spectra))
    arrived, local_sum = lax.optimization_barrier((exchange(send), sum_over(local_sum, "dp")))
    (grad_spectra,) = call(
        functools.partial(spectra_kernel, mode_scale, owned, lanes),
        "grad_spectra",
        (arrived, by_mode, rows),
        (shape((owned * lanes, both)),),
        limit=SMALL,
    )
    near = gather_near(grad_spectra, "dp")
    carried = channels * channels * tiles // inverse
    (send,) = call(
        functools.partial(backward_kernel, samples, tiles),
        "mix_backward",
        (grad_spectra, back_rows, local_sum, flat_weight),
        (shape((inverse, owned * lanes + carried)),),
        [
            pltpu.VMEM((owned * lanes, both), BF16),
            pltpu.VMEM((owned * lanes, both), BF16),
            pltpu.VMEM((owned, 2 * samples, channels * ROWS, both), F32),
            *weight_scratch,
            *early(grad_spectra, back_rows, local_sum),
            pltpu.VMEM((inverse, owned * lanes + carried), BF16),
            pltpu.SemaphoreType.DMA((owned,)),
        ],
        grid=(owned,),
        blocks={n: in_place for n in range(4)},
        out_blocks={0: in_place},
    )
    send, near = lax.optimization_barrier((send, near))
    all_grads = gather_far(near, "dp")
    arrived = exchange(send)

    groups = lax.axis_size("dp")
    total = groups * samples
    per_mode = pl.BlockSpec((lanes, both), lambda q: (q, 0))
    (mode_grad,) = call(
        functools.partial(outer_kernel, samples, groups),
        "mode_grad",
        (*all_spectra, *all_grads),
        (shape(flat_weight.shape, F32),),
        [pltpu.VMEM((total, channels, both), F32)] * 2 + [pltpu.VMEM((total, channels, both), BF16)] * 2,
        grid=(owned,),
        blocks={n: per_mode for n in range(2 * groups)},
        out_blocks={0: weight_block},
    )
    arrived, mode_grad = lax.optimization_barrier((arrived, mode_grad))

    input_grad, local_grad = call(
        functools.partial(final_kernel, spec_scale, tiles),
        "final",
        (arrived, by_height, back_cols, backward_mix, gate_rows, by_channel),
        (shape((pixel_rows, width)), shape((channels, channels), F32)),
        [
            pltpu.VMEM((th, lanes, width), BF16),
            pltpu.VMEM((pixel_rows, width), BF16),
            pltpu.SemaphoreType.DMA((lanes // PACK,)),
        ],
        out_blocks={0: in_place},
        limit=SMALL,
    )
    return (input_grad.reshape(inputs.shape), mode_grad.reshape(mode_weight.shape), local_grad)


def solution(mesh):
    return jax.shard_map(
        local,
        mesh=mesh,
        in_specs=(
            P("dp", None, "tile", None),
            P("dp", None, "tile", None),
            P("tile", None, None, None),
            P(),
        ),
        out_specs=(P("dp", None, "tile", None), P("tile", None, None, None), P()),
        check_vma=False,
    )
```

```python
import functools
import math

import jax
import jax.numpy as jnp
import numpy as np
from jax import lax
from jax.experimental import pallas as pl
from jax.experimental.pallas import tpu as pltpu
from jax.sharding import PartitionSpec as P

F32 = jnp.float32
BF16 = jnp.bfloat16
LIMIT = 56 * 1024 * 1024
SMALL = 24 * 1024 * 1024
ROWS = 8
PACK = 16
GROUP = 8
SPLIT = 4
AHEAD = 3


def row_tables(height, modes):
    index = np.arange(modes)
    signed = np.where(index < modes // 2, index, index - modes)
    phases = np.mod(np.arange(height)[:, None] * signed[None, :], height)
    angles = phases * (2.0 * math.pi / height)
    return np.cos(angles), np.sin(angles)


def column_tables(width, modes):
    phases = np.mod(np.arange(modes)[:, None] * np.arange(width)[None, :], width)
    angles = phases * (2.0 * math.pi / width)
    return np.stack([np.cos(angles), -np.sin(angles)])


def constant(table):
    return jnp.asarray(np.asarray(table, np.float32)).astype(BF16)


def tables(tiles, owned, th, width, modes):
    cols = column_tables(width, tiles * owned)
    split = cols.reshape(2, tiles, owned, width)
    send_cols = split.transpose(1, 0, 2, 3).reshape(tiles, 2 * owned, width)
    send_cols = np.pad(send_cols, ((0, 0), (0, padded(2 * owned) - 2 * owned), (0, 0))).reshape(-1, width)
    back_cols = split.transpose(2, 1, 0, 3).reshape(-1, width)
    cosine, sine = row_tables(th * tiles, modes)
    real = np.concatenate([cosine, -sine], axis=1)
    imag = np.concatenate([sine, cosine], axis=1)
    pair = np.stack([real, imag]).reshape(2, tiles, th, 2 * modes)
    rows = pair.transpose(2, 1, 0, 3).reshape(-1, 2 * modes)
    back_rows = pair.transpose(1, 0, 2, 3).reshape(-1, 2 * modes)
    return constant(send_cols), constant(rows), constant(back_rows), constant(back_cols)


def padded(rows):
    return -(-rows // PACK) * PACK


def order(outer, inner):
    take = np.arange(outer * inner).reshape(outer, inner).T.reshape(-1)
    return constant(np.eye(outer * inner)[take])


def mode_order(tiles, owned):
    rows = np.arange(tiles * padded(2 * owned)).reshape(tiles, -1)
    take = rows[:, : 2 * owned].reshape(tiles, 2, owned).transpose(2, 0, 1).reshape(-1)
    return constant(np.eye(rows.size)[take])


def dot(left, right, dims):
    return lax.dot_general(left, right, (dims, ((), ())), preferred_element_type=F32)


def low_half(shape, half):
    return lax.broadcasted_iota(jnp.int32, shape, 1) < half


def gelu_slope(values):
    size = jnp.abs(values)
    expo = jnp.exp(-0.5 * values * values)
    t = 1.0 / (1.0 + (0.3275911 / math.sqrt(2.0)) * size)
    poly = 0.5 * 1.061405429
    for factor in (-1.453152027, 1.421413741, -0.284496736, 0.254829592):
        poly = poly * t + 0.5 * factor
    tail = poly * t * expo
    cumulative = jnp.where(values < 0.0, tail, 1.0 - tail)
    return cumulative + values * expo * (1.0 / math.sqrt(2.0 * math.pi))


def shuffle(order_ref, value):
    return dot(order_ref[...], value, ((1,), (0,))).astype(BF16)


def by_rows(order_ref, field_refs, rows_ref):
    heights, lanes, _ = rows_ref.shape
    block = PACK * heights
    quarter = lanes // len(field_refs)
    for first in range(0, lanes, PACK):
        start = first % quarter * heights
        moved = shuffle(order_ref, field_refs[first // quarter][start : start + block, :])
        for h in range(heights):
            rows_ref[h, first : first + PACK, :] = moved[h * PACK : (h + 1) * PACK]


def columns_kernel(order_ref, table_ref, *rest):
    field_refs, (rows_ref, send_ref) = rest[:SPLIT], rest[SPLIT:]
    heights, lanes, _ = rows_ref.shape
    by_rows(order_ref, field_refs, rows_ref)
    for h in range(heights):
        send_ref[:, h * lanes : (h + 1) * lanes] = dot(table_ref[...], rows_ref[h], ((1,), (1,))).astype(BF16)


def relayout_kernel(order_ref, *rest):
    by_rows(order_ref, rest[:SPLIT], rest[SPLIT])


def shuffle_groups(order_ref, recv_ref, width):
    size = order_ref.shape[0]
    return [shuffle(order_ref, recv_ref[n : n + size, :width]) for n in range(0, recv_ref.shape[0], size)]


def stack(groups, index, count, lanes):
    return jnp.concatenate(
        [
            group[index * count : (index + 1) * count, n : n + lanes]
            for n in range(0, groups[0].shape[1], lanes)
            for group in groups
        ],
        axis=0,
    )


def spectra_into(scale, owned, lanes, recv_ref, order_ref, rows_ref, spec_ref):
    count = order_ref.shape[0] // owned
    fields = rows_ref.shape[0] // count * lanes
    ordered = [shuffle(order_ref, recv_ref[:, :fields])]
    for q in range(owned):
        stacked = stack(ordered, q, count, lanes)
        spec_ref[q * lanes : (q + 1) * lanes, :] = (
            scale * dot(stacked, rows_ref[...], ((0,), (0,)))
        ).astype(BF16)


def to_piece(value, rows):
    return jnp.concatenate([value[n : n + rows] for n in range(0, value.shape[0], rows)], axis=1)


def from_piece(value, extent):
    return jnp.concatenate([value[:, n : n + extent] for n in range(0, value.shape[1], extent)], axis=0)


def spectra_kernel(scale, owned, lanes, recv_ref, order_ref, rows_ref, spec_ref):
    spectra_into(scale, owned, lanes, recv_ref, order_ref, rows_ref, spec_ref)


def running(pairs):
    waiting = []
    for left, right in pairs:
        value, level = left * right, 0
        while waiting and waiting[-1][1] == level:
            value, level = waiting.pop()[0] + value, level + 1
        waiting.append((value, level))
    return sum((value for value, _ in reversed(waiting[:-1])), waiting[-1][0])


def rows_of(store, block, extent):
    return store.at[pl.ds(pl.multiple_of(block * extent, extent), extent), :]


def packed_row(view, index):
    row = view[index : index + 1, :]
    return jnp.broadcast_to(row, (PACK, row.shape[1])).astype(BF16)


def duplicates(spec, half):
    value = spec.astype(F32)
    other = pltpu.roll(value, half, 1)
    low = low_half(value.shape, half)
    return jnp.where(low, value, other), jnp.where(low, other, value)


def finish(back_ref, sums, send_ref, stage, sems, mix):
    @pl.when(pl.program_id(0) == pl.num_programs(0) - 1)
    def _():
        moves = []
        for q in range(sums.shape[0]):
            mixed = mix(sums.at[q]).astype(BF16)
            column = pl.ds(q * mixed.shape[0], mixed.shape[0])
            stage[:, column] = dot(back_ref[...], mixed, ((1,), (1,))).astype(BF16)
            moves.append(pltpu.make_async_copy(stage.at[:, column], send_ref.at[:, column], sems.at[q]))
            moves[-1].start()
        for move in moves:
            move.wait()


def fetch(sources, targets, sems):
    moves = [
        pltpu.make_async_copy(source, target, sems.at[n]) for n, (source, target) in enumerate(zip(sources, targets))
    ]

    @pl.when(pl.program_id(0) == 0)
    def _():
        for move in moves:
            move.start()

    return moves


def fetch_weights(moves, source_ref, weights, sems):
    q = pl.program_id(0)
    owned = sems.shape[0]
    size = weights.shape[0] // owned

    def move(mode):
        part = pl.ds(pl.multiple_of(mode * size, size), size)
        return pltpu.make_async_copy(source_ref.at[part, :], weights.at[part, :], sems.at[mode])

    @pl.when(q == 0)
    def _():
        move(0).start()
        for early in moves:
            early.wait()
        for mode in range(1, min(AHEAD, owned)):
            move(mode).start()

    @pl.when(q + AHEAD < owned)
    def _():
        move(q + AHEAD).start()

    return move(q), weights.at[pl.ds(pl.multiple_of(q * size, size), size), :]


def forward_kernel(scale, samples, owned, *rest):
    sources, source_ref, spec_ref, send_ref, real, imag, sums, weights, sems = rest[:4], *rest[4:12]
    targets, early, stage, late = rest[12:16], *rest[16:19]
    recv_ref, order_ref, rows_ref, back_ref = targets
    _, _, outs, both = sums.shape
    channels = weights.shape[0] // outs // owned
    half = both // 2
    lanes = samples * channels
    q = pl.program_id(0)
    moves = fetch(sources, targets, early)
    coming, weight_ref = fetch_weights(moves, source_ref, weights, sems)

    @pl.when(q == 0)
    def _():
        spectra_into(scale, owned, lanes, recv_ref, order_ref, rows_ref, spec_ref)
        real[...], imag[...] = duplicates(spec_ref[...], half)
        sums[...] = jnp.zeros_like(sums)

    coming.wait()

    def body(block, carry):
        view = rows_of(weight_ref, block, GROUP * outs)
        into = sums.at[q]
        for s in range(samples):
            rows = []
            for store in (real, imag):
                part = rows_of(store, (q * lanes + s * channels) // GROUP + block, GROUP)
                rows.append([packed_row(part, step) for step in range(GROUP)])
            for o in range(0, outs, PACK):
                column = [view[step * outs + o : step * outs + o + PACK, :] for step in range(GROUP)]
                for n, row in enumerate(rows):
                    into[2 * s + n, o : o + PACK, :] += running([(w, r) for w, r in zip(column, row)]).astype(F32)
        return carry

    lax.fori_loop(0, channels // GROUP, body, 0)

    def mix(parts):
        low = low_half((outs, both), half)
        result = []
        for s in range(samples):
            crossed = pltpu.roll(parts[2 * s + 1], half, 1)
            result.append(parts[2 * s] + jnp.where(low, -crossed, crossed))
        return jnp.concatenate(result, axis=0)

    finish(back_ref, sums, send_ref, stage, late, mix)


def backward_kernel(samples, tiles, *rest):
    sources, source_ref, send_ref, real, imag, sums, weights, sems = rest[:3], *rest[3:10]
    targets, early, stage, late = rest[10:13], *rest[13:16]
    spec_ref, back_ref, local_ref = targets

    def carried():
        column = pl.ds(sums.shape[0] * lanes, stage.shape[1] - sums.shape[0] * lanes)
        return pltpu.make_async_copy(stage.at[:, column], send_ref.at[:, column], late.at[0])

    channels, both = sums.shape[2] // ROWS, sums.shape[3]
    outs = weights.shape[0] // channels // sums.shape[0]
    half = both // 2
    lanes = samples * outs
    q = pl.program_id(0)
    moves = fetch(sources, targets, early)
    coming, weight_ref = fetch_weights(moves, source_ref, weights, sems)

    @pl.when(q == 0)
    def _():
        first, second = duplicates(spec_ref[...], half)
        real[...], imag[...] = first.astype(BF16), second.astype(BF16)
        extent = stage.shape[0] // tiles
        partial = to_piece(local_ref[...].astype(BF16), extent)
        for n in range(0, stage.shape[0], extent):
            stage[n : n + extent, sums.shape[0] * lanes :] = partial
        move = carried()
        move.start()
        move.wait()

    coming.wait()
    grads = [
        [store[pl.ds(pl.multiple_of(q * lanes + s * outs + o, PACK), PACK), :] for o in range(0, outs, PACK)]
        for s in range(samples)
        for store in (real, imag)
    ]

    def body(block, carry):
        view = rows_of(weight_ref, block, GROUP * outs)
        into = [rows_of(sums.at[q, n], block, GROUP * ROWS) for n in range(len(grads))]
        for first in range(0, GROUP, 4):
            totals = []
            for step in range(first, first + 4):
                column = [view[step * outs + o : step * outs + o + PACK, :] for o in range(0, outs, PACK)]
                for n, grad in enumerate(grads):
                    total = running([(w, g) for w, g in zip(column, grad)]).astype(F32)
                    totals.append((n, step, total[:ROWS] + total[ROWS:]))
            for n, step, total in totals:
                into[n][step * ROWS : (step + 1) * ROWS, :] = total
        return carry

    lax.fori_loop(0, channels // GROUP, body, 0)

    def mix(parts):
        low = low_half((channels, both), half)
        result = []
        for s in range(samples):
            straight, crossed = (
                sum(parts[n, pl.ds(row, channels, stride=ROWS), :] for row in range(ROWS)) for n in (2 * s, 2 * s + 1)
            )
            result.append(jnp.where(low, straight, -straight) + pltpu.roll(crossed, half, 1))
        return jnp.concatenate(result, axis=0)

    finish(back_ref, sums, send_ref, stage, late, mix)


def pixels_kernel(scale, heights, recv_ref, order_ref, back_ref, local_ref, field_ref, cot_ref, table_ref, *rest):
    grad_ref, send_ref, sum_ref, ordered, total = rest
    steps, lanes, _ = field_ref.shape
    count = order_ref.shape[0] // heights
    size = order_ref.shape[0]
    group = pl.program_id(0)

    @pl.when(group == 0)
    def _():
        for n in range(0, recv_ref.shape[0], size):
            ordered[n : n + size, :] = shuffle(order_ref, recv_ref[n : n + size, :])
        total[...] = jnp.zeros_like(total)

    local = jnp.zeros(total.shape, F32)
    for step in range(steps):
        parts = []
        for n in range(0, recv_ref.shape[0], size):
            first = pl.multiple_of(n + (group * steps + step) * count, count)
            parts.append(ordered[pl.ds(first, count), :])
        inner = stack(parts, 0, count, lanes)
        pre = scale * dot(inner, back_ref[...], ((0,), (0,)))
        pre = pre + dot(local_ref[...], field_ref[step], ((1,), (0,)))
        grad = (cot_ref[step].astype(F32) * gelu_slope(pre)).astype(BF16)
        grad_ref[step] = grad
        send_ref[:, step * lanes : (step + 1) * lanes] = dot(table_ref[...], grad, ((1,), (1,))).astype(BF16)
        local = local + dot(field_ref[step], grad, ((1,), (1,)))
    total[...] += local

    @pl.when(group == pl.num_programs(0) - 1)
    def _():
        extent = sum_ref.shape[0]
        sum_ref[...] = sum(total[n : n + extent, n : n + extent] for n in range(0, lanes, extent))


def final_kernel(scale, tiles, recv_ref, order_ref, back_ref, local_ref, grad_ref, restore_ref, *rest):
    out_ref, sum_ref, result = rest
    heights, lanes, _ = grad_ref.shape
    extent = recv_ref.shape[0] // tiles
    first = back_ref.shape[0] // (2 * tiles) * lanes
    partials = sum(recv_ref[n : n + extent, first:].astype(F32) for n in range(0, recv_ref.shape[0], extent))
    sum_ref[...] = from_piece(partials, sum_ref.shape[1])
    count = order_ref.shape[0] // heights
    ordered = shuffle_groups(order_ref, recv_ref, first)
    for h in range(heights):
        inner = stack(ordered, h, count, lanes)
        value = scale * dot(inner, back_ref[...], ((0,), (0,)))
        result[h] = (value + dot(local_ref[...], grad_ref[h], ((1,), (0,)))).astype(BF16)
    block = PACK * heights
    for first in range(0, lanes, PACK):
        part = jnp.concatenate([result[h, first : first + PACK, :] for h in range(heights)], axis=0)
        out_ref[first * heights : first * heights + block, :] = shuffle(restore_ref, part)


def outer_kernel(samples, groups, *refs):
    specs, grads = refs[:groups], refs[groups : 2 * groups]
    out_ref, real, imag, crossed = refs[2 * groups :]
    total, channels, both = real.shape
    outs = crossed.shape[1]
    half = both // 2
    low = low_half((channels, both), half)

    for g in range(groups):
        for s in range(samples):
            n = g * samples + s
            spec = specs[g][s * channels : (s + 1) * channels, :].astype(F32)
            other = pltpu.roll(spec, half, 1)
            real[n] = jnp.where(low, spec, other)
            imag[n] = jnp.where(low, other, -spec)
            grad = grads[g][s * outs : (s + 1) * outs, :]
            crossed[n] = pltpu.roll(grad.astype(F32), half, 1).astype(BF16)

    def body(block, carry):
        into = rows_of(out_ref, block, GROUP * outs)
        views = [rows_of(store.at[n], block, GROUP) for n in range(total) for store in (real, imag)]
        for first in range(0, GROUP, 2):
            pair = range(first, first + 2)
            lefts = [[packed_row(view, c) for view in views] for c in pair]
            for o in range(0, outs, PACK):
                right = []
                for n in range(total):
                    at = n % samples * outs + o
                    right += [grads[n // samples][at : at + PACK, :], crossed[n, o : o + PACK, :]]
                results = [running(list(zip(left, right))) for left in lefts]
                for c, result in zip(pair, results):
                    into[c * outs + o : c * outs + o + PACK, :] = result.astype(F32)
        return carry

    lax.fori_loop(0, channels // GROUP, body, 0)


def whole(extent):
    return pl.BlockSpec(extent, lambda *_: (0,) * len(extent))


def call(kernel, name, operands, outs, scratch=(), grid=(1,), blocks=None, out_blocks=None, limit=LIMIT):
    blocks, out_blocks = blocks or {}, out_blocks or {}
    in_specs = [blocks.get(n) or whole(operand.shape) for n, operand in enumerate(operands)]
    out_specs = [out_blocks.get(n, whole(out.shape)) for n, out in enumerate(outs)]
    return pl.pallas_call(
        kernel,
        out_shape=tuple(outs),
        grid=grid,
        in_specs=in_specs,
        out_specs=tuple(out_specs),
        scratch_shapes=list(scratch),
        compiler_params=pltpu.CompilerParams(vmem_limit_bytes=limit),
        name=name,
    )(*operands)


def swap(values, axis, step):
    return lax.ppermute(values, axis, [(i, i ^ step) for i in range(lax.axis_size(axis))])


def gather_near(values, axis):
    size = lax.axis_size(axis)
    return {0: values} | {1 << bit: swap(values, axis, 1 << bit) for bit in range(size.bit_length() - 1)}


def gather_far(near, axis):
    whole_set = dict(near)
    for step in range(1, lax.axis_size(axis)):
        if step not in whole_set:
            whole_set[step] = swap(whole_set[step & (step - 1)], axis, step & -step)
    return [whole_set[step] for step in sorted(whole_set)]


def sum_over(values, axis):
    step = 1
    while step < lax.axis_size(axis):
        values = values + swap(values, axis, step)
        step *= 2
    return values


def block_diagonal(matrix, copies):
    zero = jnp.zeros_like(matrix)
    return jnp.concatenate(
        [
            jnp.concatenate([matrix if i == j else zero for j in range(copies)], axis=1)
            for i in range(copies)
        ],
        axis=0,
    )


def shape(extent, kind=BF16):
    return jax.ShapeDtypeStruct(extent, kind)


def local(inputs, cotangent, mode_weight, local_weight):
    tiles = lax.axis_size("tile")
    samples, channels, th, width = inputs.shape
    owned, _, _, both = mode_weight.shape
    modes = both // 2
    lanes = samples * channels
    parts = width // 128
    spec_scale = 1.0 / math.sqrt(tiles * th * width)
    mode_scale = 1.0 / math.sqrt(modes * tiles * owned)
    send_cols, rows, back_rows, back_cols = tables(tiles, owned, th, width, modes)
    pixel_rows = samples * channels * th
    halves = tiles * padded(2 * owned)
    inverse = 2 * tiles * th

    def exchange(values):
        split = values.reshape(tiles, values.shape[0] // tiles, values.shape[1])
        moved = lax.all_to_all(split, "tile", split_axis=0, concat_axis=0, tiled=False)
        return moved.reshape(values.shape)

    forward_mix = block_diagonal(local_weight.T, samples)
    backward_mix = block_diagonal(local_weight, samples)
    by_row = order(PACK, th)
    by_channel = order(th, PACK)
    by_mode = mode_order(tiles, owned)
    by_height = order(2 * min(tiles, 8), th)
    flat_weight = mode_weight.reshape(-1, both)
    weight_block = pl.BlockSpec((flat_weight.shape[0] // owned, both), lambda q: (q, 0))
    weight_scratch = [pltpu.VMEM(flat_weight.shape, BF16), pltpu.SemaphoreType.DMA((owned,))]
    in_place = pl.BlockSpec(memory_space=pl.ANY)
    to_modes = shape((halves, th * lanes))
    to_pixels = shape((inverse, owned * lanes))
    field_shape = shape((th, lanes, width))

    def kept(*operands):
        return [pltpu.VMEM(operand.shape, operand.dtype) for operand in operands]

    def early(*operands):
        return kept(*operands) + [pltpu.SemaphoreType.DMA((len(operands),))]

    def field_blocks(first):
        return {first + n: pl.BlockSpec((pixel_rows // SPLIT, width), lambda _, n=n: (n, 0)) for n in range(SPLIT)}

    field_rows, send = call(
        columns_kernel,
        "columns",
        (by_row, send_cols, *[inputs.reshape(pixel_rows, width)] * SPLIT),
        (field_shape, to_modes),
        blocks=field_blocks(2),
    )
    arrived = exchange(send)
    (cot_rows,) = call(
        relayout_kernel,
        "relayout",
        (by_row, *[cotangent.reshape(pixel_rows, width)] * SPLIT),
        (field_shape,),
        blocks=field_blocks(1),
    )
    spectra, send = call(
        functools.partial(forward_kernel, spec_scale, samples, owned),
        "mix_forward",
        (arrived, by_mode, rows, back_rows, flat_weight),
        (shape((owned * lanes, both)), to_pixels),
        [
            pltpu.VMEM((owned * lanes, both), F32),
            pltpu.VMEM((owned * lanes, both), F32),
            pltpu.VMEM((owned, 2 * samples, channels, both), F32),
            *weight_scratch,
            *early(arrived, by_mode, rows, back_rows),
            pltpu.VMEM((inverse, owned * lanes), BF16),
            pltpu.SemaphoreType.DMA((owned,)),
        ],
        grid=(owned,),
        blocks={n: in_place for n in range(5)},
        out_blocks={1: in_place},
    )
    all_spectra = gather_far(gather_near(spectra, "dp"), "dp")
    arrived = exchange(send)
    steps = 4
    row_block = pl.BlockSpec((steps, lanes, width), lambda n: (n, 0, 0))
    gate_rows, send, local_sum = call(
        functools.partial(pixels_kernel, mode_scale, th),
        "pixels",
        (arrived, by_height, back_cols, forward_mix, field_rows, cot_rows, send_cols),
        (field_shape, to_modes, shape((channels, channels), F32)),
        [pltpu.VMEM((inverse, owned * lanes), BF16), pltpu.VMEM((lanes, lanes), F32)],
        grid=(th // steps,),
        blocks={4: row_block, 5: row_block},
        out_blocks={0: row_block, 1: pl.BlockSpec((halves, steps * lanes), lambda n: (0, n))},
        limit=SMALL,
    )
    send, *all_spectra = lax.optimization_barrier((send, *all_spectra))
    arrived, local_sum = lax.optimization_barrier((exchange(send), sum_over(local_sum, "dp")))
    (grad_spectra,) = call(
        functools.partial(spectra_kernel, mode_scale, owned, lanes),
        "grad_spectra",
        (arrived, by_mode, rows),
        (shape((owned * lanes, both)),),
        limit=SMALL,
    )
    near = gather_near(grad_spectra, "dp")
    carried = channels * channels * tiles // inverse
    (send,) = call(
        functools.partial(backward_kernel, samples, tiles),
        "mix_backward",
        (grad_spectra, back_rows, local_sum, flat_weight),
        (shape((inverse, owned * lanes + carried)),),
        [
            pltpu.VMEM((owned * lanes, both), BF16),
            pltpu.VMEM((owned * lanes, both), BF16),
            pltpu.VMEM((owned, 2 * samples, channels * ROWS, both), F32),
            *weight_scratch,
            *early(grad_spectra, back_rows, local_sum),
            pltpu.VMEM((inverse, owned * lanes + carried), BF16),
            pltpu.SemaphoreType.DMA((owned,)),
        ],
        grid=(owned,),
        blocks={n: in_place for n in range(4)},
        out_blocks={0: in_place},
    )
    send, near = lax.optimization_barrier((send, near))
    all_grads = gather_far(near, "dp")
    arrived = exchange(send)

    groups = lax.axis_size("dp")
    total = groups * samples
    per_mode = pl.BlockSpec((lanes, both), lambda q: (q, 0))
    (mode_grad,) = call(
        functools.partial(outer_kernel, samples, groups),
        "mode_grad",
        (*all_spectra, *all_grads),
        (shape(flat_weight.shape, F32),),
        [pltpu.VMEM((total, channels, both), F32)] * 2 + [pltpu.VMEM((total, channels, both), BF16)],
        grid=(owned,),
        blocks={n: per_mode for n in range(2 * groups)},
        out_blocks={0: weight_block},
    )
    arrived, mode_grad = lax.optimization_barrier((arrived, mode_grad))

    input_grad, local_grad = call(
        functools.partial(final_kernel, spec_scale, tiles),
        "final",
        (arrived, by_height, back_cols, backward_mix, gate_rows, by_channel),
        (shape((pixel_rows, width)), shape((channels, channels), F32)),
        [pltpu.VMEM((th, lanes, width), BF16)],
        limit=SMALL,
    )
    return (input_grad.reshape(inputs.shape), mode_grad.reshape(mode_weight.shape), local_grad)


def solution(mesh):
    return jax.shard_map(
        local,
        mesh=mesh,
        in_specs=(
            P("dp", None, "tile", None),
            P("dp", None, "tile", None),
            P("tile", None, None, None),
            P(),
        ),
        out_specs=(P("dp", None, "tile", None), P("tile", None, None, None), P()),
        check_vma=False,
    )
```

```python
import functools
import math

import jax
import jax.numpy as jnp
import numpy as np
from jax import lax
from jax.experimental import pallas as pl
from jax.experimental.pallas import tpu as pltpu
from jax.sharding import PartitionSpec as P

F32 = jnp.float32
BF16 = jnp.bfloat16
LIMIT = 56 * 1024 * 1024
SMALL = 24 * 1024 * 1024
ROWS = 8
PACK = 16
GROUP = 8
SPLIT = 4
AHEAD = 3


def row_tables(height, modes):
    index = np.arange(modes)
    signed = np.where(index < modes // 2, index, index - modes)
    phases = np.mod(np.arange(height)[:, None] * signed[None, :], height)
    angles = phases * (2.0 * math.pi / height)
    return np.cos(angles), np.sin(angles)


def column_tables(width, modes):
    phases = np.mod(np.arange(modes)[:, None] * np.arange(width)[None, :], width)
    angles = phases * (2.0 * math.pi / width)
    return np.stack([np.cos(angles), -np.sin(angles)])


def constant(table):
    return jnp.asarray(np.asarray(table, np.float32)).astype(BF16)


def tables(tiles, owned, th, width, modes):
    cols = column_tables(width, tiles * owned)
    split = cols.reshape(2, tiles, owned, width)
    send_cols = split.transpose(1, 0, 2, 3).reshape(tiles, 2 * owned, width)
    send_cols = np.pad(send_cols, ((0, 0), (0, padded(2 * owned) - 2 * owned), (0, 0))).reshape(-1, width)
    back_cols = split.transpose(2, 1, 0, 3).reshape(-1, width)
    cosine, sine = row_tables(th * tiles, modes)
    real = np.concatenate([cosine, -sine], axis=1)
    imag = np.concatenate([sine, cosine], axis=1)
    pair = np.stack([real, imag]).reshape(2, tiles, th, 2 * modes)
    rows = pair.transpose(2, 1, 0, 3).reshape(-1, 2 * modes)
    back_rows = pair.transpose(1, 0, 2, 3).reshape(-1, 2 * modes)
    return constant(send_cols), constant(rows), constant(back_rows), constant(back_cols)


def padded(rows):
    return -(-rows // PACK) * PACK


def order(outer, inner):
    take = np.arange(outer * inner).reshape(outer, inner).T.reshape(-1)
    return constant(np.eye(outer * inner)[take])


def mode_order(tiles, owned):
    rows = np.arange(tiles * padded(2 * owned)).reshape(tiles, -1)
    take = rows[:, : 2 * owned].reshape(tiles, 2, owned).transpose(2, 0, 1).reshape(-1)
    return constant(np.eye(rows.size)[take])


def dot(left, right, dims):
    return lax.dot_general(left, right, (dims, ((), ())), preferred_element_type=F32)


def low_half(shape, half):
    return lax.broadcasted_iota(jnp.int32, shape, 1) < half


def gelu_slope(values):
    size = jnp.abs(values)
    expo = jnp.exp(-0.5 * values * values)
    t = 1.0 / (1.0 + (0.3275911 / math.sqrt(2.0)) * size)
    poly = 0.5 * 1.061405429
    for factor in (-1.453152027, 1.421413741, -0.284496736, 0.254829592):
        poly = poly * t + 0.5 * factor
    tail = poly * t * expo
    cumulative = jnp.where(values < 0.0, tail, 1.0 - tail)
    return cumulative + values * expo * (1.0 / math.sqrt(2.0 * math.pi))


def shuffle(order_ref, value):
    return dot(order_ref[...], value, ((1,), (0,))).astype(BF16)


def by_rows(order_ref, field_refs, rows_ref):
    heights, lanes, _ = rows_ref.shape
    block = PACK * heights
    quarter = lanes // len(field_refs)
    for first in range(0, lanes, PACK):
        start = first % quarter * heights
        moved = shuffle(order_ref, field_refs[first // quarter][start : start + block, :])
        for h in range(heights):
            rows_ref[h, first : first + PACK, :] = moved[h * PACK : (h + 1) * PACK]


def columns_kernel(order_ref, table_ref, *rest):
    field_refs, (rows_ref, send_ref) = rest[:SPLIT], rest[SPLIT:]
    heights, lanes, _ = rows_ref.shape
    by_rows(order_ref, field_refs, rows_ref)
    for h in range(heights):
        send_ref[:, h * lanes : (h + 1) * lanes] = dot(table_ref[...], rows_ref[h], ((1,), (1,))).astype(BF16)


def relayout_kernel(order_ref, *rest):
    by_rows(order_ref, rest[:SPLIT], rest[SPLIT])


def shuffle_groups(order_ref, recv_ref, width):
    size = order_ref.shape[0]
    return [shuffle(order_ref, recv_ref[n : n + size, :width]) for n in range(0, recv_ref.shape[0], size)]


def stack(groups, index, count, lanes):
    return jnp.concatenate(
        [
            group[index * count : (index + 1) * count, n : n + lanes]
            for n in range(0, groups[0].shape[1], lanes)
            for group in groups
        ],
        axis=0,
    )


def spectra_into(scale, owned, lanes, recv_ref, order_ref, rows_ref, spec_ref):
    count = order_ref.shape[0] // owned
    fields = rows_ref.shape[0] // count * lanes
    ordered = [shuffle(order_ref, recv_ref[:, :fields])]
    for q in range(owned):
        stacked = stack(ordered, q, count, lanes)
        spec_ref[q * lanes : (q + 1) * lanes, :] = (
            scale * dot(stacked, rows_ref[...], ((0,), (0,)))
        ).astype(BF16)


def to_piece(value, rows):
    return jnp.concatenate([value[n : n + rows] for n in range(0, value.shape[0], rows)], axis=1)


def from_piece(value, extent):
    return jnp.concatenate([value[:, n : n + extent] for n in range(0, value.shape[1], extent)], axis=0)


def spectra_kernel(scale, owned, lanes, recv_ref, order_ref, rows_ref, spec_ref):
    spectra_into(scale, owned, lanes, recv_ref, order_ref, rows_ref, spec_ref)


def running(pairs):
    waiting = []
    for left, right in pairs:
        value, level = left * right, 0
        while waiting and waiting[-1][1] == level:
            value, level = waiting.pop()[0] + value, level + 1
        waiting.append((value, level))
    return sum((value for value, _ in reversed(waiting[:-1])), waiting[-1][0])


def rows_of(store, block, extent):
    return store.at[pl.ds(pl.multiple_of(block * extent, extent), extent), :]


def packed_row(view, index):
    row = view[index : index + 1, :]
    return jnp.broadcast_to(row, (PACK, row.shape[1])).astype(BF16)


def duplicates(spec, half):
    value = spec.astype(F32)
    other = pltpu.roll(value, half, 1)
    low = low_half(value.shape, half)
    return jnp.where(low, value, other), jnp.where(low, other, value)


def finish(back_ref, sums, send_ref, stage, sems, mix):
    @pl.when(pl.program_id(0) == pl.num_programs(0) - 1)
    def _():
        moves = []
        for q in range(sums.shape[0]):
            mixed = mix(sums.at[q]).astype(BF16)
            column = pl.ds(q * mixed.shape[0], mixed.shape[0])
            stage[:, column] = dot(back_ref[...], mixed, ((1,), (1,))).astype(BF16)
            moves.append(pltpu.make_async_copy(stage.at[:, column], send_ref.at[:, column], sems.at[q]))
            moves[-1].start()
        for move in moves:
            move.wait()


def fetch(sources, targets, sems):
    moves = [
        pltpu.make_async_copy(source, target, sems.at[n]) for n, (source, target) in enumerate(zip(sources, targets))
    ]

    @pl.when(pl.program_id(0) == 0)
    def _():
        for move in moves:
            move.start()

    return moves


def fetch_weights(moves, source_ref, weights, sems):
    q = pl.program_id(0)
    owned = sems.shape[0]
    size = weights.shape[0] // owned

    def move(mode):
        part = pl.ds(pl.multiple_of(mode * size, size), size)
        return pltpu.make_async_copy(source_ref.at[part, :], weights.at[part, :], sems.at[mode])

    @pl.when(q == 0)
    def _():
        move(0).start()
        for early in moves:
            early.wait()
        for mode in range(1, min(AHEAD, owned)):
            move(mode).start()

    @pl.when(q + AHEAD < owned)
    def _():
        move(q + AHEAD).start()

    return move(q), weights.at[pl.ds(pl.multiple_of(q * size, size), size), :]


def forward_kernel(scale, samples, owned, *rest):
    sources, source_ref, spec_ref, send_ref, real, imag, sums, weights, sems = rest[:4], *rest[4:12]
    targets, early, stage, late = rest[12:16], *rest[16:19]
    recv_ref, order_ref, rows_ref, back_ref = targets
    _, _, outs, both = sums.shape
    channels = weights.shape[0] // outs // owned
    half = both // 2
    lanes = samples * channels
    q = pl.program_id(0)
    moves = fetch(sources, targets, early)
    coming, weight_ref = fetch_weights(moves, source_ref, weights, sems)

    @pl.when(q == 0)
    def _():
        spectra_into(scale, owned, lanes, recv_ref, order_ref, rows_ref, spec_ref)
        real[...], imag[...] = duplicates(spec_ref[...], half)
        sums[...] = jnp.zeros_like(sums)

    coming.wait()

    def body(block, carry):
        view = rows_of(weight_ref, block, GROUP * outs)
        into = sums.at[q]
        for s in range(samples):
            rows = []
            for store in (real, imag):
                part = rows_of(store, (q * lanes + s * channels) // GROUP + block, GROUP)
                rows.append([packed_row(part, step) for step in range(GROUP)])
            for o in range(0, outs, PACK):
                column = [view[step * outs + o : step * outs + o + PACK, :] for step in range(GROUP)]
                for n, row in enumerate(rows):
                    into[2 * s + n, o : o + PACK, :] += running([(w, r) for w, r in zip(column, row)]).astype(F32)
        return carry

    lax.fori_loop(0, channels // GROUP, body, 0)

    def mix(parts):
        low = low_half((outs, both), half)
        result = []
        for s in range(samples):
            crossed = pltpu.roll(parts[2 * s + 1], half, 1)
            result.append(parts[2 * s] + jnp.where(low, -crossed, crossed))
        return jnp.concatenate(result, axis=0)

    finish(back_ref, sums, send_ref, stage, late, mix)


def backward_kernel(samples, tiles, *rest):
    sources, source_ref, send_ref, real, imag, sums, weights, sems = rest[:3], *rest[3:10]
    targets, early, stage, late = rest[10:13], *rest[13:16]
    spec_ref, back_ref, local_ref = targets

    def carried():
        column = pl.ds(sums.shape[0] * lanes, stage.shape[1] - sums.shape[0] * lanes)
        return pltpu.make_async_copy(stage.at[:, column], send_ref.at[:, column], late.at[0])

    channels, both = sums.shape[2] // ROWS, sums.shape[3]
    outs = weights.shape[0] // channels // sums.shape[0]
    half = both // 2
    lanes = samples * outs
    q = pl.program_id(0)
    moves = fetch(sources, targets, early)
    coming, weight_ref = fetch_weights(moves, source_ref, weights, sems)

    @pl.when(q == 0)
    def _():
        first, second = duplicates(spec_ref[...], half)
        real[...], imag[...] = first.astype(BF16), second.astype(BF16)
        extent = stage.shape[0] // tiles
        partial = to_piece(local_ref[...].astype(BF16), extent)
        for n in range(0, stage.shape[0], extent):
            stage[n : n + extent, sums.shape[0] * lanes :] = partial
        move = carried()
        move.start()
        move.wait()

    coming.wait()
    grads = [
        [store[pl.ds(pl.multiple_of(q * lanes + s * outs + o, PACK), PACK), :] for o in range(0, outs, PACK)]
        for s in range(samples)
        for store in (real, imag)
    ]

    def body(block, carry):
        view = rows_of(weight_ref, block, GROUP * outs)
        into = [rows_of(sums.at[q, n], block, GROUP * ROWS) for n in range(len(grads))]
        for first in range(0, GROUP, 4):
            totals = []
            for step in range(first, first + 4):
                column = [view[step * outs + o : step * outs + o + PACK, :] for o in range(0, outs, PACK)]
                for n, grad in enumerate(grads):
                    total = running([(w, g) for w, g in zip(column, grad)]).astype(F32)
                    totals.append((n, step, total[:ROWS] + total[ROWS:]))
            for n, step, total in totals:
                into[n][step * ROWS : (step + 1) * ROWS, :] = total
        return carry

    lax.fori_loop(0, channels // GROUP, body, 0)

    def mix(parts):
        low = low_half((channels, both), half)
        result = []
        for s in range(samples):
            straight, crossed = (
                sum(parts[n, pl.ds(row, channels, stride=ROWS), :] for row in range(ROWS)) for n in (2 * s, 2 * s + 1)
            )
            result.append(jnp.where(low, straight, -straight) + pltpu.roll(crossed, half, 1))
        return jnp.concatenate(result, axis=0)

    finish(back_ref, sums, send_ref, stage, late, mix)


def pixels_kernel(scale, heights, recv_ref, order_ref, back_ref, local_ref, field_ref, cot_ref, table_ref, *rest):
    grad_ref, send_ref, sum_ref, ordered, total = rest
    steps, lanes, _ = field_ref.shape
    count = order_ref.shape[0] // heights
    size = order_ref.shape[0]
    group = pl.program_id(0)

    @pl.when(group == 0)
    def _():
        for n in range(0, recv_ref.shape[0], size):
            ordered[n : n + size, :] = shuffle(order_ref, recv_ref[n : n + size, :])
        total[...] = jnp.zeros_like(total)

    local = jnp.zeros(total.shape, F32)
    for step in range(steps):
        parts = []
        for n in range(0, recv_ref.shape[0], size):
            first = pl.multiple_of(n + (group * steps + step) * count, count)
            parts.append(ordered[pl.ds(first, count), :])
        inner = stack(parts, 0, count, lanes)
        pre = scale * dot(inner, back_ref[...], ((0,), (0,)))
        pre = pre + dot(local_ref[...], field_ref[step], ((1,), (0,)))
        grad = (cot_ref[step].astype(F32) * gelu_slope(pre)).astype(BF16)
        grad_ref[step] = grad
        send_ref[:, step * lanes : (step + 1) * lanes] = dot(table_ref[...], grad, ((1,), (1,))).astype(BF16)
        local = local + dot(field_ref[step], grad, ((1,), (1,)))
    total[...] += local

    @pl.when(group == pl.num_programs(0) - 1)
    def _():
        extent = sum_ref.shape[0]
        sum_ref[...] = sum(total[n : n + extent, n : n + extent] for n in range(0, lanes, extent))


def final_kernel(scale, tiles, recv_ref, order_ref, back_ref, local_ref, grad_ref, restore_ref, *rest):
    out_ref, sum_ref, result = rest
    heights, lanes, _ = grad_ref.shape
    extent = recv_ref.shape[0] // tiles
    first = back_ref.shape[0] // (2 * tiles) * lanes
    partials = sum(recv_ref[n : n + extent, first:].astype(F32) for n in range(0, recv_ref.shape[0], extent))
    sum_ref[...] = from_piece(partials, sum_ref.shape[1])
    count = order_ref.shape[0] // heights
    ordered = shuffle_groups(order_ref, recv_ref, first)
    for h in range(heights):
        inner = stack(ordered, h, count, lanes)
        value = scale * dot(inner, back_ref[...], ((0,), (0,)))
        result[h] = (value + dot(local_ref[...], grad_ref[h], ((1,), (0,)))).astype(BF16)
    block = PACK * heights
    for first in range(0, lanes, PACK):
        part = jnp.concatenate([result[h, first : first + PACK, :] for h in range(heights)], axis=0)
        out_ref[first * heights : first * heights + block, :] = shuffle(restore_ref, part)


def outer_kernel(samples, groups, *refs):
    specs, grads = refs[:groups], refs[groups : 2 * groups]
    out_ref, real, imag, crossed, exact = refs[2 * groups :]
    total, channels, both = real.shape
    outs = crossed.shape[1]
    half = both // 2
    low = low_half((channels, both), half)

    for g in range(groups):
        for s in range(samples):
            n = g * samples + s
            spec = specs[g][s * channels : (s + 1) * channels, :].astype(F32)
            other = pltpu.roll(spec, half, 1)
            real[n] = jnp.where(low, spec, other)
            imag[n] = jnp.where(low, other, -spec)
            grad = grads[g][s * outs : (s + 1) * outs, :]
            swapped = pltpu.roll(grad.astype(F32), half, 1)
            crossed[n] = swapped.astype(BF16)
            exact[2 * n] = grad[outs - PACK :, :].astype(F32)
            exact[2 * n + 1] = swapped[outs - PACK :, :]

    def body(block, carry):
        into = rows_of(out_ref, block, GROUP * outs)
        views = [rows_of(store.at[n], block, GROUP) for n in range(total) for store in (real, imag)]
        for first in range(0, GROUP, 2):
            pair = range(first, first + 2)
            lefts = [[packed_row(view, c) for view in views] for c in pair]
            for c in pair:
                value = running([(view[c : c + 1, :], exact[n]) for n, view in enumerate(views)])
                into[(c + 1) * outs - PACK : (c + 1) * outs, :] = value
            for o in range(0, outs - PACK, PACK):
                right = []
                for n in range(total):
                    at = n % samples * outs + o
                    right += [grads[n // samples][at : at + PACK, :], crossed[n, o : o + PACK, :]]
                results = [running(list(zip(left, right))) for left in lefts]
                for c, result in zip(pair, results):
                    into[c * outs + o : c * outs + o + PACK, :] = result.astype(F32)
        return carry

    lax.fori_loop(0, channels // GROUP, body, 0)


def whole(extent):
    return pl.BlockSpec(extent, lambda *_: (0,) * len(extent))


def call(kernel, name, operands, outs, scratch=(), grid=(1,), blocks=None, out_blocks=None, limit=LIMIT):
    blocks, out_blocks = blocks or {}, out_blocks or {}
    in_specs = [blocks.get(n) or whole(operand.shape) for n, operand in enumerate(operands)]
    out_specs = [out_blocks.get(n, whole(out.shape)) for n, out in enumerate(outs)]
    return pl.pallas_call(
        kernel,
        out_shape=tuple(outs),
        grid=grid,
        in_specs=in_specs,
        out_specs=tuple(out_specs),
        scratch_shapes=list(scratch),
        compiler_params=pltpu.CompilerParams(vmem_limit_bytes=limit),
        name=name,
    )(*operands)


def swap(values, axis, step):
    return lax.ppermute(values, axis, [(i, i ^ step) for i in range(lax.axis_size(axis))])


def gather_near(values, axis):
    size = lax.axis_size(axis)
    return {0: values} | {1 << bit: swap(values, axis, 1 << bit) for bit in range(size.bit_length() - 1)}


def gather_far(near, axis):
    whole_set = dict(near)
    for step in range(1, lax.axis_size(axis)):
        if step not in whole_set:
            whole_set[step] = swap(whole_set[step & (step - 1)], axis, step & -step)
    return [whole_set[step] for step in sorted(whole_set)]


def sum_over(values, axis):
    step = 1
    while step < lax.axis_size(axis):
        values = values + swap(values, axis, step)
        step *= 2
    return values


def block_diagonal(matrix, copies):
    zero = jnp.zeros_like(matrix)
    return jnp.concatenate(
        [
            jnp.concatenate([matrix if i == j else zero for j in range(copies)], axis=1)
            for i in range(copies)
        ],
        axis=0,
    )


def shape(extent, kind=BF16):
    return jax.ShapeDtypeStruct(extent, kind)


def local(inputs, cotangent, mode_weight, local_weight):
    tiles = lax.axis_size("tile")
    samples, channels, th, width = inputs.shape
    owned, _, _, both = mode_weight.shape
    modes = both // 2
    lanes = samples * channels
    parts = width // 128
    spec_scale = 1.0 / math.sqrt(tiles * th * width)
    mode_scale = 1.0 / math.sqrt(modes * tiles * owned)
    send_cols, rows, back_rows, back_cols = tables(tiles, owned, th, width, modes)
    pixel_rows = samples * channels * th
    halves = tiles * padded(2 * owned)
    inverse = 2 * tiles * th

    def exchange(values):
        split = values.reshape(tiles, values.shape[0] // tiles, values.shape[1])
        moved = lax.all_to_all(split, "tile", split_axis=0, concat_axis=0, tiled=False)
        return moved.reshape(values.shape)

    forward_mix = block_diagonal(local_weight.T, samples)
    backward_mix = block_diagonal(local_weight, samples)
    by_row = order(PACK, th)
    by_channel = order(th, PACK)
    by_mode = mode_order(tiles, owned)
    by_height = order(2 * min(tiles, 8), th)
    flat_weight = mode_weight.reshape(-1, both)
    weight_block = pl.BlockSpec((flat_weight.shape[0] // owned, both), lambda q: (q, 0))
    weight_scratch = [pltpu.VMEM(flat_weight.shape, BF16), pltpu.SemaphoreType.DMA((owned,))]
    in_place = pl.BlockSpec(memory_space=pl.ANY)
    to_modes = shape((halves, th * lanes))
    to_pixels = shape((inverse, owned * lanes))
    field_shape = shape((th, lanes, width))

    def kept(*operands):
        return [pltpu.VMEM(operand.shape, operand.dtype) for operand in operands]

    def early(*operands):
        return kept(*operands) + [pltpu.SemaphoreType.DMA((len(operands),))]

    def field_blocks(first):
        return {first + n: pl.BlockSpec((pixel_rows // SPLIT, width), lambda _, n=n: (n, 0)) for n in range(SPLIT)}

    field_rows, send = call(
        columns_kernel,
        "columns",
        (by_row, send_cols, *[inputs.reshape(pixel_rows, width)] * SPLIT),
        (field_shape, to_modes),
        blocks=field_blocks(2),
    )
    arrived = exchange(send)
    (cot_rows,) = call(
        relayout_kernel,
        "relayout",
        (by_row, *[cotangent.reshape(pixel_rows, width)] * SPLIT),
        (field_shape,),
        blocks=field_blocks(1),
    )
    spectra, send = call(
        functools.partial(forward_kernel, spec_scale, samples, owned),
        "mix_forward",
        (arrived, by_mode, rows, back_rows, flat_weight),
        (shape((owned * lanes, both)), to_pixels),
        [
            pltpu.VMEM((owned * lanes, both), F32),
            pltpu.VMEM((owned * lanes, both), F32),
            pltpu.VMEM((owned, 2 * samples, channels, both), F32),
            *weight_scratch,
            *early(arrived, by_mode, rows, back_rows),
            pltpu.VMEM((inverse, owned * lanes), BF16),
            pltpu.SemaphoreType.DMA((owned,)),
        ],
        grid=(owned,),
        blocks={n: in_place for n in range(5)},
        out_blocks={1: in_place},
    )
    all_spectra = gather_far(gather_near(spectra, "dp"), "dp")
    arrived = exchange(send)
    steps = 4
    row_block = pl.BlockSpec((steps, lanes, width), lambda n: (n, 0, 0))
    gate_rows, send, local_sum = call(
        functools.partial(pixels_kernel, mode_scale, th),
        "pixels",
        (arrived, by_height, back_cols, forward_mix, field_rows, cot_rows, send_cols),
        (field_shape, to_modes, shape((channels, channels), F32)),
        [pltpu.VMEM((inverse, owned * lanes), BF16), pltpu.VMEM((lanes, lanes), F32)],
        grid=(th // steps,),
        blocks={4: row_block, 5: row_block},
        out_blocks={0: row_block, 1: pl.BlockSpec((halves, steps * lanes), lambda n: (0, n))},
        limit=SMALL,
    )
    send, *all_spectra = lax.optimization_barrier((send, *all_spectra))
    arrived, local_sum = lax.optimization_barrier((exchange(send), sum_over(local_sum, "dp")))
    (grad_spectra,) = call(
        functools.partial(spectra_kernel, mode_scale, owned, lanes),
        "grad_spectra",
        (arrived, by_mode, rows),
        (shape((owned * lanes, both)),),
        limit=SMALL,
    )
    near = gather_near(grad_spectra, "dp")
    carried = channels * channels * tiles // inverse
    (send,) = call(
        functools.partial(backward_kernel, samples, tiles),
        "mix_backward",
        (grad_spectra, back_rows, local_sum, flat_weight),
        (shape((inverse, owned * lanes + carried)),),
        [
            pltpu.VMEM((owned * lanes, both), BF16),
            pltpu.VMEM((owned * lanes, both), BF16),
            pltpu.VMEM((owned, 2 * samples, channels * ROWS, both), F32),
            *weight_scratch,
            *early(grad_spectra, back_rows, local_sum),
            pltpu.VMEM((inverse, owned * lanes + carried), BF16),
            pltpu.SemaphoreType.DMA((owned,)),
        ],
        grid=(owned,),
        blocks={n: in_place for n in range(4)},
        out_blocks={0: in_place},
    )
    send, near = lax.optimization_barrier((send, near))
    all_grads = gather_far(near, "dp")
    arrived = exchange(send)

    groups = lax.axis_size("dp")
    total = groups * samples
    per_mode = pl.BlockSpec((lanes, both), lambda q: (q, 0))
    (mode_grad,) = call(
        functools.partial(outer_kernel, samples, groups),
        "mode_grad",
        (*all_spectra, *all_grads),
        (shape(flat_weight.shape, F32),),
        [pltpu.VMEM((total, channels, both), F32)] * 2
        + [pltpu.VMEM((total, channels, both), BF16), pltpu.VMEM((2 * total, PACK, both), F32)],
        grid=(owned,),
        blocks={n: per_mode for n in range(2 * groups)},
        out_blocks={0: weight_block},
    )
    arrived, mode_grad = lax.optimization_barrier((arrived, mode_grad))

    input_grad, local_grad = call(
        functools.partial(final_kernel, spec_scale, tiles),
        "final",
        (arrived, by_height, back_cols, backward_mix, gate_rows, by_channel),
        (shape((pixel_rows, width)), shape((channels, channels), F32)),
        [pltpu.VMEM((th, lanes, width), BF16)],
        limit=SMALL,
    )
    return (input_grad.reshape(inputs.shape), mode_grad.reshape(mode_weight.shape), local_grad)


def solution(mesh):
    return jax.shard_map(
        local,
        mesh=mesh,
        in_specs=(
            P("dp", None, "tile", None),
            P("dp", None, "tile", None),
            P("tile", None, None, None),
            P(),
        ),
        out_specs=(P("dp", None, "tile", None), P("tile", None, None, None), P()),
        check_vma=False,
    )
```

```python
import functools
import math

import jax
import jax.numpy as jnp
import numpy as np
from jax import lax
from jax.experimental import pallas as pl
from jax.experimental.pallas import tpu as pltpu
from jax.sharding import PartitionSpec as P

F32 = jnp.float32
BF16 = jnp.bfloat16
LIMIT = 56 * 1024 * 1024
SMALL = 24 * 1024 * 1024
ROWS = 8
PACK = 16
GROUP = 8
SPLIT = 4
AHEAD = 3


def row_tables(height, modes):
    index = np.arange(modes)
    signed = np.where(index < modes // 2, index, index - modes)
    phases = np.mod(np.arange(height)[:, None] * signed[None, :], height)
    angles = phases * (2.0 * math.pi / height)
    return np.cos(angles), np.sin(angles)


def column_tables(width, modes):
    phases = np.mod(np.arange(modes)[:, None] * np.arange(width)[None, :], width)
    angles = phases * (2.0 * math.pi / width)
    return np.stack([np.cos(angles), -np.sin(angles)])


def constant(table):
    return jnp.asarray(np.asarray(table, np.float32)).astype(BF16)


def tables(tiles, owned, th, width, modes):
    cols = column_tables(width, tiles * owned)
    split = cols.reshape(2, tiles, owned, width)
    send_cols = split.transpose(1, 0, 2, 3).reshape(tiles, 2 * owned, width)
    send_cols = np.pad(send_cols, ((0, 0), (0, padded(2 * owned) - 2 * owned), (0, 0))).reshape(-1, width)
    back_cols = split.transpose(2, 1, 0, 3).reshape(-1, width)
    cosine, sine = row_tables(th * tiles, modes)
    real = np.concatenate([cosine, -sine], axis=1)
    imag = np.concatenate([sine, cosine], axis=1)
    pair = np.stack([real, imag]).reshape(2, tiles, th, 2 * modes)
    rows = pair.transpose(2, 1, 0, 3).reshape(-1, 2 * modes)
    back_rows = pair.transpose(1, 0, 2, 3).reshape(-1, 2 * modes)
    return constant(send_cols), constant(rows), constant(back_rows), constant(back_cols)


def padded(rows):
    return -(-rows // PACK) * PACK


def order(outer, inner):
    take = np.arange(outer * inner).reshape(outer, inner).T.reshape(-1)
    return constant(np.eye(outer * inner)[take])


def mode_order(tiles, owned):
    rows = np.arange(tiles * padded(2 * owned)).reshape(tiles, -1)
    take = rows[:, : 2 * owned].reshape(tiles, 2, owned).transpose(2, 0, 1).reshape(-1)
    return constant(np.eye(rows.size)[take])


def dot(left, right, dims):
    return lax.dot_general(left, right, (dims, ((), ())), preferred_element_type=F32)


def low_half(shape, half):
    return lax.broadcasted_iota(jnp.int32, shape, 1) < half


def gelu_slope(values):
    size = jnp.abs(values)
    expo = jnp.exp(-0.5 * values * values)
    t = 1.0 / (1.0 + (0.3275911 / math.sqrt(2.0)) * size)
    poly = 0.5 * 1.061405429
    for factor in (-1.453152027, 1.421413741, -0.284496736, 0.254829592):
        poly = poly * t + 0.5 * factor
    tail = poly * t * expo
    cumulative = jnp.where(values < 0.0, tail, 1.0 - tail)
    return cumulative + values * expo * (1.0 / math.sqrt(2.0 * math.pi))


def shuffle(order_ref, value):
    return dot(order_ref[...], value, ((1,), (0,))).astype(BF16)


def by_rows(order_ref, field_refs, rows_ref):
    heights, lanes, _ = rows_ref.shape
    block = PACK * heights
    quarter = lanes // len(field_refs)
    for first in range(0, lanes, PACK):
        start = first % quarter * heights
        moved = shuffle(order_ref, field_refs[first // quarter][start : start + block, :])
        for h in range(heights):
            rows_ref[h, first : first + PACK, :] = moved[h * PACK : (h + 1) * PACK]


def columns_kernel(order_ref, table_ref, *rest):
    field_refs, (rows_ref, send_ref) = rest[:SPLIT], rest[SPLIT:]
    heights, lanes, _ = rows_ref.shape
    by_rows(order_ref, field_refs, rows_ref)
    for h in range(heights):
        send_ref[:, h * lanes : (h + 1) * lanes] = dot(table_ref[...], rows_ref[h], ((1,), (1,))).astype(BF16)


def relayout_kernel(order_ref, *rest):
    by_rows(order_ref, rest[:SPLIT], rest[SPLIT])


def shuffle_groups(order_ref, recv_ref, width):
    size = order_ref.shape[0]
    return [shuffle(order_ref, recv_ref[n : n + size, :width]) for n in range(0, recv_ref.shape[0], size)]


def stack(groups, index, count, lanes):
    return jnp.concatenate(
        [
            group[index * count : (index + 1) * count, n : n + lanes]
            for n in range(0, groups[0].shape[1], lanes)
            for group in groups
        ],
        axis=0,
    )


def spectra_into(scale, owned, lanes, recv_ref, order_ref, rows_ref, spec_ref):
    count = order_ref.shape[0] // owned
    fields = rows_ref.shape[0] // count * lanes
    ordered = [shuffle(order_ref, recv_ref[:, :fields])]
    for q in range(owned):
        stacked = stack(ordered, q, count, lanes)
        spec_ref[q * lanes : (q + 1) * lanes, :] = (
            scale * dot(stacked, rows_ref[...], ((0,), (0,)))
        ).astype(BF16)


def to_piece(value, rows):
    return jnp.concatenate([value[n : n + rows] for n in range(0, value.shape[0], rows)], axis=1)


def from_piece(value, extent):
    return jnp.concatenate([value[:, n : n + extent] for n in range(0, value.shape[1], extent)], axis=0)


def spectra_kernel(scale, owned, lanes, recv_ref, order_ref, rows_ref, spec_ref):
    spectra_into(scale, owned, lanes, recv_ref, order_ref, rows_ref, spec_ref)


def running(pairs):
    waiting = []
    for left, right in pairs:
        value, level = left * right, 0
        while waiting and waiting[-1][1] == level:
            value, level = waiting.pop()[0] + value, level + 1
        waiting.append((value, level))
    return sum((value for value, _ in reversed(waiting[:-1])), waiting[-1][0])


def rows_of(store, block, extent):
    return store.at[pl.ds(pl.multiple_of(block * extent, extent), extent), :]


def packed_row(view, index):
    row = view[index : index + 1, :]
    return jnp.broadcast_to(row, (PACK, row.shape[1])).astype(BF16)


def duplicates(spec, half):
    value = spec.astype(F32)
    other = pltpu.roll(value, half, 1)
    low = low_half(value.shape, half)
    return jnp.where(low, value, other), jnp.where(low, other, value)


def finish(back_ref, sums, send_ref, stage, sems, mix):
    @pl.when(pl.program_id(0) == pl.num_programs(0) - 1)
    def _():
        moves = []
        for q in range(sums.shape[0]):
            mixed = mix(sums.at[q]).astype(BF16)
            column = pl.ds(q * mixed.shape[0], mixed.shape[0])
            stage[:, column] = dot(back_ref[...], mixed, ((1,), (1,))).astype(BF16)
            moves.append(pltpu.make_async_copy(stage.at[:, column], send_ref.at[:, column], sems.at[q]))
            moves[-1].start()
        for move in moves:
            move.wait()


def fetch(sources, targets, sems):
    moves = [
        pltpu.make_async_copy(source, target, sems.at[n]) for n, (source, target) in enumerate(zip(sources, targets))
    ]

    @pl.when(pl.program_id(0) == 0)
    def _():
        for move in moves:
            move.start()

    return moves


def fetch_weights(moves, source_ref, weights, sems):
    q = pl.program_id(0)
    owned = sems.shape[0]
    size = weights.shape[0] // owned

    def move(mode):
        part = pl.ds(pl.multiple_of(mode * size, size), size)
        return pltpu.make_async_copy(source_ref.at[part, :], weights.at[part, :], sems.at[mode])

    @pl.when(q == 0)
    def _():
        move(0).start()
        for early in moves:
            early.wait()
        for mode in range(1, min(AHEAD, owned)):
            move(mode).start()

    @pl.when(q + AHEAD < owned)
    def _():
        move(q + AHEAD).start()

    return move(q), weights.at[pl.ds(pl.multiple_of(q * size, size), size), :]


def forward_kernel(scale, samples, owned, *rest):
    sources, source_ref, spec_ref, send_ref, real, imag, sums, weights, sems = rest[:4], *rest[4:12]
    targets, early, stage, late = rest[12:16], *rest[16:19]
    recv_ref, order_ref, rows_ref, back_ref = targets
    _, _, outs, both = sums.shape
    channels = weights.shape[0] // outs // owned
    half = both // 2
    lanes = samples * channels
    q = pl.program_id(0)
    moves = fetch(sources, targets, early)
    coming, weight_ref = fetch_weights(moves, source_ref, weights, sems)

    @pl.when(q == 0)
    def _():
        spectra_into(scale, owned, lanes, recv_ref, order_ref, rows_ref, spec_ref)
        real[...], imag[...] = duplicates(spec_ref[...], half)
        sums[...] = jnp.zeros_like(sums)

    coming.wait()

    def body(block, carry):
        view = rows_of(weight_ref, block, GROUP * outs)
        into = sums.at[q]
        for s in range(samples):
            rows = []
            for store in (real, imag):
                part = rows_of(store, (q * lanes + s * channels) // GROUP + block, GROUP)
                rows.append([packed_row(part, step) for step in range(GROUP)])
            for o in range(0, outs, PACK):
                column = [view[step * outs + o : step * outs + o + PACK, :] for step in range(GROUP)]
                for n, row in enumerate(rows):
                    into[2 * s + n, o : o + PACK, :] += running([(w, r) for w, r in zip(column, row)]).astype(F32)
        return carry

    lax.fori_loop(0, channels // GROUP, body, 0)

    def mix(parts):
        low = low_half((outs, both), half)
        result = []
        for s in range(samples):
            crossed = pltpu.roll(parts[2 * s + 1], half, 1)
            result.append(parts[2 * s] + jnp.where(low, -crossed, crossed))
        return jnp.concatenate(result, axis=0)

    finish(back_ref, sums, send_ref, stage, late, mix)


def backward_kernel(samples, tiles, *rest):
    sources, source_ref, send_ref, real, imag, sums, weights, sems = rest[:3], *rest[3:10]
    targets, early, stage, late = rest[10:13], *rest[13:16]
    spec_ref, back_ref, local_ref = targets

    def carried():
        column = pl.ds(sums.shape[0] * lanes, stage.shape[1] - sums.shape[0] * lanes)
        return pltpu.make_async_copy(stage.at[:, column], send_ref.at[:, column], late.at[0])

    channels, both = sums.shape[2] // ROWS, sums.shape[3]
    outs = weights.shape[0] // channels // sums.shape[0]
    half = both // 2
    lanes = samples * outs
    q = pl.program_id(0)
    moves = fetch(sources, targets, early)
    coming, weight_ref = fetch_weights(moves, source_ref, weights, sems)

    @pl.when(q == 0)
    def _():
        first, second = duplicates(spec_ref[...], half)
        real[...], imag[...] = first.astype(BF16), second.astype(BF16)
        extent = stage.shape[0] // tiles
        partial = to_piece(local_ref[...].astype(BF16), extent)
        for n in range(0, stage.shape[0], extent):
            stage[n : n + extent, sums.shape[0] * lanes :] = partial
        move = carried()
        move.start()
        move.wait()

    coming.wait()
    grads = [
        [store[pl.ds(pl.multiple_of(q * lanes + s * outs + o, PACK), PACK), :] for o in range(0, outs, PACK)]
        for s in range(samples)
        for store in (real, imag)
    ]

    def body(block, carry):
        view = rows_of(weight_ref, block, GROUP * outs)
        into = [rows_of(sums.at[q, n], block, GROUP * ROWS) for n in range(len(grads))]
        for first in range(0, GROUP, 4):
            totals = []
            for step in range(first, first + 4):
                column = [view[step * outs + o : step * outs + o + PACK, :] for o in range(0, outs, PACK)]
                for n, grad in enumerate(grads):
                    total = running([(w, g) for w, g in zip(column, grad)]).astype(F32)
                    totals.append((n, step, total[:ROWS] + total[ROWS:]))
            for n, step, total in totals:
                into[n][step * ROWS : (step + 1) * ROWS, :] = total
        return carry

    lax.fori_loop(0, channels // GROUP, body, 0)

    def mix(parts):
        low = low_half((channels, both), half)
        result = []
        for s in range(samples):
            straight, crossed = (
                sum(parts[n, pl.ds(row, channels, stride=ROWS), :] for row in range(ROWS)) for n in (2 * s, 2 * s + 1)
            )
            result.append(jnp.where(low, straight, -straight) + pltpu.roll(crossed, half, 1))
        return jnp.concatenate(result, axis=0)

    finish(back_ref, sums, send_ref, stage, late, mix)


def pixels_kernel(scale, heights, recv_ref, order_ref, back_ref, local_ref, field_ref, cot_ref, table_ref, *rest):
    grad_ref, send_ref, sum_ref, ordered, total = rest
    steps, lanes, _ = field_ref.shape
    count = order_ref.shape[0] // heights
    size = order_ref.shape[0]
    group = pl.program_id(0)

    @pl.when(group == 0)
    def _():
        for n in range(0, recv_ref.shape[0], size):
            ordered[n : n + size, :] = shuffle(order_ref, recv_ref[n : n + size, :])
        total[...] = jnp.zeros_like(total)

    local = jnp.zeros(total.shape, F32)
    for step in range(steps):
        parts = []
        for n in range(0, recv_ref.shape[0], size):
            first = pl.multiple_of(n + (group * steps + step) * count, count)
            parts.append(ordered[pl.ds(first, count), :])
        inner = stack(parts, 0, count, lanes)
        pre = scale * dot(inner, back_ref[...], ((0,), (0,)))
        pre = pre + dot(local_ref[...], field_ref[step], ((1,), (0,)))
        grad = (cot_ref[step].astype(F32) * gelu_slope(pre)).astype(BF16)
        grad_ref[step] = grad
        send_ref[:, step * lanes : (step + 1) * lanes] = dot(table_ref[...], grad, ((1,), (1,))).astype(BF16)
        local = local + dot(field_ref[step], grad, ((1,), (1,)))
    total[...] += local

    @pl.when(group == pl.num_programs(0) - 1)
    def _():
        extent = sum_ref.shape[0]
        sum_ref[...] = sum(total[n : n + extent, n : n + extent] for n in range(0, lanes, extent))


def final_kernel(scale, tiles, recv_ref, order_ref, back_ref, local_ref, grad_ref, restore_ref, *rest):
    out_ref, sum_ref, result = rest
    heights, lanes, _ = grad_ref.shape
    extent = recv_ref.shape[0] // tiles
    first = back_ref.shape[0] // (2 * tiles) * lanes
    partials = sum(recv_ref[n : n + extent, first:].astype(F32) for n in range(0, recv_ref.shape[0], extent))
    sum_ref[...] = from_piece(partials, sum_ref.shape[1])
    count = order_ref.shape[0] // heights
    ordered = shuffle_groups(order_ref, recv_ref, first)
    for h in range(heights):
        inner = stack(ordered, h, count, lanes)
        value = scale * dot(inner, back_ref[...], ((0,), (0,)))
        result[h] = (value + dot(local_ref[...], grad_ref[h], ((1,), (0,)))).astype(BF16)
    block = PACK * heights
    for first in range(0, lanes, PACK):
        part = jnp.concatenate([result[h, first : first + PACK, :] for h in range(heights)], axis=0)
        out_ref[first * heights : first * heights + block, :] = shuffle(restore_ref, part)


def outer_kernel(samples, groups, *refs):
    specs, grads = refs[:groups], refs[groups : 2 * groups]
    out_ref, plain, joint, right, apart = refs[2 * groups :]
    total, channels, both = plain.shape
    outs = right.shape[1]
    half = both // 2
    low = low_half((channels, both), half)
    for g in range(groups):
        for s in range(samples):
            n = g * samples + s
            spec = specs[g][s * channels : (s + 1) * channels, :].astype(F32)
            plain[n] = spec
            added = spec + pltpu.roll(spec, half, 1)
            joint[n] = jnp.where(low[: channels // 2], added[: channels // 2], added[channels // 2 :])
            grad = grads[g][s * outs : (s + 1) * outs, :].astype(F32)
            right[n] = grad
            difference = pltpu.roll(grad, half, 1) - grad
            apart[n] = jnp.where(low, difference, -difference)
    blocks = channels // 2 // GROUP
    tile_low = low_half((ROWS, both), half)

    def body(block, carry):
        near, far = rows_of(out_ref, block, GROUP * outs), rows_of(out_ref, block + blocks, GROUP * outs)
        first = [rows_of(plain.at[n], block, GROUP) for n in range(total)]
        second = [rows_of(plain.at[n], block + blocks, GROUP) for n in range(total)]
        third = [rows_of(joint.at[n], block, GROUP) for n in range(total)]
        for c in range(GROUP):
            rows = [[view[c : c + 1, :] for view in views] for views in (first, second, third)]
            for o in range(0, outs, ROWS):
                tiles = [right[n, o : o + ROWS, :] for n in range(total)]
                others = [apart[n, o : o + ROWS, :] for n in range(total)]
                one, two = (running(list(zip(row, tiles))) for row in rows[:2])
                both_joint = running(list(zip(rows[2], others)))
                for value, extra, into in (
                    (one, pltpu.roll(both_joint, half, 1), near),
                    (two, both_joint, far),
                ):
                    result = pltpu.roll(value, half, 1) + jnp.where(tile_low, value, extra - value)
                    into[c * outs + o : c * outs + o + ROWS, :] = result
        return carry

    lax.fori_loop(0, blocks, body, 0)


def whole(extent):
    return pl.BlockSpec(extent, lambda *_: (0,) * len(extent))


def call(kernel, name, operands, outs, scratch=(), grid=(1,), blocks=None, out_blocks=None, limit=LIMIT):
    blocks, out_blocks = blocks or {}, out_blocks or {}
    in_specs = [blocks.get(n) or whole(operand.shape) for n, operand in enumerate(operands)]
    out_specs = [out_blocks.get(n, whole(out.shape)) for n, out in enumerate(outs)]
    return pl.pallas_call(
        kernel,
        out_shape=tuple(outs),
        grid=grid,
        in_specs=in_specs,
        out_specs=tuple(out_specs),
        scratch_shapes=list(scratch),
        compiler_params=pltpu.CompilerParams(vmem_limit_bytes=limit),
        name=name,
    )(*operands)


def swap(values, axis, step):
    return lax.ppermute(values, axis, [(i, i ^ step) for i in range(lax.axis_size(axis))])


def gather_near(values, axis):
    size = lax.axis_size(axis)
    return {0: values} | {1 << bit: swap(values, axis, 1 << bit) for bit in range(size.bit_length() - 1)}


def gather_far(near, axis):
    whole_set = dict(near)
    for step in range(1, lax.axis_size(axis)):
        if step not in whole_set:
            whole_set[step] = swap(whole_set[step & (step - 1)], axis, step & -step)
    return [whole_set[step] for step in sorted(whole_set)]


def sum_over(values, axis):
    step = 1
    while step < lax.axis_size(axis):
        values = values + swap(values, axis, step)
        step *= 2
    return values


def block_diagonal(matrix, copies):
    zero = jnp.zeros_like(matrix)
    return jnp.concatenate(
        [
            jnp.concatenate([matrix if i == j else zero for j in range(copies)], axis=1)
            for i in range(copies)
        ],
        axis=0,
    )


def shape(extent, kind=BF16):
    return jax.ShapeDtypeStruct(extent, kind)


def local(inputs, cotangent, mode_weight, local_weight):
    tiles = lax.axis_size("tile")
    samples, channels, th, width = inputs.shape
    owned, _, _, both = mode_weight.shape
    modes = both // 2
    lanes = samples * channels
    parts = width // 128
    spec_scale = 1.0 / math.sqrt(tiles * th * width)
    mode_scale = 1.0 / math.sqrt(modes * tiles * owned)
    send_cols, rows, back_rows, back_cols = tables(tiles, owned, th, width, modes)
    pixel_rows = samples * channels * th
    halves = tiles * padded(2 * owned)
    inverse = 2 * tiles * th

    def exchange(values):
        split = values.reshape(tiles, values.shape[0] // tiles, values.shape[1])
        moved = lax.all_to_all(split, "tile", split_axis=0, concat_axis=0, tiled=False)
        return moved.reshape(values.shape)

    forward_mix = block_diagonal(local_weight.T, samples)
    backward_mix = block_diagonal(local_weight, samples)
    by_row = order(PACK, th)
    by_channel = order(th, PACK)
    by_mode = mode_order(tiles, owned)
    by_height = order(2 * min(tiles, 8), th)
    flat_weight = mode_weight.reshape(-1, both)
    weight_block = pl.BlockSpec((flat_weight.shape[0] // owned, both), lambda q: (q, 0))
    weight_scratch = [pltpu.VMEM(flat_weight.shape, BF16), pltpu.SemaphoreType.DMA((owned,))]
    in_place = pl.BlockSpec(memory_space=pl.ANY)
    to_modes = shape((halves, th * lanes))
    to_pixels = shape((inverse, owned * lanes))
    field_shape = shape((th, lanes, width))

    def kept(*operands):
        return [pltpu.VMEM(operand.shape, operand.dtype) for operand in operands]

    def early(*operands):
        return kept(*operands) + [pltpu.SemaphoreType.DMA((len(operands),))]

    def field_blocks(first):
        return {first + n: pl.BlockSpec((pixel_rows // SPLIT, width), lambda _, n=n: (n, 0)) for n in range(SPLIT)}

    field_rows, send = call(
        columns_kernel,
        "columns",
        (by_row, send_cols, *[inputs.reshape(pixel_rows, width)] * SPLIT),
        (field_shape, to_modes),
        blocks=field_blocks(2),
    )
    arrived = exchange(send)
    (cot_rows,) = call(
        relayout_kernel,
        "relayout",
        (by_row, *[cotangent.reshape(pixel_rows, width)] * SPLIT),
        (field_shape,),
        blocks=field_blocks(1),
    )
    spectra, send = call(
        functools.partial(forward_kernel, spec_scale, samples, owned),
        "mix_forward",
        (arrived, by_mode, rows, back_rows, flat_weight),
        (shape((owned * lanes, both)), to_pixels),
        [
            pltpu.VMEM((owned * lanes, both), F32),
            pltpu.VMEM((owned * lanes, both), F32),
            pltpu.VMEM((owned, 2 * samples, channels, both), F32),
            *weight_scratch,
            *early(arrived, by_mode, rows, back_rows),
            pltpu.VMEM((inverse, owned * lanes), BF16),
            pltpu.SemaphoreType.DMA((owned,)),
        ],
        grid=(owned,),
        blocks={n: in_place for n in range(5)},
        out_blocks={1: in_place},
    )
    all_spectra = gather_far(gather_near(spectra, "dp"), "dp")
    arrived = exchange(send)
    steps = 4
    row_block = pl.BlockSpec((steps, lanes, width), lambda n: (n, 0, 0))
    gate_rows, send, local_sum = call(
        functools.partial(pixels_kernel, mode_scale, th),
        "pixels",
        (arrived, by_height, back_cols, forward_mix, field_rows, cot_rows, send_cols),
        (field_shape, to_modes, shape((channels, channels), F32)),
        [pltpu.VMEM((inverse, owned * lanes), BF16), pltpu.VMEM((lanes, lanes), F32)],
        grid=(th // steps,),
        blocks={4: row_block, 5: row_block},
        out_blocks={0: row_block, 1: pl.BlockSpec((halves, steps * lanes), lambda n: (0, n))},
        limit=SMALL,
    )
    send, *all_spectra = lax.optimization_barrier((send, *all_spectra))
    arrived, local_sum = lax.optimization_barrier((exchange(send), sum_over(local_sum, "dp")))
    (grad_spectra,) = call(
        functools.partial(spectra_kernel, mode_scale, owned, lanes),
        "grad_spectra",
        (arrived, by_mode, rows),
        (shape((owned * lanes, both)),),
        limit=SMALL,
    )
    near = gather_near(grad_spectra, "dp")
    carried = channels * channels * tiles // inverse
    (send,) = call(
        functools.partial(backward_kernel, samples, tiles),
        "mix_backward",
        (grad_spectra, back_rows, local_sum, flat_weight),
        (shape((inverse, owned * lanes + carried)),),
        [
            pltpu.VMEM((owned * lanes, both), BF16),
            pltpu.VMEM((owned * lanes, both), BF16),
            pltpu.VMEM((owned, 2 * samples, channels * ROWS, both), F32),
            *weight_scratch,
            *early(grad_spectra, back_rows, local_sum),
            pltpu.VMEM((inverse, owned * lanes + carried), BF16),
            pltpu.SemaphoreType.DMA((owned,)),
        ],
        grid=(owned,),
        blocks={n: in_place for n in range(4)},
        out_blocks={0: in_place},
    )
    send, near = lax.optimization_barrier((send, near))
    all_grads = gather_far(near, "dp")
    arrived = exchange(send)

    groups = lax.axis_size("dp")
    total = groups * samples
    per_mode = pl.BlockSpec((lanes, both), lambda q: (q, 0))
    (mode_grad,) = call(
        functools.partial(outer_kernel, samples, groups),
        "mode_grad",
        (*all_spectra, *all_grads),
        (shape(flat_weight.shape, F32),),
        [
            pltpu.VMEM((total, channels, both), F32),
            pltpu.VMEM((total, channels // 2, both), F32),
            pltpu.VMEM((total, channels, both), F32),
            pltpu.VMEM((total, channels, both), F32),
        ],
        grid=(owned,),
        blocks={n: per_mode for n in range(2 * groups)},
        out_blocks={0: weight_block},
    )
    arrived, mode_grad = lax.optimization_barrier((arrived, mode_grad))

    input_grad, local_grad = call(
        functools.partial(final_kernel, spec_scale, tiles),
        "final",
        (arrived, by_height, back_cols, backward_mix, gate_rows, by_channel),
        (shape((pixel_rows, width)), shape((channels, channels), F32)),
        [pltpu.VMEM((th, lanes, width), BF16)],
        limit=SMALL,
    )
    return (input_grad.reshape(inputs.shape), mode_grad.reshape(mode_weight.shape), local_grad)


def solution(mesh):
    return jax.shard_map(
        local,
        mesh=mesh,
        in_specs=(
            P("dp", None, "tile", None),
            P("dp", None, "tile", None),
            P("tile", None, None, None),
            P(),
        ),
        out_specs=(P("dp", None, "tile", None), P("tile", None, None, None), P()),
        check_vma=False,
    )
```

```python
import functools
import math

import jax
import jax.numpy as jnp
import numpy as np
from jax import lax
from jax.experimental import pallas as pl
from jax.experimental.pallas import tpu as pltpu
from jax.sharding import PartitionSpec as P

F32 = jnp.float32
BF16 = jnp.bfloat16
LIMIT = 56 * 1024 * 1024
SMALL = 24 * 1024 * 1024
ROWS = 8
PACK = 16
GROUP = 8
SPLIT = 4
AHEAD = 3


def row_tables(height, modes):
    index = np.arange(modes)
    signed = np.where(index < modes // 2, index, index - modes)
    phases = np.mod(np.arange(height)[:, None] * signed[None, :], height)
    angles = phases * (2.0 * math.pi / height)
    return np.cos(angles), np.sin(angles)


def column_tables(width, modes):
    phases = np.mod(np.arange(modes)[:, None] * np.arange(width)[None, :], width)
    angles = phases * (2.0 * math.pi / width)
    return np.stack([np.cos(angles), -np.sin(angles)])


def constant(table):
    return jnp.asarray(np.asarray(table, np.float32)).astype(BF16)


def tables(tiles, owned, th, width, modes):
    cols = column_tables(width, tiles * owned)
    split = cols.reshape(2, tiles, owned, width)
    send_cols = split.transpose(1, 0, 2, 3).reshape(tiles, 2 * owned, width)
    send_cols = np.pad(send_cols, ((0, 0), (0, padded(2 * owned) - 2 * owned), (0, 0))).reshape(-1, width)
    back_cols = split.transpose(2, 1, 0, 3).reshape(-1, width)
    cosine, sine = row_tables(th * tiles, modes)
    real = np.concatenate([cosine, -sine], axis=1)
    imag = np.concatenate([sine, cosine], axis=1)
    pair = np.stack([real, imag]).reshape(2, tiles, th, 2 * modes)
    rows = pair.transpose(2, 1, 0, 3).reshape(-1, 2 * modes)
    back_rows = pair.transpose(1, 0, 2, 3).reshape(-1, 2 * modes)
    return constant(send_cols), constant(rows), constant(back_rows), constant(back_cols)


def padded(rows):
    return -(-rows // PACK) * PACK


def order(outer, inner):
    take = np.arange(outer * inner).reshape(outer, inner).T.reshape(-1)
    return constant(np.eye(outer * inner)[take])


def mode_order(tiles, owned):
    rows = np.arange(tiles * padded(2 * owned)).reshape(tiles, -1)
    take = rows[:, : 2 * owned].reshape(tiles, 2, owned).transpose(2, 0, 1).reshape(-1)
    return constant(np.eye(rows.size)[take])


def dot(left, right, dims):
    return lax.dot_general(left, right, (dims, ((), ())), preferred_element_type=F32)


def low_half(shape, half):
    return lax.broadcasted_iota(jnp.int32, shape, 1) < half


def gelu_slope(values):
    size = jnp.abs(values)
    expo = jnp.exp(-0.5 * values * values)
    t = 1.0 / (1.0 + (0.3275911 / math.sqrt(2.0)) * size)
    poly = 0.5 * 1.061405429
    for factor in (-1.453152027, 1.421413741, -0.284496736, 0.254829592):
        poly = poly * t + 0.5 * factor
    tail = poly * t * expo
    cumulative = jnp.where(values < 0.0, tail, 1.0 - tail)
    return cumulative + values * expo * (1.0 / math.sqrt(2.0 * math.pi))


def shuffle(order_ref, value):
    return dot(order_ref[...], value, ((1,), (0,))).astype(BF16)


def by_rows(order_ref, field_refs, rows_ref):
    heights, lanes, _ = rows_ref.shape
    block = PACK * heights
    quarter = lanes // len(field_refs)
    for first in range(0, lanes, PACK):
        start = first % quarter * heights
        moved = shuffle(order_ref, field_refs[first // quarter][start : start + block, :])
        for h in range(heights):
            rows_ref[h, first : first + PACK, :] = moved[h * PACK : (h + 1) * PACK]


def columns_kernel(order_ref, table_ref, *rest):
    field_refs, (rows_ref, send_ref) = rest[:SPLIT], rest[SPLIT:]
    heights, lanes, _ = rows_ref.shape
    by_rows(order_ref, field_refs, rows_ref)
    for h in range(heights):
        send_ref[:, h * lanes : (h + 1) * lanes] = dot(table_ref[...], rows_ref[h], ((1,), (1,))).astype(BF16)


def relayout_kernel(order_ref, *rest):
    by_rows(order_ref, rest[:SPLIT], rest[SPLIT])


def shuffle_groups(order_ref, recv_ref, width):
    size = order_ref.shape[0]
    return [shuffle(order_ref, recv_ref[n : n + size, :width]) for n in range(0, recv_ref.shape[0], size)]


def stack(groups, index, count, lanes):
    return jnp.concatenate(
        [
            group[index * count : (index + 1) * count, n : n + lanes]
            for n in range(0, groups[0].shape[1], lanes)
            for group in groups
        ],
        axis=0,
    )


def spectra_into(scale, owned, lanes, recv_ref, order_ref, rows_ref, spec_ref):
    count = order_ref.shape[0] // owned
    fields = rows_ref.shape[0] // count * lanes
    ordered = [shuffle(order_ref, recv_ref[:, :fields])]
    for q in range(owned):
        stacked = stack(ordered, q, count, lanes)
        spec_ref[q * lanes : (q + 1) * lanes, :] = (
            scale * dot(stacked, rows_ref[...], ((0,), (0,)))
        ).astype(BF16)


def to_piece(value, rows):
    return jnp.concatenate([value[n : n + rows] for n in range(0, value.shape[0], rows)], axis=1)


def from_piece(value, extent):
    return jnp.concatenate([value[:, n : n + extent] for n in range(0, value.shape[1], extent)], axis=0)


def spectra_kernel(scale, owned, lanes, recv_ref, order_ref, rows_ref, spec_ref):
    spectra_into(scale, owned, lanes, recv_ref, order_ref, rows_ref, spec_ref)


def running(pairs):
    waiting = []
    for left, right in pairs:
        value, level = left * right, 0
        while waiting and waiting[-1][1] == level:
            value, level = waiting.pop()[0] + value, level + 1
        waiting.append((value, level))
    return sum((value for value, _ in reversed(waiting[:-1])), waiting[-1][0])


def rows_of(store, block, extent):
    return store.at[pl.ds(pl.multiple_of(block * extent, extent), extent), :]


def packed_row(view, index):
    row = view[index : index + 1, :]
    return jnp.broadcast_to(row, (PACK, row.shape[1])).astype(BF16)


def duplicates(spec, half):
    value = spec.astype(F32)
    other = pltpu.roll(value, half, 1)
    low = low_half(value.shape, half)
    return jnp.where(low, value, other), jnp.where(low, other, value)


def finish(back_ref, sums, send_ref, stage, sems, mix):
    @pl.when(pl.program_id(0) == pl.num_programs(0) - 1)
    def _():
        moves = []
        for q in range(sums.shape[0]):
            mixed = mix(sums.at[q]).astype(BF16)
            column = pl.ds(q * mixed.shape[0], mixed.shape[0])
            stage[:, column] = dot(back_ref[...], mixed, ((1,), (1,))).astype(BF16)
            moves.append(pltpu.make_async_copy(stage.at[:, column], send_ref.at[:, column], sems.at[q]))
            moves[-1].start()
        for move in moves:
            move.wait()


def fetch(sources, targets, sems):
    moves = [
        pltpu.make_async_copy(source, target, sems.at[n]) for n, (source, target) in enumerate(zip(sources, targets))
    ]

    @pl.when(pl.program_id(0) == 0)
    def _():
        for move in moves:
            move.start()

    return moves


def fetch_weights(moves, source_ref, weights, sems):
    q = pl.program_id(0)
    owned = sems.shape[0]
    size = weights.shape[0] // owned

    def move(mode):
        part = pl.ds(pl.multiple_of(mode * size, size), size)
        return pltpu.make_async_copy(source_ref.at[part, :], weights.at[part, :], sems.at[mode])

    @pl.when(q == 0)
    def _():
        move(0).start()
        for early in moves:
            early.wait()
        for mode in range(1, min(AHEAD, owned)):
            move(mode).start()

    @pl.when(q + AHEAD < owned)
    def _():
        move(q + AHEAD).start()

    return move(q), weights.at[pl.ds(pl.multiple_of(q * size, size), size), :]


def forward_kernel(scale, samples, owned, *rest):
    sources, source_ref, spec_ref, send_ref, real, imag, sums, weights, sems = rest[:4], *rest[4:12]
    targets, early, stage, late = rest[12:16], *rest[16:19]
    recv_ref, order_ref, rows_ref, back_ref = targets
    _, _, outs, both = sums.shape
    channels = weights.shape[0] // outs // owned
    half = both // 2
    lanes = samples * channels
    q = pl.program_id(0)
    moves = fetch(sources, targets, early)
    coming, weight_ref = fetch_weights(moves, source_ref, weights, sems)

    @pl.when(q == 0)
    def _():
        spectra_into(scale, owned, lanes, recv_ref, order_ref, rows_ref, spec_ref)
        real[...], imag[...] = duplicates(spec_ref[...], half)
        sums[...] = jnp.zeros_like(sums)

    coming.wait()

    def body(block, carry):
        view = rows_of(weight_ref, block, GROUP * outs)
        into = sums.at[q]
        for s in range(samples):
            rows = []
            for store in (real, imag):
                part = rows_of(store, (q * lanes + s * channels) // GROUP + block, GROUP)[...]
                rows.append([packed_row(part, step) for step in range(GROUP)])
            for o in range(0, outs, PACK):
                column = [view[step * outs + o : step * outs + o + PACK, :] for step in range(GROUP)]
                for n, row in enumerate(rows):
                    into[2 * s + n, o : o + PACK, :] += running([(w, r) for w, r in zip(column, row)]).astype(F32)
        return carry

    lax.fori_loop(0, channels // GROUP, body, 0)

    def mix(parts):
        low = low_half((outs, both), half)
        result = []
        for s in range(samples):
            crossed = pltpu.roll(parts[2 * s + 1], half, 1)
            result.append(parts[2 * s] + jnp.where(low, -crossed, crossed))
        return jnp.concatenate(result, axis=0)

    finish(back_ref, sums, send_ref, stage, late, mix)


def backward_kernel(samples, tiles, *rest):
    sources, source_ref, send_ref, real, imag, sums, weights, sems = rest[:3], *rest[3:10]
    targets, early, stage, late = rest[10:13], *rest[13:16]
    spec_ref, back_ref, local_ref = targets

    def carried():
        column = pl.ds(sums.shape[0] * lanes, stage.shape[1] - sums.shape[0] * lanes)
        return pltpu.make_async_copy(stage.at[:, column], send_ref.at[:, column], late.at[0])

    channels, both = sums.shape[2] // ROWS, sums.shape[3]
    outs = weights.shape[0] // channels // sums.shape[0]
    half = both // 2
    lanes = samples * outs
    q = pl.program_id(0)
    moves = fetch(sources, targets, early)
    coming, weight_ref = fetch_weights(moves, source_ref, weights, sems)

    @pl.when(q == 0)
    def _():
        first, second = duplicates(spec_ref[...], half)
        real[...], imag[...] = first.astype(BF16), second.astype(BF16)
        extent = stage.shape[0] // tiles
        partial = to_piece(local_ref[...].astype(BF16), extent)
        for n in range(0, stage.shape[0], extent):
            stage[n : n + extent, sums.shape[0] * lanes :] = partial
        move = carried()
        move.start()
        move.wait()

    coming.wait()
    grads = [
        [store[pl.ds(pl.multiple_of(q * lanes + s * outs + o, PACK), PACK), :] for o in range(0, outs, PACK)]
        for s in range(samples)
        for store in (real, imag)
    ]

    def body(block, carry):
        view = rows_of(weight_ref, block, GROUP * outs)
        into = [rows_of(sums.at[q, n], block, GROUP * ROWS) for n in range(len(grads))]
        for first in range(0, GROUP, 4):
            totals = []
            for step in range(first, first + 4):
                column = [view[step * outs + o : step * outs + o + PACK, :] for o in range(0, outs, PACK)]
                for n, grad in enumerate(grads):
                    total = running([(w, g) for w, g in zip(column, grad)]).astype(F32)
                    totals.append((n, step, total[:ROWS] + total[ROWS:]))
            for n, step, total in totals:
                into[n][step * ROWS : (step + 1) * ROWS, :] = total
        return carry

    lax.fori_loop(0, channels // GROUP, body, 0)

    def mix(parts):
        low = low_half((channels, both), half)
        result = []
        for s in range(samples):
            straight, crossed = (
                sum(parts[n, pl.ds(row, channels, stride=ROWS), :] for row in range(ROWS)) for n in (2 * s, 2 * s + 1)
            )
            result.append(jnp.where(low, straight, -straight) + pltpu.roll(crossed, half, 1))
        return jnp.concatenate(result, axis=0)

    finish(back_ref, sums, send_ref, stage, late, mix)


def pixels_kernel(scale, heights, recv_ref, order_ref, back_ref, local_ref, field_ref, cot_ref, table_ref, *rest):
    grad_ref, send_ref, sum_ref, ordered, total = rest
    steps, lanes, _ = field_ref.shape
    count = order_ref.shape[0] // heights
    size = order_ref.shape[0]
    group = pl.program_id(0)

    @pl.when(group == 0)
    def _():
        for n in range(0, recv_ref.shape[0], size):
            ordered[n : n + size, :] = shuffle(order_ref, recv_ref[n : n + size, :])
        total[...] = jnp.zeros_like(total)

    local = jnp.zeros(total.shape, F32)
    for step in range(steps):
        parts = []
        for n in range(0, recv_ref.shape[0], size):
            first = pl.multiple_of(n + (group * steps + step) * count, count)
            parts.append(ordered[pl.ds(first, count), :])
        inner = stack(parts, 0, count, lanes)
        pre = scale * dot(inner, back_ref[...], ((0,), (0,)))
        pre = pre + dot(local_ref[...], field_ref[step], ((1,), (0,)))
        grad = (cot_ref[step].astype(F32) * gelu_slope(pre)).astype(BF16)
        grad_ref[step] = grad
        send_ref[:, step * lanes : (step + 1) * lanes] = dot(table_ref[...], grad, ((1,), (1,))).astype(BF16)
        local = local + dot(field_ref[step], grad, ((1,), (1,)))
    total[...] += local

    @pl.when(group == pl.num_programs(0) - 1)
    def _():
        extent = sum_ref.shape[0]
        sum_ref[...] = sum(total[n : n + extent, n : n + extent] for n in range(0, lanes, extent))


def final_kernel(scale, tiles, recv_ref, order_ref, back_ref, local_ref, grad_ref, restore_ref, *rest):
    out_ref, sum_ref, result = rest
    heights, lanes, _ = grad_ref.shape
    extent = recv_ref.shape[0] // tiles
    first = back_ref.shape[0] // (2 * tiles) * lanes
    partials = sum(recv_ref[n : n + extent, first:].astype(F32) for n in range(0, recv_ref.shape[0], extent))
    sum_ref[...] = from_piece(partials, sum_ref.shape[1])
    count = order_ref.shape[0] // heights
    ordered = shuffle_groups(order_ref, recv_ref, first)
    for h in range(heights):
        inner = stack(ordered, h, count, lanes)
        value = scale * dot(inner, back_ref[...], ((0,), (0,)))
        result[h] = (value + dot(local_ref[...], grad_ref[h], ((1,), (0,)))).astype(BF16)
    block = PACK * heights
    for first in range(0, lanes, PACK):
        part = jnp.concatenate([result[h, first : first + PACK, :] for h in range(heights)], axis=0)
        out_ref[first * heights : first * heights + block, :] = shuffle(restore_ref, part)


def outer_kernel(samples, groups, *refs):
    specs, grads = refs[:groups], refs[groups : 2 * groups]
    out_ref, real, imag, crossed = refs[2 * groups :]
    total, channels, both = real.shape
    outs = crossed.shape[1]
    half = both // 2
    low = low_half((channels, both), half)

    for g in range(groups):
        for s in range(samples):
            n = g * samples + s
            spec = specs[g][s * channels : (s + 1) * channels, :].astype(F32)
            other = pltpu.roll(spec, half, 1)
            real[n] = jnp.where(low, spec, other)
            imag[n] = jnp.where(low, other, -spec)
            grad = grads[g][s * outs : (s + 1) * outs, :]
            crossed[n] = pltpu.roll(grad.astype(F32), half, 1).astype(BF16)

    def body(block, carry):
        into = rows_of(out_ref, block, GROUP * outs)
        views = [rows_of(store.at[n], block, GROUP)[...] for n in range(total) for store in (real, imag)]
        for first in range(0, GROUP, 2):
            pair = range(first, first + 2)
            lefts = [[packed_row(view, c) for view in views] for c in pair]
            for o in range(0, outs, PACK):
                right = []
                for n in range(total):
                    at = n % samples * outs + o
                    right += [grads[n // samples][at : at + PACK, :], crossed[n, o : o + PACK, :]]
                results = [running(list(zip(left, right))) for left in lefts]
                for c, result in zip(pair, results):
                    into[c * outs + o : c * outs + o + PACK, :] = result.astype(F32)
        return carry

    lax.fori_loop(0, channels // GROUP, body, 0)


def whole(extent):
    return pl.BlockSpec(extent, lambda *_: (0,) * len(extent))


def call(kernel, name, operands, outs, scratch=(), grid=(1,), blocks=None, out_blocks=None, limit=LIMIT):
    blocks, out_blocks = blocks or {}, out_blocks or {}
    in_specs = [blocks.get(n) or whole(operand.shape) for n, operand in enumerate(operands)]
    out_specs = [out_blocks.get(n, whole(out.shape)) for n, out in enumerate(outs)]
    return pl.pallas_call(
        kernel,
        out_shape=tuple(outs),
        grid=grid,
        in_specs=in_specs,
        out_specs=tuple(out_specs),
        scratch_shapes=list(scratch),
        compiler_params=pltpu.CompilerParams(vmem_limit_bytes=limit),
        name=name,
    )(*operands)


def swap(values, axis, step):
    return lax.ppermute(values, axis, [(i, i ^ step) for i in range(lax.axis_size(axis))])


def gather_near(values, axis):
    size = lax.axis_size(axis)
    return {0: values} | {1 << bit: swap(values, axis, 1 << bit) for bit in range(size.bit_length() - 1)}


def gather_far(near, axis):
    whole_set = dict(near)
    for step in range(1, lax.axis_size(axis)):
        if step not in whole_set:
            whole_set[step] = swap(whole_set[step & (step - 1)], axis, step & -step)
    return [whole_set[step] for step in sorted(whole_set)]


def sum_over(values, axis):
    step = 1
    while step < lax.axis_size(axis):
        values = values + swap(values, axis, step)
        step *= 2
    return values


def block_diagonal(matrix, copies):
    zero = jnp.zeros_like(matrix)
    return jnp.concatenate(
        [
            jnp.concatenate([matrix if i == j else zero for j in range(copies)], axis=1)
            for i in range(copies)
        ],
        axis=0,
    )


def shape(extent, kind=BF16):
    return jax.ShapeDtypeStruct(extent, kind)


def local(inputs, cotangent, mode_weight, local_weight):
    tiles = lax.axis_size("tile")
    samples, channels, th, width = inputs.shape
    owned, _, _, both = mode_weight.shape
    modes = both // 2
    lanes = samples * channels
    parts = width // 128
    spec_scale = 1.0 / math.sqrt(tiles * th * width)
    mode_scale = 1.0 / math.sqrt(modes * tiles * owned)
    send_cols, rows, back_rows, back_cols = tables(tiles, owned, th, width, modes)
    pixel_rows = samples * channels * th
    halves = tiles * padded(2 * owned)
    inverse = 2 * tiles * th

    def exchange(values):
        split = values.reshape(tiles, values.shape[0] // tiles, values.shape[1])
        moved = lax.all_to_all(split, "tile", split_axis=0, concat_axis=0, tiled=False)
        return moved.reshape(values.shape)

    forward_mix = block_diagonal(local_weight.T, samples)
    backward_mix = block_diagonal(local_weight, samples)
    by_row = order(PACK, th)
    by_channel = order(th, PACK)
    by_mode = mode_order(tiles, owned)
    by_height = order(2 * min(tiles, 8), th)
    flat_weight = mode_weight.reshape(-1, both)
    weight_block = pl.BlockSpec((flat_weight.shape[0] // owned, both), lambda q: (q, 0))
    weight_scratch = [pltpu.VMEM(flat_weight.shape, BF16), pltpu.SemaphoreType.DMA((owned,))]
    in_place = pl.BlockSpec(memory_space=pl.ANY)
    to_modes = shape((halves, th * lanes))
    to_pixels = shape((inverse, owned * lanes))
    field_shape = shape((th, lanes, width))

    def kept(*operands):
        return [pltpu.VMEM(operand.shape, operand.dtype) for operand in operands]

    def early(*operands):
        return kept(*operands) + [pltpu.SemaphoreType.DMA((len(operands),))]

    def field_blocks(first):
        return {first + n: pl.BlockSpec((pixel_rows // SPLIT, width), lambda _, n=n: (n, 0)) for n in range(SPLIT)}

    field_rows, send = call(
        columns_kernel,
        "columns",
        (by_row, send_cols, *[inputs.reshape(pixel_rows, width)] * SPLIT),
        (field_shape, to_modes),
        blocks=field_blocks(2),
    )
    arrived = exchange(send)
    (cot_rows,) = call(
        relayout_kernel,
        "relayout",
        (by_row, *[cotangent.reshape(pixel_rows, width)] * SPLIT),
        (field_shape,),
        blocks=field_blocks(1),
    )
    spectra, send = call(
        functools.partial(forward_kernel, spec_scale, samples, owned),
        "mix_forward",
        (arrived, by_mode, rows, back_rows, flat_weight),
        (shape((owned * lanes, both)), to_pixels),
        [
            pltpu.VMEM((owned * lanes, both), F32),
            pltpu.VMEM((owned * lanes, both), F32),
            pltpu.VMEM((owned, 2 * samples, channels, both), F32),
            *weight_scratch,
            *early(arrived, by_mode, rows, back_rows),
            pltpu.VMEM((inverse, owned * lanes), BF16),
            pltpu.SemaphoreType.DMA((owned,)),
        ],
        grid=(owned,),
        blocks={n: in_place for n in range(5)},
        out_blocks={1: in_place},
    )
    all_spectra = gather_far(gather_near(spectra, "dp"), "dp")
    arrived = exchange(send)
    steps = 4
    row_block = pl.BlockSpec((steps, lanes, width), lambda n: (n, 0, 0))
    gate_rows, send, local_sum = call(
        functools.partial(pixels_kernel, mode_scale, th),
        "pixels",
        (arrived, by_height, back_cols, forward_mix, field_rows, cot_rows, send_cols),
        (field_shape, to_modes, shape((channels, channels), F32)),
        [pltpu.VMEM((inverse, owned * lanes), BF16), pltpu.VMEM((lanes, lanes), F32)],
        grid=(th // steps,),
        blocks={4: row_block, 5: row_block},
        out_blocks={0: row_block, 1: pl.BlockSpec((halves, steps * lanes), lambda n: (0, n))},
        limit=SMALL,
    )
    send, *all_spectra = lax.optimization_barrier((send, *all_spectra))
    arrived, local_sum = lax.optimization_barrier((exchange(send), sum_over(local_sum, "dp")))
    (grad_spectra,) = call(
        functools.partial(spectra_kernel, mode_scale, owned, lanes),
        "grad_spectra",
        (arrived, by_mode, rows),
        (shape((owned * lanes, both)),),
        limit=SMALL,
    )
    near = gather_near(grad_spectra, "dp")
    carried = channels * channels * tiles // inverse
    (send,) = call(
        functools.partial(backward_kernel, samples, tiles),
        "mix_backward",
        (grad_spectra, back_rows, local_sum, flat_weight),
        (shape((inverse, owned * lanes + carried)),),
        [
            pltpu.VMEM((owned * lanes, both), BF16),
            pltpu.VMEM((owned * lanes, both), BF16),
            pltpu.VMEM((owned, 2 * samples, channels * ROWS, both), F32),
            *weight_scratch,
            *early(grad_spectra, back_rows, local_sum),
            pltpu.VMEM((inverse, owned * lanes + carried), BF16),
            pltpu.SemaphoreType.DMA((owned,)),
        ],
        grid=(owned,),
        blocks={n: in_place for n in range(4)},
        out_blocks={0: in_place},
    )
    send, near = lax.optimization_barrier((send, near))
    all_grads = gather_far(near, "dp")
    arrived = exchange(send)

    groups = lax.axis_size("dp")
    total = groups * samples
    per_mode = pl.BlockSpec((lanes, both), lambda q: (q, 0))
    (mode_grad,) = call(
        functools.partial(outer_kernel, samples, groups),
        "mode_grad",
        (*all_spectra, *all_grads),
        (shape(flat_weight.shape, F32),),
        [pltpu.VMEM((total, channels, both), F32)] * 2 + [pltpu.VMEM((total, channels, both), BF16)],
        grid=(owned,),
        blocks={n: per_mode for n in range(2 * groups)},
        out_blocks={0: weight_block},
    )
    arrived, mode_grad = lax.optimization_barrier((arrived, mode_grad))

    input_grad, local_grad = call(
        functools.partial(final_kernel, spec_scale, tiles),
        "final",
        (arrived, by_height, back_cols, backward_mix, gate_rows, by_channel),
        (shape((pixel_rows, width)), shape((channels, channels), F32)),
        [pltpu.VMEM((th, lanes, width), BF16)],
        limit=SMALL,
    )
    return (input_grad.reshape(inputs.shape), mode_grad.reshape(mode_weight.shape), local_grad)


def solution(mesh):
    return jax.shard_map(
        local,
        mesh=mesh,
        in_specs=(
            P("dp", None, "tile", None),
            P("dp", None, "tile", None),
            P("tile", None, None, None),
            P(),
        ),
        out_specs=(P("dp", None, "tile", None), P("tile", None, None, None), P()),
        check_vma=False,
    )
```

```python
import functools
import math

import jax
import jax.numpy as jnp
import numpy as np
from jax import lax
from jax.experimental import pallas as pl
from jax.experimental.pallas import tpu as pltpu
from jax.sharding import PartitionSpec as P

F32 = jnp.float32
BF16 = jnp.bfloat16
LIMIT = 56 * 1024 * 1024
SMALL = 24 * 1024 * 1024
ROWS = 8
PACK = 16
GROUP = 8
SPLIT = 4
AHEAD = 3


def row_tables(height, modes):
    index = np.arange(modes)
    signed = np.where(index < modes // 2, index, index - modes)
    phases = np.mod(np.arange(height)[:, None] * signed[None, :], height)
    angles = phases * (2.0 * math.pi / height)
    return np.cos(angles), np.sin(angles)


def column_tables(width, modes):
    phases = np.mod(np.arange(modes)[:, None] * np.arange(width)[None, :], width)
    angles = phases * (2.0 * math.pi / width)
    return np.stack([np.cos(angles), -np.sin(angles)])


def constant(table):
    return jnp.asarray(np.asarray(table, np.float32)).astype(BF16)


def tables(tiles, owned, th, width, modes):
    cols = column_tables(width, tiles * owned)
    split = cols.reshape(2, tiles, owned, width)
    send_cols = split.transpose(1, 0, 2, 3).reshape(tiles, 2 * owned, width)
    send_cols = np.pad(send_cols, ((0, 0), (0, padded(2 * owned) - 2 * owned), (0, 0))).reshape(-1, width)
    back_cols = split.transpose(2, 1, 0, 3).reshape(-1, width)
    cosine, sine = row_tables(th * tiles, modes)
    real = np.concatenate([cosine, -sine], axis=1)
    imag = np.concatenate([sine, cosine], axis=1)
    pair = np.stack([real, imag]).reshape(2, tiles, th, 2 * modes)
    rows = pair.transpose(2, 1, 0, 3).reshape(-1, 2 * modes)
    back_rows = pair.transpose(1, 0, 2, 3).reshape(-1, 2 * modes)
    return constant(send_cols), constant(rows), constant(back_rows), constant(back_cols)


def padded(rows):
    return -(-rows // PACK) * PACK


def order(outer, inner):
    take = np.arange(outer * inner).reshape(outer, inner).T.reshape(-1)
    return constant(np.eye(outer * inner)[take])


def mode_order(tiles, owned):
    rows = np.arange(tiles * padded(2 * owned)).reshape(tiles, -1)
    take = rows[:, : 2 * owned].reshape(tiles, 2, owned).transpose(2, 0, 1).reshape(-1)
    return constant(np.eye(rows.size)[take])


def dot(left, right, dims):
    return lax.dot_general(left, right, (dims, ((), ())), preferred_element_type=F32)


def low_half(shape, half):
    return lax.broadcasted_iota(jnp.int32, shape, 1) < half


def gelu_slope(values):
    size = jnp.abs(values)
    expo = jnp.exp(-0.5 * values * values)
    t = 1.0 / (1.0 + (0.3275911 / math.sqrt(2.0)) * size)
    poly = 0.5 * 1.061405429
    for factor in (-1.453152027, 1.421413741, -0.284496736, 0.254829592):
        poly = poly * t + 0.5 * factor
    tail = poly * t * expo
    cumulative = jnp.where(values < 0.0, tail, 1.0 - tail)
    return cumulative + values * expo * (1.0 / math.sqrt(2.0 * math.pi))


def shuffle(order_ref, value):
    return dot(order_ref[...], value, ((1,), (0,))).astype(BF16)


def by_rows(order_ref, field_refs, rows_ref):
    heights, lanes, _ = rows_ref.shape
    block = PACK * heights
    quarter = lanes // len(field_refs)
    for first in range(0, lanes, PACK):
        start = first % quarter * heights
        moved = shuffle(order_ref, field_refs[first // quarter][start : start + block, :])
        for h in range(heights):
            rows_ref[h, first : first + PACK, :] = moved[h * PACK : (h + 1) * PACK]


def columns_kernel(order_ref, table_ref, *rest):
    field_refs, (rows_ref, send_ref) = rest[:SPLIT], rest[SPLIT:]
    heights, lanes, _ = rows_ref.shape
    by_rows(order_ref, field_refs, rows_ref)
    for h in range(heights):
        send_ref[:, h * lanes : (h + 1) * lanes] = dot(table_ref[...], rows_ref[h], ((1,), (1,))).astype(BF16)


def relayout_kernel(order_ref, *rest):
    by_rows(order_ref, rest[:SPLIT], rest[SPLIT])


def shuffle_groups(order_ref, recv_ref, width):
    size = order_ref.shape[0]
    return [shuffle(order_ref, recv_ref[n : n + size, :width]) for n in range(0, recv_ref.shape[0], size)]


def stack(groups, index, count, lanes):
    return jnp.concatenate(
        [
            group[index * count : (index + 1) * count, n : n + lanes]
            for n in range(0, groups[0].shape[1], lanes)
            for group in groups
        ],
        axis=0,
    )


def spectra_into(scale, owned, lanes, recv_ref, order_ref, rows_ref, spec_ref):
    count = order_ref.shape[0] // owned
    fields = rows_ref.shape[0] // count * lanes
    ordered = [shuffle(order_ref, recv_ref[:, :fields])]
    for q in range(owned):
        stacked = stack(ordered, q, count, lanes)
        spec_ref[q * lanes : (q + 1) * lanes, :] = (
            scale * dot(stacked, rows_ref[...], ((0,), (0,)))
        ).astype(BF16)


def to_piece(value, rows):
    return jnp.concatenate([value[n : n + rows] for n in range(0, value.shape[0], rows)], axis=1)


def from_piece(value, extent):
    return jnp.concatenate([value[:, n : n + extent] for n in range(0, value.shape[1], extent)], axis=0)


def spectra_kernel(scale, owned, lanes, recv_ref, order_ref, rows_ref, spec_ref):
    spectra_into(scale, owned, lanes, recv_ref, order_ref, rows_ref, spec_ref)


def running(pairs):
    waiting = []
    for left, right in pairs:
        value, level = left * right, 0
        while waiting and waiting[-1][1] == level:
            value, level = waiting.pop()[0] + value, level + 1
        waiting.append((value, level))
    return sum((value for value, _ in reversed(waiting[:-1])), waiting[-1][0])


def rows_of(store, block, extent):
    return store.at[pl.ds(pl.multiple_of(block * extent, extent), extent), :]


def packed_row(view, index):
    row = view[index : index + 1, :]
    return jnp.broadcast_to(row, (PACK, row.shape[1])).astype(BF16)


def duplicates(spec, half):
    value = spec.astype(F32)
    other = pltpu.roll(value, half, 1)
    low = low_half(value.shape, half)
    return jnp.where(low, value, other), jnp.where(low, other, value)


def finish(back_ref, sums, send_ref, stage, sems, mix):
    @pl.when(pl.program_id(0) == pl.num_programs(0) - 1)
    def _():
        moves = []
        for q in range(sums.shape[0]):
            mixed = mix(sums.at[q]).astype(BF16)
            column = pl.ds(q * mixed.shape[0], mixed.shape[0])
            stage[:, column] = dot(back_ref[...], mixed, ((1,), (1,))).astype(BF16)
            moves.append(pltpu.make_async_copy(stage.at[:, column], send_ref.at[:, column], sems.at[q]))
            moves[-1].start()
        for move in moves:
            move.wait()


def fetch(sources, targets, sems):
    moves = [
        pltpu.make_async_copy(source, target, sems.at[n]) for n, (source, target) in enumerate(zip(sources, targets))
    ]

    @pl.when(pl.program_id(0) == 0)
    def _():
        for move in moves:
            move.start()

    return moves


def fetch_weights(moves, source_ref, weights, sems):
    q = pl.program_id(0)
    owned = sems.shape[0]
    size = weights.shape[0] // owned

    def move(mode):
        part = pl.ds(pl.multiple_of(mode * size, size), size)
        return pltpu.make_async_copy(source_ref.at[part, :], weights.at[part, :], sems.at[mode])

    @pl.when(q == 0)
    def _():
        move(0).start()
        for early in moves:
            early.wait()
        for mode in range(1, min(AHEAD, owned)):
            move(mode).start()

    @pl.when(q + AHEAD < owned)
    def _():
        move(q + AHEAD).start()

    return move(q), weights.at[pl.ds(pl.multiple_of(q * size, size), size), :]


def forward_kernel(scale, samples, owned, *rest):
    sources, source_ref, spec_ref, send_ref, real, imag, sums, weights, sems = rest[:4], *rest[4:12]
    targets, early, stage, late = rest[12:16], *rest[16:19]
    recv_ref, order_ref, rows_ref, back_ref = targets
    _, _, outs, both = sums.shape
    channels = weights.shape[0] // outs // owned
    half = both // 2
    lanes = samples * channels
    q = pl.program_id(0)
    moves = fetch(sources, targets, early)
    coming, weight_ref = fetch_weights(moves, source_ref, weights, sems)

    @pl.when(q == 0)
    def _():
        spectra_into(scale, owned, lanes, recv_ref, order_ref, rows_ref, spec_ref)
        real[...], imag[...] = duplicates(spec_ref[...], half)
        sums[...] = jnp.zeros_like(sums)

    coming.wait()

    def body(block, carry):
        view = rows_of(weight_ref, block, GROUP * outs)
        into = sums.at[q]
        for s in range(samples):
            rows = []
            for store in (real, imag):
                part = rows_of(store, (q * lanes + s * channels) // GROUP + block, GROUP)[...]
                rows.append([packed_row(part, step) for step in range(GROUP)])
            for o in range(0, outs, PACK):
                column = [view[step * outs + o : step * outs + o + PACK, :] for step in range(GROUP)]
                for n, row in enumerate(rows):
                    into[2 * s + n, o : o + PACK, :] += running([(w, r) for w, r in zip(column, row)]).astype(F32)
        return carry

    lax.fori_loop(0, channels // GROUP, body, 0)

    def mix(parts):
        low = low_half((outs, both), half)
        result = []
        for s in range(samples):
            crossed = pltpu.roll(parts[2 * s + 1], half, 1)
            result.append(parts[2 * s] + jnp.where(low, -crossed, crossed))
        return jnp.concatenate(result, axis=0)

    finish(back_ref, sums, send_ref, stage, late, mix)


def backward_kernel(samples, tiles, *rest):
    sources, source_ref, send_ref, real, imag, sums, weights, sems = rest[:3], *rest[3:10]
    targets, early, stage, late = rest[10:13], *rest[13:16]
    spec_ref, back_ref, local_ref = targets

    def carried():
        column = pl.ds(sums.shape[0] * lanes, stage.shape[1] - sums.shape[0] * lanes)
        return pltpu.make_async_copy(stage.at[:, column], send_ref.at[:, column], late.at[0])

    channels, both = sums.shape[2] // ROWS, sums.shape[3]
    outs = weights.shape[0] // channels // sums.shape[0]
    half = both // 2
    lanes = samples * outs
    q = pl.program_id(0)
    moves = fetch(sources, targets, early)
    coming, weight_ref = fetch_weights(moves, source_ref, weights, sems)

    @pl.when(q == 0)
    def _():
        first, second = duplicates(spec_ref[...], half)
        real[...], imag[...] = first.astype(BF16), second.astype(BF16)
        extent = stage.shape[0] // tiles
        partial = to_piece(local_ref[...].astype(BF16), extent)
        for n in range(0, stage.shape[0], extent):
            stage[n : n + extent, sums.shape[0] * lanes :] = partial
        move = carried()
        move.start()
        move.wait()

    coming.wait()
    grads = [
        [store[pl.ds(pl.multiple_of(q * lanes + s * outs + o, PACK), PACK), :] for o in range(0, outs, PACK)]
        for s in range(samples)
        for store in (real, imag)
    ]

    def body(block, carry):
        view = rows_of(weight_ref, block, GROUP * outs)
        into = [rows_of(sums.at[q, n], block, GROUP * ROWS) for n in range(len(grads))]
        for first in range(0, GROUP, 4):
            totals = []
            for step in range(first, first + 4):
                column = [view[step * outs + o : step * outs + o + PACK, :] for o in range(0, outs, PACK)]
                for n, grad in enumerate(grads):
                    total = running([(w, g) for w, g in zip(column, grad)]).astype(F32)
                    totals.append((n, step, total[:ROWS] + total[ROWS:]))
            for n, step, total in totals:
                into[n][step * ROWS : (step + 1) * ROWS, :] = total
        return carry

    lax.fori_loop(0, channels // GROUP, body, 0)

    def mix(parts):
        low = low_half((channels, both), half)
        result = []
        for s in range(samples):
            straight, crossed = (
                sum(parts[n, pl.ds(row, channels, stride=ROWS), :] for row in range(ROWS)) for n in (2 * s, 2 * s + 1)
            )
            result.append(jnp.where(low, straight, -straight) + pltpu.roll(crossed, half, 1))
        return jnp.concatenate(result, axis=0)

    finish(back_ref, sums, send_ref, stage, late, mix)


def pixels_kernel(scale, heights, recv_ref, order_ref, back_ref, local_ref, field_ref, cot_ref, table_ref, *rest):
    grad_ref, send_ref, sum_ref, ordered, total = rest
    steps, lanes, _ = field_ref.shape
    count = order_ref.shape[0] // heights
    size = order_ref.shape[0]
    group = pl.program_id(0)

    @pl.when(group == 0)
    def _():
        for n in range(0, recv_ref.shape[0], size):
            ordered[n : n + size, :] = shuffle(order_ref, recv_ref[n : n + size, :])
        total[...] = jnp.zeros_like(total)

    local = jnp.zeros(total.shape, F32)
    for step in range(steps):
        parts = []
        for n in range(0, recv_ref.shape[0], size):
            first = pl.multiple_of(n + (group * steps + step) * count, count)
            parts.append(ordered[pl.ds(first, count), :])
        inner = stack(parts, 0, count, lanes)
        pre = scale * dot(inner, back_ref[...], ((0,), (0,)))
        pre = pre + dot(local_ref[...], field_ref[step], ((1,), (0,)))
        grad = (cot_ref[step].astype(F32) * gelu_slope(pre)).astype(BF16)
        grad_ref[step] = grad
        send_ref[:, step * lanes : (step + 1) * lanes] = dot(table_ref[...], grad, ((1,), (1,))).astype(BF16)
        local = local + dot(field_ref[step], grad, ((1,), (1,)))
    total[...] += local

    @pl.when(group == pl.num_programs(0) - 1)
    def _():
        extent = sum_ref.shape[0]
        sum_ref[...] = sum(total[n : n + extent, n : n + extent] for n in range(0, lanes, extent))


def final_kernel(scale, tiles, recv_ref, order_ref, back_ref, local_ref, grad_ref, restore_ref, *rest):
    out_ref, sum_ref, result = rest
    heights, lanes, _ = grad_ref.shape
    extent = recv_ref.shape[0] // tiles
    first = back_ref.shape[0] // (2 * tiles) * lanes
    partials = sum(recv_ref[n : n + extent, first:].astype(F32) for n in range(0, recv_ref.shape[0], extent))
    sum_ref[...] = from_piece(partials, sum_ref.shape[1])
    count = order_ref.shape[0] // heights
    ordered = shuffle_groups(order_ref, recv_ref, first)
    for h in range(heights):
        inner = stack(ordered, h, count, lanes)
        value = scale * dot(inner, back_ref[...], ((0,), (0,)))
        result[h] = (value + dot(local_ref[...], grad_ref[h], ((1,), (0,)))).astype(BF16)
    block = PACK * heights
    for first in range(0, lanes, PACK):
        part = jnp.concatenate([result[h, first : first + PACK, :] for h in range(heights)], axis=0)
        out_ref[first * heights : first * heights + block, :] = shuffle(restore_ref, part)


def outer_kernel(samples, groups, *refs):
    specs, grads = refs[:groups], refs[groups : 2 * groups]
    out_ref, real, imag, crossed = refs[2 * groups :]
    total, channels, both = real.shape
    outs = crossed.shape[1]
    half = both // 2
    low = low_half((channels, both), half)

    for g in range(groups):
        for s in range(samples):
            n = g * samples + s
            spec = specs[g][s * channels : (s + 1) * channels, :].astype(F32)
            other = pltpu.roll(spec, half, 1)
            real[n] = jnp.where(low, spec, other)
            imag[n] = jnp.where(low, other, -spec)
            grad = grads[g][s * outs : (s + 1) * outs, :]
            crossed[n] = pltpu.roll(grad.astype(F32), half, 1).astype(BF16)

    def body(block, carry):
        into = rows_of(out_ref, block, GROUP * outs)
        views = [rows_of(store.at[n], block, GROUP)[...] for n in range(total) for store in (real, imag)]
        for first in range(0, GROUP, 2):
            pair = range(first, first + 2)
            lefts = [[packed_row(view, c) for view in views] for c in pair]
            for o in range(0, outs, PACK):
                right = []
                for n in range(total):
                    at = n % samples * outs + o
                    right += [grads[n // samples][at : at + PACK, :], crossed[n, o : o + PACK, :]]
                results = [running(list(zip(left, right))) for left in lefts]
                for c, result in zip(pair, results):
                    into[c * outs + o : c * outs + o + PACK, :] = result.astype(F32)
        return carry

    lax.fori_loop(0, channels // GROUP, body, 0)


def whole(extent):
    return pl.BlockSpec(extent, lambda *_: (0,) * len(extent))


def call(kernel, name, operands, outs, scratch=(), grid=(1,), blocks=None, out_blocks=None, limit=LIMIT):
    blocks, out_blocks = blocks or {}, out_blocks or {}
    in_specs = [blocks.get(n) or whole(operand.shape) for n, operand in enumerate(operands)]
    out_specs = [out_blocks.get(n, whole(out.shape)) for n, out in enumerate(outs)]
    return pl.pallas_call(
        kernel,
        out_shape=tuple(outs),
        grid=grid,
        in_specs=in_specs,
        out_specs=tuple(out_specs),
        scratch_shapes=list(scratch),
        compiler_params=pltpu.CompilerParams(vmem_limit_bytes=limit),
        name=name,
    )(*operands)


def swap(values, axis, step):
    return lax.ppermute(values, axis, [(i, i ^ step) for i in range(lax.axis_size(axis))])


def gather_near(values, axis):
    size = lax.axis_size(axis)
    return {0: values} | {1 << bit: swap(values, axis, 1 << bit) for bit in range(size.bit_length() - 1)}


def gather_far(near, axis):
    whole_set = dict(near)
    for step in range(1, lax.axis_size(axis)):
        if step not in whole_set:
            whole_set[step] = swap(whole_set[step & (step - 1)], axis, step & -step)
    return [whole_set[step] for step in sorted(whole_set)]


def sum_over(values, axis):
    step = 1
    while step < lax.axis_size(axis):
        values = values + swap(values, axis, step)
        step *= 2
    return values


def block_diagonal(matrix, copies):
    zero = jnp.zeros_like(matrix)
    return jnp.concatenate(
        [
            jnp.concatenate([matrix if i == j else zero for j in range(copies)], axis=1)
            for i in range(copies)
        ],
        axis=0,
    )


def shape(extent, kind=BF16):
    return jax.ShapeDtypeStruct(extent, kind)


def local(inputs, cotangent, mode_weight, local_weight):
    tiles = lax.axis_size("tile")
    samples, channels, th, width = inputs.shape
    owned, _, _, both = mode_weight.shape
    modes = both // 2
    lanes = samples * channels
    parts = width // 128
    spec_scale = 1.0 / math.sqrt(tiles * th * width)
    mode_scale = 1.0 / math.sqrt(modes * tiles * owned)
    send_cols, rows, back_rows, back_cols = tables(tiles, owned, th, width, modes)
    pixel_rows = samples * channels * th
    halves = tiles * padded(2 * owned)
    inverse = 2 * tiles * th

    def exchange(values):
        split = values.reshape(tiles, values.shape[0] // tiles, values.shape[1])
        moved = lax.all_to_all(split, "tile", split_axis=0, concat_axis=0, tiled=False)
        return moved.reshape(values.shape)

    forward_mix = block_diagonal(local_weight.T, samples)
    backward_mix = block_diagonal(local_weight, samples)
    by_row = order(PACK, th)
    by_channel = order(th, PACK)
    by_mode = mode_order(tiles, owned)
    by_height = order(2 * min(tiles, 8), th)
    flat_weight = mode_weight.reshape(-1, both)
    weight_block = pl.BlockSpec((flat_weight.shape[0] // owned, both), lambda q: (q, 0))
    weight_scratch = [pltpu.VMEM(flat_weight.shape, BF16), pltpu.SemaphoreType.DMA((owned,))]
    in_place = pl.BlockSpec(memory_space=pl.ANY)
    to_modes = shape((halves, th * lanes))
    to_pixels = shape((inverse, owned * lanes))
    field_shape = shape((th, lanes, width))

    def kept(*operands):
        return [pltpu.VMEM(operand.shape, operand.dtype) for operand in operands]

    def early(*operands):
        return kept(*operands) + [pltpu.SemaphoreType.DMA((len(operands),))]

    def field_blocks(first):
        return {first + n: pl.BlockSpec((pixel_rows // SPLIT, width), lambda _, n=n: (n, 0)) for n in range(SPLIT)}

    field_rows, send = call(
        columns_kernel,
        "columns",
        (by_row, send_cols, *[inputs.reshape(pixel_rows, width)] * SPLIT),
        (field_shape, to_modes),
        blocks=field_blocks(2),
    )
    (cot_rows,) = call(
        relayout_kernel,
        "relayout",
        (by_row, *[cotangent.reshape(pixel_rows, width)] * SPLIT),
        (field_shape,),
        blocks=field_blocks(1),
    )
    arrived, cot_rows = lax.optimization_barrier((exchange(send), cot_rows))
    spectra, send = call(
        functools.partial(forward_kernel, spec_scale, samples, owned),
        "mix_forward",
        (arrived, by_mode, rows, back_rows, flat_weight),
        (shape((owned * lanes, both)), to_pixels),
        [
            pltpu.VMEM((owned * lanes, both), F32),
            pltpu.VMEM((owned * lanes, both), F32),
            pltpu.VMEM((owned, 2 * samples, channels, both), F32),
            *weight_scratch,
            *early(arrived, by_mode, rows, back_rows),
            pltpu.VMEM((inverse, owned * lanes), BF16),
            pltpu.SemaphoreType.DMA((owned,)),
        ],
        grid=(owned,),
        blocks={n: in_place for n in range(5)},
        out_blocks={1: in_place},
    )
    all_spectra = gather_far(gather_near(spectra, "dp"), "dp")
    arrived = exchange(send)
    steps = 4
    row_block = pl.BlockSpec((steps, lanes, width), lambda n: (n, 0, 0))
    gate_rows, send, local_sum = call(
        functools.partial(pixels_kernel, mode_scale, th),
        "pixels",
        (arrived, by_height, back_cols, forward_mix, field_rows, cot_rows, send_cols),
        (field_shape, to_modes, shape((channels, channels), F32)),
        [pltpu.VMEM((inverse, owned * lanes), BF16), pltpu.VMEM((lanes, lanes), F32)],
        grid=(th // steps,),
        blocks={4: row_block, 5: row_block},
        out_blocks={0: row_block, 1: pl.BlockSpec((halves, steps * lanes), lambda n: (0, n))},
        limit=SMALL,
    )
    send, *all_spectra = lax.optimization_barrier((send, *all_spectra))
    arrived, local_sum = lax.optimization_barrier((exchange(send), sum_over(local_sum, "dp")))
    (grad_spectra,) = call(
        functools.partial(spectra_kernel, mode_scale, owned, lanes),
        "grad_spectra",
        (arrived, by_mode, rows),
        (shape((owned * lanes, both)),),
        limit=SMALL,
    )
    near = gather_near(grad_spectra, "dp")
    carried = channels * channels * tiles // inverse
    (send,) = call(
        functools.partial(backward_kernel, samples, tiles),
        "mix_backward",
        (grad_spectra, back_rows, local_sum, flat_weight),
        (shape((inverse, owned * lanes + carried)),),
        [
            pltpu.VMEM((owned * lanes, both), BF16),
            pltpu.VMEM((owned * lanes, both), BF16),
            pltpu.VMEM((owned, 2 * samples, channels * ROWS, both), F32),
            *weight_scratch,
            *early(grad_spectra, back_rows, local_sum),
            pltpu.VMEM((inverse, owned * lanes + carried), BF16),
            pltpu.SemaphoreType.DMA((owned,)),
        ],
        grid=(owned,),
        blocks={n: in_place for n in range(4)},
        out_blocks={0: in_place},
    )
    send, near = lax.optimization_barrier((send, near))
    send, *all_grads = lax.optimization_barrier((send, *gather_far(near, "dp")))
    arrived = exchange(send)

    groups = lax.axis_size("dp")
    total = groups * samples
    per_mode = pl.BlockSpec((lanes, both), lambda q: (q, 0))
    (mode_grad,) = call(
        functools.partial(outer_kernel, samples, groups),
        "mode_grad",
        (*all_spectra, *all_grads),
        (shape(flat_weight.shape, F32),),
        [pltpu.VMEM((total, channels, both), F32)] * 2 + [pltpu.VMEM((total, channels, both), BF16)],
        grid=(owned,),
        blocks={n: per_mode for n in range(2 * groups)},
        out_blocks={0: weight_block},
    )
    arrived, mode_grad = lax.optimization_barrier((arrived, mode_grad))

    input_grad, local_grad = call(
        functools.partial(final_kernel, spec_scale, tiles),
        "final",
        (arrived, by_height, back_cols, backward_mix, gate_rows, by_channel),
        (shape((pixel_rows, width)), shape((channels, channels), F32)),
        [pltpu.VMEM((th, lanes, width), BF16)],
        limit=SMALL,
    )
    return (input_grad.reshape(inputs.shape), mode_grad.reshape(mode_weight.shape), local_grad)


def solution(mesh):
    return jax.shard_map(
        local,
        mesh=mesh,
        in_specs=(
            P("dp", None, "tile", None),
            P("dp", None, "tile", None),
            P("tile", None, None, None),
            P(),
        ),
        out_specs=(P("dp", None, "tile", None), P("tile", None, None, None), P()),
        check_vma=False,
    )
```

```python
import functools
import math

import jax
import jax.numpy as jnp
import numpy as np
from jax import lax
from jax.experimental import pallas as pl
from jax.experimental.pallas import tpu as pltpu
from jax.sharding import PartitionSpec as P

F32 = jnp.float32
BF16 = jnp.bfloat16
LIMIT = 56 * 1024 * 1024
SMALL = 24 * 1024 * 1024
ROWS = 8
PACK = 16
GROUP = 8
SPLIT = 4
AHEAD = 3


def row_tables(height, modes):
    index = np.arange(modes)
    signed = np.where(index < modes // 2, index, index - modes)
    phases = np.mod(np.arange(height)[:, None] * signed[None, :], height)
    angles = phases * (2.0 * math.pi / height)
    return np.cos(angles), np.sin(angles)


def column_tables(width, modes):
    phases = np.mod(np.arange(modes)[:, None] * np.arange(width)[None, :], width)
    angles = phases * (2.0 * math.pi / width)
    return np.stack([np.cos(angles), -np.sin(angles)])


def constant(table):
    return jnp.asarray(np.asarray(table, np.float32)).astype(BF16)


def tables(tiles, owned, th, width, modes):
    cols = column_tables(width, tiles * owned)
    split = cols.reshape(2, tiles, owned, width)
    send_cols = split.transpose(1, 0, 2, 3).reshape(tiles, 2 * owned, width)
    send_cols = np.pad(send_cols, ((0, 0), (0, padded(2 * owned) - 2 * owned), (0, 0))).reshape(-1, width)
    back_cols = split.transpose(2, 1, 0, 3).reshape(-1, width)
    cosine, sine = row_tables(th * tiles, modes)
    real = np.concatenate([cosine, -sine], axis=1)
    imag = np.concatenate([sine, cosine], axis=1)
    pair = np.stack([real, imag]).reshape(2, tiles, th, 2 * modes)
    rows = pair.transpose(2, 1, 0, 3).reshape(-1, 2 * modes)
    back_rows = pair.transpose(1, 0, 2, 3).reshape(-1, 2 * modes)
    return constant(send_cols), constant(rows), constant(back_rows), constant(back_cols)


def padded(rows):
    return -(-rows // PACK) * PACK


def order(outer, inner):
    take = np.arange(outer * inner).reshape(outer, inner).T.reshape(-1)
    return constant(np.eye(outer * inner)[take])


def mode_order(tiles, owned):
    rows = np.arange(tiles * padded(2 * owned)).reshape(tiles, -1)
    take = rows[:, : 2 * owned].reshape(tiles, 2, owned).transpose(2, 0, 1).reshape(-1)
    return constant(np.eye(rows.size)[take])


def dot(left, right, dims):
    return lax.dot_general(left, right, (dims, ((), ())), preferred_element_type=F32)


def low_half(shape, half):
    return lax.broadcasted_iota(jnp.int32, shape, 1) < half


def gelu_slope(values):
    size = jnp.abs(values)
    expo = jnp.exp(-0.5 * values * values)
    t = 1.0 / (1.0 + (0.3275911 / math.sqrt(2.0)) * size)
    poly = 0.5 * 1.061405429
    for factor in (-1.453152027, 1.421413741, -0.284496736, 0.254829592):
        poly = poly * t + 0.5 * factor
    tail = poly * t * expo
    cumulative = jnp.where(values < 0.0, tail, 1.0 - tail)
    return cumulative + values * expo * (1.0 / math.sqrt(2.0 * math.pi))


def shuffle(order_ref, value):
    return dot(order_ref[...], value, ((1,), (0,))).astype(BF16)


def by_rows(order_ref, field_refs, rows_ref):
    heights, lanes, _ = rows_ref.shape
    block = PACK * heights
    quarter = lanes // len(field_refs)
    for first in range(0, lanes, PACK):
        start = first % quarter * heights
        moved = shuffle(order_ref, field_refs[first // quarter][start : start + block, :])
        for h in range(heights):
            rows_ref[h, first : first + PACK, :] = moved[h * PACK : (h + 1) * PACK]


def columns_kernel(order_ref, table_ref, *rest):
    field_refs, (rows_ref, send_ref) = rest[:SPLIT], rest[SPLIT:]
    heights, lanes, _ = rows_ref.shape
    by_rows(order_ref, field_refs, rows_ref)
    for h in range(heights):
        send_ref[:, h * lanes : (h + 1) * lanes] = dot(table_ref[...], rows_ref[h], ((1,), (1,))).astype(BF16)


def relayout_kernel(order_ref, *rest):
    by_rows(order_ref, rest[:SPLIT], rest[SPLIT])


def shuffle_groups(order_ref, recv_ref, width):
    size = order_ref.shape[0]
    return [shuffle(order_ref, recv_ref[n : n + size, :width]) for n in range(0, recv_ref.shape[0], size)]


def stack(groups, index, count, lanes):
    return jnp.concatenate(
        [
            group[index * count : (index + 1) * count, n : n + lanes]
            for n in range(0, groups[0].shape[1], lanes)
            for group in groups
        ],
        axis=0,
    )


def spectra_into(scale, owned, lanes, recv_ref, order_ref, rows_ref, spec_ref):
    count = order_ref.shape[0] // owned
    fields = rows_ref.shape[0] // count * lanes
    ordered = [shuffle(order_ref, recv_ref[:, :fields])]
    for q in range(owned):
        stacked = stack(ordered, q, count, lanes)
        spec_ref[q * lanes : (q + 1) * lanes, :] = (
            scale * dot(stacked, rows_ref[...], ((0,), (0,)))
        ).astype(BF16)


def to_piece(value, rows):
    return jnp.concatenate([value[n : n + rows] for n in range(0, value.shape[0], rows)], axis=1)


def from_piece(value, extent):
    return jnp.concatenate([value[:, n : n + extent] for n in range(0, value.shape[1], extent)], axis=0)


def spectra_kernel(scale, owned, lanes, recv_ref, order_ref, rows_ref, spec_ref):
    spectra_into(scale, owned, lanes, recv_ref, order_ref, rows_ref, spec_ref)


def running(pairs):
    waiting = []
    for left, right in pairs:
        value, level = left * right, 0
        while waiting and waiting[-1][1] == level:
            value, level = waiting.pop()[0] + value, level + 1
        waiting.append((value, level))
    return sum((value for value, _ in reversed(waiting[:-1])), waiting[-1][0])


def rows_of(store, block, extent):
    return store.at[pl.ds(pl.multiple_of(block * extent, extent), extent), :]


def packed_row(view, index):
    row = view[index : index + 1, :]
    return jnp.broadcast_to(row, (PACK, row.shape[1])).astype(BF16)


def duplicates(spec, half):
    value = spec.astype(F32)
    other = pltpu.roll(value, half, 1)
    low = low_half(value.shape, half)
    return jnp.where(low, value, other), jnp.where(low, other, value)


def finish(back_ref, sums, send_ref, stage, sems, mix):
    @pl.when(pl.program_id(0) == pl.num_programs(0) - 1)
    def _():
        moves = []
        for q in range(sums.shape[0]):
            mixed = mix(sums.at[q]).astype(BF16)
            column = pl.ds(q * mixed.shape[0], mixed.shape[0])
            stage[:, column] = dot(back_ref[...], mixed, ((1,), (1,))).astype(BF16)
            moves.append(pltpu.make_async_copy(stage.at[:, column], send_ref.at[:, column], sems.at[q]))
            moves[-1].start()
        for move in moves:
            move.wait()


def fetch(sources, targets, sems):
    moves = [
        pltpu.make_async_copy(source, target, sems.at[n]) for n, (source, target) in enumerate(zip(sources, targets))
    ]

    @pl.when(pl.program_id(0) == 0)
    def _():
        for move in moves:
            move.start()

    return moves


def fetch_weights(moves, source_ref, weights, sems):
    q = pl.program_id(0)
    owned = sems.shape[0]
    size = weights.shape[0] // owned

    def move(mode):
        part = pl.ds(pl.multiple_of(mode * size, size), size)
        return pltpu.make_async_copy(source_ref.at[part, :], weights.at[part, :], sems.at[mode])

    @pl.when(q == 0)
    def _():
        move(0).start()
        for early in moves:
            early.wait()
        for mode in range(1, min(AHEAD, owned)):
            move(mode).start()

    @pl.when(q + AHEAD < owned)
    def _():
        move(q + AHEAD).start()

    return move(q), weights.at[pl.ds(pl.multiple_of(q * size, size), size), :]


def forward_kernel(scale, samples, owned, *rest):
    sources, source_ref, spec_ref, send_ref, real, imag, sums, weights, sems = rest[:4], *rest[4:12]
    targets, early, stage, late = rest[12:16], *rest[16:19]
    recv_ref, order_ref, rows_ref, back_ref = targets
    _, _, outs, both = sums.shape
    channels = weights.shape[0] // outs // owned
    half = both // 2
    lanes = samples * channels
    q = pl.program_id(0)
    moves = fetch(sources, targets, early)
    coming, weight_ref = fetch_weights(moves, source_ref, weights, sems)

    @pl.when(q == 0)
    def _():
        spectra_into(scale, owned, lanes, recv_ref, order_ref, rows_ref, spec_ref)
        real[...], imag[...] = duplicates(spec_ref[...], half)
        sums[...] = jnp.zeros_like(sums)

    coming.wait()

    def body(block, carry):
        view = rows_of(weight_ref, block, GROUP * outs)
        into = sums.at[q]
        for s in range(samples):
            rows = []
            for store in (real, imag):
                part = rows_of(store, (q * lanes + s * channels) // GROUP + block, GROUP)[...]
                rows.append([packed_row(part, step) for step in range(GROUP)])
            for o in range(0, outs, PACK):
                column = [view[step * outs + o : step * outs + o + PACK, :] for step in range(GROUP)]
                for n, row in enumerate(rows):
                    into[2 * s + n, o : o + PACK, :] += running([(w, r) for w, r in zip(column, row)]).astype(F32)
        return carry

    lax.fori_loop(0, channels // GROUP, body, 0)

    def mix(parts):
        low = low_half((outs, both), half)
        result = []
        for s in range(samples):
            crossed = pltpu.roll(parts[2 * s + 1], half, 1)
            result.append(parts[2 * s] + jnp.where(low, -crossed, crossed))
        return jnp.concatenate(result, axis=0)

    finish(back_ref, sums, send_ref, stage, late, mix)


def backward_kernel(samples, tiles, *rest):
    sources, source_ref, send_ref, real, imag, sums, weights, sems = rest[:3], *rest[3:10]
    targets, early, stage, late = rest[10:13], *rest[13:16]
    spec_ref, back_ref, local_ref = targets

    def carried():
        column = pl.ds(sums.shape[0] * lanes, stage.shape[1] - sums.shape[0] * lanes)
        return pltpu.make_async_copy(stage.at[:, column], send_ref.at[:, column], late.at[0])

    channels, both = sums.shape[2] // ROWS, sums.shape[3]
    outs = weights.shape[0] // channels // sums.shape[0]
    half = both // 2
    lanes = samples * outs
    q = pl.program_id(0)
    moves = fetch(sources, targets, early)
    coming, weight_ref = fetch_weights(moves, source_ref, weights, sems)

    @pl.when(q == 0)
    def _():
        first, second = duplicates(spec_ref[...], half)
        real[...], imag[...] = first.astype(BF16), second.astype(BF16)
        extent = stage.shape[0] // tiles
        partial = to_piece(local_ref[...].astype(BF16), extent)
        for n in range(0, stage.shape[0], extent):
            stage[n : n + extent, sums.shape[0] * lanes :] = partial
        move = carried()
        move.start()
        move.wait()

    coming.wait()
    grads = [
        [store[pl.ds(pl.multiple_of(q * lanes + s * outs + o, PACK), PACK), :] for o in range(0, outs, PACK)]
        for s in range(samples)
        for store in (real, imag)
    ]

    def body(block, carry):
        view = rows_of(weight_ref, block, GROUP * outs)
        into = [rows_of(sums.at[q, n], block, GROUP * ROWS) for n in range(len(grads))]
        for first in range(0, GROUP, 4):
            totals = []
            for step in range(first, first + 4):
                column = [view[step * outs + o : step * outs + o + PACK, :] for o in range(0, outs, PACK)]
                for n, grad in enumerate(grads):
                    total = running([(w, g) for w, g in zip(column, grad)]).astype(F32)
                    totals.append((n, step, total[:ROWS] + total[ROWS:]))
            for n, step, total in totals:
                into[n][step * ROWS : (step + 1) * ROWS, :] = total
        return carry

    lax.fori_loop(0, channels // GROUP, body, 0)

    def mix(parts):
        low = low_half((channels, both), half)
        result = []
        for s in range(samples):
            straight, crossed = (
                sum(parts[n, pl.ds(row, channels, stride=ROWS), :] for row in range(ROWS)) for n in (2 * s, 2 * s + 1)
            )
            result.append(jnp.where(low, straight, -straight) + pltpu.roll(crossed, half, 1))
        return jnp.concatenate(result, axis=0)

    finish(back_ref, sums, send_ref, stage, late, mix)


def pixels_kernel(scale, heights, recv_ref, order_ref, back_ref, local_ref, field_ref, cot_ref, table_ref, *rest):
    grad_ref, send_ref, sum_ref, ordered, total = rest
    steps, lanes, _ = field_ref.shape
    count = order_ref.shape[0] // heights
    size = order_ref.shape[0]
    group = pl.program_id(0)

    @pl.when(group == 0)
    def _():
        for n in range(0, recv_ref.shape[0], size):
            ordered[n : n + size, :] = shuffle(order_ref, recv_ref[n : n + size, :])
        total[...] = jnp.zeros_like(total)

    local = jnp.zeros(total.shape, F32)
    for step in range(steps):
        parts = []
        for n in range(0, recv_ref.shape[0], size):
            first = pl.multiple_of(n + (group * steps + step) * count, count)
            parts.append(ordered[pl.ds(first, count), :])
        inner = stack(parts, 0, count, lanes)
        pre = scale * dot(inner, back_ref[...], ((0,), (0,)))
        pre = pre + dot(local_ref[...], field_ref[step], ((1,), (0,)))
        grad = (cot_ref[step].astype(F32) * gelu_slope(pre)).astype(BF16)
        grad_ref[step] = grad
        send_ref[:, step * lanes : (step + 1) * lanes] = dot(table_ref[...], grad, ((1,), (1,))).astype(BF16)
        local = local + dot(field_ref[step], grad, ((1,), (1,)))
    total[...] += local

    @pl.when(group == pl.num_programs(0) - 1)
    def _():
        extent = sum_ref.shape[0]
        sum_ref[...] = sum(total[n : n + extent, n : n + extent] for n in range(0, lanes, extent))


def final_kernel(scale, tiles, recv_ref, order_ref, back_ref, local_ref, grad_ref, restore_ref, *rest):
    out_ref, sum_ref, result = rest
    heights, lanes, _ = grad_ref.shape
    extent = recv_ref.shape[0] // tiles
    first = back_ref.shape[0] // (2 * tiles) * lanes
    partials = sum(recv_ref[n : n + extent, first:].astype(F32) for n in range(0, recv_ref.shape[0], extent))
    sum_ref[...] = from_piece(partials, sum_ref.shape[1])
    count = order_ref.shape[0] // heights
    ordered = shuffle_groups(order_ref, recv_ref, first)
    for h in range(heights):
        inner = stack(ordered, h, count, lanes)
        value = scale * dot(inner, back_ref[...], ((0,), (0,)))
        result[h] = (value + dot(local_ref[...], grad_ref[h], ((1,), (0,)))).astype(BF16)
    block = PACK * heights
    for first in range(0, lanes, PACK):
        part = jnp.concatenate([result[h, first : first + PACK, :] for h in range(heights)], axis=0)
        out_ref[first * heights : first * heights + block, :] = shuffle(restore_ref, part)


def outer_kernel(samples, groups, *refs):
    specs, grads = refs[:groups], refs[groups : 2 * groups]
    out_ref, real, imag, crossed = refs[2 * groups :]
    total, channels, both = real.shape
    outs = crossed.shape[1]
    half = both // 2
    low = low_half((channels, both), half)

    for g in range(groups):
        for s in range(samples):
            n = g * samples + s
            spec = specs[g][s * channels : (s + 1) * channels, :].astype(F32)
            other = pltpu.roll(spec, half, 1)
            real[n] = jnp.where(low, spec, other)
            imag[n] = jnp.where(low, other, -spec)
            grad = grads[g][s * outs : (s + 1) * outs, :]
            crossed[n] = pltpu.roll(grad.astype(F32), half, 1).astype(BF16)

    def body(block, carry):
        into = rows_of(out_ref, block, GROUP * outs)
        views = [rows_of(store.at[n], block, GROUP)[...] for n in range(total) for store in (real, imag)]
        for first in range(0, GROUP, 2):
            pair = range(first, first + 2)
            lefts = [[packed_row(view, c) for view in views] for c in pair]
            for o in range(0, outs, PACK):
                right = []
                for n in range(total):
                    at = n % samples * outs + o
                    right += [grads[n // samples][at : at + PACK, :], crossed[n, o : o + PACK, :]]
                results = [running(list(zip(left, right))) for left in lefts]
                for c, result in zip(pair, results):
                    into[c * outs + o : c * outs + o + PACK, :] = result.astype(F32)
        return carry

    lax.fori_loop(0, channels // GROUP, body, 0)


def whole(extent):
    return pl.BlockSpec(extent, lambda *_: (0,) * len(extent))


def call(kernel, name, operands, outs, scratch=(), grid=(1,), blocks=None, out_blocks=None, limit=LIMIT):
    blocks, out_blocks = blocks or {}, out_blocks or {}
    in_specs = [blocks.get(n) or whole(operand.shape) for n, operand in enumerate(operands)]
    out_specs = [out_blocks.get(n, whole(out.shape)) for n, out in enumerate(outs)]
    return pl.pallas_call(
        kernel,
        out_shape=tuple(outs),
        grid=grid,
        in_specs=in_specs,
        out_specs=tuple(out_specs),
        scratch_shapes=list(scratch),
        compiler_params=pltpu.CompilerParams(vmem_limit_bytes=limit),
        name=name,
    )(*operands)


def swap(values, axis, step):
    return lax.ppermute(values, axis, [(i, i ^ step) for i in range(lax.axis_size(axis))])


def gather_near(values, axis):
    size = lax.axis_size(axis)
    return {0: values} | {1 << bit: swap(values, axis, 1 << bit) for bit in range(size.bit_length() - 1)}


def gather_far(near, axis):
    whole_set = dict(near)
    for step in range(1, lax.axis_size(axis)):
        if step not in whole_set:
            whole_set[step] = swap(whole_set[step & (step - 1)], axis, step & -step)
    return [whole_set[step] for step in sorted(whole_set)]


def sum_over(values, axis):
    step = 1
    while step < lax.axis_size(axis):
        values = values + swap(values, axis, step)
        step *= 2
    return values


def block_diagonal(matrix, copies):
    zero = jnp.zeros_like(matrix)
    return jnp.concatenate(
        [
            jnp.concatenate([matrix if i == j else zero for j in range(copies)], axis=1)
            for i in range(copies)
        ],
        axis=0,
    )


def shape(extent, kind=BF16):
    return jax.ShapeDtypeStruct(extent, kind)


def local(inputs, cotangent, mode_weight, local_weight):
    tiles = lax.axis_size("tile")
    samples, channels, th, width = inputs.shape
    owned, _, _, both = mode_weight.shape
    modes = both // 2
    lanes = samples * channels
    parts = width // 128
    spec_scale = 1.0 / math.sqrt(tiles * th * width)
    mode_scale = 1.0 / math.sqrt(modes * tiles * owned)
    send_cols, rows, back_rows, back_cols = tables(tiles, owned, th, width, modes)
    pixel_rows = samples * channels * th
    halves = tiles * padded(2 * owned)
    inverse = 2 * tiles * th

    def exchange(values):
        split = values.reshape(tiles, values.shape[0] // tiles, values.shape[1])
        moved = lax.all_to_all(split, "tile", split_axis=0, concat_axis=0, tiled=False)
        return moved.reshape(values.shape)

    forward_mix = block_diagonal(local_weight.T, samples)
    backward_mix = block_diagonal(local_weight, samples)
    by_row = order(PACK, th)
    by_channel = order(th, PACK)
    by_mode = mode_order(tiles, owned)
    by_height = order(2 * min(tiles, 8), th)
    flat_weight = mode_weight.reshape(-1, both)
    weight_block = pl.BlockSpec((flat_weight.shape[0] // owned, both), lambda q: (q, 0))
    weight_scratch = [pltpu.VMEM(flat_weight.shape, BF16), pltpu.SemaphoreType.DMA((owned,))]
    in_place = pl.BlockSpec(memory_space=pl.ANY)
    to_modes = shape((halves, th * lanes))
    to_pixels = shape((inverse, owned * lanes))
    field_shape = shape((th, lanes, width))

    def kept(*operands):
        return [pltpu.VMEM(operand.shape, operand.dtype) for operand in operands]

    def early(*operands):
        return kept(*operands) + [pltpu.SemaphoreType.DMA((len(operands),))]

    def field_blocks(first):
        return {first + n: pl.BlockSpec((pixel_rows // SPLIT, width), lambda _, n=n: (n, 0)) for n in range(SPLIT)}

    field_rows, send = call(
        columns_kernel,
        "columns",
        (by_row, send_cols, *[inputs.reshape(pixel_rows, width)] * SPLIT),
        (field_shape, to_modes),
        blocks=field_blocks(2),
    )
    arrived = exchange(send)
    (cot_rows,) = call(
        relayout_kernel,
        "relayout",
        (by_row, *[cotangent.reshape(pixel_rows, width)] * SPLIT),
        (field_shape,),
        blocks=field_blocks(1),
    )
    spectra, send = call(
        functools.partial(forward_kernel, spec_scale, samples, owned),
        "mix_forward",
        (arrived, by_mode, rows, back_rows, flat_weight),
        (shape((owned * lanes, both)), to_pixels),
        [
            pltpu.VMEM((owned * lanes, both), F32),
            pltpu.VMEM((owned * lanes, both), F32),
            pltpu.VMEM((owned, 2 * samples, channels, both), F32),
            *weight_scratch,
            *early(arrived, by_mode, rows, back_rows),
            pltpu.VMEM((inverse, owned * lanes), BF16),
            pltpu.SemaphoreType.DMA((owned,)),
        ],
        grid=(owned,),
        blocks={n: in_place for n in range(5)},
        out_blocks={1: in_place},
    )
    all_spectra = gather_far(gather_near(spectra, "dp"), "dp")
    arrived = exchange(send)
    steps = 4
    row_block = pl.BlockSpec((steps, lanes, width), lambda n: (n, 0, 0))
    gate_rows, send, local_sum = call(
        functools.partial(pixels_kernel, mode_scale, th),
        "pixels",
        (arrived, by_height, back_cols, forward_mix, field_rows, cot_rows, send_cols),
        (field_shape, to_modes, shape((channels, channels), F32)),
        [pltpu.VMEM((inverse, owned * lanes), BF16), pltpu.VMEM((lanes, lanes), F32)],
        grid=(th // steps,),
        blocks={4: row_block, 5: row_block},
        out_blocks={0: row_block, 1: pl.BlockSpec((halves, steps * lanes), lambda n: (0, n))},
        limit=SMALL,
    )
    send, *all_spectra = lax.optimization_barrier((send, *all_spectra))
    arrived, local_sum = lax.optimization_barrier((exchange(send), sum_over(local_sum, "dp")))
    (grad_spectra,) = call(
        functools.partial(spectra_kernel, mode_scale, owned, lanes),
        "grad_spectra",
        (arrived, by_mode, rows),
        (shape((owned * lanes, both)),),
        limit=SMALL,
    )
    near = gather_near(grad_spectra, "dp")
    carried = channels * channels * tiles // inverse
    (send,) = call(
        functools.partial(backward_kernel, samples, tiles),
        "mix_backward",
        (grad_spectra, back_rows, local_sum, flat_weight),
        (shape((inverse, owned * lanes + carried)),),
        [
            pltpu.VMEM((owned * lanes, both), BF16),
            pltpu.VMEM((owned * lanes, both), BF16),
            pltpu.VMEM((owned, 2 * samples, channels * ROWS, both), F32),
            *weight_scratch,
            *early(grad_spectra, back_rows, local_sum),
            pltpu.VMEM((inverse, owned * lanes + carried), BF16),
            pltpu.SemaphoreType.DMA((owned,)),
        ],
        grid=(owned,),
        blocks={n: in_place for n in range(4)},
        out_blocks={0: in_place},
    )
    send, near = lax.optimization_barrier((send, near))
    send, *all_grads = lax.optimization_barrier((send, *gather_far(near, "dp")))
    arrived = exchange(send)

    groups = lax.axis_size("dp")
    total = groups * samples
    per_mode = pl.BlockSpec((lanes, both), lambda q: (q, 0))
    (mode_grad,) = call(
        functools.partial(outer_kernel, samples, groups),
        "mode_grad",
        (*all_spectra, *all_grads),
        (shape(flat_weight.shape, F32),),
        [pltpu.VMEM((total, channels, both), F32)] * 2 + [pltpu.VMEM((total, channels, both), BF16)],
        grid=(owned,),
        blocks={n: per_mode for n in range(2 * groups)},
        out_blocks={0: weight_block},
    )
    arrived, mode_grad = lax.optimization_barrier((arrived, mode_grad))

    input_grad, local_grad = call(
        functools.partial(final_kernel, spec_scale, tiles),
        "final",
        (arrived, by_height, back_cols, backward_mix, gate_rows, by_channel),
        (shape((pixel_rows, width)), shape((channels, channels), F32)),
        [pltpu.VMEM((th, lanes, width), BF16)],
        limit=SMALL,
    )
    return (input_grad.reshape(inputs.shape), mode_grad.reshape(mode_weight.shape), local_grad)


def solution(mesh):
    return jax.shard_map(
        local,
        mesh=mesh,
        in_specs=(
            P("dp", None, "tile", None),
            P("dp", None, "tile", None),
            P("tile", None, None, None),
            P(),
        ),
        out_specs=(P("dp", None, "tile", None), P("tile", None, None, None), P()),
        check_vma=False,
    )
```

```python
import functools
import math

import jax
import jax.numpy as jnp
import numpy as np
from jax import lax
from jax.experimental import pallas as pl
from jax.experimental.pallas import tpu as pltpu
from jax.sharding import PartitionSpec as P

F32 = jnp.float32
BF16 = jnp.bfloat16
LIMIT = 56 * 1024 * 1024
SMALL = 24 * 1024 * 1024
ROWS = 8
PACK = 16
GROUP = 8
SPLIT = 4
AHEAD = 2


def row_tables(height, modes):
    index = np.arange(modes)
    signed = np.where(index < modes // 2, index, index - modes)
    phases = np.mod(np.arange(height)[:, None] * signed[None, :], height)
    angles = phases * (2.0 * math.pi / height)
    return np.cos(angles), np.sin(angles)


def column_tables(width, modes):
    phases = np.mod(np.arange(modes)[:, None] * np.arange(width)[None, :], width)
    angles = phases * (2.0 * math.pi / width)
    return np.stack([np.cos(angles), -np.sin(angles)])


def constant(table):
    return jnp.asarray(np.asarray(table, np.float32)).astype(BF16)


def tables(tiles, owned, th, width, modes):
    cols = column_tables(width, tiles * owned)
    split = cols.reshape(2, tiles, owned, width)
    send_cols = split.transpose(1, 0, 2, 3).reshape(tiles, 2 * owned, width)
    send_cols = np.pad(send_cols, ((0, 0), (0, padded(2 * owned) - 2 * owned), (0, 0))).reshape(-1, width)
    back_cols = split.transpose(2, 1, 0, 3).reshape(-1, width)
    cosine, sine = row_tables(th * tiles, modes)
    real = np.concatenate([cosine, -sine], axis=1)
    imag = np.concatenate([sine, cosine], axis=1)
    pair = np.stack([real, imag]).reshape(2, tiles, th, 2 * modes)
    rows = pair.transpose(2, 1, 0, 3).reshape(-1, 2 * modes)
    back_rows = pair.transpose(1, 0, 2, 3).reshape(-1, 2 * modes)
    return constant(send_cols), constant(rows), constant(back_rows), constant(back_cols)


def padded(rows):
    return -(-rows // PACK) * PACK


def order(outer, inner):
    take = np.arange(outer * inner).reshape(outer, inner).T.reshape(-1)
    return constant(np.eye(outer * inner)[take])


def mode_order(tiles, owned):
    rows = np.arange(tiles * padded(2 * owned)).reshape(tiles, -1)
    take = rows[:, : 2 * owned].reshape(tiles, 2, owned).transpose(2, 0, 1).reshape(-1)
    return constant(np.eye(rows.size)[take])


def dot(left, right, dims):
    return lax.dot_general(left, right, (dims, ((), ())), preferred_element_type=F32)


def low_half(shape, half):
    return lax.broadcasted_iota(jnp.int32, shape, 1) < half


def gelu_slope(values):
    size = jnp.abs(values)
    expo = jnp.exp(-0.5 * values * values)
    t = 1.0 / (1.0 + (0.3275911 / math.sqrt(2.0)) * size)
    poly = 0.5 * 1.061405429
    for factor in (-1.453152027, 1.421413741, -0.284496736, 0.254829592):
        poly = poly * t + 0.5 * factor
    tail = poly * t * expo
    cumulative = jnp.where(values < 0.0, tail, 1.0 - tail)
    return cumulative + values * expo * (1.0 / math.sqrt(2.0 * math.pi))


def shuffle(order_ref, value):
    return dot(order_ref[...], value, ((1,), (0,))).astype(BF16)


def by_rows(order_ref, field_refs, rows_ref):
    heights, lanes, _ = rows_ref.shape
    block = PACK * heights
    quarter = lanes // len(field_refs)
    for first in range(0, lanes, PACK):
        start = first % quarter * heights
        moved = shuffle(order_ref, field_refs[first // quarter][start : start + block, :])
        for h in range(heights):
            rows_ref[h, first : first + PACK, :] = moved[h * PACK : (h + 1) * PACK]


def columns_kernel(order_ref, table_ref, *rest):
    field_refs, (rows_ref, send_ref) = rest[:SPLIT], rest[SPLIT:]
    heights, lanes, _ = rows_ref.shape
    by_rows(order_ref, field_refs, rows_ref)
    for h in range(heights):
        send_ref[:, h * lanes : (h + 1) * lanes] = dot(table_ref[...], rows_ref[h], ((1,), (1,))).astype(BF16)


def relayout_kernel(order_ref, *rest):
    by_rows(order_ref, rest[:SPLIT], rest[SPLIT])


def shuffle_groups(order_ref, recv_ref, width):
    size = order_ref.shape[0]
    return [shuffle(order_ref, recv_ref[n : n + size, :width]) for n in range(0, recv_ref.shape[0], size)]


def stack(groups, index, count, lanes):
    return jnp.concatenate(
        [
            group[index * count : (index + 1) * count, n : n + lanes]
            for n in range(0, groups[0].shape[1], lanes)
            for group in groups
        ],
        axis=0,
    )


def spectra_into(scale, owned, lanes, recv_ref, order_ref, rows_ref, spec_ref):
    count = order_ref.shape[0] // owned
    fields = rows_ref.shape[0] // count * lanes
    ordered = [shuffle(order_ref, recv_ref[:, :fields])]
    for q in range(owned):
        stacked = stack(ordered, q, count, lanes)
        spec_ref[q * lanes : (q + 1) * lanes, :] = (
            scale * dot(stacked, rows_ref[...], ((0,), (0,)))
        ).astype(BF16)


def to_piece(value, rows):
    return jnp.concatenate([value[n : n + rows] for n in range(0, value.shape[0], rows)], axis=1)


def from_piece(value, extent):
    return jnp.concatenate([value[:, n : n + extent] for n in range(0, value.shape[1], extent)], axis=0)


def spectra_kernel(scale, owned, lanes, recv_ref, order_ref, rows_ref, spec_ref):
    spectra_into(scale, owned, lanes, recv_ref, order_ref, rows_ref, spec_ref)


def running(pairs):
    waiting = []
    for left, right in pairs:
        value, level = left * right, 0
        while waiting and waiting[-1][1] == level:
            value, level = waiting.pop()[0] + value, level + 1
        waiting.append((value, level))
    return sum((value for value, _ in reversed(waiting[:-1])), waiting[-1][0])


def rows_of(store, block, extent):
    return store.at[pl.ds(pl.multiple_of(block * extent, extent), extent), :]


def packed_row(view, index):
    row = view[index : index + 1, :]
    return jnp.broadcast_to(row, (PACK, row.shape[1])).astype(BF16)


def duplicates(spec, half):
    value = spec.astype(F32)
    other = pltpu.roll(value, half, 1)
    low = low_half(value.shape, half)
    return jnp.where(low, value, other), jnp.where(low, other, value)


def finish(back_ref, sums, send_ref, stage, sems, mix):
    @pl.when(pl.program_id(0) == pl.num_programs(0) - 1)
    def _():
        moves = []
        for q in range(sums.shape[0]):
            mixed = mix(sums.at[q]).astype(BF16)
            column = pl.ds(q * mixed.shape[0], mixed.shape[0])
            stage[:, column] = dot(back_ref[...], mixed, ((1,), (1,))).astype(BF16)
            moves.append(pltpu.make_async_copy(stage.at[:, column], send_ref.at[:, column], sems.at[q]))
            moves[-1].start()
        for move in moves:
            move.wait()


def fetch(sources, targets, sems):
    moves = [
        pltpu.make_async_copy(source, target, sems.at[n]) for n, (source, target) in enumerate(zip(sources, targets))
    ]

    @pl.when(pl.program_id(0) == 0)
    def _():
        for move in moves:
            move.start()

    return moves


def fetch_weights(moves, source_ref, weights, sems):
    q = pl.program_id(0)
    owned = sems.shape[0]
    size = weights.shape[0] // owned

    def move(mode):
        part = pl.ds(pl.multiple_of(mode * size, size), size)
        return pltpu.make_async_copy(source_ref.at[part, :], weights.at[part, :], sems.at[mode])

    @pl.when(q == 0)
    def _():
        move(0).start()
        for early in moves:
            early.wait()
        for mode in range(1, min(AHEAD, owned)):
            move(mode).start()

    @pl.when(q + AHEAD < owned)
    def _():
        move(q + AHEAD).start()

    return move(q), weights.at[pl.ds(pl.multiple_of(q * size, size), size), :]


def forward_kernel(scale, samples, owned, *rest):
    sources, source_ref, spec_ref, send_ref, real, imag, sums, weights, sems = rest[:4], *rest[4:12]
    targets, early, stage, late = rest[12:16], *rest[16:19]
    recv_ref, order_ref, rows_ref, back_ref = targets
    _, _, outs, both = sums.shape
    channels = weights.shape[0] // outs // owned
    half = both // 2
    lanes = samples * channels
    q = pl.program_id(0)
    moves = fetch(sources, targets, early)
    coming, weight_ref = fetch_weights(moves, source_ref, weights, sems)

    @pl.when(q == 0)
    def _():
        spectra_into(scale, owned, lanes, recv_ref, order_ref, rows_ref, spec_ref)
        real[...], imag[...] = duplicates(spec_ref[...], half)
        sums[...] = jnp.zeros_like(sums)

    coming.wait()

    def body(block, carry):
        view = rows_of(weight_ref, block, GROUP * outs)
        into = sums.at[q]
        for s in range(samples):
            rows = []
            for store in (real, imag):
                part = rows_of(store, (q * lanes + s * channels) // GROUP + block, GROUP)[...]
                rows.append([packed_row(part, step) for step in range(GROUP)])
            for o in range(0, outs, PACK):
                column = [view[step * outs + o : step * outs + o + PACK, :] for step in range(GROUP)]
                for n, row in enumerate(rows):
                    into[2 * s + n, o : o + PACK, :] += running([(w, r) for w, r in zip(column, row)]).astype(F32)
        return carry

    lax.fori_loop(0, channels // GROUP, body, 0)

    def mix(parts):
        low = low_half((outs, both), half)
        result = []
        for s in range(samples):
            crossed = pltpu.roll(parts[2 * s + 1], half, 1)
            result.append(parts[2 * s] + jnp.where(low, -crossed, crossed))
        return jnp.concatenate(result, axis=0)

    finish(back_ref, sums, send_ref, stage, late, mix)


def backward_kernel(samples, tiles, *rest):
    sources, source_ref, send_ref, real, imag, sums, weights, sems = rest[:3], *rest[3:10]
    targets, early, stage, late = rest[10:13], *rest[13:16]
    spec_ref, back_ref, local_ref = targets

    def carried():
        column = pl.ds(sums.shape[0] * lanes, stage.shape[1] - sums.shape[0] * lanes)
        return pltpu.make_async_copy(stage.at[:, column], send_ref.at[:, column], late.at[0])

    channels, both = sums.shape[2] // ROWS, sums.shape[3]
    outs = weights.shape[0] // channels // sums.shape[0]
    half = both // 2
    lanes = samples * outs
    q = pl.program_id(0)
    moves = fetch(sources, targets, early)
    coming, weight_ref = fetch_weights(moves, source_ref, weights, sems)

    @pl.when(q == 0)
    def _():
        first, second = duplicates(spec_ref[...], half)
        real[...], imag[...] = first.astype(BF16), second.astype(BF16)
        extent = stage.shape[0] // tiles
        partial = to_piece(local_ref[...].astype(BF16), extent)
        for n in range(0, stage.shape[0], extent):
            stage[n : n + extent, sums.shape[0] * lanes :] = partial
        move = carried()
        move.start()
        move.wait()

    coming.wait()
    grads = [
        [store[pl.ds(pl.multiple_of(q * lanes + s * outs + o, PACK), PACK), :] for o in range(0, outs, PACK)]
        for s in range(samples)
        for store in (real, imag)
    ]

    def body(block, carry):
        view = rows_of(weight_ref, block, GROUP * outs)
        into = [rows_of(sums.at[q, n], block, GROUP * ROWS) for n in range(len(grads))]
        for first in range(0, GROUP, 4):
            totals = []
            for step in range(first, first + 4):
                column = [view[step * outs + o : step * outs + o + PACK, :] for o in range(0, outs, PACK)]
                for n, grad in enumerate(grads):
                    total = running([(w, g) for w, g in zip(column, grad)]).astype(F32)
                    totals.append((n, step, total[:ROWS] + total[ROWS:]))
            for n, step, total in totals:
                into[n][step * ROWS : (step + 1) * ROWS, :] = total
        return carry

    lax.fori_loop(0, channels // GROUP, body, 0)

    def mix(parts):
        low = low_half((channels, both), half)
        result = []
        for s in range(samples):
            straight, crossed = (
                sum(parts[n, pl.ds(row, channels, stride=ROWS), :] for row in range(ROWS)) for n in (2 * s, 2 * s + 1)
            )
            result.append(jnp.where(low, straight, -straight) + pltpu.roll(crossed, half, 1))
        return jnp.concatenate(result, axis=0)

    finish(back_ref, sums, send_ref, stage, late, mix)


def pixels_kernel(scale, heights, recv_ref, order_ref, back_ref, local_ref, field_ref, cot_ref, table_ref, *rest):
    grad_ref, send_ref, sum_ref, ordered, total = rest
    steps, lanes, _ = field_ref.shape
    count = order_ref.shape[0] // heights
    size = order_ref.shape[0]
    group = pl.program_id(0)

    @pl.when(group == 0)
    def _():
        for n in range(0, recv_ref.shape[0], size):
            ordered[n : n + size, :] = shuffle(order_ref, recv_ref[n : n + size, :])
        total[...] = jnp.zeros_like(total)

    local = jnp.zeros(total.shape, F32)
    for step in range(steps):
        parts = []
        for n in range(0, recv_ref.shape[0], size):
            first = pl.multiple_of(n + (group * steps + step) * count, count)
            parts.append(ordered[pl.ds(first, count), :])
        inner = stack(parts, 0, count, lanes)
        pre = scale * dot(inner, back_ref[...], ((0,), (0,)))
        pre = pre + dot(local_ref[...], field_ref[step], ((1,), (0,)))
        grad = (cot_ref[step].astype(F32) * gelu_slope(pre)).astype(BF16)
        grad_ref[step] = grad
        send_ref[:, step * lanes : (step + 1) * lanes] = dot(table_ref[...], grad, ((1,), (1,))).astype(BF16)
        local = local + dot(field_ref[step], grad, ((1,), (1,)))
    total[...] += local

    @pl.when(group == pl.num_programs(0) - 1)
    def _():
        extent = sum_ref.shape[0]
        sum_ref[...] = sum(total[n : n + extent, n : n + extent] for n in range(0, lanes, extent))


def final_kernel(scale, tiles, recv_ref, order_ref, back_ref, local_ref, grad_ref, restore_ref, *rest):
    out_ref, sum_ref, result = rest
    heights, lanes, _ = grad_ref.shape
    extent = recv_ref.shape[0] // tiles
    first = back_ref.shape[0] // (2 * tiles) * lanes
    partials = sum(recv_ref[n : n + extent, first:].astype(F32) for n in range(0, recv_ref.shape[0], extent))
    sum_ref[...] = from_piece(partials, sum_ref.shape[1])
    count = order_ref.shape[0] // heights
    ordered = shuffle_groups(order_ref, recv_ref, first)
    for h in range(heights):
        inner = stack(ordered, h, count, lanes)
        value = scale * dot(inner, back_ref[...], ((0,), (0,)))
        result[h] = (value + dot(local_ref[...], grad_ref[h], ((1,), (0,)))).astype(BF16)
    block = PACK * heights
    for first in range(0, lanes, PACK):
        part = jnp.concatenate([result[h, first : first + PACK, :] for h in range(heights)], axis=0)
        out_ref[first * heights : first * heights + block, :] = shuffle(restore_ref, part)


def outer_kernel(samples, groups, *refs):
    specs, grads = refs[:groups], refs[groups : 2 * groups]
    out_ref, real, imag, crossed = refs[2 * groups :]
    total, channels, both = real.shape
    outs = crossed.shape[1]
    half = both // 2
    low = low_half((channels, both), half)

    for g in range(groups):
        for s in range(samples):
            n = g * samples + s
            spec = specs[g][s * channels : (s + 1) * channels, :].astype(F32)
            other = pltpu.roll(spec, half, 1)
            real[n] = jnp.where(low, spec, other)
            imag[n] = jnp.where(low, other, -spec)
            grad = grads[g][s * outs : (s + 1) * outs, :]
            crossed[n] = pltpu.roll(grad.astype(F32), half, 1).astype(BF16)

    def body(block, carry):
        into = rows_of(out_ref, block, GROUP * outs)
        views = [rows_of(store.at[n], block, GROUP)[...] for n in range(total) for store in (real, imag)]
        for first in range(0, GROUP, 2):
            pair = range(first, first + 2)
            lefts = [[packed_row(view, c) for view in views] for c in pair]
            for o in range(0, outs, PACK):
                right = []
                for n in range(total):
                    at = n % samples * outs + o
                    right += [grads[n // samples][at : at + PACK, :], crossed[n, o : o + PACK, :]]
                results = [running(list(zip(left, right))) for left in lefts]
                for c, result in zip(pair, results):
                    into[c * outs + o : c * outs + o + PACK, :] = result.astype(F32)
        return carry

    lax.fori_loop(0, channels // GROUP, body, 0)


def whole(extent):
    return pl.BlockSpec(extent, lambda *_: (0,) * len(extent))


def call(kernel, name, operands, outs, scratch=(), grid=(1,), blocks=None, out_blocks=None, limit=LIMIT):
    blocks, out_blocks = blocks or {}, out_blocks or {}
    in_specs = [blocks.get(n) or whole(operand.shape) for n, operand in enumerate(operands)]
    out_specs = [out_blocks.get(n, whole(out.shape)) for n, out in enumerate(outs)]
    return pl.pallas_call(
        kernel,
        out_shape=tuple(outs),
        grid=grid,
        in_specs=in_specs,
        out_specs=tuple(out_specs),
        scratch_shapes=list(scratch),
        compiler_params=pltpu.CompilerParams(vmem_limit_bytes=limit),
        name=name,
    )(*operands)


def swap(values, axis, step):
    return lax.ppermute(values, axis, [(i, i ^ step) for i in range(lax.axis_size(axis))])


def gather_near(values, axis):
    size = lax.axis_size(axis)
    return {0: values} | {1 << bit: swap(values, axis, 1 << bit) for bit in range(size.bit_length() - 1)}


def gather_far(near, axis):
    whole_set = dict(near)
    for step in range(1, lax.axis_size(axis)):
        if step not in whole_set:
            whole_set[step] = swap(whole_set[step & (step - 1)], axis, step & -step)
    return [whole_set[step] for step in sorted(whole_set)]


def sum_over(values, axis):
    step = 1
    while step < lax.axis_size(axis):
        values = values + swap(values, axis, step)
        step *= 2
    return values


def block_diagonal(matrix, copies):
    zero = jnp.zeros_like(matrix)
    return jnp.concatenate(
        [
            jnp.concatenate([matrix if i == j else zero for j in range(copies)], axis=1)
            for i in range(copies)
        ],
        axis=0,
    )


def shape(extent, kind=BF16):
    return jax.ShapeDtypeStruct(extent, kind)


def local(inputs, cotangent, mode_weight, local_weight):
    tiles = lax.axis_size("tile")
    samples, channels, th, width = inputs.shape
    owned, _, _, both = mode_weight.shape
    modes = both // 2
    lanes = samples * channels
    parts = width // 128
    spec_scale = 1.0 / math.sqrt(tiles * th * width)
    mode_scale = 1.0 / math.sqrt(modes * tiles * owned)
    send_cols, rows, back_rows, back_cols = tables(tiles, owned, th, width, modes)
    pixel_rows = samples * channels * th
    halves = tiles * padded(2 * owned)
    inverse = 2 * tiles * th

    def exchange(values):
        split = values.reshape(tiles, values.shape[0] // tiles, values.shape[1])
        moved = lax.all_to_all(split, "tile", split_axis=0, concat_axis=0, tiled=False)
        return moved.reshape(values.shape)

    forward_mix = block_diagonal(local_weight.T, samples)
    backward_mix = block_diagonal(local_weight, samples)
    by_row = order(PACK, th)
    by_channel = order(th, PACK)
    by_mode = mode_order(tiles, owned)
    by_height = order(2 * min(tiles, 8), th)
    flat_weight = mode_weight.reshape(-1, both)
    weight_block = pl.BlockSpec((flat_weight.shape[0] // owned, both), lambda q: (q, 0))
    weight_scratch = [pltpu.VMEM(flat_weight.shape, BF16), pltpu.SemaphoreType.DMA((owned,))]
    in_place = pl.BlockSpec(memory_space=pl.ANY)
    to_modes = shape((halves, th * lanes))
    to_pixels = shape((inverse, owned * lanes))
    field_shape = shape((th, lanes, width))

    def kept(*operands):
        return [pltpu.VMEM(operand.shape, operand.dtype) for operand in operands]

    def early(*operands):
        return kept(*operands) + [pltpu.SemaphoreType.DMA((len(operands),))]

    def field_blocks(first):
        return {first + n: pl.BlockSpec((pixel_rows // SPLIT, width), lambda _, n=n: (n, 0)) for n in range(SPLIT)}

    field_rows, send = call(
        columns_kernel,
        "columns",
        (by_row, send_cols, *[inputs.reshape(pixel_rows, width)] * SPLIT),
        (field_shape, to_modes),
        blocks=field_blocks(2),
    )
    arrived = exchange(send)
    (cot_rows,) = call(
        relayout_kernel,
        "relayout",
        (by_row, *[cotangent.reshape(pixel_rows, width)] * SPLIT),
        (field_shape,),
        blocks=field_blocks(1),
    )
    spectra, send = call(
        functools.partial(forward_kernel, spec_scale, samples, owned),
        "mix_forward",
        (arrived, by_mode, rows, back_rows, flat_weight),
        (shape((owned * lanes, both)), to_pixels),
        [
            pltpu.VMEM((owned * lanes, both), F32),
            pltpu.VMEM((owned * lanes, both), F32),
            pltpu.VMEM((owned, 2 * samples, channels, both), F32),
            *weight_scratch,
            *early(arrived, by_mode, rows, back_rows),
            pltpu.VMEM((inverse, owned * lanes), BF16),
            pltpu.SemaphoreType.DMA((owned,)),
        ],
        grid=(owned,),
        blocks={n: in_place for n in range(5)},
        out_blocks={1: in_place},
    )
    all_spectra = gather_far(gather_near(spectra, "dp"), "dp")
    arrived = exchange(send)
    steps = 8
    row_block = pl.BlockSpec((steps, lanes, width), lambda n: (n, 0, 0))
    gate_rows, send, local_sum = call(
        functools.partial(pixels_kernel, mode_scale, th),
        "pixels",
        (arrived, by_height, back_cols, forward_mix, field_rows, cot_rows, send_cols),
        (field_shape, to_modes, shape((channels, channels), F32)),
        [pltpu.VMEM((inverse, owned * lanes), BF16), pltpu.VMEM((lanes, lanes), F32)],
        grid=(th // steps,),
        blocks={4: row_block, 5: row_block},
        out_blocks={0: row_block, 1: pl.BlockSpec((halves, steps * lanes), lambda n: (0, n))},
        limit=SMALL,
    )
    send, *all_spectra = lax.optimization_barrier((send, *all_spectra))
    arrived, local_sum = lax.optimization_barrier((exchange(send), sum_over(local_sum, "dp")))
    (grad_spectra,) = call(
        functools.partial(spectra_kernel, mode_scale, owned, lanes),
        "grad_spectra",
        (arrived, by_mode, rows),
        (shape((owned * lanes, both)),),
        limit=SMALL,
    )
    near = gather_near(grad_spectra, "dp")
    carried = channels * channels * tiles // inverse
    (send,) = call(
        functools.partial(backward_kernel, samples, tiles),
        "mix_backward",
        (grad_spectra, back_rows, local_sum, flat_weight),
        (shape((inverse, owned * lanes + carried)),),
        [
            pltpu.VMEM((owned * lanes, both), BF16),
            pltpu.VMEM((owned * lanes, both), BF16),
            pltpu.VMEM((owned, 2 * samples, channels * ROWS, both), F32),
            *weight_scratch,
            *early(grad_spectra, back_rows, local_sum),
            pltpu.VMEM((inverse, owned * lanes + carried), BF16),
            pltpu.SemaphoreType.DMA((owned,)),
        ],
        grid=(owned,),
        blocks={n: in_place for n in range(4)},
        out_blocks={0: in_place},
    )
    send, near = lax.optimization_barrier((send, near))
    send, *all_grads = lax.optimization_barrier((send, *gather_far(near, "dp")))
    arrived = exchange(send)

    groups = lax.axis_size("dp")
    total = groups * samples
    per_mode = pl.BlockSpec((lanes, both), lambda q: (q, 0))
    (mode_grad,) = call(
        functools.partial(outer_kernel, samples, groups),
        "mode_grad",
        (*all_spectra, *all_grads),
        (shape(flat_weight.shape, F32),),
        [pltpu.VMEM((total, channels, both), F32)] * 2 + [pltpu.VMEM((total, channels, both), BF16)],
        grid=(owned,),
        blocks={n: per_mode for n in range(2 * groups)},
        out_blocks={0: weight_block},
    )
    arrived, mode_grad = lax.optimization_barrier((arrived, mode_grad))

    input_grad, local_grad = call(
        functools.partial(final_kernel, spec_scale, tiles),
        "final",
        (arrived, by_height, back_cols, backward_mix, gate_rows, by_channel),
        (shape((pixel_rows, width)), shape((channels, channels), F32)),
        [pltpu.VMEM((th, lanes, width), BF16)],
        limit=SMALL,
    )
    return (input_grad.reshape(inputs.shape), mode_grad.reshape(mode_weight.shape), local_grad)


def solution(mesh):
    return jax.shard_map(
        local,
        mesh=mesh,
        in_specs=(
            P("dp", None, "tile", None),
            P("dp", None, "tile", None),
            P("tile", None, None, None),
            P(),
        ),
        out_specs=(P("dp", None, "tile", None), P("tile", None, None, None), P()),
        check_vma=False,
    )
```

```python
import functools
import math

import jax
import jax.numpy as jnp
import numpy as np
from jax import lax
from jax.experimental import pallas as pl
from jax.experimental.pallas import tpu as pltpu
from jax.sharding import PartitionSpec as P

F32 = jnp.float32
BF16 = jnp.bfloat16
LIMIT = 56 * 1024 * 1024
SMALL = 24 * 1024 * 1024
ROWS = 8
PACK = 16
GROUP = 8
SPLIT = 4
AHEAD = 2


def row_tables(height, modes):
    index = np.arange(modes)
    signed = np.where(index < modes // 2, index, index - modes)
    phases = np.mod(np.arange(height)[:, None] * signed[None, :], height)
    angles = phases * (2.0 * math.pi / height)
    return np.cos(angles), np.sin(angles)


def column_tables(width, modes):
    phases = np.mod(np.arange(modes)[:, None] * np.arange(width)[None, :], width)
    angles = phases * (2.0 * math.pi / width)
    return np.stack([np.cos(angles), -np.sin(angles)])


def constant(table):
    return jnp.asarray(np.asarray(table, np.float32)).astype(BF16)


def tables(tiles, owned, th, width, modes):
    cols = column_tables(width, tiles * owned)
    split = cols.reshape(2, tiles, owned, width)
    send_cols = split.transpose(1, 0, 2, 3).reshape(tiles, 2 * owned, width)
    send_cols = np.pad(send_cols, ((0, 0), (0, padded(2 * owned) - 2 * owned), (0, 0))).reshape(-1, width)
    back_cols = split.transpose(2, 1, 0, 3).reshape(-1, width)
    cosine, sine = row_tables(th * tiles, modes)
    real = np.concatenate([cosine, -sine], axis=1)
    imag = np.concatenate([sine, cosine], axis=1)
    pair = np.stack([real, imag]).reshape(2, tiles, th, 2 * modes)
    rows = pair.transpose(2, 1, 0, 3).reshape(-1, 2 * modes)
    back_rows = pair.transpose(1, 0, 2, 3).reshape(-1, 2 * modes)
    return constant(send_cols), constant(rows), constant(back_rows), constant(back_cols)


def padded(rows):
    return -(-rows // PACK) * PACK


def order(outer, inner):
    take = np.arange(outer * inner).reshape(outer, inner).T.reshape(-1)
    return constant(np.eye(outer * inner)[take])


def mode_order(tiles, owned):
    rows = np.arange(tiles * padded(2 * owned)).reshape(tiles, -1)
    take = rows[:, : 2 * owned].reshape(tiles, 2, owned).transpose(2, 0, 1).reshape(-1)
    return constant(np.eye(rows.size)[take])


def dot(left, right, dims):
    return lax.dot_general(left, right, (dims, ((), ())), preferred_element_type=F32)


def low_half(shape, half):
    return lax.broadcasted_iota(jnp.int32, shape, 1) < half


def gelu_slope(values):
    size = jnp.abs(values)
    expo = jnp.exp(-0.5 * values * values)
    t = 1.0 / (1.0 + (0.3275911 / math.sqrt(2.0)) * size)
    poly = 0.5 * 1.061405429
    for factor in (-1.453152027, 1.421413741, -0.284496736, 0.254829592):
        poly = poly * t + 0.5 * factor
    tail = poly * t * expo
    cumulative = jnp.where(values < 0.0, tail, 1.0 - tail)
    return cumulative + values * expo * (1.0 / math.sqrt(2.0 * math.pi))


def shuffle(order_ref, value):
    return dot(order_ref[...], value, ((1,), (0,))).astype(BF16)


def by_rows(order_ref, field_refs, rows_ref):
    heights, lanes, _ = rows_ref.shape
    block = PACK * heights
    quarter = lanes // len(field_refs)
    for first in range(0, lanes, PACK):
        start = first % quarter * heights
        moved = shuffle(order_ref, field_refs[first // quarter][start : start + block, :])
        for h in range(heights):
            rows_ref[h, first : first + PACK, :] = moved[h * PACK : (h + 1) * PACK]


def columns_kernel(order_ref, table_ref, *rest):
    field_refs, (rows_ref, send_ref) = rest[:SPLIT], rest[SPLIT:]
    heights, lanes, _ = rows_ref.shape
    by_rows(order_ref, field_refs, rows_ref)
    for h in range(heights):
        send_ref[:, h * lanes : (h + 1) * lanes] = dot(table_ref[...], rows_ref[h], ((1,), (1,))).astype(BF16)


def relayout_kernel(order_ref, *rest):
    by_rows(order_ref, rest[:SPLIT], rest[SPLIT])


def shuffle_groups(order_ref, recv_ref, width):
    size = order_ref.shape[0]
    return [shuffle(order_ref, recv_ref[n : n + size, :width]) for n in range(0, recv_ref.shape[0], size)]


def stack(groups, index, count, lanes):
    return jnp.concatenate(
        [
            group[index * count : (index + 1) * count, n : n + lanes]
            for n in range(0, groups[0].shape[1], lanes)
            for group in groups
        ],
        axis=0,
    )


def spectra_into(scale, owned, lanes, recv_ref, order_ref, rows_ref, spec_ref):
    count = order_ref.shape[0] // owned
    fields = rows_ref.shape[0] // count * lanes
    ordered = [shuffle(order_ref, recv_ref[:, :fields])]
    for q in range(owned):
        stacked = stack(ordered, q, count, lanes)
        spec_ref[q * lanes : (q + 1) * lanes, :] = (
            scale * dot(stacked, rows_ref[...], ((0,), (0,)))
        ).astype(BF16)


def to_piece(value, rows):
    return jnp.concatenate([value[n : n + rows] for n in range(0, value.shape[0], rows)], axis=1)


def from_piece(value, extent):
    return jnp.concatenate([value[:, n : n + extent] for n in range(0, value.shape[1], extent)], axis=0)


def spectra_kernel(scale, owned, lanes, recv_ref, order_ref, rows_ref, spec_ref):
    spectra_into(scale, owned, lanes, recv_ref, order_ref, rows_ref, spec_ref)


def running(pairs):
    waiting = []
    for left, right in pairs:
        value, level = left * right, 0
        while waiting and waiting[-1][1] == level:
            value, level = waiting.pop()[0] + value, level + 1
        waiting.append((value, level))
    return sum((value for value, _ in reversed(waiting[:-1])), waiting[-1][0])


def rows_of(store, block, extent):
    return store.at[pl.ds(pl.multiple_of(block * extent, extent), extent), :]


def packed_row(view, index):
    row = view[index : index + 1, :]
    return jnp.broadcast_to(row, (PACK, row.shape[1])).astype(BF16)


def duplicates(spec, half):
    value = spec.astype(F32)
    other = pltpu.roll(value, half, 1)
    low = low_half(value.shape, half)
    return jnp.where(low, value, other), jnp.where(low, other, value)


def finish(back_ref, sums, send_ref, stage, sems, mix):
    @pl.when(pl.program_id(0) == pl.num_programs(0) - 1)
    def _():
        moves = []
        for q in range(sums.shape[0]):
            mixed = mix(sums.at[q]).astype(BF16)
            column = pl.ds(q * mixed.shape[0], mixed.shape[0])
            stage[:, column] = dot(back_ref[...], mixed, ((1,), (1,))).astype(BF16)
            moves.append(pltpu.make_async_copy(stage.at[:, column], send_ref.at[:, column], sems.at[q]))
            moves[-1].start()
        for move in moves:
            move.wait()


def fetch(sources, targets, sems):
    moves = [
        pltpu.make_async_copy(source, target, sems.at[n]) for n, (source, target) in enumerate(zip(sources, targets))
    ]

    @pl.when(pl.program_id(0) == 0)
    def _():
        for move in moves:
            move.start()

    return moves


def fetch_weights(moves, source_ref, weights, sems):
    q = pl.program_id(0)
    owned = sems.shape[0]
    size = weights.shape[0] // owned

    def move(mode):
        part = pl.ds(pl.multiple_of(mode * size, size), size)
        return pltpu.make_async_copy(source_ref.at[part, :], weights.at[part, :], sems.at[mode])

    @pl.when(q == 0)
    def _():
        move(0).start()
        for early in moves:
            early.wait()
        for mode in range(1, min(AHEAD, owned)):
            move(mode).start()

    @pl.when(q + AHEAD < owned)
    def _():
        move(q + AHEAD).start()

    return move(q), weights.at[pl.ds(pl.multiple_of(q * size, size), size), :]


def forward_kernel(scale, samples, owned, *rest):
    sources, source_ref, spec_ref, send_ref, real, imag, sums, weights, sems = rest[:4], *rest[4:12]
    targets, early, stage, late = rest[12:16], *rest[16:19]
    recv_ref, order_ref, rows_ref, back_ref = targets
    _, _, outs, both = sums.shape
    channels = weights.shape[0] // outs // owned
    half = both // 2
    lanes = samples * channels
    q = pl.program_id(0)
    moves = fetch(sources, targets, early)
    coming, weight_ref = fetch_weights(moves, source_ref, weights, sems)

    @pl.when(q == 0)
    def _():
        spectra_into(scale, owned, lanes, recv_ref, order_ref, rows_ref, spec_ref)
        real[...], imag[...] = duplicates(spec_ref[...], half)
        sums[...] = jnp.zeros_like(sums)

    coming.wait()

    def body(block, carry):
        view = rows_of(weight_ref, block, GROUP * outs)
        into = sums.at[q]
        for s in range(samples):
            rows = []
            for store in (real, imag):
                part = rows_of(store, (q * lanes + s * channels) // GROUP + block, GROUP)[...]
                rows.append([packed_row(part, step) for step in range(GROUP)])
            for o in range(0, outs, PACK):
                column = [view[step * outs + o : step * outs + o + PACK, :] for step in range(GROUP)]
                for n, row in enumerate(rows):
                    into[2 * s + n, o : o + PACK, :] += running([(w, r) for w, r in zip(column, row)]).astype(F32)
        return carry

    lax.fori_loop(0, channels // GROUP, body, 0)

    def mix(parts):
        low = low_half((outs, both), half)
        result = []
        for s in range(samples):
            crossed = pltpu.roll(parts[2 * s + 1], half, 1)
            result.append(parts[2 * s] + jnp.where(low, -crossed, crossed))
        return jnp.concatenate(result, axis=0)

    finish(back_ref, sums, send_ref, stage, late, mix)


def backward_kernel(samples, tiles, *rest):
    sources, source_ref, send_ref, real, imag, sums, weights, sems = rest[:3], *rest[3:10]
    targets, early, stage, late = rest[10:13], *rest[13:16]
    spec_ref, back_ref, local_ref = targets

    def carried():
        column = pl.ds(sums.shape[0] * lanes, stage.shape[1] - sums.shape[0] * lanes)
        return pltpu.make_async_copy(stage.at[:, column], send_ref.at[:, column], late.at[0])

    channels, both = sums.shape[2] // ROWS, sums.shape[3]
    outs = weights.shape[0] // channels // sums.shape[0]
    half = both // 2
    lanes = samples * outs
    q = pl.program_id(0)
    moves = fetch(sources, targets, early)
    coming, weight_ref = fetch_weights(moves, source_ref, weights, sems)

    @pl.when(q == 0)
    def _():
        first, second = duplicates(spec_ref[...], half)
        real[...], imag[...] = first.astype(BF16), second.astype(BF16)
        extent = stage.shape[0] // tiles
        partial = to_piece(local_ref[...].astype(BF16), extent)
        for n in range(0, stage.shape[0], extent):
            stage[n : n + extent, sums.shape[0] * lanes :] = partial
        move = carried()
        move.start()
        move.wait()

    coming.wait()
    grads = [
        [store[pl.ds(pl.multiple_of(q * lanes + s * outs + o, PACK), PACK), :] for o in range(0, outs, PACK)]
        for s in range(samples)
        for store in (real, imag)
    ]

    def body(block, carry):
        view = rows_of(weight_ref, block, GROUP * outs)
        into = [rows_of(sums.at[q, n], block, GROUP * ROWS) for n in range(len(grads))]
        for first in range(0, GROUP, 4):
            totals = []
            for step in range(first, first + 4):
                column = [view[step * outs + o : step * outs + o + PACK, :] for o in range(0, outs, PACK)]
                for n, grad in enumerate(grads):
                    total = running([(w, g) for w, g in zip(column, grad)]).astype(F32)
                    totals.append((n, step, total[:ROWS] + total[ROWS:]))
            for n, step, total in totals:
                into[n][step * ROWS : (step + 1) * ROWS, :] = total
        return carry

    lax.fori_loop(0, channels // GROUP, body, 0)

    def mix(parts):
        low = low_half((channels, both), half)
        result = []
        for s in range(samples):
            straight, crossed = (
                sum(parts[n, pl.ds(row, channels, stride=ROWS), :] for row in range(ROWS)) for n in (2 * s, 2 * s + 1)
            )
            result.append(jnp.where(low, straight, -straight) + pltpu.roll(crossed, half, 1))
        return jnp.concatenate(result, axis=0)

    finish(back_ref, sums, send_ref, stage, late, mix)


def pixels_kernel(scale, heights, recv_ref, order_ref, back_ref, local_ref, field_ref, cot_ref, table_ref, *rest):
    grad_ref, send_ref, sum_ref, ordered, total = rest
    steps, lanes, _ = field_ref.shape
    count = order_ref.shape[0] // heights
    size = order_ref.shape[0]
    group = pl.program_id(0)

    @pl.when(group == 0)
    def _():
        for n in range(0, recv_ref.shape[0], size):
            ordered[n : n + size, :] = shuffle(order_ref, recv_ref[n : n + size, :])
        total[...] = jnp.zeros_like(total)

    local = jnp.zeros(total.shape, F32)
    for step in range(steps):
        parts = []
        for n in range(0, recv_ref.shape[0], size):
            first = pl.multiple_of(n + (group * steps + step) * count, count)
            parts.append(ordered[pl.ds(first, count), :])
        inner = stack(parts, 0, count, lanes)
        pre = scale * dot(inner, back_ref[...], ((0,), (0,)))
        pre = pre + dot(local_ref[...], field_ref[step], ((1,), (0,)))
        grad = (cot_ref[step].astype(F32) * gelu_slope(pre)).astype(BF16)
        grad_ref[step] = grad
        send_ref[:, step * lanes : (step + 1) * lanes] = dot(table_ref[...], grad, ((1,), (1,))).astype(BF16)
        local = local + dot(field_ref[step], grad, ((1,), (1,)))
    total[...] += local

    @pl.when(group == pl.num_programs(0) - 1)
    def _():
        extent = sum_ref.shape[0]
        sum_ref[...] = sum(total[n : n + extent, n : n + extent] for n in range(0, lanes, extent))


def final_kernel(scale, tiles, recv_ref, order_ref, back_ref, local_ref, grad_ref, restore_ref, *rest):
    out_ref, sum_ref, result = rest
    heights, lanes, _ = grad_ref.shape
    extent = recv_ref.shape[0] // tiles
    first = back_ref.shape[0] // (2 * tiles) * lanes
    partials = sum(recv_ref[n : n + extent, first:].astype(F32) for n in range(0, recv_ref.shape[0], extent))
    sum_ref[...] = from_piece(partials, sum_ref.shape[1])
    count = order_ref.shape[0] // heights
    ordered = shuffle_groups(order_ref, recv_ref, first)
    for h in range(heights):
        inner = stack(ordered, h, count, lanes)
        value = scale * dot(inner, back_ref[...], ((0,), (0,)))
        result[h] = (value + dot(local_ref[...], grad_ref[h], ((1,), (0,)))).astype(BF16)
    block = PACK * heights
    for first in range(0, lanes, PACK):
        part = jnp.concatenate([result[h, first : first + PACK, :] for h in range(heights)], axis=0)
        out_ref[first * heights : first * heights + block, :] = shuffle(restore_ref, part)


def outer_kernel(samples, groups, *refs):
    specs, grads = refs[:groups], refs[groups : 2 * groups]
    out_ref, real, imag, crossed = refs[2 * groups :]
    total, channels, both = real.shape
    outs = crossed.shape[1]
    half = both // 2
    low = low_half((channels, both), half)

    for g in range(groups):
        for s in range(samples):
            n = g * samples + s
            spec = specs[g][s * channels : (s + 1) * channels, :].astype(F32)
            other = pltpu.roll(spec, half, 1)
            real[n] = jnp.where(low, spec, other)
            imag[n] = jnp.where(low, other, -spec)
            grad = grads[g][s * outs : (s + 1) * outs, :]
            crossed[n] = pltpu.roll(grad.astype(F32), half, 1).astype(BF16)

    def body(block, carry):
        into = rows_of(out_ref, block, GROUP * outs)
        views = [rows_of(store.at[n], block, GROUP)[...] for n in range(total) for store in (real, imag)]
        for first in range(0, GROUP, 2):
            pair = range(first, first + 2)
            lefts = [[packed_row(view, c) for view in views] for c in pair]
            for o in range(0, outs, PACK):
                right = []
                for n in range(total):
                    at = n % samples * outs + o
                    right += [grads[n // samples][at : at + PACK, :], crossed[n, o : o + PACK, :]]
                results = [running(list(zip(left, right))) for left in lefts]
                for c, result in zip(pair, results):
                    into[c * outs + o : c * outs + o + PACK, :] = result.astype(F32)
        return carry

    lax.fori_loop(0, channels // GROUP, body, 0)


def whole(extent):
    return pl.BlockSpec(extent, lambda *_: (0,) * len(extent))


def call(kernel, name, operands, outs, scratch=(), grid=(1,), blocks=None, out_blocks=None, limit=LIMIT):
    blocks, out_blocks = blocks or {}, out_blocks or {}
    in_specs = [blocks.get(n) or whole(operand.shape) for n, operand in enumerate(operands)]
    out_specs = [out_blocks.get(n, whole(out.shape)) for n, out in enumerate(outs)]
    return pl.pallas_call(
        kernel,
        out_shape=tuple(outs),
        grid=grid,
        in_specs=in_specs,
        out_specs=tuple(out_specs),
        scratch_shapes=list(scratch),
        compiler_params=pltpu.CompilerParams(vmem_limit_bytes=limit),
        name=name,
    )(*operands)


def swap(values, axis, step):
    return lax.ppermute(values, axis, [(i, i ^ step) for i in range(lax.axis_size(axis))])


def gather_near(values, axis):
    size = lax.axis_size(axis)
    return {0: values} | {1 << bit: swap(values, axis, 1 << bit) for bit in range(size.bit_length() - 1)}


def gather_far(near, axis):
    whole_set = dict(near)
    for step in range(1, lax.axis_size(axis)):
        if step not in whole_set:
            whole_set[step] = swap(whole_set[step & (step - 1)], axis, step & -step)
    return [whole_set[step] for step in sorted(whole_set)]


def sum_over(values, axis):
    step = 1
    while step < lax.axis_size(axis):
        values = values + swap(values, axis, step)
        step *= 2
    return values


def block_diagonal(matrix, copies):
    zero = jnp.zeros_like(matrix)
    return jnp.concatenate(
        [
            jnp.concatenate([matrix if i == j else zero for j in range(copies)], axis=1)
            for i in range(copies)
        ],
        axis=0,
    )


def shape(extent, kind=BF16):
    return jax.ShapeDtypeStruct(extent, kind)


def local(inputs, cotangent, mode_weight, local_weight):
    tiles = lax.axis_size("tile")
    samples, channels, th, width = inputs.shape
    owned, _, _, both = mode_weight.shape
    modes = both // 2
    lanes = samples * channels
    parts = width // 128
    spec_scale = 1.0 / math.sqrt(tiles * th * width)
    mode_scale = 1.0 / math.sqrt(modes * tiles * owned)
    send_cols, rows, back_rows, back_cols = tables(tiles, owned, th, width, modes)
    pixel_rows = samples * channels * th
    halves = tiles * padded(2 * owned)
    inverse = 2 * tiles * th

    def exchange(values):
        split = values.reshape(tiles, values.shape[0] // tiles, values.shape[1])
        moved = lax.all_to_all(split, "tile", split_axis=0, concat_axis=0, tiled=False)
        return moved.reshape(values.shape)

    forward_mix = block_diagonal(local_weight.T, samples)
    backward_mix = block_diagonal(local_weight, samples)
    by_row = order(PACK, th)
    by_channel = order(th, PACK)
    by_mode = mode_order(tiles, owned)
    by_height = order(2 * min(tiles, 8), th)
    flat_weight = mode_weight.reshape(-1, both)
    weight_block = pl.BlockSpec((flat_weight.shape[0] // owned, both), lambda q: (q, 0))
    weight_scratch = [pltpu.VMEM(flat_weight.shape, BF16), pltpu.SemaphoreType.DMA((owned,))]
    in_place = pl.BlockSpec(memory_space=pl.ANY)
    to_modes = shape((halves, th * lanes))
    to_pixels = shape((inverse, owned * lanes))
    field_shape = shape((th, lanes, width))

    def kept(*operands):
        return [pltpu.VMEM(operand.shape, operand.dtype) for operand in operands]

    def early(*operands):
        return kept(*operands) + [pltpu.SemaphoreType.DMA((len(operands),))]

    def field_blocks(first):
        return {first + n: pl.BlockSpec((pixel_rows // SPLIT, width), lambda _, n=n: (n, 0)) for n in range(SPLIT)}

    field_rows, send = call(
        columns_kernel,
        "columns",
        (by_row, send_cols, *[inputs.reshape(pixel_rows, width)] * SPLIT),
        (field_shape, to_modes),
        blocks=field_blocks(2),
    )
    arrived = exchange(send)
    (cot_rows,) = call(
        relayout_kernel,
        "relayout",
        (by_row, *[cotangent.reshape(pixel_rows, width)] * SPLIT),
        (field_shape,),
        blocks=field_blocks(1),
    )
    spectra, send = call(
        functools.partial(forward_kernel, spec_scale, samples, owned),
        "mix_forward",
        (arrived, by_mode, rows, back_rows, flat_weight),
        (shape((owned * lanes, both)), to_pixels),
        [
            pltpu.VMEM((owned * lanes, both), F32),
            pltpu.VMEM((owned * lanes, both), F32),
            pltpu.VMEM((owned, 2 * samples, channels, both), F32),
            *weight_scratch,
            *early(arrived, by_mode, rows, back_rows),
            pltpu.VMEM((inverse, owned * lanes), BF16),
            pltpu.SemaphoreType.DMA((owned,)),
        ],
        grid=(owned,),
        blocks={n: in_place for n in range(5)},
        out_blocks={1: in_place},
    )
    all_spectra = gather_far(gather_near(spectra, "dp"), "dp")
    arrived = exchange(send)
    steps = th
    row_block = pl.BlockSpec((steps, lanes, width), lambda n: (n, 0, 0))
    gate_rows, send, local_sum = call(
        functools.partial(pixels_kernel, mode_scale, th),
        "pixels",
        (arrived, by_height, back_cols, forward_mix, field_rows, cot_rows, send_cols),
        (field_shape, to_modes, shape((channels, channels), F32)),
        [pltpu.VMEM((inverse, owned * lanes), BF16), pltpu.VMEM((lanes, lanes), F32)],
        grid=(th // steps,),
        blocks={4: row_block, 5: row_block},
        out_blocks={0: row_block, 1: pl.BlockSpec((halves, steps * lanes), lambda n: (0, n))},
        limit=SMALL,
    )
    send, *all_spectra = lax.optimization_barrier((send, *all_spectra))
    arrived, local_sum = lax.optimization_barrier((exchange(send), sum_over(local_sum, "dp")))
    (grad_spectra,) = call(
        functools.partial(spectra_kernel, mode_scale, owned, lanes),
        "grad_spectra",
        (arrived, by_mode, rows),
        (shape((owned * lanes, both)),),
        limit=SMALL,
    )
    near = gather_near(grad_spectra, "dp")
    carried = channels * channels * tiles // inverse
    (send,) = call(
        functools.partial(backward_kernel, samples, tiles),
        "mix_backward",
        (grad_spectra, back_rows, local_sum, flat_weight),
        (shape((inverse, owned * lanes + carried)),),
        [
            pltpu.VMEM((owned * lanes, both), BF16),
            pltpu.VMEM((owned * lanes, both), BF16),
            pltpu.VMEM((owned, 2 * samples, channels * ROWS, both), F32),
            *weight_scratch,
            *early(grad_spectra, back_rows, local_sum),
            pltpu.VMEM((inverse, owned * lanes + carried), BF16),
            pltpu.SemaphoreType.DMA((owned,)),
        ],
        grid=(owned,),
        blocks={n: in_place for n in range(4)},
        out_blocks={0: in_place},
    )
    send, near = lax.optimization_barrier((send, near))
    send, *all_grads = lax.optimization_barrier((send, *gather_far(near, "dp")))
    arrived = exchange(send)

    groups = lax.axis_size("dp")
    total = groups * samples
    per_mode = pl.BlockSpec((lanes, both), lambda q: (q, 0))
    (mode_grad,) = call(
        functools.partial(outer_kernel, samples, groups),
        "mode_grad",
        (*all_spectra, *all_grads),
        (shape(flat_weight.shape, F32),),
        [pltpu.VMEM((total, channels, both), F32)] * 2 + [pltpu.VMEM((total, channels, both), BF16)],
        grid=(owned,),
        blocks={n: per_mode for n in range(2 * groups)},
        out_blocks={0: weight_block},
    )
    arrived, mode_grad = lax.optimization_barrier((arrived, mode_grad))

    input_grad, local_grad = call(
        functools.partial(final_kernel, spec_scale, tiles),
        "final",
        (arrived, by_height, back_cols, backward_mix, gate_rows, by_channel),
        (shape((pixel_rows, width)), shape((channels, channels), F32)),
        [pltpu.VMEM((th, lanes, width), BF16)],
        limit=SMALL,
    )
    return (input_grad.reshape(inputs.shape), mode_grad.reshape(mode_weight.shape), local_grad)


def solution(mesh):
    return jax.shard_map(
        local,
        mesh=mesh,
        in_specs=(
            P("dp", None, "tile", None),
            P("dp", None, "tile", None),
            P("tile", None, None, None),
            P(),
        ),
        out_specs=(P("dp", None, "tile", None), P("tile", None, None, None), P()),
        check_vma=False,
    )
```
